32 devices in a mesh: items: 4 (over y, core), rows: 8 (over z, x).
Axes of the slice: x: 2, y: 2, z: 4, core: 2. Of those that a mesh axis runs over, the one named last changes fastest.
Arguments:
- hidden_in: float32 [4, 1024, 1536], P('items', 'rows'), may hold values from -6 to 6
- cotangent: float32 [4, 1024, 1536], P('items', 'rows'), may hold values from -6 to 6
- text_states: bfloat16 [4, 2, 128, 4096], P('items', None, 'rows'), may hold values from -6 to 6
- time_embed: bfloat16 [4, 2, 1024], P('items'), may hold values from -6 to 6
- live_rows: int32 [4, 8, 2], P('items', 'rows'), may hold values from 1 to 2, as said below
- frame_rows: int32 [4, 2], P('items'), may hold values from 4 to 16
- text_len: int32 [4, 2], P('items'), may hold values from 64 to 128
- w_qkv: bfloat16 [1536, 4608], P('rows'), may hold values from -0.15625 to 0.15625
- w_out: bfloat16 [1536, 1536], P('rows'), may hold values from -0.15625 to 0.15625
- w_text: bfloat16 [4096, 3072], P('rows'), may hold values from -0.09375 to 0.09375
- w_gu: bfloat16 [1536, 8192], P('rows'), may hold values from -0.15625 to 0.15625
- w_down: bfloat16 [4096, 1536], P('rows'), may hold values from -0.09375 to 0.09375
- w_ada: bfloat16 [1024, 6144], P('rows'), may hold values from -0.1875 to 0.1875
- gains: float32 [7, 1536], replicated, may hold values from 0.1 to 1.9
- cross_gate: float32 [24], replicated, may hold values from -1.5 to 1.5
- ada_bias: float32 [6144], replicated, may hold values from -3 to 3
- text_gain: float32 [4096], replicated, may hold values from 0.1 to 1.9
Outputs:
- output: float32 [4, 1024, 1536], P('items', 'rows')
- grad_x: float32 [4, 1024, 1536], P('items', 'rows')
- grad_w_qkv: float32 [1536, 4608], P('rows')
- grad_w_out: float32 [1536, 1536], P('rows')
- grad_w_text: float32 [4096, 3072], P('rows')
- grad_w_gu: float32 [1536, 8192], P('rows')
- grad_w_down: float32 [4096, 1536], P('rows')
- grad_w_ada: float32 [1024, 6144], P('rows')
- grad_gains: float32 [7, 1536], replicated
- grad_cross_gate: float32 [24], replicated
- grad_ada_bias: float32 [6144], replicated
- grad_text_gain: float32 [4096], replicated
The draws below stay inside these ranges and needn't reach their ends.
Inputs may be any that keep to these rules, and one draw needn't show every extreme that they name: The first live_rows[g, r, s] row slots of item s on device r hold its rows, in order of the devices; every item has at least one live row on every device of its group.
All inputs are finite; a program needn't handle non-finite values.
Results may differ from the reference program's by a relative error of at most 0.023.
Values may be sent and summed in bfloat16 or wider, within the bound.
A program may use at most 384 MiB of HBM per device.

```python
import jax
import jax.numpy as jnp
from jax import lax

D = 1536
HEADS = 24
HEAD = 64
FF = 4096
TD = 4096
TE = 1024
COLS = 32
CAP = 2
IG = 2
TEXT = 128
SLOTS = 128
N_ITEMS = 4
N_ROWS = 8


def draw_live_rows(key, part):
    key = jax.random.fold_in(key, 11)
    first_key, second_key = jax.random.split(key)
    base_rows = jax.random.randint(first_key, (N_ITEMS, N_ROWS, IG), 1, CAP + 1)
    full_rank = jax.random.randint(second_key, (N_ITEMS, 1, IG), 0, N_ROWS)
    ranks = jnp.arange(N_ROWS)[None, :, None]
    return jnp.where(ranks == full_rank, CAP, base_rows).astype(jnp.int32)


def draw_text_len(key, part):
    key = jax.random.fold_in(key, 23)
    first_key, second_key = jax.random.split(key)
    base_len = jax.random.randint(first_key, (N_ITEMS, IG), TEXT // 2, TEXT + 1)
    full_item = jax.random.randint(second_key, (N_ITEMS, 1), 0, IG)
    places = jnp.arange(IG)[None, :]
    return jnp.where(places == full_item, TEXT, base_len).astype(jnp.int32)


def touch_ends(drawn, key, least, top_value):
    longest = drawn.shape.index(max(drawn.shape))
    spots = []
    for shift in (0, 1):
        where = [jax.random.randint(jax.random.fold_in(key, axis), (), 0, length) for axis, length in enumerate(drawn.shape)]
        where[longest] = (where[longest] + shift) % drawn.shape[longest]
        spots.append(tuple(where))
    return drawn.at[spots[0]].set(least).at[spots[1]].set(top_value)


def levels(key, extent, shards, low, high):
    level = 1.0
    for dim, blocks in shards:
        draws = jax.random.uniform(jax.random.fold_in(jax.random.fold_in(key, 6), dim), (blocks,), jnp.float32, low / len(shards), high / len(shards))
        level = level * jnp.repeat(jnp.exp(draws), extent[dim] // blocks).reshape((-1,) + (1,) * (len(extent) - 1 - dim))
    return level


def bell_draw(rng, shape, deviation, bound, pieces=(), kind=jnp.bfloat16):
    gain = levels(rng, shape, pieces, -0.22, 0.18) if pieces else 1.0
    values = jax.random.normal(rng, shape, jnp.float32) * deviation * gain
    return jnp.minimum(jnp.maximum(values, -bound), bound).astype(kind)


def setup_inputs(seed: int = 0) -> dict:
    seeds = jax.random.split(jax.random.key(seed), 18)
    return {
        "hidden_in": bell_draw(seeds[0], (N_ITEMS, N_ROWS * SLOTS, D), 1.0, 6.0, ((0, 4), (1, 8)), jnp.float32),
        "cotangent": bell_draw(seeds[1], (N_ITEMS, N_ROWS * SLOTS, D), 1.0, 6.0, ((0, 4), (1, 8)), jnp.float32),
        "text_states": bell_draw(seeds[2], (N_ITEMS, IG, TEXT, TD), 1.0, 6.0, ((0, 4), (2, 8))),
        "time_embed": bell_draw(seeds[3], (N_ITEMS, IG, TE), 1.0, 6.0, ((0, 4),)),
        "live_rows": draw_live_rows(jax.random.fold_in(seeds[17], 71), 0),
        "frame_rows": touch_ends(jax.random.randint(seeds[5], (N_ITEMS, IG), 2 * CAP, 8 * CAP + 1), jax.random.fold_in(seeds[5], 1), 2 * CAP, 8 * CAP).astype(jnp.int32),
        "text_len": draw_text_len(jax.random.fold_in(seeds[17], 71), 0),
        "w_qkv": bell_draw(seeds[7], (D, 3 * D), D ** -0.5, 0.15625, ((0, 8),)),
        "w_out": bell_draw(seeds[8], (D, D), D ** -0.5, 0.15625, ((0, 8),)),
        "w_text": bell_draw(seeds[9], (TD, 2 * D), TD ** -0.5, 0.09375, ((0, 8),)),
        "w_gu": bell_draw(seeds[10], (D, 2 * FF), D ** -0.5, 0.15625, ((0, 8),)),
        "w_down": bell_draw(seeds[11], (FF, D), FF ** -0.5, 0.09375, ((0, 8),)),
        "w_ada": bell_draw(seeds[12], (TE, 4 * D), TE ** -0.5, 0.1875, ((0, 8),)),
        "gains": jnp.clip(1.0 + 0.18 * jax.random.normal(seeds[13], (7, D), jnp.float32), 0.1, 1.9),
        "cross_gate": jnp.clip(jax.random.uniform(seeds[14], (HEADS,), jnp.float32, -1.5, 1.5), -1.5, 1.5),
        "ada_bias": bell_draw(seeds[15], (4 * D,), 0.5, 3.0, (), jnp.float32),
        "text_gain": jnp.clip(1.0 + 0.18 * jax.random.normal(seeds[16], (TD,), jnp.float32), 0.1, 1.9),
    }


@jax.custom_vjp
def low(v):
    return lax.optimization_barrier(v.astype(jnp.bfloat16)).astype(jnp.float32)

@jax.custom_vjp
def low_back(v):
    return v

def low_keep(v):
    return (low(v), None)

def low_pass(kept, grad):
    return (grad,)

def back_keep(v):
    return (v, None)

def back_low(kept, grad):
    return (low(grad),)
low.defvjp(low_keep, low_pass)
low_back.defvjp(back_keep, back_low)
epsilon = 1e-06
masked_score = -1e+30
highest = lax.Precision.HIGHEST

def norm_gain(values, scaling):
    return values * lax.rsqrt(lax.optimization_barrier(jnp.mean(values * values, axis=-1, keepdims=True)) + epsilon) * scaling

def matmul_full(left, right):
    return jnp.einsum('...k,kn->...n', left, right, precision=highest)

def freq_rates(number):
    return 10000.0 ** (-jnp.arange(number).astype(jnp.float32) / number)

def rotary_angles(frame_index, frame_row, column, head_size):
    frame_pairs = head_size // 8
    space_pairs = (head_size // 2 - frame_pairs) // 2
    return jnp.concatenate([frame_index.astype(jnp.float32)[..., None] * freq_rates(frame_pairs), frame_row.astype(jnp.float32)[..., None] * freq_rates(space_pairs), column.astype(jnp.float32)[..., None] * freq_rates(space_pairs)], axis=-1)

def rotate(values, cos_table, sin_table, head_count):
    shaped = values.reshape(values.shape[:-1] + (head_count, values.shape[-1] // head_count))
    half_size = shaped.shape[-1] // 2
    upper_half = shaped[..., :half_size]
    lower_half = shaped[..., half_size:]
    cos_heads = cos_table[..., None, :]
    sin_heads = sin_table[..., None, :]
    turned = jnp.concatenate([upper_half * cos_heads - lower_half * sin_heads, upper_half * sin_heads + lower_half * cos_heads], axis=-1)
    return turned.reshape(values.shape)

def softmax_rows(scores, mask):
    scores = jnp.where(mask, scores, masked_score)
    row_max = lax.optimization_barrier(jnp.max(scores, axis=-1, keepdims=True))
    exp_terms = jnp.exp(scores - row_max)
    return exp_terms / lax.optimization_barrier(jnp.sum(exp_terms, axis=-1, keepdims=True))

def reference(hidden_in, cotangent, text_states, time_embed, live_rows, frame_rows, text_len, w_qkv, w_out, w_text, w_gu, w_down, w_ada, gains, cross_gate, ada_bias, text_gain):
    single = jnp.float32
    groups = hidden_in.shape[0]
    item_slots = CAP * COLS
    seq_len = N_ROWS * item_slots
    block_rows = min(512, seq_len)

    def to_seq(array):
        shaped = array.reshape((groups, N_ROWS, IG, item_slots) + array.shape[2:])
        return jnp.swapaxes(shaped, 1, 2).reshape((groups, IG, seq_len) + array.shape[2:])

    def from_seq(array):
        shaped = array.reshape((groups, IG, N_ROWS, item_slots) + array.shape[3:])
        return jnp.swapaxes(shaped, 1, 2).reshape((groups, N_ROWS * IG * item_slots) + array.shape[3:])

    def grid_seq(array):
        return jnp.swapaxes(array, 1, 2).reshape(groups, IG, seq_len)
    slot_row = (jnp.arange(item_slots) // COLS).astype(jnp.int32)
    column = (jnp.arange(item_slots) % COLS).astype(jnp.int32)
    rows_below = jnp.cumsum(live_rows, axis=1, dtype=jnp.int32) - live_rows
    row_index = rows_below[..., None] + slot_row
    heights = frame_rows[:, None, :, None]
    frame_index = row_index // heights
    frame_row = row_index % heights
    columns = jnp.broadcast_to(column, row_index.shape)
    live_grid = slot_row < live_rows[..., None]
    key_live = grid_seq(live_grid)
    live_seq = key_live.astype(single)
    angles = rotary_angles(grid_seq(frame_index), grid_seq(frame_row), grid_seq(columns), HEAD)
    cos_table = jnp.cos(angles)
    sin_table = jnp.sin(angles)
    text_live = jnp.arange(TEXT).astype(jnp.int32)[None, None, :] < text_len[..., None]

    def self_attention(queries, keys_low, values_low):
        seq_count = groups * IG
        query_blocks = queries.reshape(seq_count, seq_len // block_rows, block_rows, HEADS, HEAD)
        key_seqs = keys_low.reshape(seq_count, seq_len, HEADS, HEAD)
        value_seqs = values_low.reshape(seq_count, seq_len, HEADS, HEAD)
        mask_seqs = key_live.reshape(seq_count, seq_len)

        def one_sequence(packed):
            query_seq, key_seq, value_seq, mask_seq = packed

            def one_block(query_block):
                scores = low_back(jnp.einsum('phe,khe->hpk', query_block, key_seq, precision=highest) * HEAD ** (-0.5))
                attn_probs = softmax_rows(scores, mask_seq[None, None, :])
                return jnp.einsum('hpk,khe->phe', low(attn_probs), value_seq, precision=highest)
            return lax.map(jax.checkpoint(one_block), query_seq)
        attended = lax.map(jax.checkpoint(one_sequence), (query_blocks, key_seqs, value_seqs, mask_seqs))
        return attended.reshape(groups, IG, seq_len, D)

    def cross_attention(queries, text_keys, text_values):
        query_heads = queries.reshape(groups, IG, seq_len, HEADS, HEAD)
        key_heads = text_keys.reshape(groups, IG, TEXT, HEADS, HEAD)
        value_heads = text_values.reshape(groups, IG, TEXT, HEADS, HEAD)
        scores = low_back(jnp.einsum('gsphe,gskhe->gshpk', query_heads, key_heads, precision=highest) * HEAD ** (-0.5))
        attn_probs = softmax_rows(scores, text_live[:, :, None, None, :])
        mixed = jnp.einsum('gshpk,gskhe->gsphe', low(attn_probs), value_heads, precision=highest)
        return mixed.reshape(groups, IG, seq_len, D)

    def forward(hidden_full, qkv_full, out_full, text_full, gu_full, down_full, ada_full, gains_full, gate_full, bias_full, tgain_full):
        states = to_seq(hidden_full)
        time_silu = low(jax.nn.silu(time_embed.astype(single)))
        modulation = matmul_full(time_silu, ada_full) + bias_full
        scale_attn = modulation[:, :, None, 0:D]
        gate_attn = modulation[:, :, None, D:2 * D]
        scale_ffn = modulation[:, :, None, 2 * D:3 * D]
        gate_ffn = modulation[:, :, None, 3 * D:]
        attn_in = low(norm_gain(states, gains_full[0]) * (1.0 + scale_attn))
        qkv_proj = low_back(matmul_full(attn_in, qkv_full))
        queries = low(rotate(norm_gain(qkv_proj[..., 0:D], gains_full[1]), cos_table, sin_table, HEADS))
        keys_low = low(rotate(norm_gain(qkv_proj[..., D:2 * D], gains_full[2]), cos_table, sin_table, HEADS))
        values_low = low(qkv_proj[..., 2 * D:])
        text_norm = low(norm_gain(text_states.astype(single), tgain_full))
        text_proj = low_back(matmul_full(text_norm, text_full))
        text_keys = low(norm_gain(text_proj[..., 0:D], gains_full[6]))
        text_values = low(text_proj[..., D:])
        self_out = low_back(self_attention(queries, keys_low, values_low))
        cross_out = low_back(cross_attention(queries, text_keys, text_values))
        head_gate = jnp.repeat(jnp.tanh(gate_full), HEAD)
        combined = low(self_out + head_gate * cross_out)
        projected = low_back(matmul_full(combined, out_full))
        middle = states + jnp.tanh(gate_attn) * norm_gain(projected, gains_full[3])
        ffn_in = low(norm_gain(middle, gains_full[4]) * (1.0 + scale_ffn))
        gate_up = low_back(matmul_full(ffn_in, gu_full))
        inner_act = low(jax.nn.silu(gate_up[..., 0:FF]) * gate_up[..., FF:])
        ffn_out = low_back(matmul_full(inner_act, down_full))
        result = middle + jnp.tanh(gate_ffn) * norm_gain(ffn_out, gains_full[5])
        return from_seq(live_seq[..., None] * result)
    primals = (hidden_in, w_qkv.astype(single), w_out.astype(single), w_text.astype(single), w_gu.astype(single), w_down.astype(single), w_ada.astype(single), gains, cross_gate, ada_bias, text_gain)
    result, pullback = jax.vjp(forward, *primals)
    grads = pullback(cotangent)
    return (result, grads[0], grads[1], grads[2], grads[3], grads[4], grads[5], grads[6], grads[7], grads[8], grads[9], grads[10])
```

```python
import jax
import jax.numpy as jnp
from jax import lax
from jax.sharding import PartitionSpec as P

COLS = 32


epsilon = 1e-06
masked_score = -1e30
group_heads = 4


def norm_gain(values, scaling):
    return values * lax.rsqrt(jnp.mean(values * values, axis=-1, keepdims=True) + epsilon) * scaling


def pre_norm(values, shift_scale, scaling):
    return norm_gain(values, scaling) * (1.0 + shift_scale)


def post_add(residual, branch, gate_in, scaling):
    return residual + jnp.tanh(gate_in) * norm_gain(branch, scaling)


def swiglu(gate_up):
    middle_col = gate_up.shape[-1] // 2
    return jax.nn.silu(gate_up[..., :middle_col]) * gate_up[..., middle_col:]


def freq_rates(number):
    return 10000.0 ** (-jnp.arange(number).astype(jnp.float32) / number)


def rotary_angles(frame_index, frame_row, column, head_size):
    frame_pairs = head_size // 8
    space_pairs = (head_size // 2 - frame_pairs) // 2
    return jnp.concatenate(
        [
            frame_index.astype(jnp.float32)[..., None] * freq_rates(frame_pairs),
            frame_row.astype(jnp.float32)[..., None] * freq_rates(space_pairs),
            column.astype(jnp.float32)[..., None] * freq_rates(space_pairs),
        ],
        axis=-1,
    )


def rotate(values, cos_table, sin_table, head_count):
    shaped = values.reshape(values.shape[:-1] + (head_count, values.shape[-1] // head_count))
    half_size = shaped.shape[-1] // 2
    upper_half = shaped[..., :half_size]
    lower_half = shaped[..., half_size:]
    cos_heads = cos_table[..., None, :]
    sin_heads = sin_table[..., None, :]
    turned = jnp.concatenate(
        [
            upper_half * cos_heads - lower_half * sin_heads,
            upper_half * sin_heads + lower_half * cos_heads,
        ],
        axis=-1,
    )
    return turned.reshape(values.shape)


def text_split(projected, key_gain):
    half_cols = projected.shape[-1] // 2
    return (norm_gain(projected[..., :half_cols], key_gain), projected[..., half_cols:])


def gathered_plan(
    hidden_in,
    cotangent,
    text_states,
    time_embed,
    live_rows,
    frame_rows,
    text_len,
    w_qkv,
    w_out,
    w_text,
    w_gu,
    w_down,
    w_ada,
    gains,
    cross_gate,
    ada_bias,
    text_gain,
):
    single = jnp.float32
    narrow = jnp.bfloat16
    model_width = hidden_in.shape[2]
    head_count = cross_gate.shape[0]
    head_size = model_width // head_count
    score_scale = head_size ** (-0.5)
    item_count = time_embed.shape[1]
    item_slots = hidden_in.shape[1] // item_count
    row_devices = lax.axis_size("rows")
    seq_len = row_devices * item_slots
    text_local = text_states.shape[2]
    text_all = text_local * row_devices
    text_width = text_states.shape[3]
    group_span = group_heads * head_size
    block_count = head_count // group_heads
    token_count = item_count * item_slots

    def weight_term(left, right, accuracy):
        return jnp.einsum(
            "tk,tn->kn", left, right, precision=accuracy, preferred_element_type=single
        )

    def reduce_term(term):
        return lax.psum_scatter(
            term.astype(jnp.bfloat16), "rows", scatter_dimension=0, tiled=True
        ).astype(jnp.float32)

    full_qkv, full_out, full_text, full_gu, full_down, full_ada = (
        lax.all_gather(w_qkv, "rows", axis=0, tiled=True),
        lax.all_gather(w_out, "rows", axis=0, tiled=True),
        lax.all_gather(w_text, "rows", axis=0, tiled=True),
        lax.all_gather(w_gu, "rows", axis=0, tiled=True),
        lax.all_gather(w_down, "rows", axis=0, tiled=True),
        lax.all_gather(w_ada, "rows", axis=0, tiled=True),
    )
    counts_here = live_rows[0]
    every_count = lax.all_gather(counts_here, "rows", axis=0, tiled=True)
    device_place = lax.axis_index("rows")
    ranks = jnp.arange(row_devices)
    rows_below = jnp.sum(jnp.where(ranks[:, None] < device_place, every_count, 0), axis=0)
    slot_row = jnp.arange(item_slots) // COLS
    column = jnp.arange(item_slots) % COLS
    row_index = rows_below[:, None] + slot_row[None, :]
    heights = frame_rows[0][:, None]
    frame_index = row_index // heights
    frame_row = row_index % heights
    live_mask = (slot_row[None, :] < counts_here[0][:, None]).astype(single)
    key_live = (slot_row[None, None, :] < jnp.transpose(every_count)[:, :, None]).reshape(
        item_count, seq_len
    )
    text_live = jnp.arange(text_all)[None, :] < text_len[0][:, None]
    angles = rotary_angles(
        frame_index, frame_row, jnp.broadcast_to(column, row_index.shape), head_size
    )
    cos_table = jnp.cos(angles)
    sin_table = jnp.sin(angles)

    def qkv_split(projected, gain_query, gain_key):
        queries = rotate(
            norm_gain(projected[..., :model_width], gain_query), cos_table, sin_table, head_count
        )
        keys_here = rotate(
            norm_gain(projected[..., model_width : 2 * model_width], gain_key),
            cos_table,
            sin_table,
            head_count,
        )
        return (queries, keys_here, projected[..., 2 * model_width :])

    states = hidden_in[0].reshape(item_count, item_slots, model_width)
    time_silu = jax.nn.silu(time_embed[0].astype(single)).astype(narrow)
    modulation = jnp.dot(time_silu, full_ada, preferred_element_type=single) + ada_bias
    scale_attn = modulation[:, None, 0:model_width]
    gate_attn = modulation[:, None, model_width : 2 * model_width]
    scale_ffn = modulation[:, None, 2 * model_width : 3 * model_width]
    gate_ffn = modulation[:, None, 3 * model_width :]
    attn_in = (
        pre_norm(states, scale_attn, gains[0]).astype(narrow).reshape(token_count, model_width)
    )
    qkv_proj = jnp.dot(attn_in, full_qkv, preferred_element_type=single).reshape(
        item_count, item_slots, 3 * model_width
    )
    query_full, key_full, value_full = qkv_split(qkv_proj, gains[1], gains[2])
    query_low = query_full.astype(narrow)
    key_low = key_full.astype(narrow)
    value_low = value_full.astype(narrow)
    text_float = text_states[0].astype(single)
    text_norm = norm_gain(text_float, text_gain).astype(narrow)
    text_proj = jnp.einsum("ctd,dn->ctn", text_norm, full_text, preferred_element_type=single)
    tkey_full, tval_full = text_split(text_proj, gains[6])
    key_all, value_all, tkey_all, tval_all = (
        lax.all_gather(key_low, "rows", axis=1, tiled=True),
        lax.all_gather(value_low, "rows", axis=1, tiled=True),
        lax.all_gather(tkey_full.astype(narrow), "rows", axis=1, tiled=True),
        lax.all_gather(tval_full.astype(narrow), "rows", axis=1, tiled=True),
    )

    def block_slices(block_index, key_source, value_source):
        offset = block_index * group_span
        query_part = lax.dynamic_slice_in_dim(query_low, offset, group_span, 2).reshape(
            item_count, item_slots, group_heads, head_size
        )
        key_part = lax.dynamic_slice_in_dim(key_source, offset, group_span, 2).reshape(
            item_count, seq_len, group_heads, head_size
        )
        value_part = lax.dynamic_slice_in_dim(value_source, offset, group_span, 2).reshape(
            item_count, seq_len, group_heads, head_size
        )
        return (query_part, key_part, value_part)

    def self_step(carry, block_index):
        query_part, key_part, value_part = block_slices(block_index, key_all, value_all)
        scores = (
            jnp.einsum("iphe,ikhe->ihpk", query_part, key_part, preferred_element_type=single)
            * score_scale
        )
        scores = jnp.where(key_live[:, None, None, :], scores, masked_score)
        row_max = jnp.max(scores, axis=-1, keepdims=True)
        exp_terms = jnp.exp(scores - row_max)
        exp_total = jnp.sum(exp_terms, axis=-1, keepdims=True)
        probs_low = (exp_terms / exp_total).astype(narrow)
        attended = jnp.einsum(
            "ihpk,ikhe->iphe", probs_low, value_part, preferred_element_type=single
        )
        return (
            carry,
            (
                attended.reshape(item_count, item_slots, group_span),
                (row_max + jnp.log(exp_total))[..., 0],
            ),
        )

    _, (self_parts, log_totals) = lax.scan(
        self_step, jnp.zeros((), single), jnp.arange(block_count)
    )

    def heads_last(parts):
        return jnp.transpose(parts, (1, 2, 0, 3)).reshape(item_count, item_slots, model_width)

    self_out = heads_last(self_parts)
    query_heads = query_low.reshape(item_count, item_slots, head_count, head_size)
    tkey_heads = tkey_all.reshape(item_count, text_all, head_count, head_size)
    tval_heads = tval_all.reshape(item_count, text_all, head_count, head_size)
    cross_scores = (
        jnp.einsum("iphe,ikhe->ihpk", query_heads, tkey_heads, preferred_element_type=single)
        * score_scale
    )
    cross_scores = jnp.where(text_live[:, None, None, :], cross_scores, masked_score)
    cross_max = jnp.max(cross_scores, axis=-1, keepdims=True)
    cross_exp = jnp.exp(cross_scores - cross_max)
    cross_probs = cross_exp / jnp.sum(cross_exp, axis=-1, keepdims=True)
    cross_low = cross_probs.astype(narrow)
    cross_out = jnp.einsum("ihpk,ikhe->iphe", cross_low, tval_heads, preferred_element_type=single)
    tanh_gate = jnp.tanh(cross_gate)
    combined = (
        self_out.reshape(item_count, item_slots, head_count, head_size)
        + tanh_gate[:, None] * cross_out
    )
    combined = combined.reshape(token_count, model_width).astype(narrow)
    projected = jnp.dot(combined, full_out, preferred_element_type=single).reshape(
        item_count, item_slots, model_width
    )
    middle = post_add(states, projected, gate_attn, gains[3])
    ffn_in = pre_norm(middle, scale_ffn, gains[4]).astype(narrow).reshape(token_count, model_width)
    gate_up = jnp.dot(ffn_in, full_gu, preferred_element_type=single)
    inner_act = swiglu(gate_up).astype(narrow)
    ffn_out = jnp.dot(inner_act, full_down, preferred_element_type=single).reshape(
        item_count, item_slots, model_width
    )
    result = post_add(middle, ffn_out, gate_ffn, gains[5])
    output = (live_mask[..., None] * result).reshape(1, token_count, model_width)
    grad_result = live_mask[..., None] * cotangent[0].reshape(item_count, item_slots, model_width)
    _, back_ffn_out = jax.vjp(post_add, middle, ffn_out, gate_ffn, gains[5])
    grad_middle, grad_ffn_out, grad_gate_ffn, grad_gain_five = back_ffn_out(grad_result)
    ffn_low = grad_ffn_out.astype(narrow).reshape(token_count, model_width)
    shard_down = reduce_term(weight_term(inner_act, ffn_low, None))
    grad_inner = jnp.einsum("tn,kn->tk", ffn_low, full_down, preferred_element_type=single)
    _, back_glu = jax.vjp(swiglu, gate_up)
    gate_up_low = back_glu(grad_inner)[0].astype(narrow)
    shard_gu = reduce_term(weight_term(ffn_in, gate_up_low, None))
    grad_ffn_in = jnp.einsum("tn,kn->tk", gate_up_low, full_gu, preferred_element_type=single)
    _, back_ffn_in = jax.vjp(pre_norm, middle, scale_ffn, gains[4])
    part_middle, grad_scale_ffn, grad_gain_four = back_ffn_in(
        grad_ffn_in.reshape(item_count, item_slots, model_width)
    )
    grad_middle = grad_middle + part_middle
    _, back_attn_out = jax.vjp(post_add, states, projected, gate_attn, gains[3])
    grad_hidden, grad_projected, grad_gate_attn, grad_gain_three = back_attn_out(grad_middle)
    projected_low = grad_projected.astype(narrow).reshape(token_count, model_width)
    shard_out = reduce_term(weight_term(combined, projected_low, None))
    grad_combined = jnp.einsum("tn,kn->tk", projected_low, full_out, preferred_element_type=single)
    grad_combined = grad_combined.reshape(item_count, item_slots, head_count, head_size)
    self_low = grad_combined.reshape(item_count, item_slots, model_width).astype(narrow)
    cross_grad_low = (tanh_gate[:, None] * grad_combined).astype(narrow)
    grad_cross_gate = (1.0 - tanh_gate * tanh_gate) * jnp.sum(
        grad_combined * cross_out, axis=(0, 1, 3)
    )

    def self_back(carry, packed):
        block_index, log_total = packed
        query_part, key_part, value_part = block_slices(block_index, key_all, value_all)
        offset = block_index * group_span
        grad_part = lax.dynamic_slice_in_dim(self_low, offset, group_span, 2).reshape(
            item_count, item_slots, group_heads, head_size
        )
        scores = (
            jnp.einsum("iphe,ikhe->ihpk", query_part, key_part, preferred_element_type=single)
            * score_scale
        )
        scores = jnp.where(key_live[:, None, None, :], scores, masked_score)
        attn_probs = jnp.exp(scores - log_total[..., None])
        grad_probs = jnp.einsum(
            "iphe,ikhe->ihpk", grad_part, value_part, preferred_element_type=single
        )
        row_inner = jnp.sum(attn_probs * grad_probs, axis=-1, keepdims=True)
        score_low = (attn_probs * (grad_probs - row_inner)).astype(narrow)
        grad_query = (
            jnp.einsum("ihpk,ikhe->iphe", score_low, key_part, preferred_element_type=single)
            * score_scale
        )
        grad_value = jnp.einsum(
            "ihpk,iphe->ikhe", attn_probs.astype(narrow), grad_part, preferred_element_type=single
        )
        grad_key = (
            jnp.einsum("ihpk,iphe->ikhe", score_low, query_part, preferred_element_type=single)
            * score_scale
        )
        owned_key, owned_value = (
            lax.psum_scatter(
                grad_key.reshape(item_count, seq_len, group_span).astype(jnp.bfloat16),
                "rows",
                scatter_dimension=1,
                tiled=True,
            ).astype(jnp.float32),
            lax.psum_scatter(
                grad_value.reshape(item_count, seq_len, group_span).astype(jnp.bfloat16),
                "rows",
                scatter_dimension=1,
                tiled=True,
            ).astype(jnp.float32),
        )
        return (
            carry,
            (grad_query.reshape(item_count, item_slots, group_span), owned_key, owned_value),
        )

    _, (query_parts, key_parts, value_parts) = lax.scan(
        self_back, jnp.zeros((), single), (jnp.arange(block_count), log_totals)
    )
    cross_grad_probs = jnp.einsum(
        "iphe,ikhe->ihpk", cross_grad_low, tval_heads, preferred_element_type=single
    )
    cross_inner = jnp.sum(cross_probs * cross_grad_probs, axis=-1, keepdims=True)
    cross_score_low = (cross_probs * (cross_grad_probs - cross_inner)).astype(narrow)
    grad_query_cross = (
        jnp.einsum("ihpk,ikhe->iphe", cross_score_low, tkey_heads, preferred_element_type=single)
        * score_scale
    )
    grad_text_key = (
        jnp.einsum("ihpk,iphe->ikhe", cross_score_low, query_heads, preferred_element_type=single)
        * score_scale
    )
    grad_text_value = jnp.einsum(
        "ihpk,iphe->ikhe", cross_low, cross_grad_low, preferred_element_type=single
    )
    owned_tkey, owned_tval = (
        lax.psum_scatter(
            grad_text_key.reshape(item_count, text_all, model_width).astype(jnp.bfloat16),
            "rows",
            scatter_dimension=1,
            tiled=True,
        ).astype(jnp.float32),
        lax.psum_scatter(
            grad_text_value.reshape(item_count, text_all, model_width).astype(jnp.bfloat16),
            "rows",
            scatter_dimension=1,
            tiled=True,
        ).astype(jnp.float32),
    )
    grad_query_all = heads_last(query_parts) + grad_query_cross.reshape(
        item_count, item_slots, model_width
    )
    _, back_qkv = jax.vjp(qkv_split, qkv_proj, gains[1], gains[2])
    grad_qkv, grad_gain_one, grad_gain_two = back_qkv(
        (grad_query_all, heads_last(key_parts), heads_last(value_parts))
    )
    qkv_low = grad_qkv.astype(narrow).reshape(token_count, 3 * model_width)
    shard_qkv = reduce_term(weight_term(attn_in, qkv_low, None))
    grad_attn_in = jnp.einsum("tn,kn->tk", qkv_low, full_qkv, preferred_element_type=single)
    _, back_attn_in = jax.vjp(pre_norm, states, scale_attn, gains[0])
    part_states, grad_scale_attn, grad_gain_zero = back_attn_in(
        grad_attn_in.reshape(item_count, item_slots, model_width)
    )
    grad_x = (grad_hidden + part_states).reshape(1, token_count, model_width)
    _, back_text = jax.vjp(text_split, text_proj, gains[6])
    grad_text_proj, grad_gain_six = back_text((owned_tkey, owned_tval))
    text_low = grad_text_proj.astype(narrow).reshape(item_count * text_local, 2 * model_width)
    shard_text = reduce_term(
        weight_term(text_norm.reshape(item_count * text_local, text_width), text_low, None)
    )
    grad_text_norm = jnp.einsum("tn,kn->tk", text_low, full_text, preferred_element_type=single)
    _, back_text_norm = jax.vjp(norm_gain, text_float, text_gain)
    grad_text_gain = back_text_norm(grad_text_norm.reshape(text_float.shape))[1]
    grad_modulation = jnp.concatenate(
        [grad_scale_attn, grad_gate_attn, grad_scale_ffn, grad_gate_ffn], axis=-1
    )[:, 0, :]
    shard_ada = reduce_term(
        weight_term(time_silu.astype(single), grad_modulation, lax.Precision.HIGHEST)
    )
    grad_ada_bias = jnp.sum(grad_modulation, axis=0)
    grad_gains = jnp.stack(
        [
            grad_gain_zero,
            grad_gain_one,
            grad_gain_two,
            grad_gain_three,
            grad_gain_four,
            grad_gain_five,
            grad_gain_six,
        ],
        axis=0,
    )
    final_qkv, final_out, final_text, final_gu, final_down, final_ada = (
        lax.psum(shard_qkv.astype(jnp.bfloat16), "items").astype(jnp.float32),
        lax.psum(shard_out.astype(jnp.bfloat16), "items").astype(jnp.float32),
        lax.psum(shard_text.astype(jnp.bfloat16), "items").astype(jnp.float32),
        lax.psum(shard_gu.astype(jnp.bfloat16), "items").astype(jnp.float32),
        lax.psum(shard_down.astype(jnp.bfloat16), "items").astype(jnp.float32),
        lax.psum(shard_ada.astype(jnp.bfloat16), "items").astype(jnp.float32),
    )
    total_gains, total_gate, total_bias, total_text_gain = lax.psum(
        (grad_gains, grad_cross_gate, grad_ada_bias, grad_text_gain), ("items", "rows")
    )
    return (
        output,
        grad_x,
        final_qkv,
        final_out,
        final_text,
        final_gu,
        final_down,
        final_ada,
        total_gains,
        total_gate,
        total_bias,
        total_text_gain,
    )


def norm_parts(values):
    inverse = lax.rsqrt(jnp.mean(values * values, axis=-1, keepdims=True) + epsilon)
    return values * inverse, inverse


def norm_back(unit, inverse, scaled_grad):
    return inverse * (scaled_grad - unit * jnp.mean(scaled_grad * unit, axis=-1, keepdims=True))


def gather_tokens(block):
    return lax.all_gather(block, "rows", axis=1, tiled=True)


def scatter_tokens(partial):
    return lax.psum_scatter(
        partial.astype(jnp.bfloat16), "rows", scatter_dimension=1, tiled=True
    ).astype(jnp.float32)


def columns_here(weight, pieces):
    ranks = lax.axis_size("rows")
    depth, width = weight.shape
    shaped = weight.reshape(depth, pieces, ranks, width // (pieces * ranks))
    moved = lax.all_to_all(shaped, "rows", split_axis=2, concat_axis=0, tiled=True)
    return moved.reshape(depth * ranks, width // ranks)


def rows_here(grad, pieces):
    ranks = lax.axis_size("rows")
    depth, width = grad.shape
    low = grad.astype(jnp.bfloat16).reshape(depth, pieces, 1, width // pieces)
    moved = lax.all_to_all(low, "rows", split_axis=0, concat_axis=2, tiled=True)
    return moved.reshape(depth // ranks, width * ranks)


def head_parallel_plan(
    hidden_in,
    cotangent,
    text_states,
    time_embed,
    live_rows,
    frame_rows,
    text_len,
    w_qkv,
    w_out,
    w_text,
    w_gu,
    w_down,
    w_ada,
    gains,
    cross_gate,
    ada_bias,
    text_gain,
):
    single = jnp.float32
    narrow = jnp.bfloat16
    ranks = lax.axis_size("rows")
    place = lax.axis_index("rows")
    width = hidden_in.shape[2]
    heads = cross_gate.shape[0]
    head_size = width // heads
    score_scale = head_size ** (-0.5)
    items = time_embed.shape[1]
    slots = hidden_in.shape[1] // items
    row_slots = slots // COLS
    seq_len = ranks * slots
    text_local = text_states.shape[2]
    text_all = text_local * ranks
    text_width = text_states.shape[3]
    span = width // ranks
    heads_here = heads // ranks
    tokens = items * seq_len

    def dot(left, right):
        return jnp.dot(left, right, preferred_element_type=single)

    def dot_back(left, weight):
        return jnp.einsum("tn,kn->tk", left, weight, preferred_element_type=single)

    def weight_grad(left, right):
        return jnp.einsum("tk,tn->kn", left, right, preferred_element_type=single)

    time_silu = jax.nn.silu(time_embed[0].astype(single)).astype(narrow)
    ada_depth = w_ada.shape[0]
    time_here = lax.dynamic_slice_in_dim(time_silu, place * ada_depth, ada_depth, 1)
    modulation = lax.psum(dot(time_here, w_ada), "rows") + ada_bias
    scale_attn = modulation[:, None, 0:width]
    gate_attn = jnp.tanh(modulation[:, None, width : 2 * width])
    scale_ffn = modulation[:, None, 2 * width : 3 * width]
    gate_ffn = jnp.tanh(modulation[:, None, 3 * width :])

    counts_here = live_rows[0]
    counts = lax.all_gather(counts_here, "rows", axis=0, tiled=True)
    below = jnp.cumsum(counts, axis=0) - counts
    slot_row = jnp.arange(row_slots)
    row_index = jnp.transpose(below)[:, :, None] + slot_row
    heights = frame_rows[0][:, None, None]
    frame_pairs = head_size // 8
    space_pairs = (head_size // 2 - frame_pairs) // 2
    row_angles = jnp.concatenate(
        [
            (row_index // heights).astype(single)[..., None] * freq_rates(frame_pairs),
            (row_index % heights).astype(single)[..., None] * freq_rates(space_pairs),
        ],
        axis=-1,
    )
    column_angles = jnp.arange(COLS).astype(single)[:, None] * freq_rates(space_pairs)

    def table(function):
        by_row = function(row_angles)
        by_column = function(column_angles)
        shape = (items, ranks, row_slots, COLS)
        whole = jnp.concatenate(
            [
                jnp.broadcast_to(by_row[:, :, :, None, :], shape + by_row.shape[-1:]),
                jnp.broadcast_to(by_column, shape + by_column.shape[-1:]),
            ],
            axis=-1,
        )
        return whole.reshape(tokens, 1, head_size // 2)

    cos_table = table(jnp.cos)
    sin_table = table(jnp.sin)

    def turn(values, sign):
        shaped = values.reshape(tokens, heads_here, head_size)
        upper = shaped[..., : head_size // 2]
        lower = shaped[..., head_size // 2 :]
        sines = sign * sin_table
        turned = jnp.concatenate(
            [upper * cos_table - lower * sines, upper * sines + lower * cos_table], axis=-1
        )
        return turned.reshape(tokens, width // ranks)

    slot_in_row = jnp.arange(slots) // COLS
    live_mask = (slot_in_row[None, :] < counts_here[0][:, None]).astype(single)[..., None]
    key_live = (slot_in_row < jnp.transpose(counts)[:, :, None]).reshape(items, seq_len)
    text_live = jnp.arange(text_all)[None, :] < text_len[0][:, None]

    def gain_here(index):
        return lax.dynamic_slice_in_dim(gains[index], place * span, span, 0)

    states = hidden_in[0].reshape(items, slots, width)
    unit_in, inverse_in = norm_parts(states)
    norm_in = unit_in * gains[0]
    attn_in = gather_tokens((norm_in * (1.0 + scale_attn)).astype(narrow)).reshape(tokens, width)
    qkv_here = columns_here(w_qkv, 3)
    qkv_proj = dot(attn_in, qkv_here)
    query_proj, key_proj, value_proj = jnp.split(qkv_proj, 3, axis=1)

    text_in = lax.all_gather(text_states[0], "rows", axis=1, tiled=True)
    text_unit, _ = norm_parts(text_in.astype(single).reshape(items * text_all, text_width))
    text_norm = (text_unit * text_gain).astype(narrow)
    text_here = columns_here(w_text, 2)
    text_proj = dot(text_norm, text_here)
    tkey_proj, tval_proj = jnp.split(text_proj, 2, axis=1)

    def squares(values):
        return jnp.sum(values * values, axis=-1)

    totals = lax.psum(
        jnp.concatenate([squares(query_proj), squares(key_proj), squares(tkey_proj)]), "rows"
    )
    inverses = lax.rsqrt(totals / width + epsilon)[:, None]
    inverse_q, inverse_k, inverse_t = (
        inverses[:tokens],
        inverses[tokens : 2 * tokens],
        inverses[2 * tokens :],
    )
    gain_q, gain_k, gain_t = gain_here(1), gain_here(2), gain_here(6)
    unit_q, unit_k, unit_t = query_proj * inverse_q, key_proj * inverse_k, tkey_proj * inverse_t

    def by_head(values):
        return values.reshape(items, -1, heads_here, head_size)

    query = by_head(turn(unit_q * gain_q, 1.0).astype(narrow))
    key = by_head(turn(unit_k * gain_k, 1.0).astype(narrow))
    value = by_head(value_proj.astype(narrow))
    tkey = by_head((unit_t * gain_t).astype(narrow))
    tval = by_head(tval_proj.astype(narrow))

    def soft(keys, mask):
        scores = jnp.einsum("iphe,ikhe->ihpk", query, keys, preferred_element_type=single)
        scores = jnp.where(mask[:, None, None, :], scores * score_scale, masked_score)
        terms = jnp.exp(scores - jnp.max(scores, axis=-1, keepdims=True))
        return terms / jnp.sum(terms, axis=-1, keepdims=True)

    def mix(weights, values):
        return jnp.einsum("ihpk,ikhe->iphe", weights, values, preferred_element_type=single)

    probs = soft(key, key_live)
    self_out = mix(probs.astype(narrow), value)
    cross_probs = soft(tkey, text_live)
    cross_out = mix(cross_probs.astype(narrow), tval)
    gate_here = jnp.tanh(lax.dynamic_slice_in_dim(cross_gate, place * heads_here, heads_here, 0))
    combined = (self_out + gate_here[:, None] * cross_out).astype(narrow).reshape(tokens, span)
    projected = scatter_tokens(dot(combined, w_out).reshape(items, seq_len, width))

    unit_proj, inverse_proj = norm_parts(projected)
    norm_proj = unit_proj * gains[3]
    middle = states + gate_attn * norm_proj
    unit_mid, inverse_mid = norm_parts(middle)
    norm_mid = unit_mid * gains[4]
    ffn_in = gather_tokens((norm_mid * (1.0 + scale_ffn)).astype(narrow)).reshape(tokens, width)
    gu_here = columns_here(w_gu, 2)
    gate_up = dot(ffn_in, gu_here)
    gate_part, up_part = jnp.split(gate_up, 2, axis=1)
    sigmoid = 1.0 / (1.0 + jnp.exp(-gate_part))
    inner_act = (gate_part * sigmoid * up_part).astype(narrow)
    ffn_out = scatter_tokens(dot(inner_act, w_down).reshape(items, seq_len, width))
    unit_ffn, inverse_ffn = norm_parts(ffn_out)
    norm_ffn = unit_ffn * gains[5]
    output = live_mask * (middle + gate_ffn * norm_ffn)

    def over_tokens(values):
        return jnp.sum(values, axis=(0, 1))

    grad_result = live_mask * cotangent[0].reshape(items, slots, width)
    grad_gate_ffn = (1.0 - gate_ffn * gate_ffn)[:, 0] * jnp.sum(grad_result * norm_ffn, axis=1)
    grad_norm = gate_ffn * grad_result
    grad_five = over_tokens(grad_norm * unit_ffn)
    ffn_low = gather_tokens(
        norm_back(unit_ffn, inverse_ffn, grad_norm * gains[5]).astype(narrow)
    ).reshape(tokens, width)
    grad_down = weight_grad(inner_act, ffn_low)
    grad_inner = dot_back(ffn_low, w_down)
    gate_up_low = jnp.concatenate(
        [
            grad_inner * up_part * sigmoid * (1.0 + gate_part * (1.0 - sigmoid)),
            grad_inner * gate_part * sigmoid,
        ],
        axis=1,
    ).astype(narrow)
    grad_gu = weight_grad(ffn_in, gate_up_low)
    grad_ffn_in = scatter_tokens(
        dot_back(gate_up_low, gu_here).reshape(items, seq_len, width)
    )
    grad_scale_ffn = jnp.sum(grad_ffn_in * norm_mid, axis=1)
    grad_norm = grad_ffn_in * (1.0 + scale_ffn)
    grad_four = over_tokens(grad_norm * unit_mid)
    grad_middle = grad_result + norm_back(unit_mid, inverse_mid, grad_norm * gains[4])

    grad_gate_attn = (1.0 - gate_attn * gate_attn)[:, 0] * jnp.sum(grad_middle * norm_proj, axis=1)
    grad_norm = gate_attn * grad_middle
    grad_three = over_tokens(grad_norm * unit_proj)
    projected_low = gather_tokens(
        norm_back(unit_proj, inverse_proj, grad_norm * gains[3]).astype(narrow)
    ).reshape(tokens, width)
    grad_out = weight_grad(combined, projected_low)
    grad_combined = by_head(dot_back(projected_low, w_out))
    self_low = grad_combined.astype(narrow)
    cross_grad_low = (gate_here[:, None] * grad_combined).astype(narrow)
    grad_gate = (1.0 - gate_here * gate_here) * jnp.sum(grad_combined * cross_out, axis=(0, 1, 3))

    def soft_back(weights, low_grad, keys, values):
        grad_weights = jnp.einsum(
            "iphe,ikhe->ihpk", low_grad, values, preferred_element_type=single
        )
        inner = jnp.sum(weights * grad_weights, axis=-1, keepdims=True)
        score_low = (weights * (grad_weights - inner)).astype(narrow)
        grad_values = jnp.einsum(
            "ihpk,iphe->ikhe", weights.astype(narrow), low_grad, preferred_element_type=single
        )
        grad_keys = jnp.einsum(
            "ihpk,iphe->ikhe", score_low, query, preferred_element_type=single
        )
        grad_queries = mix(score_low, keys)
        return (
            grad_queries * score_scale,
            (grad_keys * score_scale).reshape(-1, span),
            grad_values.reshape(-1, span),
        )

    grad_query, grad_key, grad_value = soft_back(probs, self_low, key, value)
    grad_query_text, grad_tkey, grad_tval = soft_back(cross_probs, cross_grad_low, tkey, tval)
    grad_query = (grad_query + grad_query_text).reshape(tokens, span)
    grad_query = turn(grad_query, -1.0)
    grad_key = turn(grad_key, -1.0)
    scaled_q, scaled_k, scaled_t = grad_query * gain_q, grad_key * gain_k, grad_tkey * gain_t
    means = (
        lax.psum(
            jnp.concatenate(
                [
                    jnp.sum(scaled_q * unit_q, axis=-1),
                    jnp.sum(scaled_k * unit_k, axis=-1),
                    jnp.sum(scaled_t * unit_t, axis=-1),
                ]
            ),
            "rows",
        )[:, None]
        / width
    )
    qkv_low = jnp.concatenate(
        [
            inverse_q * (scaled_q - unit_q * means[:tokens]),
            inverse_k * (scaled_k - unit_k * means[tokens : 2 * tokens]),
            grad_value,
        ],
        axis=1,
    ).astype(narrow)
    text_low = jnp.concatenate(
        [inverse_t * (scaled_t - unit_t * means[2 * tokens :]), grad_tval], axis=1
    ).astype(narrow)
    grad_qkv = weight_grad(attn_in, qkv_low)
    grad_attn_in = scatter_tokens(dot_back(qkv_low, qkv_here).reshape(items, seq_len, width))
    grad_scale_attn = jnp.sum(grad_attn_in * norm_in, axis=1)
    grad_norm = grad_attn_in * (1.0 + scale_attn)
    grad_zero = over_tokens(grad_norm * unit_in)
    grad_x = grad_middle + norm_back(unit_in, inverse_in, grad_norm * gains[0])

    grad_text = weight_grad(text_norm, text_low)
    grad_text_gain = jnp.sum(dot_back(text_low, text_here) * text_unit, axis=0)
    grad_modulation = jnp.concatenate(
        [grad_scale_attn, grad_gate_attn, grad_scale_ffn, grad_gate_ffn], axis=-1
    )
    all_modulation = lax.all_gather(
        lax.psum(grad_modulation, "rows"), "items", axis=0, tiled=True
    )
    all_time = lax.all_gather(time_here, "items", axis=0, tiled=True)
    final_ada = jnp.einsum(
        "tk,tn->kn",
        all_time.astype(single),
        all_modulation,
        precision=lax.Precision.HIGHEST,
        preferred_element_type=single,
    )
    total_bias = jnp.sum(all_modulation, axis=0)

    def spread(part, whole):
        return lax.dynamic_update_slice_in_dim(
            jnp.zeros((whole,), single), part, place * part.shape[0], 0
        )

    grad_gains = jnp.stack(
        [
            grad_zero,
            spread(jnp.sum(grad_query * unit_q, axis=0), width),
            spread(jnp.sum(grad_key * unit_k, axis=0), width),
            grad_three,
            grad_four,
            grad_five,
            spread(jnp.sum(grad_tkey * unit_t, axis=0), width),
        ]
    )
    total_gains, total_gate, total_text_gain = lax.psum(
        (grad_gains, spread(grad_gate, heads), grad_text_gain), ("items", "rows")
    )
    sums = [
        lax.psum(part.astype(narrow), "items").astype(single)
        for part in (
            rows_here(grad_qkv, 3),
            grad_out,
            rows_here(grad_text, 2),
            rows_here(grad_gu, 2),
            grad_down,
        )
    ]
    return (
        output.reshape(1, items * slots, width),
        grad_x.reshape(1, items * slots, width),
        *sums,
        final_ada,
        total_gains,
        total_gate,
        total_bias,
        total_text_gain,
    )


def per_device(*arrays):
    heads = arrays[14].shape[0]
    plan = gathered_plan if heads % lax.axis_size("rows") else head_parallel_plan
    return plan(*arrays)


def solution(mesh):
    in_specs = (
        P("items", "rows", None),
        P("items", "rows", None),
        P("items", None, "rows", None),
        P("items", None, None),
        P("items", "rows", None),
        P("items", None),
        P("items", None),
        P("rows", None),
        P("rows", None),
        P("rows", None),
        P("rows", None),
        P("rows", None),
        P("rows", None),
        P(),
        P(),
        P(),
        P(),
    )
    out_specs = (
        P("items", "rows", None),
        P("items", "rows", None),
        P("rows", None),
        P("rows", None),
        P("rows", None),
        P("rows", None),
        P("rows", None),
        P("rows", None),
        P(),
        P(),
        P(),
        P(),
    )
    return jax.shard_map(
        per_device, mesh=mesh, in_specs=in_specs, out_specs=out_specs, check_vma=False
    )
```

```python
import functools

import jax
import jax.numpy as jnp
from jax import lax
from jax.experimental import pallas as pl
from jax.experimental.pallas import tpu as pltpu
from jax.sharding import PartitionSpec as P

COLS = 32


epsilon = 1e-06
masked_score = -1e30
group_heads = 4


def norm_gain(values, scaling):
    return values * lax.rsqrt(jnp.mean(values * values, axis=-1, keepdims=True) + epsilon) * scaling


def pre_norm(values, shift_scale, scaling):
    return norm_gain(values, scaling) * (1.0 + shift_scale)


def post_add(residual, branch, gate_in, scaling):
    return residual + jnp.tanh(gate_in) * norm_gain(branch, scaling)


def swiglu(gate_up):
    middle_col = gate_up.shape[-1] // 2
    return jax.nn.silu(gate_up[..., :middle_col]) * gate_up[..., middle_col:]


def freq_rates(number):
    return 10000.0 ** (-jnp.arange(number).astype(jnp.float32) / number)


def rotary_angles(frame_index, frame_row, column, head_size):
    frame_pairs = head_size // 8
    space_pairs = (head_size // 2 - frame_pairs) // 2
    return jnp.concatenate(
        [
            frame_index.astype(jnp.float32)[..., None] * freq_rates(frame_pairs),
            frame_row.astype(jnp.float32)[..., None] * freq_rates(space_pairs),
            column.astype(jnp.float32)[..., None] * freq_rates(space_pairs),
        ],
        axis=-1,
    )


def rotate(values, cos_table, sin_table, head_count):
    shaped = values.reshape(values.shape[:-1] + (head_count, values.shape[-1] // head_count))
    half_size = shaped.shape[-1] // 2
    upper_half = shaped[..., :half_size]
    lower_half = shaped[..., half_size:]
    cos_heads = cos_table[..., None, :]
    sin_heads = sin_table[..., None, :]
    turned = jnp.concatenate(
        [
            upper_half * cos_heads - lower_half * sin_heads,
            upper_half * sin_heads + lower_half * cos_heads,
        ],
        axis=-1,
    )
    return turned.reshape(values.shape)


def text_split(projected, key_gain):
    half_cols = projected.shape[-1] // 2
    return (norm_gain(projected[..., :half_cols], key_gain), projected[..., half_cols:])


def gathered_plan(
    hidden_in,
    cotangent,
    text_states,
    time_embed,
    live_rows,
    frame_rows,
    text_len,
    w_qkv,
    w_out,
    w_text,
    w_gu,
    w_down,
    w_ada,
    gains,
    cross_gate,
    ada_bias,
    text_gain,
):
    single = jnp.float32
    narrow = jnp.bfloat16
    model_width = hidden_in.shape[2]
    head_count = cross_gate.shape[0]
    head_size = model_width // head_count
    score_scale = head_size ** (-0.5)
    item_count = time_embed.shape[1]
    item_slots = hidden_in.shape[1] // item_count
    row_devices = lax.axis_size("rows")
    seq_len = row_devices * item_slots
    text_local = text_states.shape[2]
    text_all = text_local * row_devices
    text_width = text_states.shape[3]
    group_span = group_heads * head_size
    block_count = head_count // group_heads
    token_count = item_count * item_slots

    def weight_term(left, right, accuracy):
        return jnp.einsum(
            "tk,tn->kn", left, right, precision=accuracy, preferred_element_type=single
        )

    def reduce_term(term):
        return lax.psum_scatter(
            term.astype(jnp.bfloat16), "rows", scatter_dimension=0, tiled=True
        ).astype(jnp.float32)

    full_qkv, full_out, full_text, full_gu, full_down, full_ada = (
        lax.all_gather(w_qkv, "rows", axis=0, tiled=True),
        lax.all_gather(w_out, "rows", axis=0, tiled=True),
        lax.all_gather(w_text, "rows", axis=0, tiled=True),
        lax.all_gather(w_gu, "rows", axis=0, tiled=True),
        lax.all_gather(w_down, "rows", axis=0, tiled=True),
        lax.all_gather(w_ada, "rows", axis=0, tiled=True),
    )
    counts_here = live_rows[0]
    every_count = lax.all_gather(counts_here, "rows", axis=0, tiled=True)
    device_place = lax.axis_index("rows")
    ranks = jnp.arange(row_devices)
    rows_below = jnp.sum(jnp.where(ranks[:, None] < device_place, every_count, 0), axis=0)
    slot_row = jnp.arange(item_slots) // COLS
    column = jnp.arange(item_slots) % COLS
    row_index = rows_below[:, None] + slot_row[None, :]
    heights = frame_rows[0][:, None]
    frame_index = row_index // heights
    frame_row = row_index % heights
    live_mask = (slot_row[None, :] < counts_here[0][:, None]).astype(single)
    key_live = (slot_row[None, None, :] < jnp.transpose(every_count)[:, :, None]).reshape(
        item_count, seq_len
    )
    text_live = jnp.arange(text_all)[None, :] < text_len[0][:, None]
    angles = rotary_angles(
        frame_index, frame_row, jnp.broadcast_to(column, row_index.shape), head_size
    )
    cos_table = jnp.cos(angles)
    sin_table = jnp.sin(angles)

    def qkv_split(projected, gain_query, gain_key):
        queries = rotate(
            norm_gain(projected[..., :model_width], gain_query), cos_table, sin_table, head_count
        )
        keys_here = rotate(
            norm_gain(projected[..., model_width : 2 * model_width], gain_key),
            cos_table,
            sin_table,
            head_count,
        )
        return (queries, keys_here, projected[..., 2 * model_width :])

    states = hidden_in[0].reshape(item_count, item_slots, model_width)
    time_silu = jax.nn.silu(time_embed[0].astype(single)).astype(narrow)
    modulation = jnp.dot(time_silu, full_ada, preferred_element_type=single) + ada_bias
    scale_attn = modulation[:, None, 0:model_width]
    gate_attn = modulation[:, None, model_width : 2 * model_width]
    scale_ffn = modulation[:, None, 2 * model_width : 3 * model_width]
    gate_ffn = modulation[:, None, 3 * model_width :]
    attn_in = (
        pre_norm(states, scale_attn, gains[0]).astype(narrow).reshape(token_count, model_width)
    )
    qkv_proj = jnp.dot(attn_in, full_qkv, preferred_element_type=single).reshape(
        item_count, item_slots, 3 * model_width
    )
    query_full, key_full, value_full = qkv_split(qkv_proj, gains[1], gains[2])
    query_low = query_full.astype(narrow)
    key_low = key_full.astype(narrow)
    value_low = value_full.astype(narrow)
    text_float = text_states[0].astype(single)
    text_norm = norm_gain(text_float, text_gain).astype(narrow)
    text_proj = jnp.einsum("ctd,dn->ctn", text_norm, full_text, preferred_element_type=single)
    tkey_full, tval_full = text_split(text_proj, gains[6])
    key_all, value_all, tkey_all, tval_all = (
        lax.all_gather(key_low, "rows", axis=1, tiled=True),
        lax.all_gather(value_low, "rows", axis=1, tiled=True),
        lax.all_gather(tkey_full.astype(narrow), "rows", axis=1, tiled=True),
        lax.all_gather(tval_full.astype(narrow), "rows", axis=1, tiled=True),
    )

    def block_slices(block_index, key_source, value_source):
        offset = block_index * group_span
        query_part = lax.dynamic_slice_in_dim(query_low, offset, group_span, 2).reshape(
            item_count, item_slots, group_heads, head_size
        )
        key_part = lax.dynamic_slice_in_dim(key_source, offset, group_span, 2).reshape(
            item_count, seq_len, group_heads, head_size
        )
        value_part = lax.dynamic_slice_in_dim(value_source, offset, group_span, 2).reshape(
            item_count, seq_len, group_heads, head_size
        )
        return (query_part, key_part, value_part)

    def self_step(carry, block_index):
        query_part, key_part, value_part = block_slices(block_index, key_all, value_all)
        scores = (
            jnp.einsum("iphe,ikhe->ihpk", query_part, key_part, preferred_element_type=single)
            * score_scale
        )
        scores = jnp.where(key_live[:, None, None, :], scores, masked_score)
        row_max = jnp.max(scores, axis=-1, keepdims=True)
        exp_terms = jnp.exp(scores - row_max)
        exp_total = jnp.sum(exp_terms, axis=-1, keepdims=True)
        probs_low = (exp_terms / exp_total).astype(narrow)
        attended = jnp.einsum(
            "ihpk,ikhe->iphe", probs_low, value_part, preferred_element_type=single
        )
        return (
            carry,
            (
                attended.reshape(item_count, item_slots, group_span),
                (row_max + jnp.log(exp_total))[..., 0],
            ),
        )

    _, (self_parts, log_totals) = lax.scan(
        self_step, jnp.zeros((), single), jnp.arange(block_count)
    )

    def heads_last(parts):
        return jnp.transpose(parts, (1, 2, 0, 3)).reshape(item_count, item_slots, model_width)

    self_out = heads_last(self_parts)
    query_heads = query_low.reshape(item_count, item_slots, head_count, head_size)
    tkey_heads = tkey_all.reshape(item_count, text_all, head_count, head_size)
    tval_heads = tval_all.reshape(item_count, text_all, head_count, head_size)
    cross_scores = (
        jnp.einsum("iphe,ikhe->ihpk", query_heads, tkey_heads, preferred_element_type=single)
        * score_scale
    )
    cross_scores = jnp.where(text_live[:, None, None, :], cross_scores, masked_score)
    cross_max = jnp.max(cross_scores, axis=-1, keepdims=True)
    cross_exp = jnp.exp(cross_scores - cross_max)
    cross_probs = cross_exp / jnp.sum(cross_exp, axis=-1, keepdims=True)
    cross_low = cross_probs.astype(narrow)
    cross_out = jnp.einsum("ihpk,ikhe->iphe", cross_low, tval_heads, preferred_element_type=single)
    tanh_gate = jnp.tanh(cross_gate)
    combined = (
        self_out.reshape(item_count, item_slots, head_count, head_size)
        + tanh_gate[:, None] * cross_out
    )
    combined = combined.reshape(token_count, model_width).astype(narrow)
    projected = jnp.dot(combined, full_out, preferred_element_type=single).reshape(
        item_count, item_slots, model_width
    )
    middle = post_add(states, projected, gate_attn, gains[3])
    ffn_in = pre_norm(middle, scale_ffn, gains[4]).astype(narrow).reshape(token_count, model_width)
    gate_up = jnp.dot(ffn_in, full_gu, preferred_element_type=single)
    inner_act = swiglu(gate_up).astype(narrow)
    ffn_out = jnp.dot(inner_act, full_down, preferred_element_type=single).reshape(
        item_count, item_slots, model_width
    )
    result = post_add(middle, ffn_out, gate_ffn, gains[5])
    output = (live_mask[..., None] * result).reshape(1, token_count, model_width)
    grad_result = live_mask[..., None] * cotangent[0].reshape(item_count, item_slots, model_width)
    _, back_ffn_out = jax.vjp(post_add, middle, ffn_out, gate_ffn, gains[5])
    grad_middle, grad_ffn_out, grad_gate_ffn, grad_gain_five = back_ffn_out(grad_result)
    ffn_low = grad_ffn_out.astype(narrow).reshape(token_count, model_width)
    shard_down = reduce_term(weight_term(inner_act, ffn_low, None))
    grad_inner = jnp.einsum("tn,kn->tk", ffn_low, full_down, preferred_element_type=single)
    _, back_glu = jax.vjp(swiglu, gate_up)
    gate_up_low = back_glu(grad_inner)[0].astype(narrow)
    shard_gu = reduce_term(weight_term(ffn_in, gate_up_low, None))
    grad_ffn_in = jnp.einsum("tn,kn->tk", gate_up_low, full_gu, preferred_element_type=single)
    _, back_ffn_in = jax.vjp(pre_norm, middle, scale_ffn, gains[4])
    part_middle, grad_scale_ffn, grad_gain_four = back_ffn_in(
        grad_ffn_in.reshape(item_count, item_slots, model_width)
    )
    grad_middle = grad_middle + part_middle
    _, back_attn_out = jax.vjp(post_add, states, projected, gate_attn, gains[3])
    grad_hidden, grad_projected, grad_gate_attn, grad_gain_three = back_attn_out(grad_middle)
    projected_low = grad_projected.astype(narrow).reshape(token_count, model_width)
    shard_out = reduce_term(weight_term(combined, projected_low, None))
    grad_combined = jnp.einsum("tn,kn->tk", projected_low, full_out, preferred_element_type=single)
    grad_combined = grad_combined.reshape(item_count, item_slots, head_count, head_size)
    self_low = grad_combined.reshape(item_count, item_slots, model_width).astype(narrow)
    cross_grad_low = (tanh_gate[:, None] * grad_combined).astype(narrow)
    grad_cross_gate = (1.0 - tanh_gate * tanh_gate) * jnp.sum(
        grad_combined * cross_out, axis=(0, 1, 3)
    )

    def self_back(carry, packed):
        block_index, log_total = packed
        query_part, key_part, value_part = block_slices(block_index, key_all, value_all)
        offset = block_index * group_span
        grad_part = lax.dynamic_slice_in_dim(self_low, offset, group_span, 2).reshape(
            item_count, item_slots, group_heads, head_size
        )
        scores = (
            jnp.einsum("iphe,ikhe->ihpk", query_part, key_part, preferred_element_type=single)
            * score_scale
        )
        scores = jnp.where(key_live[:, None, None, :], scores, masked_score)
        attn_probs = jnp.exp(scores - log_total[..., None])
        grad_probs = jnp.einsum(
            "iphe,ikhe->ihpk", grad_part, value_part, preferred_element_type=single
        )
        row_inner = jnp.sum(attn_probs * grad_probs, axis=-1, keepdims=True)
        score_low = (attn_probs * (grad_probs - row_inner)).astype(narrow)
        grad_query = (
            jnp.einsum("ihpk,ikhe->iphe", score_low, key_part, preferred_element_type=single)
            * score_scale
        )
        grad_value = jnp.einsum(
            "ihpk,iphe->ikhe", attn_probs.astype(narrow), grad_part, preferred_element_type=single
        )
        grad_key = (
            jnp.einsum("ihpk,iphe->ikhe", score_low, query_part, preferred_element_type=single)
            * score_scale
        )
        owned_key, owned_value = (
            lax.psum_scatter(
                grad_key.reshape(item_count, seq_len, group_span).astype(jnp.bfloat16),
                "rows",
                scatter_dimension=1,
                tiled=True,
            ).astype(jnp.float32),
            lax.psum_scatter(
                grad_value.reshape(item_count, seq_len, group_span).astype(jnp.bfloat16),
                "rows",
                scatter_dimension=1,
                tiled=True,
            ).astype(jnp.float32),
        )
        return (
            carry,
            (grad_query.reshape(item_count, item_slots, group_span), owned_key, owned_value),
        )

    _, (query_parts, key_parts, value_parts) = lax.scan(
        self_back, jnp.zeros((), single), (jnp.arange(block_count), log_totals)
    )
    cross_grad_probs = jnp.einsum(
        "iphe,ikhe->ihpk", cross_grad_low, tval_heads, preferred_element_type=single
    )
    cross_inner = jnp.sum(cross_probs * cross_grad_probs, axis=-1, keepdims=True)
    cross_score_low = (cross_probs * (cross_grad_probs - cross_inner)).astype(narrow)
    grad_query_cross = (
        jnp.einsum("ihpk,ikhe->iphe", cross_score_low, tkey_heads, preferred_element_type=single)
        * score_scale
    )
    grad_text_key = (
        jnp.einsum("ihpk,iphe->ikhe", cross_score_low, query_heads, preferred_element_type=single)
        * score_scale
    )
    grad_text_value = jnp.einsum(
        "ihpk,iphe->ikhe", cross_low, cross_grad_low, preferred_element_type=single
    )
    owned_tkey, owned_tval = (
        lax.psum_scatter(
            grad_text_key.reshape(item_count, text_all, model_width).astype(jnp.bfloat16),
            "rows",
            scatter_dimension=1,
            tiled=True,
        ).astype(jnp.float32),
        lax.psum_scatter(
            grad_text_value.reshape(item_count, text_all, model_width).astype(jnp.bfloat16),
            "rows",
            scatter_dimension=1,
            tiled=True,
        ).astype(jnp.float32),
    )
    grad_query_all = heads_last(query_parts) + grad_query_cross.reshape(
        item_count, item_slots, model_width
    )
    _, back_qkv = jax.vjp(qkv_split, qkv_proj, gains[1], gains[2])
    grad_qkv, grad_gain_one, grad_gain_two = back_qkv(
        (grad_query_all, heads_last(key_parts), heads_last(value_parts))
    )
    qkv_low = grad_qkv.astype(narrow).reshape(token_count, 3 * model_width)
    shard_qkv = reduce_term(weight_term(attn_in, qkv_low, None))
    grad_attn_in = jnp.einsum("tn,kn->tk", qkv_low, full_qkv, preferred_element_type=single)
    _, back_attn_in = jax.vjp(pre_norm, states, scale_attn, gains[0])
    part_states, grad_scale_attn, grad_gain_zero = back_attn_in(
        grad_attn_in.reshape(item_count, item_slots, model_width)
    )
    grad_x = (grad_hidden + part_states).reshape(1, token_count, model_width)
    _, back_text = jax.vjp(text_split, text_proj, gains[6])
    grad_text_proj, grad_gain_six = back_text((owned_tkey, owned_tval))
    text_low = grad_text_proj.astype(narrow).reshape(item_count * text_local, 2 * model_width)
    shard_text = reduce_term(
        weight_term(text_norm.reshape(item_count * text_local, text_width), text_low, None)
    )
    grad_text_norm = jnp.einsum("tn,kn->tk", text_low, full_text, preferred_element_type=single)
    _, back_text_norm = jax.vjp(norm_gain, text_float, text_gain)
    grad_text_gain = back_text_norm(grad_text_norm.reshape(text_float.shape))[1]
    grad_modulation = jnp.concatenate(
        [grad_scale_attn, grad_gate_attn, grad_scale_ffn, grad_gate_ffn], axis=-1
    )[:, 0, :]
    shard_ada = reduce_term(
        weight_term(time_silu.astype(single), grad_modulation, lax.Precision.HIGHEST)
    )
    grad_ada_bias = jnp.sum(grad_modulation, axis=0)
    grad_gains = jnp.stack(
        [
            grad_gain_zero,
            grad_gain_one,
            grad_gain_two,
            grad_gain_three,
            grad_gain_four,
            grad_gain_five,
            grad_gain_six,
        ],
        axis=0,
    )
    final_qkv, final_out, final_text, final_gu, final_down, final_ada = (
        lax.psum(shard_qkv.astype(jnp.bfloat16), "items").astype(jnp.float32),
        lax.psum(shard_out.astype(jnp.bfloat16), "items").astype(jnp.float32),
        lax.psum(shard_text.astype(jnp.bfloat16), "items").astype(jnp.float32),
        lax.psum(shard_gu.astype(jnp.bfloat16), "items").astype(jnp.float32),
        lax.psum(shard_down.astype(jnp.bfloat16), "items").astype(jnp.float32),
        lax.psum(shard_ada.astype(jnp.bfloat16), "items").astype(jnp.float32),
    )
    total_gains, total_gate, total_bias, total_text_gain = lax.psum(
        (grad_gains, grad_cross_gate, grad_ada_bias, grad_text_gain), ("items", "rows")
    )
    return (
        output,
        grad_x,
        final_qkv,
        final_out,
        final_text,
        final_gu,
        final_down,
        final_ada,
        total_gains,
        total_gate,
        total_bias,
        total_text_gain,
    )


def norm_parts(values):
    inverse = lax.rsqrt(jnp.mean(values * values, axis=-1, keepdims=True) + epsilon)
    return values * inverse, inverse


def norm_back(unit, inverse, scaled_grad):
    return inverse * (scaled_grad - unit * jnp.mean(scaled_grad * unit, axis=-1, keepdims=True))


MESH = pl.DeviceIdType.MESH
DEPTH, BREADTH = 4, 2


def row_place():
    place = lax.axis_index("rows")
    return place // BREADTH, lax.rem(place, BREADTH)


def on_rows(line, side):
    return {"rows": line * BREADTH + side}


def greet(devices):
    barrier = pltpu.get_barrier_semaphore()
    for condition, device in devices:

        @pl.when(condition)
        def _(device=device):
            pl.semaphore_signal(barrier, inc=1, device_id=device, device_id_type=MESH)

    count = 0
    for condition, _ in devices:
        count = count + jnp.where(condition, 1, 0)
    pl.semaphore_wait(barrier, count)


def remote(source, target, send, receive, device):
    return pltpu.make_async_remote_copy(
        src_ref=source,
        dst_ref=target,
        send_sem=send,
        recv_sem=receive,
        device_id=device,
        device_id_type=MESH,
    )


def shard_of(ref, place, axis):
    return ref.at[place] if axis == 0 else ref.at[:, place]


def gather_kernel(axis, own, whole, local, z_send, z_recv, x_send, x_recv):
    line, side = row_place()
    above, below, across = on_rows(line + 1, side), on_rows(line - 1, side), on_rows(line, 1 - side)
    has_above, has_below = line < DEPTH - 1, line > 0
    greet([(has_above, above), (has_below, below), (line >= 0, across)])

    def block(at, which):
        return shard_of(whole, at * BREADTH + which, axis)

    def pass_on(source, at, way, device):
        return remote(source, block(at, side), z_send.at[way, at], z_recv.at[at], device)

    def cross(source, at):
        return remote(source, block(at, side), x_send.at[at], x_recv.at[at], across)

    cross(own, line).start()

    @pl.when(has_above)
    def _():
        pass_on(own, line, 0, above).start()

    @pl.when(has_below)
    def _():
        pass_on(own, line, 1, below).start()

    keep = pltpu.make_async_copy(own, block(line, side), local)
    keep.start()
    for step in range(1, DEPTH):

        @pl.when(line - step >= 0)
        def _(at=line - step):
            pass_on(own, at, 0, below).wait_recv()

            @pl.when(has_above)
            def _():
                pass_on(block(at, side), at, 0, above).start()

            cross(block(at, side), at).start()

        @pl.when(line + step < DEPTH)
        def _(at=line + step):
            pass_on(own, at, 1, above).wait_recv()

            @pl.when(has_below)
            def _():
                pass_on(block(at, side), at, 1, below).start()

            cross(block(at, side), at).start()

    keep.wait()
    for at in range(DEPTH):
        cross(own, at).wait_recv()
        cross(own, at).wait_send()

        @pl.when(has_above & (at <= line))
        def _(at=at):
            pass_on(own, at, 0, above).wait_send()

        @pl.when(has_below & (at >= line))
        def _(at=at):
            pass_on(own, at, 1, below).wait_send()


def gather_rows(block, ident, axis):
    ranks = DEPTH * BREADTH
    shape = block.shape[:axis] + (ranks,) + block.shape[axis:]
    anywhere = pl.BlockSpec(memory_space=pl.ANY)
    return pl.pallas_call(
        functools.partial(gather_kernel, axis),
        out_shape=jax.ShapeDtypeStruct(shape, block.dtype),
        in_specs=[anywhere],
        out_specs=anywhere,
        scratch_shapes=[
            pltpu.SemaphoreType.DMA,
            pltpu.SemaphoreType.DMA((2, DEPTH)),
            pltpu.SemaphoreType.DMA((DEPTH,)),
            pltpu.SemaphoreType.DMA((DEPTH,)),
            pltpu.SemaphoreType.DMA((DEPTH,)),
        ],
        name=f"gather_rows_{ident}",
        compiler_params=pltpu.CompilerParams(collective_id=ident, has_side_effects=True),
    )(block)


def scatter_kernel(axis, parts, total, crossed, risen, sunk, up, down, x_send, x_recv, z_send, z_recv):
    line, side = row_place()
    above, below, across = on_rows(line + 1, side), on_rows(line - 1, side), on_rows(line, 1 - side)
    has_above, has_below = line < DEPTH - 1, line > 0
    greet([(has_above, above), (has_below, below), (line >= 0, across)])

    def part(at, which):
        return shard_of(parts, at * BREADTH + which, axis)

    def cross(at):
        return remote(part(at, 1 - side), crossed.at[at], x_send.at[at], x_recv.at[at], across)

    def rise(at):
        return remote(up.at[at], risen.at[at], z_send.at[0, at], z_recv.at[0, at], above)

    def sink(at):
        return remote(down.at[at], sunk.at[at], z_send.at[1, at], z_recv.at[1, at], below)

    def add_up(at, others, target):
        mine = part(at, side)
        whole = mine.shape
        value = mine[...].astype(jnp.float32) + crossed[at].astype(jnp.float32)
        for other in others:
            value = value + other[at].astype(jnp.float32)
        target[...] = value.astype(target.dtype)

    for step in range(DEPTH - 1, 0, -1):
        for at, there in ((line + step, line + step < DEPTH), (line - step, line - step >= 0)):

            @pl.when(there)
            def _(at=at):
                cross(at).start()

    cross(line).start()
    for step in range(DEPTH - 1, 0, -1):

        @pl.when(line + step < DEPTH)
        def _(at=line + step):
            cross(at).wait_recv()

            @pl.when(has_below)
            def _():
                rise(at).wait_recv()
                add_up(at, [risen], up.at[at])

            @pl.when(jnp.logical_not(has_below))
            def _():
                add_up(at, [], up.at[at])

            rise(at).start()

        @pl.when(line - step >= 0)
        def _(at=line - step):
            cross(at).wait_recv()

            @pl.when(has_above)
            def _():
                sink(at).wait_recv()
                add_up(at, [sunk], down.at[at])

            @pl.when(jnp.logical_not(has_above))
            def _():
                add_up(at, [], down.at[at])

            sink(at).start()

    cross(line).wait_recv()

    @pl.when(has_below & has_above)
    def _():
        rise(line).wait_recv()
        sink(line).wait_recv()
        add_up(line, [risen, sunk], total)

    @pl.when(jnp.logical_not(has_above))
    def _():
        rise(line).wait_recv()
        add_up(line, [risen], total)

    @pl.when(jnp.logical_not(has_below))
    def _():
        sink(line).wait_recv()
        add_up(line, [sunk], total)

    for at in range(DEPTH):
        cross(at).wait_send()

        @pl.when(at > line)
        def _(at=at):
            rise(at).wait_send()

        @pl.when(at < line)
        def _(at=at):
            sink(at).wait_send()


def scatter_rows(parts, ident, axis):
    shape = parts.shape[:axis] + parts.shape[axis + 1 :]
    near = pl.BlockSpec(memory_space=pltpu.VMEM)
    slots = pltpu.VMEM((DEPTH,) + shape, parts.dtype)
    return pl.pallas_call(
        functools.partial(scatter_kernel, axis),
        out_shape=jax.ShapeDtypeStruct(shape, jnp.float32),
        in_specs=[near],
        out_specs=near,
        scratch_shapes=[slots] * 5
        + [
            pltpu.SemaphoreType.DMA((DEPTH,)),
            pltpu.SemaphoreType.DMA((DEPTH,)),
            pltpu.SemaphoreType.DMA((2, DEPTH)),
            pltpu.SemaphoreType.DMA((2, DEPTH)),
        ],
        name=f"scatter_rows_{ident}",
        compiler_params=pltpu.CompilerParams(
            collective_id=ident, has_side_effects=True, vmem_limit_bytes=32 << 20
        ),
    )(parts)


def sum_kernel(own, total, held, send, receive):
    ranks = DEPTH * BREADTH
    place = lax.axis_index("rows")
    others = [lax.rem(place + step, ranks) for step in range(1, ranks)]
    greet([(place >= 0, {"rows": other}) for other in others])

    def push(step, other, slot):
        return remote(own, held.at[slot], send.at[step], receive.at[slot], {"rows": other})

    for step, other in enumerate(others):
        push(step, other, place).start()
    held[pl.ds(place, 1)] = own[...][None]
    for step, other in enumerate(others):
        push(step, other, other).wait_recv()
    value = held[0]
    for rank in range(1, ranks):
        value = value + held[rank]
    total[...] = value
    for step, other in enumerate(others):
        push(step, other, place).wait_send()


def sum_rows(own, ident):
    ranks = DEPTH * BREADTH
    near = pl.BlockSpec(memory_space=pltpu.VMEM)
    return pl.pallas_call(
        sum_kernel,
        out_shape=jax.ShapeDtypeStruct(own.shape, own.dtype),
        in_specs=[near],
        out_specs=near,
        scratch_shapes=[
            pltpu.VMEM((ranks,) + own.shape, own.dtype),
            pltpu.SemaphoreType.DMA((ranks,)),
            pltpu.SemaphoreType.DMA((ranks,)),
        ],
        name=f"sum_rows_{ident}",
        compiler_params=pltpu.CompilerParams(collective_id=ident, has_side_effects=True),
    )(own)


def final_kernel(ranks, groups, sums, own, out, held, kept, part, h_send, h_recv, g_send, g_recv, o_send, o_recv):
    place, group = lax.axis_index("rows"), lax.axis_index("items")
    rows = [lax.rem(place + step, ranks) for step in range(1, ranks)]
    items = [lax.rem(group + step, groups) for step in range(1, groups)]
    greet([(place >= 0, {"rows": other}) for other in rows] + [(place >= 0, {"items": other}) for other in items])

    def push(step, other, slot):
        return remote(own.at[other], held.at[slot], h_send.at[step], h_recv.at[slot], {"rows": other})

    def swap(step, other, slot):
        return remote(part, kept.at[slot], g_send.at[step], g_recv.at[slot], {"items": other})

    def share(step, other, slot):
        return remote(out.at[place], out.at[slot], o_send.at[step], o_recv.at[slot], {"rows": other})

    for step, other in enumerate(rows):
        push(step, other, place).start()
    held[pl.ds(place, 1)] = own[pl.ds(place, 1)]
    for step, other in enumerate(rows):
        push(step, other, other).wait_recv()
    value = held[0]
    for rank in range(1, ranks):
        value = value + held[rank]
    part[...] = value
    for step, other in enumerate(items):
        swap(step, other, group).start()
    kept[pl.ds(group, 1)] = value[None]
    for step, other in enumerate(items):
        swap(step, other, other).wait_recv()
    total = kept[0, :sums]
    for item in range(1, groups):
        total = total + kept[item, :sums]
    depth = own.shape[1] - sums
    out[pl.ds(place, 1), :sums] = total[None]
    for item in range(groups):
        out[pl.ds(place, 1), sums + item * depth : sums + (item + 1) * depth] = kept[item, sums:][None]
    for step, other in enumerate(rows):
        share(step, other, place).start()
    for step, other in enumerate(rows):
        share(step, other, other).wait_recv()
    for step, other in enumerate(rows):
        push(step, other, place).wait_send()
        share(step, other, place).wait_send()
    for step, other in enumerate(items):
        swap(step, other, group).wait_send()


def final_sums(own, sums, ident):
    ranks, groups = lax.axis_size("rows"), lax.axis_size("items")
    near = pl.BlockSpec(memory_space=pltpu.VMEM)
    depth = own.shape[1]
    return pl.pallas_call(
        functools.partial(final_kernel, ranks, groups, sums),
        out_shape=jax.ShapeDtypeStruct((ranks, sums + groups * (depth - sums), 128), own.dtype),
        in_specs=[near],
        out_specs=near,
        scratch_shapes=[
            pltpu.VMEM(own.shape, own.dtype),
            pltpu.VMEM((groups,) + own.shape[1:], own.dtype),
            pltpu.VMEM(own.shape[1:], own.dtype),
            pltpu.SemaphoreType.DMA((ranks,)),
            pltpu.SemaphoreType.DMA((ranks,)),
            pltpu.SemaphoreType.DMA((groups,)),
            pltpu.SemaphoreType.DMA((groups,)),
            pltpu.SemaphoreType.DMA((ranks,)),
            pltpu.SemaphoreType.DMA((ranks,)),
        ],
        name=f"final_sums_{ident}",
        compiler_params=pltpu.CompilerParams(collective_id=ident, has_side_effects=True),
    )(own)


def gather_tokens(block, ident):
    whole = gather_rows(block, ident, 1)
    return whole.reshape(-1, block.shape[-1])


def scatter_tokens(partial, items, ident):
    ranks = lax.axis_size("rows")
    blocks = partial.astype(jnp.bfloat16).reshape(items, ranks, -1, partial.shape[-1])
    return scatter_rows(blocks, ident, 1)


def sum_vectors(vectors, ident):
    sizes = [vector.size for vector in vectors]
    flat = jnp.concatenate([vector.reshape(-1) for vector in vectors])
    rows = -(-flat.size // 1024) * 8
    flat = jnp.pad(flat, (0, rows * 128 - flat.size))
    total = sum_rows(flat.reshape(rows, 128), ident).reshape(-1)
    parts, start = [], 0
    for vector, size in zip(vectors, sizes):
        parts.append(total[start : start + size].reshape(vector.shape))
        start += size
    return parts


def columns_here(weight, pieces):
    ranks = lax.axis_size("rows")
    depth, width = weight.shape
    shaped = weight.reshape(depth, pieces, ranks, width // (pieces * ranks))
    moved = lax.all_to_all(shaped, "rows", split_axis=2, concat_axis=0, tiled=True)
    return moved.reshape(depth * ranks, width // ranks)


def rows_here(grad, pieces):
    ranks = lax.axis_size("rows")
    depth, width = grad.shape
    low = grad.astype(jnp.bfloat16).reshape(depth, pieces, 1, width // pieces)
    moved = lax.all_to_all(low, "rows", split_axis=0, concat_axis=2, tiled=True)
    return moved.reshape(depth // ranks, width * ranks)


def head_parallel_plan(
    hidden_in,
    cotangent,
    text_states,
    time_embed,
    live_rows,
    frame_rows,
    text_len,
    w_qkv,
    w_out,
    w_text,
    w_gu,
    w_down,
    w_ada,
    gains,
    cross_gate,
    ada_bias,
    text_gain,
):
    single = jnp.float32
    narrow = jnp.bfloat16
    ranks = lax.axis_size("rows")
    place = lax.axis_index("rows")
    width = hidden_in.shape[2]
    heads = cross_gate.shape[0]
    head_size = width // heads
    score_scale = head_size ** (-0.5)
    items = time_embed.shape[1]
    slots = hidden_in.shape[1] // items
    row_slots = slots // COLS
    seq_len = ranks * slots
    text_local = text_states.shape[2]
    text_all = text_local * ranks
    text_width = text_states.shape[3]
    span = width // ranks
    heads_here = heads // ranks
    tokens = items * seq_len

    def dot(left, right):
        return jnp.dot(left, right, preferred_element_type=single)

    def dot_back(left, weight):
        return jnp.einsum("tn,kn->tk", left, weight, preferred_element_type=single)

    def weight_grad(left, right):
        return jnp.einsum("tk,tn->kn", left, right, preferred_element_type=single)

    time_silu = jax.nn.silu(time_embed[0].astype(single)).astype(narrow)
    ada_depth = w_ada.shape[0]
    time_here = lax.dynamic_slice_in_dim(time_silu, place * ada_depth, ada_depth, 1)

    def spread(part, whole):
        return lax.dynamic_update_slice_in_dim(
            jnp.zeros((whole,), single), part.reshape(-1), place * part.size, 0
        )

    counts_here = live_rows[0]
    text_float = text_states[0].astype(single).reshape(items * text_local, text_width)
    text_inverse = norm_parts(text_float)[1]
    modulation, counts, text_inverse = sum_vectors(
        [
            dot(time_here, w_ada),
            spread(counts_here.astype(single), ranks * items),
            spread(text_inverse, ranks * items * text_local),
        ],
        0,
    )
    modulation = modulation + ada_bias
    counts = counts.astype(jnp.int32).reshape(ranks, items)
    text_inverse = text_inverse.reshape(-1, 1)
    scale_attn = modulation[:, None, 0:width]
    gate_attn = jnp.tanh(modulation[:, None, width : 2 * width])
    scale_ffn = modulation[:, None, 2 * width : 3 * width]
    gate_ffn = jnp.tanh(modulation[:, None, 3 * width :])

    below = jnp.cumsum(counts, axis=0) - counts
    slot_row = jnp.arange(row_slots)
    row_index = jnp.transpose(below)[:, :, None] + slot_row
    heights = frame_rows[0][:, None, None]
    frame_pairs = head_size // 8
    space_pairs = (head_size // 2 - frame_pairs) // 2
    row_angles = jnp.concatenate(
        [
            (row_index // heights).astype(single)[..., None] * freq_rates(frame_pairs),
            (row_index % heights).astype(single)[..., None] * freq_rates(space_pairs),
        ],
        axis=-1,
    )
    column_angles = jnp.arange(COLS).astype(single)[:, None] * freq_rates(space_pairs)

    def table(function):
        by_row = function(row_angles)
        by_column = function(column_angles)
        shape = (items, ranks, row_slots, COLS)
        whole = jnp.concatenate(
            [
                jnp.broadcast_to(by_row[:, :, :, None, :], shape + by_row.shape[-1:]),
                jnp.broadcast_to(by_column, shape + by_column.shape[-1:]),
            ],
            axis=-1,
        )
        return whole.reshape(tokens, 1, head_size // 2)

    cos_table = table(jnp.cos)
    sin_table = table(jnp.sin)

    def turn(values, sign):
        shaped = values.reshape(tokens, heads_here, head_size)
        upper = shaped[..., : head_size // 2]
        lower = shaped[..., head_size // 2 :]
        sines = sign * sin_table
        turned = jnp.concatenate(
            [upper * cos_table - lower * sines, upper * sines + lower * cos_table], axis=-1
        )
        return turned.reshape(tokens, width // ranks)

    slot_in_row = jnp.arange(slots) // COLS
    live_mask = (slot_in_row[None, :] < counts_here[0][:, None]).astype(single)[..., None]
    key_live = (slot_in_row < jnp.transpose(counts)[:, :, None]).reshape(items, seq_len)
    text_live = jnp.arange(text_all)[None, :] < text_len[0][:, None]

    def gain_here(index):
        return lax.dynamic_slice_in_dim(gains[index], place * span, span, 0)

    states = hidden_in[0].reshape(items, slots, width)
    unit_in, inverse_in = norm_parts(states)
    norm_in = unit_in * gains[0]
    attn_in = gather_tokens((norm_in * (1.0 + scale_attn)).astype(narrow), 1)
    qkv_here = columns_here(w_qkv, 3)
    qkv_proj = dot(attn_in, qkv_here)
    query_proj, key_proj, value_proj = jnp.split(qkv_proj, 3, axis=1)

    features = text_width // ranks
    text_in = lax.all_to_all(
        text_states[0].reshape(items * text_local, ranks, features),
        "rows",
        split_axis=1,
        concat_axis=0,
        tiled=True,
    ).reshape(items * text_all, features)
    text_unit = text_in.astype(single) * text_inverse
    gain_text = lax.dynamic_slice_in_dim(text_gain, place * features, features, 0)
    text_norm = (text_unit * gain_text).astype(narrow)

    def by_rank(values):
        pieces = values.reshape(-1, 2, ranks, span)
        return jnp.transpose(pieces, (2, 0, 1, 3)).reshape(ranks, -1, 2 * span)

    def text_rows(values):
        shaped = values.reshape(ranks, items, text_local, -1)
        return jnp.swapaxes(shaped, 0, 1).reshape(items * text_all, -1)

    text_proj = scatter_rows(by_rank(dot(text_norm, w_text).astype(narrow)), 2, 0)
    tkey_proj, tval_proj = jnp.split(text_rows(text_proj), 2, axis=1)

    def squares(values):
        return jnp.sum(values * values, axis=-1)

    totals = sum_vectors([squares(query_proj), squares(key_proj), squares(tkey_proj)], 3)
    inverse_q, inverse_k, inverse_t = (
        lax.rsqrt(total / width + epsilon)[:, None] for total in totals
    )
    gain_q, gain_k, gain_t = gain_here(1), gain_here(2), gain_here(6)
    unit_q, unit_k, unit_t = query_proj * inverse_q, key_proj * inverse_k, tkey_proj * inverse_t

    def by_head(values):
        return values.reshape(items, -1, heads_here, head_size)

    query = by_head(turn(unit_q * gain_q, 1.0).astype(narrow))
    key = by_head(turn(unit_k * gain_k, 1.0).astype(narrow))
    value = by_head(value_proj.astype(narrow))
    tkey = by_head((unit_t * gain_t).astype(narrow))
    tval = by_head(tval_proj.astype(narrow))

    def soft(keys, mask):
        scores = jnp.einsum("iphe,ikhe->ihpk", query, keys, preferred_element_type=single)
        scores = jnp.where(mask[:, None, None, :], scores * score_scale, masked_score)
        terms = jnp.exp(scores - jnp.max(scores, axis=-1, keepdims=True))
        return terms / jnp.sum(terms, axis=-1, keepdims=True)

    def mix(weights, values):
        return jnp.einsum("ihpk,ikhe->iphe", weights, values, preferred_element_type=single)

    probs = soft(key, key_live)
    self_out = mix(probs.astype(narrow), value)
    cross_probs = soft(tkey, text_live)
    cross_out = mix(cross_probs.astype(narrow), tval)
    gate_here = jnp.tanh(lax.dynamic_slice_in_dim(cross_gate, place * heads_here, heads_here, 0))
    combined = (self_out + gate_here[:, None] * cross_out).astype(narrow).reshape(tokens, span)
    projected = scatter_tokens(dot(combined, w_out), items, 4)

    unit_proj, inverse_proj = norm_parts(projected)
    norm_proj = unit_proj * gains[3]
    middle = states + gate_attn * norm_proj
    unit_mid, inverse_mid = norm_parts(middle)
    norm_mid = unit_mid * gains[4]
    ffn_in = gather_tokens((norm_mid * (1.0 + scale_ffn)).astype(narrow), 5)
    gu_here = columns_here(w_gu, 2)
    gate_up = dot(ffn_in, gu_here)
    gate_part, up_part = jnp.split(gate_up, 2, axis=1)
    sigmoid = 1.0 / (1.0 + jnp.exp(-gate_part))
    inner_act = (gate_part * sigmoid * up_part).astype(narrow)
    ffn_out = scatter_tokens(dot(inner_act, w_down), items, 6)
    unit_ffn, inverse_ffn = norm_parts(ffn_out)
    norm_ffn = unit_ffn * gains[5]
    output = live_mask * (middle + gate_ffn * norm_ffn)

    def over_tokens(values):
        return jnp.sum(values, axis=(0, 1))

    grad_result = live_mask * cotangent[0].reshape(items, slots, width)
    grad_gate_ffn = (1.0 - gate_ffn * gate_ffn)[:, 0] * jnp.sum(grad_result * norm_ffn, axis=1)
    grad_norm = gate_ffn * grad_result
    grad_five = over_tokens(grad_norm * unit_ffn)
    ffn_low = gather_tokens(
        norm_back(unit_ffn, inverse_ffn, grad_norm * gains[5]).astype(narrow), 7
    )
    grad_down = weight_grad(inner_act, ffn_low)
    grad_inner = dot_back(ffn_low, w_down)
    gate_up_low = jnp.concatenate(
        [
            grad_inner * up_part * sigmoid * (1.0 + gate_part * (1.0 - sigmoid)),
            grad_inner * gate_part * sigmoid,
        ],
        axis=1,
    ).astype(narrow)
    grad_gu = weight_grad(ffn_in, gate_up_low)
    grad_ffn_in = scatter_tokens(dot_back(gate_up_low, gu_here), items, 8)
    grad_scale_ffn = jnp.sum(grad_ffn_in * norm_mid, axis=1)
    grad_norm = grad_ffn_in * (1.0 + scale_ffn)
    grad_four = over_tokens(grad_norm * unit_mid)
    grad_middle = grad_result + norm_back(unit_mid, inverse_mid, grad_norm * gains[4])

    grad_gate_attn = (1.0 - gate_attn * gate_attn)[:, 0] * jnp.sum(grad_middle * norm_proj, axis=1)
    grad_norm = gate_attn * grad_middle
    grad_three = over_tokens(grad_norm * unit_proj)
    projected_low = gather_tokens(
        norm_back(unit_proj, inverse_proj, grad_norm * gains[3]).astype(narrow), 9
    )
    grad_out = weight_grad(combined, projected_low)
    grad_combined = by_head(dot_back(projected_low, w_out))
    self_low = grad_combined.astype(narrow)
    cross_grad_low = (gate_here[:, None] * grad_combined).astype(narrow)
    grad_gate = (1.0 - gate_here * gate_here) * jnp.sum(grad_combined * cross_out, axis=(0, 1, 3))

    def soft_back(weights, low_grad, keys, values):
        grad_weights = jnp.einsum(
            "iphe,ikhe->ihpk", low_grad, values, preferred_element_type=single
        )
        inner = jnp.sum(weights * grad_weights, axis=-1, keepdims=True)
        score_low = (weights * (grad_weights - inner)).astype(narrow)
        grad_values = jnp.einsum(
            "ihpk,iphe->ikhe", weights.astype(narrow), low_grad, preferred_element_type=single
        )
        grad_keys = jnp.einsum(
            "ihpk,iphe->ikhe", score_low, query, preferred_element_type=single
        )
        grad_queries = mix(score_low, keys)
        return (
            grad_queries * score_scale,
            (grad_keys * score_scale).reshape(-1, span),
            grad_values.reshape(-1, span),
        )

    grad_query, grad_key, grad_value = soft_back(probs, self_low, key, value)
    grad_query_text, grad_tkey, grad_tval = soft_back(cross_probs, cross_grad_low, tkey, tval)
    grad_query = (grad_query + grad_query_text).reshape(tokens, span)
    grad_query = turn(grad_query, -1.0)
    grad_key = turn(grad_key, -1.0)
    scaled_q, scaled_k, scaled_t = grad_query * gain_q, grad_key * gain_k, grad_tkey * gain_t
    mean_q, mean_k, mean_t = (
        total[:, None] / width
        for total in sum_vectors(
            [
                jnp.sum(scaled_q * unit_q, axis=-1),
                jnp.sum(scaled_k * unit_k, axis=-1),
                jnp.sum(scaled_t * unit_t, axis=-1),
            ],
            10,
        )
    )
    qkv_low = jnp.concatenate(
        [
            inverse_q * (scaled_q - unit_q * mean_q),
            inverse_k * (scaled_k - unit_k * mean_k),
            grad_value,
        ],
        axis=1,
    ).astype(narrow)
    text_low = jnp.concatenate(
        [inverse_t * (scaled_t - unit_t * mean_t), grad_tval], axis=1
    ).astype(narrow)
    grad_qkv = weight_grad(attn_in, qkv_low)
    grad_attn_in = scatter_tokens(dot_back(qkv_low, qkv_here), items, 11)
    grad_scale_attn = jnp.sum(grad_attn_in * norm_in, axis=1)
    grad_norm = grad_attn_in * (1.0 + scale_attn)
    grad_zero = over_tokens(grad_norm * unit_in)
    grad_x = grad_middle + norm_back(unit_in, inverse_in, grad_norm * gains[0])

    text_low = text_low.reshape(items, ranks, text_local, 2 * span)
    text_low = jnp.swapaxes(text_low, 0, 1).reshape(items * text_all, 2 * span)
    all_low = gather_rows(text_low, 12, 0).reshape(ranks, -1, 2, span)
    all_low = jnp.transpose(all_low, (1, 2, 0, 3)).reshape(items * text_all, 2 * width)
    grad_text = weight_grad(text_norm, all_low)
    grad_text_gain = jnp.sum(dot_back(all_low, w_text) * text_unit, axis=0)
    grad_modulation = jnp.stack([grad_scale_attn, grad_gate_attn, grad_scale_ffn, grad_gate_ffn], 1)
    grad_gains = jnp.stack(
        [
            grad_zero,
            spread(jnp.sum(grad_query * unit_q, axis=0), width),
            spread(jnp.sum(grad_key * unit_k, axis=0), width),
            grad_three,
            grad_four,
            grad_five,
            spread(jnp.sum(grad_tkey * unit_t, axis=0), width),
        ]
    )
    flat = jnp.concatenate(
        [
            grad_gains.reshape(-1),
            spread(grad_text_gain, text_width),
            spread(grad_gate, heads),
        ]
    )
    lanes = ranks * 128
    sum_depth = -(-flat.size // lanes)
    flat = jnp.pad(flat, (0, sum_depth * lanes - flat.size)).reshape(ranks, sum_depth, 128)
    keep_depth = grad_modulation.size // lanes
    reduced = final_sums(
        jnp.concatenate([flat, grad_modulation.reshape(ranks, keep_depth, 128)], axis=1),
        sum_depth,
        13,
    )
    flat = reduced[:, :sum_depth].reshape(-1)
    total_gains = flat[: gains.size].reshape(gains.shape)
    total_text_gain = flat[gains.size : gains.size + text_width]
    total_gate = flat[gains.size + text_width : gains.size + text_width + heads]
    groups = lax.axis_size("items")
    all_modulation = jnp.swapaxes(
        reduced[:, sum_depth:].reshape(ranks, groups, keep_depth * 128), 0, 1
    ).reshape(groups * items, 4 * width)
    all_time = lax.all_gather(time_here, "items", axis=0, tiled=True)
    final_ada = jnp.einsum(
        "tk,tn->kn",
        all_time.astype(single),
        all_modulation,
        precision=lax.Precision.HIGHEST,
        preferred_element_type=single,
    )
    total_bias = jnp.sum(all_modulation, axis=0)
    sums = [
        lax.psum(part.astype(narrow), "items").astype(single)
        for part in (
            rows_here(grad_qkv, 3),
            grad_out,
            grad_text,
            rows_here(grad_gu, 2),
            grad_down,
        )
    ]
    return (
        output.reshape(1, items * slots, width),
        grad_x.reshape(1, items * slots, width),
        *sums,
        final_ada,
        total_gains,
        total_gate,
        total_bias,
        total_text_gain,
    )


def per_device(*arrays):
    heads = arrays[14].shape[0]
    plan = gathered_plan if heads % lax.axis_size("rows") else head_parallel_plan
    return plan(*arrays)


def solution(mesh):
    in_specs = (
        P("items", "rows", None),
        P("items", "rows", None),
        P("items", None, "rows", None),
        P("items", None, None),
        P("items", "rows", None),
        P("items", None),
        P("items", None),
        P("rows", None),
        P("rows", None),
        P("rows", None),
        P("rows", None),
        P("rows", None),
        P("rows", None),
        P(),
        P(),
        P(),
        P(),
    )
    out_specs = (
        P("items", "rows", None),
        P("items", "rows", None),
        P("rows", None),
        P("rows", None),
        P("rows", None),
        P("rows", None),
        P("rows", None),
        P("rows", None),
        P(),
        P(),
        P(),
        P(),
    )
    return jax.shard_map(
        per_device, mesh=mesh, in_specs=in_specs, out_specs=out_specs, check_vma=False
    )
```

```python
import functools

import jax
import jax.numpy as jnp
from jax import lax
from jax.experimental import pallas as pl
from jax.experimental.pallas import tpu as pltpu
from jax.sharding import PartitionSpec as P

COLS = 32


epsilon = 1e-06
masked_score = -1e30
group_heads = 4


def norm_gain(values, scaling):
    return values * lax.rsqrt(jnp.mean(values * values, axis=-1, keepdims=True) + epsilon) * scaling


def pre_norm(values, shift_scale, scaling):
    return norm_gain(values, scaling) * (1.0 + shift_scale)


def post_add(residual, branch, gate_in, scaling):
    return residual + jnp.tanh(gate_in) * norm_gain(branch, scaling)


def swiglu(gate_up):
    middle_col = gate_up.shape[-1] // 2
    return jax.nn.silu(gate_up[..., :middle_col]) * gate_up[..., middle_col:]


def freq_rates(number):
    return 10000.0 ** (-jnp.arange(number).astype(jnp.float32) / number)


def rotary_angles(frame_index, frame_row, column, head_size):
    frame_pairs = head_size // 8
    space_pairs = (head_size // 2 - frame_pairs) // 2
    return jnp.concatenate(
        [
            frame_index.astype(jnp.float32)[..., None] * freq_rates(frame_pairs),
            frame_row.astype(jnp.float32)[..., None] * freq_rates(space_pairs),
            column.astype(jnp.float32)[..., None] * freq_rates(space_pairs),
        ],
        axis=-1,
    )


def rotate(values, cos_table, sin_table, head_count):
    shaped = values.reshape(values.shape[:-1] + (head_count, values.shape[-1] // head_count))
    half_size = shaped.shape[-1] // 2
    upper_half = shaped[..., :half_size]
    lower_half = shaped[..., half_size:]
    cos_heads = cos_table[..., None, :]
    sin_heads = sin_table[..., None, :]
    turned = jnp.concatenate(
        [
            upper_half * cos_heads - lower_half * sin_heads,
            upper_half * sin_heads + lower_half * cos_heads,
        ],
        axis=-1,
    )
    return turned.reshape(values.shape)


def text_split(projected, key_gain):
    half_cols = projected.shape[-1] // 2
    return (norm_gain(projected[..., :half_cols], key_gain), projected[..., half_cols:])


def gathered_plan(
    hidden_in,
    cotangent,
    text_states,
    time_embed,
    live_rows,
    frame_rows,
    text_len,
    w_qkv,
    w_out,
    w_text,
    w_gu,
    w_down,
    w_ada,
    gains,
    cross_gate,
    ada_bias,
    text_gain,
):
    single = jnp.float32
    narrow = jnp.bfloat16
    model_width = hidden_in.shape[2]
    head_count = cross_gate.shape[0]
    head_size = model_width // head_count
    score_scale = head_size ** (-0.5)
    item_count = time_embed.shape[1]
    item_slots = hidden_in.shape[1] // item_count
    row_devices = lax.axis_size("rows")
    seq_len = row_devices * item_slots
    text_local = text_states.shape[2]
    text_all = text_local * row_devices
    text_width = text_states.shape[3]
    group_span = group_heads * head_size
    block_count = head_count // group_heads
    token_count = item_count * item_slots

    def weight_term(left, right, accuracy):
        return jnp.einsum(
            "tk,tn->kn", left, right, precision=accuracy, preferred_element_type=single
        )

    def reduce_term(term):
        return lax.psum_scatter(
            term.astype(jnp.bfloat16), "rows", scatter_dimension=0, tiled=True
        ).astype(jnp.float32)

    full_qkv, full_out, full_text, full_gu, full_down, full_ada = (
        lax.all_gather(w_qkv, "rows", axis=0, tiled=True),
        lax.all_gather(w_out, "rows", axis=0, tiled=True),
        lax.all_gather(w_text, "rows", axis=0, tiled=True),
        lax.all_gather(w_gu, "rows", axis=0, tiled=True),
        lax.all_gather(w_down, "rows", axis=0, tiled=True),
        lax.all_gather(w_ada, "rows", axis=0, tiled=True),
    )
    counts_here = live_rows[0]
    every_count = lax.all_gather(counts_here, "rows", axis=0, tiled=True)
    device_place = lax.axis_index("rows")
    ranks = jnp.arange(row_devices)
    rows_below = jnp.sum(jnp.where(ranks[:, None] < device_place, every_count, 0), axis=0)
    slot_row = jnp.arange(item_slots) // COLS
    column = jnp.arange(item_slots) % COLS
    row_index = rows_below[:, None] + slot_row[None, :]
    heights = frame_rows[0][:, None]
    frame_index = row_index // heights
    frame_row = row_index % heights
    live_mask = (slot_row[None, :] < counts_here[0][:, None]).astype(single)
    key_live = (slot_row[None, None, :] < jnp.transpose(every_count)[:, :, None]).reshape(
        item_count, seq_len
    )
    text_live = jnp.arange(text_all)[None, :] < text_len[0][:, None]
    angles = rotary_angles(
        frame_index, frame_row, jnp.broadcast_to(column, row_index.shape), head_size
    )
    cos_table = jnp.cos(angles)
    sin_table = jnp.sin(angles)

    def qkv_split(projected, gain_query, gain_key):
        queries = rotate(
            norm_gain(projected[..., :model_width], gain_query), cos_table, sin_table, head_count
        )
        keys_here = rotate(
            norm_gain(projected[..., model_width : 2 * model_width], gain_key),
            cos_table,
            sin_table,
            head_count,
        )
        return (queries, keys_here, projected[..., 2 * model_width :])

    states = hidden_in[0].reshape(item_count, item_slots, model_width)
    time_silu = jax.nn.silu(time_embed[0].astype(single)).astype(narrow)
    modulation = jnp.dot(time_silu, full_ada, preferred_element_type=single) + ada_bias
    scale_attn = modulation[:, None, 0:model_width]
    gate_attn = modulation[:, None, model_width : 2 * model_width]
    scale_ffn = modulation[:, None, 2 * model_width : 3 * model_width]
    gate_ffn = modulation[:, None, 3 * model_width :]
    attn_in = (
        pre_norm(states, scale_attn, gains[0]).astype(narrow).reshape(token_count, model_width)
    )
    qkv_proj = jnp.dot(attn_in, full_qkv, preferred_element_type=single).reshape(
        item_count, item_slots, 3 * model_width
    )
    query_full, key_full, value_full = qkv_split(qkv_proj, gains[1], gains[2])
    query_low = query_full.astype(narrow)
    key_low = key_full.astype(narrow)
    value_low = value_full.astype(narrow)
    text_float = text_states[0].astype(single)
    text_norm = norm_gain(text_float, text_gain).astype(narrow)
    text_proj = jnp.einsum("ctd,dn->ctn", text_norm, full_text, preferred_element_type=single)
    tkey_full, tval_full = text_split(text_proj, gains[6])
    key_all, value_all, tkey_all, tval_all = (
        lax.all_gather(key_low, "rows", axis=1, tiled=True),
        lax.all_gather(value_low, "rows", axis=1, tiled=True),
        lax.all_gather(tkey_full.astype(narrow), "rows", axis=1, tiled=True),
        lax.all_gather(tval_full.astype(narrow), "rows", axis=1, tiled=True),
    )

    def block_slices(block_index, key_source, value_source):
        offset = block_index * group_span
        query_part = lax.dynamic_slice_in_dim(query_low, offset, group_span, 2).reshape(
            item_count, item_slots, group_heads, head_size
        )
        key_part = lax.dynamic_slice_in_dim(key_source, offset, group_span, 2).reshape(
            item_count, seq_len, group_heads, head_size
        )
        value_part = lax.dynamic_slice_in_dim(value_source, offset, group_span, 2).reshape(
            item_count, seq_len, group_heads, head_size
        )
        return (query_part, key_part, value_part)

    def self_step(carry, block_index):
        query_part, key_part, value_part = block_slices(block_index, key_all, value_all)
        scores = (
            jnp.einsum("iphe,ikhe->ihpk", query_part, key_part, preferred_element_type=single)
            * score_scale
        )
        scores = jnp.where(key_live[:, None, None, :], scores, masked_score)
        row_max = jnp.max(scores, axis=-1, keepdims=True)
        exp_terms = jnp.exp(scores - row_max)
        exp_total = jnp.sum(exp_terms, axis=-1, keepdims=True)
        probs_low = (exp_terms / exp_total).astype(narrow)
        attended = jnp.einsum(
            "ihpk,ikhe->iphe", probs_low, value_part, preferred_element_type=single
        )
        return (
            carry,
            (
                attended.reshape(item_count, item_slots, group_span),
                (row_max + jnp.log(exp_total))[..., 0],
            ),
        )

    _, (self_parts, log_totals) = lax.scan(
        self_step, jnp.zeros((), single), jnp.arange(block_count)
    )

    def heads_last(parts):
        return jnp.transpose(parts, (1, 2, 0, 3)).reshape(item_count, item_slots, model_width)

    self_out = heads_last(self_parts)
    query_heads = query_low.reshape(item_count, item_slots, head_count, head_size)
    tkey_heads = tkey_all.reshape(item_count, text_all, head_count, head_size)
    tval_heads = tval_all.reshape(item_count, text_all, head_count, head_size)
    cross_scores = (
        jnp.einsum("iphe,ikhe->ihpk", query_heads, tkey_heads, preferred_element_type=single)
        * score_scale
    )
    cross_scores = jnp.where(text_live[:, None, None, :], cross_scores, masked_score)
    cross_max = jnp.max(cross_scores, axis=-1, keepdims=True)
    cross_exp = jnp.exp(cross_scores - cross_max)
    cross_probs = cross_exp / jnp.sum(cross_exp, axis=-1, keepdims=True)
    cross_low = cross_probs.astype(narrow)
    cross_out = jnp.einsum("ihpk,ikhe->iphe", cross_low, tval_heads, preferred_element_type=single)
    tanh_gate = jnp.tanh(cross_gate)
    combined = (
        self_out.reshape(item_count, item_slots, head_count, head_size)
        + tanh_gate[:, None] * cross_out
    )
    combined = combined.reshape(token_count, model_width).astype(narrow)
    projected = jnp.dot(combined, full_out, preferred_element_type=single).reshape(
        item_count, item_slots, model_width
    )
    middle = post_add(states, projected, gate_attn, gains[3])
    ffn_in = pre_norm(middle, scale_ffn, gains[4]).astype(narrow).reshape(token_count, model_width)
    gate_up = jnp.dot(ffn_in, full_gu, preferred_element_type=single)
    inner_act = swiglu(gate_up).astype(narrow)
    ffn_out = jnp.dot(inner_act, full_down, preferred_element_type=single).reshape(
        item_count, item_slots, model_width
    )
    result = post_add(middle, ffn_out, gate_ffn, gains[5])
    output = (live_mask[..., None] * result).reshape(1, token_count, model_width)
    grad_result = live_mask[..., None] * cotangent[0].reshape(item_count, item_slots, model_width)
    _, back_ffn_out = jax.vjp(post_add, middle, ffn_out, gate_ffn, gains[5])
    grad_middle, grad_ffn_out, grad_gate_ffn, grad_gain_five = back_ffn_out(grad_result)
    ffn_low = grad_ffn_out.astype(narrow).reshape(token_count, model_width)
    shard_down = reduce_term(weight_term(inner_act, ffn_low, None))
    grad_inner = jnp.einsum("tn,kn->tk", ffn_low, full_down, preferred_element_type=single)
    _, back_glu = jax.vjp(swiglu, gate_up)
    gate_up_low = back_glu(grad_inner)[0].astype(narrow)
    shard_gu = reduce_term(weight_term(ffn_in, gate_up_low, None))
    grad_ffn_in = jnp.einsum("tn,kn->tk", gate_up_low, full_gu, preferred_element_type=single)
    _, back_ffn_in = jax.vjp(pre_norm, middle, scale_ffn, gains[4])
    part_middle, grad_scale_ffn, grad_gain_four = back_ffn_in(
        grad_ffn_in.reshape(item_count, item_slots, model_width)
    )
    grad_middle = grad_middle + part_middle
    _, back_attn_out = jax.vjp(post_add, states, projected, gate_attn, gains[3])
    grad_hidden, grad_projected, grad_gate_attn, grad_gain_three = back_attn_out(grad_middle)
    projected_low = grad_projected.astype(narrow).reshape(token_count, model_width)
    shard_out = reduce_term(weight_term(combined, projected_low, None))
    grad_combined = jnp.einsum("tn,kn->tk", projected_low, full_out, preferred_element_type=single)
    grad_combined = grad_combined.reshape(item_count, item_slots, head_count, head_size)
    self_low = grad_combined.reshape(item_count, item_slots, model_width).astype(narrow)
    cross_grad_low = (tanh_gate[:, None] * grad_combined).astype(narrow)
    grad_cross_gate = (1.0 - tanh_gate * tanh_gate) * jnp.sum(
        grad_combined * cross_out, axis=(0, 1, 3)
    )

    def self_back(carry, packed):
        block_index, log_total = packed
        query_part, key_part, value_part = block_slices(block_index, key_all, value_all)
        offset = block_index * group_span
        grad_part = lax.dynamic_slice_in_dim(self_low, offset, group_span, 2).reshape(
            item_count, item_slots, group_heads, head_size
        )
        scores = (
            jnp.einsum("iphe,ikhe->ihpk", query_part, key_part, preferred_element_type=single)
            * score_scale
        )
        scores = jnp.where(key_live[:, None, None, :], scores, masked_score)
        attn_probs = jnp.exp(scores - log_total[..., None])
        grad_probs = jnp.einsum(
            "iphe,ikhe->ihpk", grad_part, value_part, preferred_element_type=single
        )
        row_inner = jnp.sum(attn_probs * grad_probs, axis=-1, keepdims=True)
        score_low = (attn_probs * (grad_probs - row_inner)).astype(narrow)
        grad_query = (
            jnp.einsum("ihpk,ikhe->iphe", score_low, key_part, preferred_element_type=single)
            * score_scale
        )
        grad_value = jnp.einsum(
            "ihpk,iphe->ikhe", attn_probs.astype(narrow), grad_part, preferred_element_type=single
        )
        grad_key = (
            jnp.einsum("ihpk,iphe->ikhe", score_low, query_part, preferred_element_type=single)
            * score_scale
        )
        owned_key, owned_value = (
            lax.psum_scatter(
                grad_key.reshape(item_count, seq_len, group_span).astype(jnp.bfloat16),
                "rows",
                scatter_dimension=1,
                tiled=True,
            ).astype(jnp.float32),
            lax.psum_scatter(
                grad_value.reshape(item_count, seq_len, group_span).astype(jnp.bfloat16),
                "rows",
                scatter_dimension=1,
                tiled=True,
            ).astype(jnp.float32),
        )
        return (
            carry,
            (grad_query.reshape(item_count, item_slots, group_span), owned_key, owned_value),
        )

    _, (query_parts, key_parts, value_parts) = lax.scan(
        self_back, jnp.zeros((), single), (jnp.arange(block_count), log_totals)
    )
    cross_grad_probs = jnp.einsum(
        "iphe,ikhe->ihpk", cross_grad_low, tval_heads, preferred_element_type=single
    )
    cross_inner = jnp.sum(cross_probs * cross_grad_probs, axis=-1, keepdims=True)
    cross_score_low = (cross_probs * (cross_grad_probs - cross_inner)).astype(narrow)
    grad_query_cross = (
        jnp.einsum("ihpk,ikhe->iphe", cross_score_low, tkey_heads, preferred_element_type=single)
        * score_scale
    )
    grad_text_key = (
        jnp.einsum("ihpk,iphe->ikhe", cross_score_low, query_heads, preferred_element_type=single)
        * score_scale
    )
    grad_text_value = jnp.einsum(
        "ihpk,iphe->ikhe", cross_low, cross_grad_low, preferred_element_type=single
    )
    owned_tkey, owned_tval = (
        lax.psum_scatter(
            grad_text_key.reshape(item_count, text_all, model_width).astype(jnp.bfloat16),
            "rows",
            scatter_dimension=1,
            tiled=True,
        ).astype(jnp.float32),
        lax.psum_scatter(
            grad_text_value.reshape(item_count, text_all, model_width).astype(jnp.bfloat16),
            "rows",
            scatter_dimension=1,
            tiled=True,
        ).astype(jnp.float32),
    )
    grad_query_all = heads_last(query_parts) + grad_query_cross.reshape(
        item_count, item_slots, model_width
    )
    _, back_qkv = jax.vjp(qkv_split, qkv_proj, gains[1], gains[2])
    grad_qkv, grad_gain_one, grad_gain_two = back_qkv(
        (grad_query_all, heads_last(key_parts), heads_last(value_parts))
    )
    qkv_low = grad_qkv.astype(narrow).reshape(token_count, 3 * model_width)
    shard_qkv = reduce_term(weight_term(attn_in, qkv_low, None))
    grad_attn_in = jnp.einsum("tn,kn->tk", qkv_low, full_qkv, preferred_element_type=single)
    _, back_attn_in = jax.vjp(pre_norm, states, scale_attn, gains[0])
    part_states, grad_scale_attn, grad_gain_zero = back_attn_in(
        grad_attn_in.reshape(item_count, item_slots, model_width)
    )
    grad_x = (grad_hidden + part_states).reshape(1, token_count, model_width)
    _, back_text = jax.vjp(text_split, text_proj, gains[6])
    grad_text_proj, grad_gain_six = back_text((owned_tkey, owned_tval))
    text_low = grad_text_proj.astype(narrow).reshape(item_count * text_local, 2 * model_width)
    shard_text = reduce_term(
        weight_term(text_norm.reshape(item_count * text_local, text_width), text_low, None)
    )
    grad_text_norm = jnp.einsum("tn,kn->tk", text_low, full_text, preferred_element_type=single)
    _, back_text_norm = jax.vjp(norm_gain, text_float, text_gain)
    grad_text_gain = back_text_norm(grad_text_norm.reshape(text_float.shape))[1]
    grad_modulation = jnp.concatenate(
        [grad_scale_attn, grad_gate_attn, grad_scale_ffn, grad_gate_ffn], axis=-1
    )[:, 0, :]
    shard_ada = reduce_term(
        weight_term(time_silu.astype(single), grad_modulation, lax.Precision.HIGHEST)
    )
    grad_ada_bias = jnp.sum(grad_modulation, axis=0)
    grad_gains = jnp.stack(
        [
            grad_gain_zero,
            grad_gain_one,
            grad_gain_two,
            grad_gain_three,
            grad_gain_four,
            grad_gain_five,
            grad_gain_six,
        ],
        axis=0,
    )
    final_qkv, final_out, final_text, final_gu, final_down, final_ada = (
        lax.psum(shard_qkv.astype(jnp.bfloat16), "items").astype(jnp.float32),
        lax.psum(shard_out.astype(jnp.bfloat16), "items").astype(jnp.float32),
        lax.psum(shard_text.astype(jnp.bfloat16), "items").astype(jnp.float32),
        lax.psum(shard_gu.astype(jnp.bfloat16), "items").astype(jnp.float32),
        lax.psum(shard_down.astype(jnp.bfloat16), "items").astype(jnp.float32),
        lax.psum(shard_ada.astype(jnp.bfloat16), "items").astype(jnp.float32),
    )
    total_gains, total_gate, total_bias, total_text_gain = lax.psum(
        (grad_gains, grad_cross_gate, grad_ada_bias, grad_text_gain), ("items", "rows")
    )
    return (
        output,
        grad_x,
        final_qkv,
        final_out,
        final_text,
        final_gu,
        final_down,
        final_ada,
        total_gains,
        total_gate,
        total_bias,
        total_text_gain,
    )


def norm_parts(values):
    inverse = lax.rsqrt(jnp.mean(values * values, axis=-1, keepdims=True) + epsilon)
    return values * inverse, inverse


def norm_back(unit, inverse, scaled_grad):
    return inverse * (scaled_grad - unit * jnp.mean(scaled_grad * unit, axis=-1, keepdims=True))


MESH = pl.DeviceIdType.MESH
DEPTH, BREADTH = 4, 2


def row_place():
    place = lax.axis_index("rows")
    return place // BREADTH, lax.rem(place, BREADTH)


def on_rows(line, side):
    return {"rows": line * BREADTH + side}


def greet(devices):
    barrier = pltpu.get_barrier_semaphore()
    for condition, device in devices:

        @pl.when(condition)
        def _(device=device):
            pl.semaphore_signal(barrier, inc=1, device_id=device, device_id_type=MESH)

    count = 0
    for condition, _ in devices:
        count = count + jnp.where(condition, 1, 0)
    pl.semaphore_wait(barrier, count)


def remote(source, target, send, receive, device):
    return pltpu.make_async_remote_copy(
        src_ref=source,
        dst_ref=target,
        send_sem=send,
        recv_sem=receive,
        device_id=device,
        device_id_type=MESH,
    )


def shard_of(ref, place, axis):
    return ref.at[place] if axis == 0 else ref.at[:, place]


def gather_kernel(axis, count, own, *rest):
    whole, local, z_send, z_recv, x_send, x_recv = rest[count:]
    line, side = row_place()
    above, below, across = on_rows(line + 1, side), on_rows(line - 1, side), on_rows(line, 1 - side)
    has_above, has_below = line < DEPTH - 1, line > 0
    greet([(has_above, above), (has_below, below), (line >= 0, across)])

    def block(at, which):
        return shard_of(whole, at * BREADTH + which, axis)

    def pass_on(source, at, way, device):
        return remote(source, block(at, side), z_send.at[way, at], z_recv.at[at], device)

    def cross(source, at):
        return remote(source, block(at, side), x_send.at[at], x_recv.at[at], across)

    cross(own, line).start()

    @pl.when(has_above)
    def _():
        pass_on(own, line, 0, above).start()

    @pl.when(has_below)
    def _():
        pass_on(own, line, 1, below).start()

    keep = pltpu.make_async_copy(own, block(line, side), local)
    keep.start()
    for step in range(1, DEPTH):

        @pl.when(line - step >= 0)
        def _(at=line - step):
            pass_on(own, at, 0, below).wait_recv()

            @pl.when(has_above)
            def _():
                pass_on(block(at, side), at, 0, above).start()

            cross(block(at, side), at).start()

        @pl.when(line + step < DEPTH)
        def _(at=line + step):
            pass_on(own, at, 1, above).wait_recv()

            @pl.when(has_below)
            def _():
                pass_on(block(at, side), at, 1, below).start()

            cross(block(at, side), at).start()

    keep.wait()
    for at in range(DEPTH):
        cross(own, at).wait_recv()
        cross(own, at).wait_send()

        @pl.when(has_above & (at <= line))
        def _(at=at):
            pass_on(own, at, 0, above).wait_send()

        @pl.when(has_below & (at >= line))
        def _(at=at):
            pass_on(own, at, 1, below).wait_send()


def gather_rows(block, ident, axis, after=()):
    ranks = DEPTH * BREADTH
    shape = block.shape[:axis] + (ranks,) + block.shape[axis:]
    anywhere = pl.BlockSpec(memory_space=pl.ANY)
    return pl.pallas_call(
        functools.partial(gather_kernel, axis, len(after)),
        out_shape=jax.ShapeDtypeStruct(shape, block.dtype),
        in_specs=[anywhere] * (1 + len(after)),
        out_specs=anywhere,
        scratch_shapes=[
            pltpu.SemaphoreType.DMA,
            pltpu.SemaphoreType.DMA((2, DEPTH)),
            pltpu.SemaphoreType.DMA((DEPTH,)),
            pltpu.SemaphoreType.DMA((DEPTH,)),
            pltpu.SemaphoreType.DMA((DEPTH,)),
        ],
        name=f"gather_rows_{ident}",
        compiler_params=pltpu.CompilerParams(collective_id=ident, has_side_effects=True),
    )(block, *after)


def scatter_kernel(axis, count, parts, *rest):
    total, crossed, risen, sunk, up, down, x_send, x_recv, z_send, z_recv = rest[count:]
    line, side = row_place()
    above, below, across = on_rows(line + 1, side), on_rows(line - 1, side), on_rows(line, 1 - side)
    has_above, has_below = line < DEPTH - 1, line > 0
    greet([(has_above, above), (has_below, below), (line >= 0, across)])

    def part(at, which):
        return shard_of(parts, at * BREADTH + which, axis)

    def cross(at):
        return remote(part(at, 1 - side), crossed.at[at], x_send.at[at], x_recv.at[at], across)

    def rise(at):
        return remote(up.at[at], risen.at[at], z_send.at[0, at], z_recv.at[0, at], above)

    def sink(at):
        return remote(down.at[at], sunk.at[at], z_send.at[1, at], z_recv.at[1, at], below)

    def add_up(at, others, target):
        mine = part(at, side)
        whole = mine.shape
        value = mine[...].astype(jnp.float32) + crossed[at].astype(jnp.float32)
        for other in others:
            value = value + other[at].astype(jnp.float32)
        target[...] = value.astype(target.dtype)

    for step in range(DEPTH - 1, 0, -1):
        for at, there in ((line + step, line + step < DEPTH), (line - step, line - step >= 0)):

            @pl.when(there)
            def _(at=at):
                cross(at).start()

    cross(line).start()
    for step in range(DEPTH - 1, 0, -1):

        @pl.when(line + step < DEPTH)
        def _(at=line + step):
            cross(at).wait_recv()

            @pl.when(has_below)
            def _():
                rise(at).wait_recv()
                add_up(at, [risen], up.at[at])

            @pl.when(jnp.logical_not(has_below))
            def _():
                add_up(at, [], up.at[at])

            rise(at).start()

        @pl.when(line - step >= 0)
        def _(at=line - step):
            cross(at).wait_recv()

            @pl.when(has_above)
            def _():
                sink(at).wait_recv()
                add_up(at, [sunk], down.at[at])

            @pl.when(jnp.logical_not(has_above))
            def _():
                add_up(at, [], down.at[at])

            sink(at).start()

    cross(line).wait_recv()

    @pl.when(has_below & has_above)
    def _():
        rise(line).wait_recv()
        sink(line).wait_recv()
        add_up(line, [risen, sunk], total)

    @pl.when(jnp.logical_not(has_above))
    def _():
        rise(line).wait_recv()
        add_up(line, [risen], total)

    @pl.when(jnp.logical_not(has_below))
    def _():
        sink(line).wait_recv()
        add_up(line, [sunk], total)

    for at in range(DEPTH):
        cross(at).wait_send()

        @pl.when(at > line)
        def _(at=at):
            rise(at).wait_send()

        @pl.when(at < line)
        def _(at=at):
            sink(at).wait_send()


def scatter_rows(parts, ident, axis, after=()):
    shape = parts.shape[:axis] + parts.shape[axis + 1 :]
    near = pl.BlockSpec(memory_space=pltpu.VMEM)
    slots = pltpu.VMEM((DEPTH,) + shape, parts.dtype)
    return pl.pallas_call(
        functools.partial(scatter_kernel, axis, len(after)),
        out_shape=jax.ShapeDtypeStruct(shape, jnp.float32),
        in_specs=[near] + [pl.BlockSpec(memory_space=pl.ANY)] * len(after),
        out_specs=near,
        scratch_shapes=[slots] * 5
        + [
            pltpu.SemaphoreType.DMA((DEPTH,)),
            pltpu.SemaphoreType.DMA((DEPTH,)),
            pltpu.SemaphoreType.DMA((2, DEPTH)),
            pltpu.SemaphoreType.DMA((2, DEPTH)),
        ],
        name=f"scatter_rows_{ident}",
        compiler_params=pltpu.CompilerParams(
            collective_id=ident, has_side_effects=True, vmem_limit_bytes=32 << 20
        ),
    )(parts, *after)


def sum_kernel(own, total, held, send, receive):
    ranks = DEPTH * BREADTH
    place = lax.axis_index("rows")
    others = [lax.rem(place + step, ranks) for step in range(1, ranks)]
    greet([(place >= 0, {"rows": other}) for other in others])

    def push(step, other, slot):
        return remote(own, held.at[slot], send.at[step], receive.at[slot], {"rows": other})

    for step, other in enumerate(others):
        push(step, other, place).start()
    held[pl.ds(place, 1)] = own[...][None]
    for step, other in enumerate(others):
        push(step, other, other).wait_recv()
    value = held[0]
    for rank in range(1, ranks):
        value = value + held[rank]
    total[...] = value
    for step, other in enumerate(others):
        push(step, other, place).wait_send()


def sum_rows(own, ident):
    ranks = DEPTH * BREADTH
    near = pl.BlockSpec(memory_space=pltpu.VMEM)
    return pl.pallas_call(
        sum_kernel,
        out_shape=jax.ShapeDtypeStruct(own.shape, own.dtype),
        in_specs=[near],
        out_specs=near,
        scratch_shapes=[
            pltpu.VMEM((ranks,) + own.shape, own.dtype),
            pltpu.SemaphoreType.DMA((ranks,)),
            pltpu.SemaphoreType.DMA((ranks,)),
        ],
        name=f"sum_rows_{ident}",
        compiler_params=pltpu.CompilerParams(collective_id=ident, has_side_effects=True),
    )(own)


def final_kernel(ranks, groups, sums, own, out, held, kept, part, h_send, h_recv, g_send, g_recv, o_send, o_recv):
    place, group = lax.axis_index("rows"), lax.axis_index("items")
    rows = [lax.rem(place + step, ranks) for step in range(1, ranks)]
    items = [lax.rem(group + step, groups) for step in range(1, groups)]
    greet([(place >= 0, {"rows": other}) for other in rows] + [(place >= 0, {"items": other}) for other in items])

    def push(step, other, slot):
        return remote(own.at[other], held.at[slot], h_send.at[step], h_recv.at[slot], {"rows": other})

    def swap(step, other, slot):
        return remote(part, kept.at[slot], g_send.at[step], g_recv.at[slot], {"items": other})

    def share(step, other, slot):
        return remote(out.at[place], out.at[slot], o_send.at[step], o_recv.at[slot], {"rows": other})

    for step, other in enumerate(rows):
        push(step, other, place).start()
    held[pl.ds(place, 1)] = own[pl.ds(place, 1)]
    for step, other in enumerate(rows):
        push(step, other, other).wait_recv()
    value = held[0]
    for rank in range(1, ranks):
        value = value + held[rank]
    part[...] = value
    for step, other in enumerate(items):
        swap(step, other, group).start()
    kept[pl.ds(group, 1)] = value[None]
    for step, other in enumerate(items):
        swap(step, other, other).wait_recv()
    total = kept[0, :sums]
    for item in range(1, groups):
        total = total + kept[item, :sums]
    depth = own.shape[1] - sums
    out[pl.ds(place, 1), :sums] = total[None]
    for item in range(groups):
        out[pl.ds(place, 1), sums + item * depth : sums + (item + 1) * depth] = kept[item, sums:][None]
    for step, other in enumerate(rows):
        share(step, other, place).start()
    for step, other in enumerate(rows):
        share(step, other, other).wait_recv()
    for step, other in enumerate(rows):
        push(step, other, place).wait_send()
        share(step, other, place).wait_send()
    for step, other in enumerate(items):
        swap(step, other, group).wait_send()


def final_sums(own, sums, ident):
    ranks, groups = lax.axis_size("rows"), lax.axis_size("items")
    near = pl.BlockSpec(memory_space=pltpu.VMEM)
    depth = own.shape[1]
    return pl.pallas_call(
        functools.partial(final_kernel, ranks, groups, sums),
        out_shape=jax.ShapeDtypeStruct((ranks, sums + groups * (depth - sums), 128), own.dtype),
        in_specs=[near],
        out_specs=near,
        scratch_shapes=[
            pltpu.VMEM(own.shape, own.dtype),
            pltpu.VMEM((groups,) + own.shape[1:], own.dtype),
            pltpu.VMEM(own.shape[1:], own.dtype),
            pltpu.SemaphoreType.DMA((ranks,)),
            pltpu.SemaphoreType.DMA((ranks,)),
            pltpu.SemaphoreType.DMA((groups,)),
            pltpu.SemaphoreType.DMA((groups,)),
            pltpu.SemaphoreType.DMA((ranks,)),
            pltpu.SemaphoreType.DMA((ranks,)),
        ],
        name=f"final_sums_{ident}",
        compiler_params=pltpu.CompilerParams(collective_id=ident, has_side_effects=True),
    )(own)


def first_kernel(
    ranks, quarters, own, qkv, text, total, qkv_out, text_out, held, packed, local,
    s_send, s_recv, t_send, t_recv, a_send, a_recv, y_send, y_recv, c_send, c_recv,
):
    place, group = lax.axis_index("rows"), lax.axis_index("items")
    others = [lax.rem(place + step, ranks) for step in range(1, ranks)]
    far = lax.rem(group + 2, 4)
    twin = group + 1 - 2 * lax.rem(group, 2)
    depth = qkv.shape[0] // quarters
    mine = pl.ds(pl.multiple_of(group * depth, 16), depth)
    fars = pl.ds(pl.multiple_of(far * depth, 16), depth)
    features = text_out.shape[-1]
    span = qkv.shape[1] // (3 * ranks)

    def columns(other):
        return pl.ds(pl.multiple_of(other * features, features), features)

    keeps = [pltpu.make_async_copy(text.at[:, :, columns(place)], text_out.at[place], local.at[0])]
    keeps[0].start()
    greet(
        [(place >= 0, {"rows": other}) for other in others]
        + [(place >= 0, {"items": far}), (place >= 0, {"items": twin})]
    )

    def sum_push(step, other, slot):
        return remote(own, held.at[slot], s_send.at[step], s_recv.at[slot], {"rows": other})

    def text_push(step, other, slot):
        return remote(
            text.at[:, :, columns(other)], text_out.at[slot], t_send.at[step], t_recv.at[slot], {"rows": other}
        )

    def push(step, other, slot):
        return remote(
            packed.at[other, mine], qkv_out.at[slot, mine], a_send.at[step], a_recv.at[slot], {"rows": other}
        )

    def pass_far(slot):
        block = qkv_out.at[slot, mine]
        return remote(block, block, y_send.at[slot], y_recv.at[slot], {"items": far})

    def pass_twin(which, slot):
        block = qkv_out.at[slot, fars if which else mine]
        return remote(block, block, c_send.at[which, slot], c_recv.at[which, slot], {"items": twin})

    for step, other in enumerate(others):
        sum_push(step, other, place).start()
    for rank in range(ranks):
        packed[rank] = jnp.concatenate(
            [
                qkv[:, (part * ranks + rank) * span : (part * ranks + rank + 1) * span]
                for part in range(3)
            ],
            axis=1,
        )
    for step, other in enumerate(others):
        push(step, other, place).start()
    for step, other in enumerate(others):
        text_push(step, other, place).start()
    keeps.append(pltpu.make_async_copy(packed.at[place], qkv_out.at[place], local.at[1]))
    keeps[1].start()
    held[pl.ds(place, 1)] = own[...][None]
    for step, other in enumerate(others):
        sum_push(step, other, other).wait_recv()
    value = held[0]
    for rank in range(1, ranks):
        value = value + held[rank]
    total[...] = value
    for step, other in enumerate(others):
        push(step, other, other).wait_recv()
        pass_far(other).start()
        pass_twin(0, other).start()
    for other in others:
        pass_far(other).wait_recv()
        pass_twin(1, other).start()
    for step, other in enumerate(others):
        sum_push(step, other, place).wait_send()
        text_push(step, other, other).wait_recv()
        text_push(step, other, place).wait_send()
        push(step, other, place).wait_send()
        pass_far(other).wait_send()
        for which in range(2):
            pass_twin(which, other).wait_recv()
            pass_twin(which, other).wait_send()
    for copy in keeps:
        copy.wait()


def first_transfers(own, qkv, text, ident):
    ranks, quarters = lax.axis_size("rows"), lax.axis_size("items")
    depth = qkv.shape[0]
    anywhere = pl.BlockSpec(memory_space=pl.ANY)
    near = pl.BlockSpec(memory_space=pltpu.VMEM)
    outs = [
        jax.ShapeDtypeStruct(own.shape, own.dtype),
        jax.ShapeDtypeStruct((ranks, depth, qkv.shape[1] // ranks), qkv.dtype),
        jax.ShapeDtypeStruct((ranks,) + text.shape[:-1] + (text.shape[-1] // ranks,), text.dtype),
    ]
    wave = pltpu.SemaphoreType.DMA
    return pl.pallas_call(
        functools.partial(first_kernel, ranks, quarters),
        out_shape=outs,
        in_specs=[near, near, anywhere],
        out_specs=[near, anywhere, anywhere],
        scratch_shapes=[
            pltpu.VMEM((ranks,) + own.shape, own.dtype),
            pltpu.VMEM(outs[1].shape, qkv.dtype),
            wave((2,)),
        ]
        + [wave((ranks,))] * 8
        + [wave((2, ranks))] * 2,
        name=f"first_transfers_{ident}",
        compiler_params=pltpu.CompilerParams(
            collective_id=ident, has_side_effects=True, vmem_limit_bytes=24 << 20
        ),
    )(own, qkv, text)


def pack_kernel(pieces, whole, packed):
    ranks, span = packed.shape[0], packed.shape[2] // pieces
    for rank in range(ranks):
        packed[rank] = jnp.concatenate(
            [whole[:, (piece * ranks + rank) * span : (piece * ranks + rank + 1) * span] for piece in range(pieces)],
            axis=1,
        ).astype(packed.dtype)


def pack_blocks(whole, pieces, ranks, dtype):
    near = pl.BlockSpec(memory_space=pltpu.VMEM)
    return pl.pallas_call(
        functools.partial(pack_kernel, pieces),
        out_shape=jax.ShapeDtypeStruct((ranks, whole.shape[0], whole.shape[1] // ranks), dtype),
        in_specs=[near],
        out_specs=near,
        name="pack_blocks",
        compiler_params=pltpu.CompilerParams(vmem_limit_bytes=24 << 20),
    )(whole)


def unpack_kernel(pieces, packed, whole):
    ranks, span = packed.shape[0], packed.shape[2] // pieces
    for piece in range(pieces):
        for rank in range(0, ranks, 2):
            start = (piece * ranks + rank) * span
            whole[:, start : start + 2 * span] = jnp.concatenate(
                [packed[rank + k, :, piece * span : (piece + 1) * span] for k in range(2)], axis=1
            ).astype(whole.dtype)


def unpack_blocks(packed, pieces, dtype):
    near = pl.BlockSpec(memory_space=pltpu.VMEM)
    ranks, rows, width = packed.shape
    return pl.pallas_call(
        functools.partial(unpack_kernel, pieces),
        out_shape=jax.ShapeDtypeStruct((rows, ranks * width), dtype),
        in_specs=[near],
        out_specs=near,
        name="unpack_blocks",
        compiler_params=pltpu.CompilerParams(vmem_limit_bytes=24 << 20),
    )(packed)


def halves_kernel(pieces, own, other, whole):
    ranks, half, span = own.shape[0], own.shape[1], own.shape[2] // pieces
    first = lax.rem(lax.axis_index("items"), 2) == 0
    for low in range(2):

        @pl.when(first == (low == 0))
        def _(low=low):
            for source, start in ((own, low * half), (other, (1 - low) * half)):
                for piece in range(pieces):
                    for rank in range(0, ranks, 2):
                        column = (piece * ranks + rank) * span
                        whole[start : start + half, column : column + 2 * span] = jnp.concatenate(
                            [source[rank + k, :, piece * span : (piece + 1) * span] for k in range(2)], axis=1
                        ).astype(whole.dtype)


def unpack_halves(own, other, pieces):
    near = pl.BlockSpec(memory_space=pltpu.VMEM)
    ranks, half, width = own.shape
    return pl.pallas_call(
        functools.partial(halves_kernel, pieces),
        out_shape=jax.ShapeDtypeStruct((2 * half, ranks * width), jnp.float32),
        in_specs=[near, near],
        out_specs=near,
        name="unpack_halves",
        compiler_params=pltpu.CompilerParams(vmem_limit_bytes=32 << 20),
    )(own, other)


def gather_tokens(block, ident, after=()):
    whole = gather_rows(block, ident, 1, after)
    return whole.reshape(-1, block.shape[-1])


def scatter_tokens(partial, items, ident, after=()):
    ranks = lax.axis_size("rows")
    blocks = partial.astype(jnp.bfloat16).reshape(items, ranks, -1, partial.shape[-1])
    return scatter_rows(blocks, ident, 1, after)


def lay_flat(vectors):
    flat = jnp.concatenate([vector.reshape(-1) for vector in vectors])
    rows = -(-flat.size // 1024) * 8
    return jnp.pad(flat, (0, rows * 128 - flat.size)).reshape(rows, 128)


def take_apart(total, vectors):
    flat, parts, start = total.reshape(-1), [], 0
    for vector in vectors:
        parts.append(flat[start : start + vector.size].reshape(vector.shape))
        start += vector.size
    return parts


def sum_vectors(vectors, ident):
    return take_apart(sum_rows(lay_flat(vectors), ident), vectors)


def first_sums(vectors, qkv, text, ident):
    total, qkv_here, text_in = first_transfers(lay_flat(vectors), qkv, text, ident)
    return take_apart(total, vectors), qkv_here, text_in


CORES = [(0, 1), (1, 0), (2, 3), (3, 2)]
FARS = [(0, 2), (1, 3), (2, 0), (3, 1)]


def swap(array, pairs):
    return lax.ppermute(array, "items", pairs)


def give_keep(grad, index, axis):
    keep = lax.dynamic_index_in_dim(grad, index, axis, keepdims=False)
    give = lax.dynamic_index_in_dim(grad, 1 - index, axis, keepdims=False)
    return give, keep


def add_low(one, other):
    return (one.astype(jnp.float32) + other.astype(jnp.float32)).astype(jnp.bfloat16)


def join(own, other, index, axis):
    shape = own.shape[:axis] + (2,) + own.shape[axis:]
    own, other = jnp.expand_dims(own, axis), jnp.expand_dims(other, axis)
    return jnp.where(lax.broadcasted_iota(jnp.int32, shape, axis) == index, own, other)


def head_parallel_plan(
    hidden_in,
    cotangent,
    text_states,
    time_embed,
    live_rows,
    frame_rows,
    text_len,
    w_qkv,
    w_out,
    w_text,
    w_gu,
    w_down,
    w_ada,
    gains,
    cross_gate,
    ada_bias,
    text_gain,
):
    single = jnp.float32
    narrow = jnp.bfloat16
    ranks = lax.axis_size("rows")
    place = lax.axis_index("rows")
    width = hidden_in.shape[2]
    heads = cross_gate.shape[0]
    head_size = width // heads
    score_scale = head_size ** (-0.5)
    items = time_embed.shape[1]
    slots = hidden_in.shape[1] // items
    row_slots = slots // COLS
    seq_len = ranks * slots
    text_local = text_states.shape[2]
    text_all = text_local * ranks
    text_width = text_states.shape[3]
    span = width // ranks
    heads_here = heads // ranks
    tokens = items * seq_len

    def dot(left, right):
        return jnp.dot(left, right, preferred_element_type=single)

    def dot_back(left, weight):
        return jnp.einsum("tn,kn->tk", left, weight, preferred_element_type=single)

    def weight_grad(left, right):
        return jnp.einsum("tk,tn->kn", left, right, preferred_element_type=single)

    time_silu = jax.nn.silu(time_embed[0].astype(single)).astype(narrow)
    ada_depth = w_ada.shape[0]
    time_here = lax.dynamic_slice_in_dim(time_silu, place * ada_depth, ada_depth, 1)

    def spread(part, whole):
        return lax.dynamic_update_slice_in_dim(
            jnp.zeros((whole,), single), part.reshape(-1), place * part.size, 0
        )

    group = lax.axis_index("items")
    core, far = lax.rem(group, 2), group // 2
    counts_here = live_rows[0]
    text_float = text_states[0].astype(single).reshape(items * text_local, text_width)
    text_inverse = norm_parts(text_float)[1]
    (modulation, counts, text_inverse), qkv_here, text_in = first_sums(
        [
            dot(time_here, w_ada),
            spread(counts_here.astype(single), ranks * items),
            spread(text_inverse, ranks * items * text_local),
        ],
        w_qkv,
        text_states[0],
        0,
    )
    qkv_here = qkv_here.reshape(width, -1)
    modulation = modulation + ada_bias
    counts = counts.astype(jnp.int32).reshape(ranks, items)
    text_inverse = text_inverse.reshape(-1, 1)
    scale_attn = modulation[:, None, 0:width]
    gate_attn = jnp.tanh(modulation[:, None, width : 2 * width])
    scale_ffn = modulation[:, None, 2 * width : 3 * width]
    gate_ffn = jnp.tanh(modulation[:, None, 3 * width :])

    below = jnp.cumsum(counts, axis=0) - counts
    slot_row = jnp.arange(row_slots)
    row_index = jnp.transpose(below)[:, :, None] + slot_row
    heights = frame_rows[0][:, None, None]
    frame_pairs = head_size // 8
    space_pairs = (head_size // 2 - frame_pairs) // 2
    row_angles = jnp.concatenate(
        [
            (row_index // heights).astype(single)[..., None] * freq_rates(frame_pairs),
            (row_index % heights).astype(single)[..., None] * freq_rates(space_pairs),
        ],
        axis=-1,
    )
    column_angles = jnp.arange(COLS).astype(single)[:, None] * freq_rates(space_pairs)

    def table(function):
        by_row = function(row_angles)
        by_column = function(column_angles)
        shape = (items, ranks, row_slots, COLS)
        whole = jnp.concatenate(
            [
                jnp.broadcast_to(by_row[:, :, :, None, :], shape + by_row.shape[-1:]),
                jnp.broadcast_to(by_column, shape + by_column.shape[-1:]),
            ],
            axis=-1,
        )
        return whole.reshape(tokens, 1, head_size // 2)

    cos_table = table(jnp.cos)
    sin_table = table(jnp.sin)

    def turn(values, sign):
        shaped = values.reshape(tokens, heads_here, head_size)
        upper = shaped[..., : head_size // 2]
        lower = shaped[..., head_size // 2 :]
        sines = sign * sin_table
        turned = jnp.concatenate(
            [upper * cos_table - lower * sines, upper * sines + lower * cos_table], axis=-1
        )
        return turned.reshape(tokens, width // ranks)

    slot_in_row = jnp.arange(slots) // COLS
    live_mask = (slot_in_row[None, :] < counts_here[0][:, None]).astype(single)[..., None]
    key_live = (slot_in_row < jnp.transpose(counts)[:, :, None]).reshape(items, seq_len)
    text_live = jnp.arange(text_all)[None, :] < text_len[0][:, None]

    def gain_here(index):
        return lax.dynamic_slice_in_dim(gains[index], place * span, span, 0)

    states = hidden_in[0].reshape(items, slots, width)
    unit_in, inverse_in = norm_parts(states)
    norm_in = unit_in * gains[0]
    attn_in = gather_tokens((norm_in * (1.0 + scale_attn)).astype(narrow), 1)
    hidden = w_down.shape[0]
    gu_depth = w_gu.shape[0] // 4
    gu_rows = lax.dynamic_slice_in_dim(w_gu, (2 * core + far) * gu_depth, gu_depth, 0)
    gu_rows = jnp.transpose(gu_rows.reshape(gu_depth, 2, ranks, hidden), (2, 0, 1, 3))
    gu_rows, attn_in = lax.optimization_barrier(
        (gu_rows.reshape(ranks, gu_depth, 2 * hidden), attn_in)
    )
    gu_part = lax.all_to_all(gu_rows, "rows", 0, 0, tiled=True)
    gu_pair = join(gu_part, swap(gu_part, FARS), far, 1)

    qkv_proj = dot(attn_in, qkv_here)
    query_proj, key_proj, value_proj = jnp.split(qkv_proj, 3, axis=1)

    features = text_width // ranks
    features = text_width // ranks
    text_in = text_in.reshape(items * text_all, features)
    text_unit = text_in.astype(single) * text_inverse
    gain_text = lax.dynamic_slice_in_dim(text_gain, place * features, features, 0)
    text_norm = (text_unit * gain_text).astype(narrow)

    def text_rows(values):
        shaped = values.reshape(ranks, items, text_local, -1)
        return jnp.swapaxes(shaped, 0, 1).reshape(items * text_all, -1)

    text_parts = pack_blocks(dot(text_norm, w_text).astype(narrow), 2, ranks, narrow)
    text_proj = scatter_rows(text_parts, 2, 0)
    tkey_proj, tval_proj = jnp.split(text_rows(text_proj), 2, axis=1)

    def squares(values):
        return jnp.sum(values * values, axis=-1)

    totals = sum_vectors([squares(query_proj), squares(key_proj), squares(tkey_proj)], 3)
    inverse_q, inverse_k, inverse_t = (
        lax.rsqrt(total / width + epsilon)[:, None] for total in totals
    )
    gain_q, gain_k, gain_t = gain_here(1), gain_here(2), gain_here(6)
    unit_q, unit_k, unit_t = query_proj * inverse_q, key_proj * inverse_k, tkey_proj * inverse_t

    def by_head(values):
        return values.reshape(items, -1, heads_here, head_size)

    query = by_head(turn(unit_q * gain_q, 1.0).astype(narrow))
    key = by_head(turn(unit_k * gain_k, 1.0).astype(narrow))
    value = by_head(value_proj.astype(narrow))
    tkey = by_head((unit_t * gain_t).astype(narrow))
    tval = by_head(tval_proj.astype(narrow))

    def soft(keys, mask):
        scores = jnp.einsum("iphe,ikhe->ihpk", query, keys, preferred_element_type=single)
        scores = jnp.where(mask[:, None, None, :], scores * score_scale, masked_score)
        terms = jnp.exp(scores - jnp.max(scores, axis=-1, keepdims=True))
        return terms / jnp.sum(terms, axis=-1, keepdims=True)

    def mix(weights, values):
        return jnp.einsum("ihpk,ikhe->iphe", weights, values, preferred_element_type=single)

    probs = soft(key, key_live)
    self_out = mix(probs.astype(narrow), value)
    cross_probs = soft(tkey, text_live)
    cross_out = mix(cross_probs.astype(narrow), tval)
    gate_here = jnp.tanh(lax.dynamic_slice_in_dim(cross_gate, place * heads_here, heads_here, 0))
    combined = (self_out + gate_here[:, None] * cross_out).astype(narrow).reshape(tokens, span)
    projected = scatter_tokens(dot(combined, w_out), items, 4)

    unit_proj, inverse_proj = norm_parts(projected)
    norm_proj = unit_proj * gains[3]
    middle = states + gate_attn * norm_proj
    unit_mid, inverse_mid = norm_parts(middle)
    norm_mid = unit_mid * gains[4]
    ffn_in = gather_tokens((norm_mid * (1.0 + scale_ffn)).astype(narrow), 5)
    gu_columns = join(gu_pair, swap(gu_pair, CORES), core, 1)
    gu_here = gu_columns.reshape(width, 2 * w_down.shape[0])
    gate_up = dot(ffn_in, gu_here)
    gate_part, up_part = jnp.split(gate_up, 2, axis=1)
    sigmoid = 1.0 / (1.0 + jnp.exp(-gate_part))
    inner_act = (gate_part * sigmoid * up_part).astype(narrow)
    ffn_out = scatter_tokens(dot(inner_act, w_down), items, 6)
    unit_ffn, inverse_ffn = norm_parts(ffn_out)
    norm_ffn = unit_ffn * gains[5]
    output = live_mask * (middle + gate_ffn * norm_ffn)

    def over_tokens(values):
        return jnp.sum(values, axis=(0, 1))

    grad_result = live_mask * cotangent[0].reshape(items, slots, width)
    grad_gate_ffn = (1.0 - gate_ffn * gate_ffn)[:, 0] * jnp.sum(grad_result * norm_ffn, axis=1)
    grad_norm = gate_ffn * grad_result
    grad_five = over_tokens(grad_norm * unit_ffn)
    ffn_low = gather_tokens(
        norm_back(unit_ffn, inverse_ffn, grad_norm * gains[5]).astype(narrow), 7
    )
    grad_down = weight_grad(inner_act, ffn_low).astype(narrow).reshape(2, -1, width)
    give_down, keep_down = give_keep(grad_down, core, 0)
    grad_inner = dot_back(ffn_low, w_down)
    gate_up_low = jnp.concatenate(
        [
            grad_inner * up_part * sigmoid * (1.0 + gate_part * (1.0 - sigmoid)),
            grad_inner * gate_part * sigmoid,
        ],
        axis=1,
    ).astype(narrow)
    grad_gu = weight_grad(ffn_in, gate_up_low).astype(narrow)
    give_gu, keep_gu = give_keep(grad_gu.reshape(ranks, 2, -1, 2 * hidden), core, 1)
    grad_ffn_in = scatter_tokens(
        dot_back(gate_up_low, gu_here), items, 8, after=(give_down, give_gu)
    )
    half_down = add_low(keep_down, swap(give_down, CORES))
    half_gu = add_low(keep_gu, swap(give_gu, CORES))
    give_gu, keep_gu = give_keep(half_gu.reshape(ranks, 2, -1, 2 * hidden), far, 1)
    grad_scale_ffn = jnp.sum(grad_ffn_in * norm_mid, axis=1)
    grad_norm = grad_ffn_in * (1.0 + scale_ffn)
    grad_four = over_tokens(grad_norm * unit_mid)
    grad_middle = grad_result + norm_back(unit_mid, inverse_mid, grad_norm * gains[4])

    grad_gate_attn = (1.0 - gate_attn * gate_attn)[:, 0] * jnp.sum(grad_middle * norm_proj, axis=1)
    grad_norm = gate_attn * grad_middle
    grad_three = over_tokens(grad_norm * unit_proj)
    projected_low = gather_tokens(
        norm_back(unit_proj, inverse_proj, grad_norm * gains[3]).astype(narrow),
        9,
        after=(half_down, give_gu),
    )
    sum_down = add_low(half_down, swap(half_down, FARS))
    sum_gu = add_low(keep_gu, swap(give_gu, FARS))
    rows_gu = lax.all_to_all(sum_gu, "rows", 0, 0, tiled=True)
    grad_out = weight_grad(combined, projected_low).astype(narrow).reshape(2, -1, width)
    give_out, keep_out = give_keep(grad_out, core, 0)
    grad_combined = by_head(dot_back(projected_low, w_out))
    self_low = grad_combined.astype(narrow)
    cross_grad_low = (gate_here[:, None] * grad_combined).astype(narrow)
    grad_gate = (1.0 - gate_here * gate_here) * jnp.sum(grad_combined * cross_out, axis=(0, 1, 3))

    def soft_back(weights, low_grad, keys, values):
        grad_weights = jnp.einsum(
            "iphe,ikhe->ihpk", low_grad, values, preferred_element_type=single
        )
        inner = jnp.sum(weights * grad_weights, axis=-1, keepdims=True)
        score_low = (weights * (grad_weights - inner)).astype(narrow)
        grad_values = jnp.einsum(
            "ihpk,iphe->ikhe", weights.astype(narrow), low_grad, preferred_element_type=single
        )
        grad_keys = jnp.einsum(
            "ihpk,iphe->ikhe", score_low, query, preferred_element_type=single
        )
        grad_queries = mix(score_low, keys)
        return (
            grad_queries * score_scale,
            (grad_keys * score_scale).reshape(-1, span),
            grad_values.reshape(-1, span),
        )

    grad_query, grad_key, grad_value = soft_back(probs, self_low, key, value)
    grad_query_text, grad_tkey, grad_tval = soft_back(cross_probs, cross_grad_low, tkey, tval)
    grad_query = (grad_query + grad_query_text).reshape(tokens, span)
    grad_query = turn(grad_query, -1.0)
    grad_key = turn(grad_key, -1.0)
    scaled_q, scaled_k, scaled_t = grad_query * gain_q, grad_key * gain_k, grad_tkey * gain_t
    mean_q, mean_k, mean_t = (
        total[:, None] / width
        for total in sum_vectors(
            [
                jnp.sum(scaled_q * unit_q, axis=-1),
                jnp.sum(scaled_k * unit_k, axis=-1),
                jnp.sum(scaled_t * unit_t, axis=-1),
            ],
            10,
        )
    )
    qkv_low = jnp.concatenate(
        [
            inverse_q * (scaled_q - unit_q * mean_q),
            inverse_k * (scaled_k - unit_k * mean_k),
            grad_value,
        ],
        axis=1,
    ).astype(narrow)
    text_low = jnp.concatenate(
        [inverse_t * (scaled_t - unit_t * mean_t), grad_tval], axis=1
    ).astype(narrow)
    grad_qkv = weight_grad(attn_in, qkv_low).astype(narrow)
    give_qkv, keep_qkv = give_keep(grad_qkv.reshape(ranks, 2, -1, 3 * span), core, 1)

    text_low = text_low.reshape(items, ranks, text_local, 2 * span)
    text_low = jnp.swapaxes(text_low, 0, 1).reshape(items * text_all, 2 * span)
    all_low = unpack_blocks(gather_rows(text_low, 12, 0, after=(give_qkv, give_out)), 2, narrow)
    half_out = add_low(keep_out, swap(give_out, CORES))
    half_qkv = add_low(keep_qkv, swap(give_qkv, CORES))
    give_qkv, keep_qkv = give_keep(half_qkv.reshape(ranks, 2, -1, 3 * span), far, 1)
    grad_text = weight_grad(text_norm, all_low).astype(narrow).reshape(2, -1, 2 * width)
    give_text, keep_text = give_keep(grad_text, core, 0)
    half_text = add_low(keep_text, swap(give_text, CORES))
    pair_gu = join(rows_gu, swap(rows_gu, FARS), far, 1).reshape(ranks, -1, 2 * hidden)
    sum_out = add_low(half_out, swap(half_out, FARS))
    sum_qkv = add_low(keep_qkv, swap(give_qkv, FARS))
    sum_text = add_low(half_text, swap(half_text, FARS))

    grad_attn_in = scatter_tokens(
        dot_back(qkv_low, qkv_here), items, 11, after=(half_out, give_qkv, half_text)
    )
    grad_scale_attn = jnp.sum(grad_attn_in * norm_in, axis=1)
    grad_norm = grad_attn_in * (1.0 + scale_attn)
    grad_zero = over_tokens(grad_norm * unit_in)
    grad_x = grad_middle + norm_back(unit_in, inverse_in, grad_norm * gains[0])

    grad_text_gain = jnp.sum(dot_back(all_low, w_text) * text_unit, axis=0)
    grad_modulation = jnp.stack([grad_scale_attn, grad_gate_attn, grad_scale_ffn, grad_gate_ffn], 1)
    grad_gains = jnp.stack(
        [
            grad_zero,
            spread(jnp.sum(grad_query * unit_q, axis=0), width),
            spread(jnp.sum(grad_key * unit_k, axis=0), width),
            grad_three,
            grad_four,
            grad_five,
            spread(jnp.sum(grad_tkey * unit_t, axis=0), width),
        ]
    )
    flat = jnp.concatenate(
        [
            grad_gains.reshape(-1),
            spread(grad_text_gain, text_width),
            spread(grad_gate, heads),
        ]
    )
    lanes = ranks * 128
    sum_depth = -(-flat.size // lanes)
    flat = jnp.pad(flat, (0, sum_depth * lanes - flat.size)).reshape(ranks, sum_depth, 128)
    keep_depth = grad_modulation.size // lanes
    reduced = final_sums(
        jnp.concatenate([flat, grad_modulation.reshape(ranks, keep_depth, 128)], axis=1),
        sum_depth,
        13,
    )
    flat = reduced[:, :sum_depth].reshape(-1)
    total_gains = flat[: gains.size].reshape(gains.shape)
    total_text_gain = flat[gains.size : gains.size + text_width]
    total_gate = flat[gains.size + text_width : gains.size + text_width + heads]
    groups = lax.axis_size("items")
    all_modulation = jnp.swapaxes(
        reduced[:, sum_depth:].reshape(ranks, groups, keep_depth * 128), 0, 1
    ).reshape(groups * items, 4 * width)
    all_time = lax.all_gather(time_here, "items", axis=0, tiled=True)
    final_ada = jnp.einsum(
        "tk,tn->kn",
        all_time.astype(single),
        all_modulation,
        precision=lax.Precision.HIGHEST,
        preferred_element_type=single,
    )
    total_bias = jnp.sum(all_modulation, axis=0)
    rows_qkv = lax.all_to_all(sum_qkv, "rows", 0, 0, tiled=True)
    pair_qkv = join(rows_qkv, swap(rows_qkv, FARS), far, 1).reshape(ranks, -1, 3 * span)

    def whole_rows(half):
        both = join(half, swap(half, CORES), core, 0).astype(single)
        return both.reshape(-1, half.shape[-1])

    sums = [
        unpack_halves(pair_qkv, swap(pair_qkv, CORES), 3),
        whole_rows(sum_out),
        whole_rows(sum_text),
        unpack_halves(pair_gu, swap(pair_gu, CORES), 2),
        whole_rows(sum_down),
    ]
    return (
        output.reshape(1, items * slots, width),
        grad_x.reshape(1, items * slots, width),
        *sums,
        final_ada,
        total_gains,
        total_gate,
        total_bias,
        total_text_gain,
    )


def per_device(*arrays):
    heads = arrays[14].shape[0]
    plan = gathered_plan if heads % lax.axis_size("rows") else head_parallel_plan
    return plan(*arrays)


def solution(mesh):
    in_specs = (
        P("items", "rows", None),
        P("items", "rows", None),
        P("items", None, "rows", None),
        P("items", None, None),
        P("items", "rows", None),
        P("items", None),
        P("items", None),
        P("rows", None),
        P("rows", None),
        P("rows", None),
        P("rows", None),
        P("rows", None),
        P("rows", None),
        P(),
        P(),
        P(),
        P(),
    )
    out_specs = (
        P("items", "rows", None),
        P("items", "rows", None),
        P("rows", None),
        P("rows", None),
        P("rows", None),
        P("rows", None),
        P("rows", None),
        P("rows", None),
        P(),
        P(),
        P(),
        P(),
    )
    return jax.shard_map(
        per_device, mesh=mesh, in_specs=in_specs, out_specs=out_specs, check_vma=False
    )
```

```python
import functools
import math

import jax
import jax.numpy as jnp
from jax import lax
from jax.experimental import pallas as pl
from jax.experimental.pallas import tpu as pltpu
from jax.sharding import PartitionSpec as P

COLS = 32


epsilon = 1e-06
masked_score = -1e30
group_heads = 4


def norm_gain(values, scaling):
    return values * lax.rsqrt(jnp.mean(values * values, axis=-1, keepdims=True) + epsilon) * scaling


def pre_norm(values, shift_scale, scaling):
    return norm_gain(values, scaling) * (1.0 + shift_scale)


def post_add(residual, branch, gate_in, scaling):
    return residual + jnp.tanh(gate_in) * norm_gain(branch, scaling)


def swiglu(gate_up):
    middle_col = gate_up.shape[-1] // 2
    return jax.nn.silu(gate_up[..., :middle_col]) * gate_up[..., middle_col:]


def freq_rates(number):
    return 10000.0 ** (-jnp.arange(number).astype(jnp.float32) / number)


def rotary_angles(frame_index, frame_row, column, head_size):
    frame_pairs = head_size // 8
    space_pairs = (head_size // 2 - frame_pairs) // 2
    return jnp.concatenate(
        [
            frame_index.astype(jnp.float32)[..., None] * freq_rates(frame_pairs),
            frame_row.astype(jnp.float32)[..., None] * freq_rates(space_pairs),
            column.astype(jnp.float32)[..., None] * freq_rates(space_pairs),
        ],
        axis=-1,
    )


def rotate(values, cos_table, sin_table, head_count):
    shaped = values.reshape(values.shape[:-1] + (head_count, values.shape[-1] // head_count))
    half_size = shaped.shape[-1] // 2
    upper_half = shaped[..., :half_size]
    lower_half = shaped[..., half_size:]
    cos_heads = cos_table[..., None, :]
    sin_heads = sin_table[..., None, :]
    turned = jnp.concatenate(
        [
            upper_half * cos_heads - lower_half * sin_heads,
            upper_half * sin_heads + lower_half * cos_heads,
        ],
        axis=-1,
    )
    return turned.reshape(values.shape)


def text_split(projected, key_gain):
    half_cols = projected.shape[-1] // 2
    return (norm_gain(projected[..., :half_cols], key_gain), projected[..., half_cols:])


def gathered_plan(
    hidden_in,
    cotangent,
    text_states,
    time_embed,
    live_rows,
    frame_rows,
    text_len,
    w_qkv,
    w_out,
    w_text,
    w_gu,
    w_down,
    w_ada,
    gains,
    cross_gate,
    ada_bias,
    text_gain,
):
    single = jnp.float32
    narrow = jnp.bfloat16
    model_width = hidden_in.shape[2]
    head_count = cross_gate.shape[0]
    head_size = model_width // head_count
    score_scale = head_size ** (-0.5)
    item_count = time_embed.shape[1]
    item_slots = hidden_in.shape[1] // item_count
    row_devices = lax.axis_size("rows")
    seq_len = row_devices * item_slots
    text_local = text_states.shape[2]
    text_all = text_local * row_devices
    text_width = text_states.shape[3]
    group_span = group_heads * head_size
    block_count = head_count // group_heads
    token_count = item_count * item_slots

    def weight_term(left, right, accuracy):
        return jnp.einsum(
            "tk,tn->kn", left, right, precision=accuracy, preferred_element_type=single
        )

    def reduce_term(term):
        return lax.psum_scatter(
            term.astype(jnp.bfloat16), "rows", scatter_dimension=0, tiled=True
        ).astype(jnp.float32)

    full_qkv, full_out, full_text, full_gu, full_down, full_ada = (
        lax.all_gather(w_qkv, "rows", axis=0, tiled=True),
        lax.all_gather(w_out, "rows", axis=0, tiled=True),
        lax.all_gather(w_text, "rows", axis=0, tiled=True),
        lax.all_gather(w_gu, "rows", axis=0, tiled=True),
        lax.all_gather(w_down, "rows", axis=0, tiled=True),
        lax.all_gather(w_ada, "rows", axis=0, tiled=True),
    )
    counts_here = live_rows[0]
    every_count = lax.all_gather(counts_here, "rows", axis=0, tiled=True)
    device_place = lax.axis_index("rows")
    ranks = jnp.arange(row_devices)
    rows_below = jnp.sum(jnp.where(ranks[:, None] < device_place, every_count, 0), axis=0)
    slot_row = jnp.arange(item_slots) // COLS
    column = jnp.arange(item_slots) % COLS
    row_index = rows_below[:, None] + slot_row[None, :]
    heights = frame_rows[0][:, None]
    frame_index = row_index // heights
    frame_row = row_index % heights
    live_mask = (slot_row[None, :] < counts_here[0][:, None]).astype(single)
    key_live = (slot_row[None, None, :] < jnp.transpose(every_count)[:, :, None]).reshape(
        item_count, seq_len
    )
    text_live = jnp.arange(text_all)[None, :] < text_len[0][:, None]
    angles = rotary_angles(
        frame_index, frame_row, jnp.broadcast_to(column, row_index.shape), head_size
    )
    cos_table = jnp.cos(angles)
    sin_table = jnp.sin(angles)

    def qkv_split(projected, gain_query, gain_key):
        queries = rotate(
            norm_gain(projected[..., :model_width], gain_query), cos_table, sin_table, head_count
        )
        keys_here = rotate(
            norm_gain(projected[..., model_width : 2 * model_width], gain_key),
            cos_table,
            sin_table,
            head_count,
        )
        return (queries, keys_here, projected[..., 2 * model_width :])

    states = hidden_in[0].reshape(item_count, item_slots, model_width)
    time_silu = jax.nn.silu(time_embed[0].astype(single)).astype(narrow)
    modulation = jnp.dot(time_silu, full_ada, preferred_element_type=single) + ada_bias
    scale_attn = modulation[:, None, 0:model_width]
    gate_attn = modulation[:, None, model_width : 2 * model_width]
    scale_ffn = modulation[:, None, 2 * model_width : 3 * model_width]
    gate_ffn = modulation[:, None, 3 * model_width :]
    attn_in = (
        pre_norm(states, scale_attn, gains[0]).astype(narrow).reshape(token_count, model_width)
    )
    qkv_proj = jnp.dot(attn_in, full_qkv, preferred_element_type=single).reshape(
        item_count, item_slots, 3 * model_width
    )
    query_full, key_full, value_full = qkv_split(qkv_proj, gains[1], gains[2])
    query_low = query_full.astype(narrow)
    key_low = key_full.astype(narrow)
    value_low = value_full.astype(narrow)
    text_float = text_states[0].astype(single)
    text_norm = norm_gain(text_float, text_gain).astype(narrow)
    text_proj = jnp.einsum("ctd,dn->ctn", text_norm, full_text, preferred_element_type=single)
    tkey_full, tval_full = text_split(text_proj, gains[6])
    key_all, value_all, tkey_all, tval_all = (
        lax.all_gather(key_low, "rows", axis=1, tiled=True),
        lax.all_gather(value_low, "rows", axis=1, tiled=True),
        lax.all_gather(tkey_full.astype(narrow), "rows", axis=1, tiled=True),
        lax.all_gather(tval_full.astype(narrow), "rows", axis=1, tiled=True),
    )

    def block_slices(block_index, key_source, value_source):
        offset = block_index * group_span
        query_part = lax.dynamic_slice_in_dim(query_low, offset, group_span, 2).reshape(
            item_count, item_slots, group_heads, head_size
        )
        key_part = lax.dynamic_slice_in_dim(key_source, offset, group_span, 2).reshape(
            item_count, seq_len, group_heads, head_size
        )
        value_part = lax.dynamic_slice_in_dim(value_source, offset, group_span, 2).reshape(
            item_count, seq_len, group_heads, head_size
        )
        return (query_part, key_part, value_part)

    def self_step(carry, block_index):
        query_part, key_part, value_part = block_slices(block_index, key_all, value_all)
        scores = (
            jnp.einsum("iphe,ikhe->ihpk", query_part, key_part, preferred_element_type=single)
            * score_scale
        )
        scores = jnp.where(key_live[:, None, None, :], scores, masked_score)
        row_max = jnp.max(scores, axis=-1, keepdims=True)
        exp_terms = jnp.exp(scores - row_max)
        exp_total = jnp.sum(exp_terms, axis=-1, keepdims=True)
        probs_low = (exp_terms / exp_total).astype(narrow)
        attended = jnp.einsum(
            "ihpk,ikhe->iphe", probs_low, value_part, preferred_element_type=single
        )
        return (
            carry,
            (
                attended.reshape(item_count, item_slots, group_span),
                (row_max + jnp.log(exp_total))[..., 0],
            ),
        )

    _, (self_parts, log_totals) = lax.scan(
        self_step, jnp.zeros((), single), jnp.arange(block_count)
    )

    def heads_last(parts):
        return jnp.transpose(parts, (1, 2, 0, 3)).reshape(item_count, item_slots, model_width)

    self_out = heads_last(self_parts)
    query_heads = query_low.reshape(item_count, item_slots, head_count, head_size)
    tkey_heads = tkey_all.reshape(item_count, text_all, head_count, head_size)
    tval_heads = tval_all.reshape(item_count, text_all, head_count, head_size)
    cross_scores = (
        jnp.einsum("iphe,ikhe->ihpk", query_heads, tkey_heads, preferred_element_type=single)
        * score_scale
    )
    cross_scores = jnp.where(text_live[:, None, None, :], cross_scores, masked_score)
    cross_max = jnp.max(cross_scores, axis=-1, keepdims=True)
    cross_exp = jnp.exp(cross_scores - cross_max)
    cross_probs = cross_exp / jnp.sum(cross_exp, axis=-1, keepdims=True)
    cross_low = cross_probs.astype(narrow)
    cross_out = jnp.einsum("ihpk,ikhe->iphe", cross_low, tval_heads, preferred_element_type=single)
    tanh_gate = jnp.tanh(cross_gate)
    combined = (
        self_out.reshape(item_count, item_slots, head_count, head_size)
        + tanh_gate[:, None] * cross_out
    )
    combined = combined.reshape(token_count, model_width).astype(narrow)
    projected = jnp.dot(combined, full_out, preferred_element_type=single).reshape(
        item_count, item_slots, model_width
    )
    middle = post_add(states, projected, gate_attn, gains[3])
    ffn_in = pre_norm(middle, scale_ffn, gains[4]).astype(narrow).reshape(token_count, model_width)
    gate_up = jnp.dot(ffn_in, full_gu, preferred_element_type=single)
    inner_act = swiglu(gate_up).astype(narrow)
    ffn_out = jnp.dot(inner_act, full_down, preferred_element_type=single).reshape(
        item_count, item_slots, model_width
    )
    result = post_add(middle, ffn_out, gate_ffn, gains[5])
    output = (live_mask[..., None] * result).reshape(1, token_count, model_width)
    grad_result = live_mask[..., None] * cotangent[0].reshape(item_count, item_slots, model_width)
    _, back_ffn_out = jax.vjp(post_add, middle, ffn_out, gate_ffn, gains[5])
    grad_middle, grad_ffn_out, grad_gate_ffn, grad_gain_five = back_ffn_out(grad_result)
    ffn_low = grad_ffn_out.astype(narrow).reshape(token_count, model_width)
    shard_down = reduce_term(weight_term(inner_act, ffn_low, None))
    grad_inner = jnp.einsum("tn,kn->tk", ffn_low, full_down, preferred_element_type=single)
    _, back_glu = jax.vjp(swiglu, gate_up)
    gate_up_low = back_glu(grad_inner)[0].astype(narrow)
    shard_gu = reduce_term(weight_term(ffn_in, gate_up_low, None))
    grad_ffn_in = jnp.einsum("tn,kn->tk", gate_up_low, full_gu, preferred_element_type=single)
    _, back_ffn_in = jax.vjp(pre_norm, middle, scale_ffn, gains[4])
    part_middle, grad_scale_ffn, grad_gain_four = back_ffn_in(
        grad_ffn_in.reshape(item_count, item_slots, model_width)
    )
    grad_middle = grad_middle + part_middle
    _, back_attn_out = jax.vjp(post_add, states, projected, gate_attn, gains[3])
    grad_hidden, grad_projected, grad_gate_attn, grad_gain_three = back_attn_out(grad_middle)
    projected_low = grad_projected.astype(narrow).reshape(token_count, model_width)
    shard_out = reduce_term(weight_term(combined, projected_low, None))
    grad_combined = jnp.einsum("tn,kn->tk", projected_low, full_out, preferred_element_type=single)
    grad_combined = grad_combined.reshape(item_count, item_slots, head_count, head_size)
    self_low = grad_combined.reshape(item_count, item_slots, model_width).astype(narrow)
    cross_grad_low = (tanh_gate[:, None] * grad_combined).astype(narrow)
    grad_cross_gate = (1.0 - tanh_gate * tanh_gate) * jnp.sum(
        grad_combined * cross_out, axis=(0, 1, 3)
    )

    def self_back(carry, packed):
        block_index, log_total = packed
        query_part, key_part, value_part = block_slices(block_index, key_all, value_all)
        offset = block_index * group_span
        grad_part = lax.dynamic_slice_in_dim(self_low, offset, group_span, 2).reshape(
            item_count, item_slots, group_heads, head_size
        )
        scores = (
            jnp.einsum("iphe,ikhe->ihpk", query_part, key_part, preferred_element_type=single)
            * score_scale
        )
        scores = jnp.where(key_live[:, None, None, :], scores, masked_score)
        attn_probs = jnp.exp(scores - log_total[..., None])
        grad_probs = jnp.einsum(
            "iphe,ikhe->ihpk", grad_part, value_part, preferred_element_type=single
        )
        row_inner = jnp.sum(attn_probs * grad_probs, axis=-1, keepdims=True)
        score_low = (attn_probs * (grad_probs - row_inner)).astype(narrow)
        grad_query = (
            jnp.einsum("ihpk,ikhe->iphe", score_low, key_part, preferred_element_type=single)
            * score_scale
        )
        grad_value = jnp.einsum(
            "ihpk,iphe->ikhe", attn_probs.astype(narrow), grad_part, preferred_element_type=single
        )
        grad_key = (
            jnp.einsum("ihpk,iphe->ikhe", score_low, query_part, preferred_element_type=single)
            * score_scale
        )
        owned_key, owned_value = (
            lax.psum_scatter(
                grad_key.reshape(item_count, seq_len, group_span).astype(jnp.bfloat16),
                "rows",
                scatter_dimension=1,
                tiled=True,
            ).astype(jnp.float32),
            lax.psum_scatter(
                grad_value.reshape(item_count, seq_len, group_span).astype(jnp.bfloat16),
                "rows",
                scatter_dimension=1,
                tiled=True,
            ).astype(jnp.float32),
        )
        return (
            carry,
            (grad_query.reshape(item_count, item_slots, group_span), owned_key, owned_value),
        )

    _, (query_parts, key_parts, value_parts) = lax.scan(
        self_back, jnp.zeros((), single), (jnp.arange(block_count), log_totals)
    )
    cross_grad_probs = jnp.einsum(
        "iphe,ikhe->ihpk", cross_grad_low, tval_heads, preferred_element_type=single
    )
    cross_inner = jnp.sum(cross_probs * cross_grad_probs, axis=-1, keepdims=True)
    cross_score_low = (cross_probs * (cross_grad_probs - cross_inner)).astype(narrow)
    grad_query_cross = (
        jnp.einsum("ihpk,ikhe->iphe", cross_score_low, tkey_heads, preferred_element_type=single)
        * score_scale
    )
    grad_text_key = (
        jnp.einsum("ihpk,iphe->ikhe", cross_score_low, query_heads, preferred_element_type=single)
        * score_scale
    )
    grad_text_value = jnp.einsum(
        "ihpk,iphe->ikhe", cross_low, cross_grad_low, preferred_element_type=single
    )
    owned_tkey, owned_tval = (
        lax.psum_scatter(
            grad_text_key.reshape(item_count, text_all, model_width).astype(jnp.bfloat16),
            "rows",
            scatter_dimension=1,
            tiled=True,
        ).astype(jnp.float32),
        lax.psum_scatter(
            grad_text_value.reshape(item_count, text_all, model_width).astype(jnp.bfloat16),
            "rows",
            scatter_dimension=1,
            tiled=True,
        ).astype(jnp.float32),
    )
    grad_query_all = heads_last(query_parts) + grad_query_cross.reshape(
        item_count, item_slots, model_width
    )
    _, back_qkv = jax.vjp(qkv_split, qkv_proj, gains[1], gains[2])
    grad_qkv, grad_gain_one, grad_gain_two = back_qkv(
        (grad_query_all, heads_last(key_parts), heads_last(value_parts))
    )
    qkv_low = grad_qkv.astype(narrow).reshape(token_count, 3 * model_width)
    shard_qkv = reduce_term(weight_term(attn_in, qkv_low, None))
    grad_attn_in = jnp.einsum("tn,kn->tk", qkv_low, full_qkv, preferred_element_type=single)
    _, back_attn_in = jax.vjp(pre_norm, states, scale_attn, gains[0])
    part_states, grad_scale_attn, grad_gain_zero = back_attn_in(
        grad_attn_in.reshape(item_count, item_slots, model_width)
    )
    grad_x = (grad_hidden + part_states).reshape(1, token_count, model_width)
    _, back_text = jax.vjp(text_split, text_proj, gains[6])
    grad_text_proj, grad_gain_six = back_text((owned_tkey, owned_tval))
    text_low = grad_text_proj.astype(narrow).reshape(item_count * text_local, 2 * model_width)
    shard_text = reduce_term(
        weight_term(text_norm.reshape(item_count * text_local, text_width), text_low, None)
    )
    grad_text_norm = jnp.einsum("tn,kn->tk", text_low, full_text, preferred_element_type=single)
    _, back_text_norm = jax.vjp(norm_gain, text_float, text_gain)
    grad_text_gain = back_text_norm(grad_text_norm.reshape(text_float.shape))[1]
    grad_modulation = jnp.concatenate(
        [grad_scale_attn, grad_gate_attn, grad_scale_ffn, grad_gate_ffn], axis=-1
    )[:, 0, :]
    shard_ada = reduce_term(
        weight_term(time_silu.astype(single), grad_modulation, lax.Precision.HIGHEST)
    )
    grad_ada_bias = jnp.sum(grad_modulation, axis=0)
    grad_gains = jnp.stack(
        [
            grad_gain_zero,
            grad_gain_one,
            grad_gain_two,
            grad_gain_three,
            grad_gain_four,
            grad_gain_five,
            grad_gain_six,
        ],
        axis=0,
    )
    final_qkv, final_out, final_text, final_gu, final_down, final_ada = (
        lax.psum(shard_qkv.astype(jnp.bfloat16), "items").astype(jnp.float32),
        lax.psum(shard_out.astype(jnp.bfloat16), "items").astype(jnp.float32),
        lax.psum(shard_text.astype(jnp.bfloat16), "items").astype(jnp.float32),
        lax.psum(shard_gu.astype(jnp.bfloat16), "items").astype(jnp.float32),
        lax.psum(shard_down.astype(jnp.bfloat16), "items").astype(jnp.float32),
        lax.psum(shard_ada.astype(jnp.bfloat16), "items").astype(jnp.float32),
    )
    total_gains, total_gate, total_bias, total_text_gain = lax.psum(
        (grad_gains, grad_cross_gate, grad_ada_bias, grad_text_gain), ("items", "rows")
    )
    return (
        output,
        grad_x,
        final_qkv,
        final_out,
        final_text,
        final_gu,
        final_down,
        final_ada,
        total_gains,
        total_gate,
        total_bias,
        total_text_gain,
    )


def norm_parts(values):
    inverse = lax.rsqrt(jnp.mean(values * values, axis=-1, keepdims=True) + epsilon)
    return values * inverse, inverse


def norm_back(unit, inverse, scaled_grad):
    return inverse * (scaled_grad - unit * jnp.mean(scaled_grad * unit, axis=-1, keepdims=True))


MESH = pl.DeviceIdType.MESH
DEPTH, BREADTH = 4, 2


def row_place():
    place = lax.axis_index("rows")
    return place // BREADTH, lax.rem(place, BREADTH)


def on_rows(line, side):
    return {"rows": line * BREADTH + side}


def greet(devices):
    barrier = pltpu.get_barrier_semaphore()
    for condition, device in devices:

        @pl.when(condition)
        def _(device=device):
            pl.semaphore_signal(barrier, inc=1, device_id=device, device_id_type=MESH)

    count = 0
    for condition, _ in devices:
        count = count + jnp.where(condition, 1, 0)
    pl.semaphore_wait(barrier, count)


def remote(source, target, send, receive, device):
    return pltpu.make_async_remote_copy(
        src_ref=source,
        dst_ref=target,
        send_sem=send,
        recv_sem=receive,
        device_id=device,
        device_id_type=MESH,
    )


def shard_of(ref, place, axis):
    return ref.at[place] if axis == 0 else ref.at[:, place]


def gather_kernel(axis, count, own, *rest):
    whole, local, z_send, z_recv, x_send, x_recv = rest[count:]
    line, side = row_place()
    above, below, across = on_rows(line + 1, side), on_rows(line - 1, side), on_rows(line, 1 - side)
    has_above, has_below = line < DEPTH - 1, line > 0
    greet([(has_above, above), (has_below, below), (line >= 0, across)])

    def block(at, which):
        return shard_of(whole, at * BREADTH + which, axis)

    def pass_on(source, at, way, device):
        return remote(source, block(at, side), z_send.at[way, at], z_recv.at[at], device)

    def cross(source, at):
        return remote(source, block(at, side), x_send.at[at], x_recv.at[at], across)

    cross(own, line).start()

    @pl.when(has_above)
    def _():
        pass_on(own, line, 0, above).start()

    @pl.when(has_below)
    def _():
        pass_on(own, line, 1, below).start()

    keep = pltpu.make_async_copy(own, block(line, side), local)
    keep.start()
    for step in range(1, DEPTH):

        @pl.when(line - step >= 0)
        def _(at=line - step):
            pass_on(own, at, 0, below).wait_recv()

            @pl.when(has_above)
            def _():
                pass_on(block(at, side), at, 0, above).start()

            cross(block(at, side), at).start()

        @pl.when(line + step < DEPTH)
        def _(at=line + step):
            pass_on(own, at, 1, above).wait_recv()

            @pl.when(has_below)
            def _():
                pass_on(block(at, side), at, 1, below).start()

            cross(block(at, side), at).start()

    keep.wait()
    for at in range(DEPTH):
        cross(own, at).wait_recv()
        cross(own, at).wait_send()

        @pl.when(has_above & (at <= line))
        def _(at=at):
            pass_on(own, at, 0, above).wait_send()

        @pl.when(has_below & (at >= line))
        def _(at=at):
            pass_on(own, at, 1, below).wait_send()


def gather_rows(block, ident, axis, after=()):
    ranks = DEPTH * BREADTH
    shape = block.shape[:axis] + (ranks,) + block.shape[axis:]
    anywhere = pl.BlockSpec(memory_space=pl.ANY)
    return pl.pallas_call(
        functools.partial(gather_kernel, axis, len(after)),
        out_shape=jax.ShapeDtypeStruct(shape, block.dtype),
        in_specs=[anywhere] * (1 + len(after)),
        out_specs=anywhere,
        scratch_shapes=[
            pltpu.SemaphoreType.DMA,
            pltpu.SemaphoreType.DMA((2, DEPTH)),
            pltpu.SemaphoreType.DMA((DEPTH,)),
            pltpu.SemaphoreType.DMA((DEPTH,)),
            pltpu.SemaphoreType.DMA((DEPTH,)),
        ],
        name=f"gather_rows_{ident}",
        compiler_params=pltpu.CompilerParams(collective_id=ident, has_side_effects=True),
    )(block, *after)


def scatter_kernel(axis, count, parts, *rest):
    total, crossed, risen, sunk, up, down, x_send, x_recv, z_send, z_recv = rest[count:]
    line, side = row_place()
    above, below, across = on_rows(line + 1, side), on_rows(line - 1, side), on_rows(line, 1 - side)
    has_above, has_below = line < DEPTH - 1, line > 0
    greet([(has_above, above), (has_below, below), (line >= 0, across)])

    def part(at, which):
        return shard_of(parts, at * BREADTH + which, axis)

    def cross(at):
        return remote(part(at, 1 - side), crossed.at[at], x_send.at[at], x_recv.at[at], across)

    def rise(at):
        return remote(up.at[at], risen.at[at], z_send.at[0, at], z_recv.at[0, at], above)

    def sink(at):
        return remote(down.at[at], sunk.at[at], z_send.at[1, at], z_recv.at[1, at], below)

    def add_up(at, others, target):
        mine = part(at, side)
        whole = mine.shape
        value = mine[...].astype(jnp.float32) + crossed[at].astype(jnp.float32)
        for other in others:
            value = value + other[at].astype(jnp.float32)
        target[...] = value.astype(target.dtype)

    for step in range(DEPTH - 1, 0, -1):
        for at, there in ((line + step, line + step < DEPTH), (line - step, line - step >= 0)):

            @pl.when(there)
            def _(at=at):
                cross(at).start()

    cross(line).start()
    for step in range(DEPTH - 1, 0, -1):

        @pl.when(line + step < DEPTH)
        def _(at=line + step):
            cross(at).wait_recv()

            @pl.when(has_below)
            def _():
                rise(at).wait_recv()
                add_up(at, [risen], up.at[at])

            @pl.when(jnp.logical_not(has_below))
            def _():
                add_up(at, [], up.at[at])

            rise(at).start()

        @pl.when(line - step >= 0)
        def _(at=line - step):
            cross(at).wait_recv()

            @pl.when(has_above)
            def _():
                sink(at).wait_recv()
                add_up(at, [sunk], down.at[at])

            @pl.when(jnp.logical_not(has_above))
            def _():
                add_up(at, [], down.at[at])

            sink(at).start()

    cross(line).wait_recv()

    @pl.when(has_below & has_above)
    def _():
        rise(line).wait_recv()
        sink(line).wait_recv()
        add_up(line, [risen, sunk], total)

    @pl.when(jnp.logical_not(has_above))
    def _():
        rise(line).wait_recv()
        add_up(line, [risen], total)

    @pl.when(jnp.logical_not(has_below))
    def _():
        sink(line).wait_recv()
        add_up(line, [sunk], total)

    for at in range(DEPTH):
        cross(at).wait_send()

        @pl.when(at > line)
        def _(at=at):
            rise(at).wait_send()

        @pl.when(at < line)
        def _(at=at):
            sink(at).wait_send()


def scatter_rows(parts, ident, axis, after=()):
    shape = parts.shape[:axis] + parts.shape[axis + 1 :]
    near = pl.BlockSpec(memory_space=pltpu.VMEM)
    slots = pltpu.VMEM((DEPTH,) + shape, parts.dtype)
    return pl.pallas_call(
        functools.partial(scatter_kernel, axis, len(after)),
        out_shape=jax.ShapeDtypeStruct(shape, jnp.float32),
        in_specs=[near] + [pl.BlockSpec(memory_space=pl.ANY)] * len(after),
        out_specs=near,
        scratch_shapes=[slots] * 5
        + [
            pltpu.SemaphoreType.DMA((DEPTH,)),
            pltpu.SemaphoreType.DMA((DEPTH,)),
            pltpu.SemaphoreType.DMA((2, DEPTH)),
            pltpu.SemaphoreType.DMA((2, DEPTH)),
        ],
        name=f"scatter_rows_{ident}",
        compiler_params=pltpu.CompilerParams(
            collective_id=ident, has_side_effects=True, vmem_limit_bytes=32 << 20
        ),
    )(parts, *after)


def sum_kernel(own, total, held, send, receive):
    ranks = DEPTH * BREADTH
    place = lax.axis_index("rows")
    others = [lax.rem(place + step, ranks) for step in range(1, ranks)]
    greet([(place >= 0, {"rows": other}) for other in others])

    def push(step, other, slot):
        return remote(own, held.at[slot], send.at[step], receive.at[slot], {"rows": other})

    for step, other in enumerate(others):
        push(step, other, place).start()
    held[pl.ds(place, 1)] = own[...][None]
    for step, other in enumerate(others):
        push(step, other, other).wait_recv()
    value = held[0]
    for rank in range(1, ranks):
        value = value + held[rank]
    total[...] = value
    for step, other in enumerate(others):
        push(step, other, place).wait_send()


def sum_rows(own, ident):
    ranks = DEPTH * BREADTH
    near = pl.BlockSpec(memory_space=pltpu.VMEM)
    return pl.pallas_call(
        sum_kernel,
        out_shape=jax.ShapeDtypeStruct(own.shape, own.dtype),
        in_specs=[near],
        out_specs=near,
        scratch_shapes=[
            pltpu.VMEM((ranks,) + own.shape, own.dtype),
            pltpu.SemaphoreType.DMA((ranks,)),
            pltpu.SemaphoreType.DMA((ranks,)),
        ],
        name=f"sum_rows_{ident}",
        compiler_params=pltpu.CompilerParams(collective_id=ident, has_side_effects=True),
    )(own)


def final_kernel(ranks, groups, sums, own, out, held, kept, part, h_send, h_recv, g_send, g_recv, o_send, o_recv):
    place, group = lax.axis_index("rows"), lax.axis_index("items")
    rows = [lax.rem(place + step, ranks) for step in range(1, ranks)]
    items = [lax.rem(group + step, groups) for step in range(1, groups)]
    greet([(place >= 0, {"rows": other}) for other in rows] + [(place >= 0, {"items": other}) for other in items])

    def push(step, other, slot):
        return remote(own.at[other], held.at[slot], h_send.at[step], h_recv.at[slot], {"rows": other})

    def swap(step, other, slot):
        return remote(part, kept.at[slot], g_send.at[step], g_recv.at[slot], {"items": other})

    def share(step, other, slot):
        return remote(out.at[place], out.at[slot], o_send.at[step], o_recv.at[slot], {"rows": other})

    for step, other in enumerate(rows):
        push(step, other, place).start()
    held[pl.ds(place, 1)] = own[pl.ds(place, 1)]
    for step, other in enumerate(rows):
        push(step, other, other).wait_recv()
    value = held[0]
    for rank in range(1, ranks):
        value = value + held[rank]
    part[...] = value
    for step, other in enumerate(items):
        swap(step, other, group).start()
    kept[pl.ds(group, 1)] = value[None]
    for step, other in enumerate(items):
        swap(step, other, other).wait_recv()
    total = kept[0, :sums]
    for item in range(1, groups):
        total = total + kept[item, :sums]
    depth = own.shape[1] - sums
    out[pl.ds(place, 1), :sums] = total[None]
    for item in range(groups):
        out[pl.ds(place, 1), sums + item * depth : sums + (item + 1) * depth] = kept[item, sums:][None]
    for step, other in enumerate(rows):
        share(step, other, place).start()
    for step, other in enumerate(rows):
        share(step, other, other).wait_recv()
    for step, other in enumerate(rows):
        push(step, other, place).wait_send()
        share(step, other, place).wait_send()
    for step, other in enumerate(items):
        swap(step, other, group).wait_send()


def final_sums(own, sums, ident):
    ranks, groups = lax.axis_size("rows"), lax.axis_size("items")
    near = pl.BlockSpec(memory_space=pltpu.VMEM)
    depth = own.shape[1]
    return pl.pallas_call(
        functools.partial(final_kernel, ranks, groups, sums),
        out_shape=jax.ShapeDtypeStruct((ranks, sums + groups * (depth - sums), 128), own.dtype),
        in_specs=[near],
        out_specs=near,
        scratch_shapes=[
            pltpu.VMEM(own.shape, own.dtype),
            pltpu.VMEM((groups,) + own.shape[1:], own.dtype),
            pltpu.VMEM(own.shape[1:], own.dtype),
            pltpu.SemaphoreType.DMA((ranks,)),
            pltpu.SemaphoreType.DMA((ranks,)),
            pltpu.SemaphoreType.DMA((groups,)),
            pltpu.SemaphoreType.DMA((groups,)),
            pltpu.SemaphoreType.DMA((ranks,)),
            pltpu.SemaphoreType.DMA((ranks,)),
        ],
        name=f"final_sums_{ident}",
        compiler_params=pltpu.CompilerParams(collective_id=ident, has_side_effects=True),
    )(own)


def first_kernel(
    ranks, quarters, own, qkv, text, total, qkv_out, text_out, held, packed, local,
    s_send, s_recv, t_send, t_recv, a_send, a_recv, y_send, y_recv, c_send, c_recv,
):
    place, group = lax.axis_index("rows"), lax.axis_index("items")
    others = [lax.rem(place + step, ranks) for step in range(1, ranks)]
    far = lax.rem(group + 2, 4)
    twin = group + 1 - 2 * lax.rem(group, 2)
    depth = qkv.shape[0] // quarters
    mine = pl.ds(pl.multiple_of(group * depth, 16), depth)
    fars = pl.ds(pl.multiple_of(far * depth, 16), depth)
    features = text_out.shape[-1]
    span = qkv.shape[1] // (3 * ranks)

    def columns(other):
        return pl.ds(pl.multiple_of(other * features, features), features)

    keeps = [pltpu.make_async_copy(text.at[:, :, columns(place)], text_out.at[place], local.at[0])]
    keeps[0].start()
    greet(
        [(place >= 0, {"rows": other}) for other in others]
        + [(place >= 0, {"items": far}), (place >= 0, {"items": twin})]
    )

    def sum_push(step, other, slot):
        return remote(own, held.at[slot], s_send.at[step], s_recv.at[slot], {"rows": other})

    def text_push(step, other, slot):
        return remote(
            text.at[:, :, columns(other)], text_out.at[slot], t_send.at[step], t_recv.at[slot], {"rows": other}
        )

    def push(step, other, slot):
        return remote(
            packed.at[other, mine], qkv_out.at[slot, mine], a_send.at[step], a_recv.at[slot], {"rows": other}
        )

    def pass_far(slot):
        block = qkv_out.at[slot, mine]
        return remote(block, block, y_send.at[slot], y_recv.at[slot], {"items": far})

    def pass_twin(which, slot):
        block = qkv_out.at[slot, fars if which else mine]
        return remote(block, block, c_send.at[which, slot], c_recv.at[which, slot], {"items": twin})

    for step, other in enumerate(others):
        sum_push(step, other, place).start()
    for rank in range(ranks):
        packed[rank] = jnp.concatenate(
            [
                qkv[:, (part * ranks + rank) * span : (part * ranks + rank + 1) * span]
                for part in range(3)
            ],
            axis=1,
        )
    for step, other in enumerate(others):
        push(step, other, place).start()
    for step, other in enumerate(others):
        text_push(step, other, place).start()
    keeps.append(pltpu.make_async_copy(packed.at[place], qkv_out.at[place], local.at[1]))
    keeps[1].start()
    held[pl.ds(place, 1)] = own[...][None]
    for step, other in enumerate(others):
        sum_push(step, other, other).wait_recv()
    value = held[0]
    for rank in range(1, ranks):
        value = value + held[rank]
    total[...] = value
    for step, other in enumerate(others):
        push(step, other, other).wait_recv()
        pass_far(other).start()
        pass_twin(0, other).start()
    for other in others:
        pass_far(other).wait_recv()
        pass_twin(1, other).start()
    for step, other in enumerate(others):
        sum_push(step, other, place).wait_send()
        text_push(step, other, other).wait_recv()
        text_push(step, other, place).wait_send()
        push(step, other, place).wait_send()
        pass_far(other).wait_send()
        for which in range(2):
            pass_twin(which, other).wait_recv()
            pass_twin(which, other).wait_send()
    for copy in keeps:
        copy.wait()


def first_transfers(own, qkv, text, ident):
    ranks, quarters = lax.axis_size("rows"), lax.axis_size("items")
    depth = qkv.shape[0]
    anywhere = pl.BlockSpec(memory_space=pl.ANY)
    near = pl.BlockSpec(memory_space=pltpu.VMEM)
    outs = [
        jax.ShapeDtypeStruct(own.shape, own.dtype),
        jax.ShapeDtypeStruct((ranks, depth, qkv.shape[1] // ranks), qkv.dtype),
        jax.ShapeDtypeStruct((ranks,) + text.shape[:-1] + (text.shape[-1] // ranks,), text.dtype),
    ]
    wave = pltpu.SemaphoreType.DMA
    return pl.pallas_call(
        functools.partial(first_kernel, ranks, quarters),
        out_shape=outs,
        in_specs=[near, near, anywhere],
        out_specs=[near, anywhere, anywhere],
        scratch_shapes=[
            pltpu.VMEM((ranks,) + own.shape, own.dtype),
            pltpu.VMEM(outs[1].shape, qkv.dtype),
            wave((2,)),
        ]
        + [wave((ranks,))] * 8
        + [wave((2, ranks))] * 2,
        name=f"first_transfers_{ident}",
        compiler_params=pltpu.CompilerParams(
            collective_id=ident, has_side_effects=True, vmem_limit_bytes=24 << 20
        ),
    )(own, qkv, text)


def pack_kernel(pieces, whole, packed):
    ranks, span = packed.shape[0], packed.shape[2] // pieces
    for rank in range(ranks):
        packed[rank] = jnp.concatenate(
            [whole[:, (piece * ranks + rank) * span : (piece * ranks + rank + 1) * span] for piece in range(pieces)],
            axis=1,
        ).astype(packed.dtype)


def pack_blocks(whole, pieces, ranks, dtype):
    near = pl.BlockSpec(memory_space=pltpu.VMEM)
    return pl.pallas_call(
        functools.partial(pack_kernel, pieces),
        out_shape=jax.ShapeDtypeStruct((ranks, whole.shape[0], whole.shape[1] // ranks), dtype),
        in_specs=[near],
        out_specs=near,
        name="pack_blocks",
        compiler_params=pltpu.CompilerParams(vmem_limit_bytes=24 << 20),
    )(whole)


def unpack_kernel(pieces, packed, whole):
    ranks, span = packed.shape[0], packed.shape[2] // pieces
    for piece in range(pieces):
        for rank in range(0, ranks, 2):
            start = (piece * ranks + rank) * span
            whole[:, start : start + 2 * span] = jnp.concatenate(
                [packed[rank + k, :, piece * span : (piece + 1) * span] for k in range(2)], axis=1
            ).astype(whole.dtype)


def unpack_blocks(packed, pieces, dtype):
    near = pl.BlockSpec(memory_space=pltpu.VMEM)
    ranks, rows, width = packed.shape
    return pl.pallas_call(
        functools.partial(unpack_kernel, pieces),
        out_shape=jax.ShapeDtypeStruct((rows, ranks * width), dtype),
        in_specs=[near],
        out_specs=near,
        name="unpack_blocks",
        compiler_params=pltpu.CompilerParams(vmem_limit_bytes=24 << 20),
    )(packed)


def halves_kernel(pieces, own, other, whole):
    ranks, half, span = own.shape[0], own.shape[1], own.shape[2] // pieces
    first = lax.rem(lax.axis_index("items"), 2) == 0
    for low in range(2):

        @pl.when(first == (low == 0))
        def _(low=low):
            for source, start in ((own, low * half), (other, (1 - low) * half)):
                for piece in range(pieces):
                    for rank in range(0, ranks, 2):
                        column = (piece * ranks + rank) * span
                        whole[start : start + half, column : column + 2 * span] = jnp.concatenate(
                            [source[rank + k, :, piece * span : (piece + 1) * span] for k in range(2)], axis=1
                        ).astype(whole.dtype)


def unpack_halves(own, other, pieces):
    near = pl.BlockSpec(memory_space=pltpu.VMEM)
    ranks, half, width = own.shape
    return pl.pallas_call(
        functools.partial(halves_kernel, pieces),
        out_shape=jax.ShapeDtypeStruct((2 * half, ranks * width), jnp.float32),
        in_specs=[near, near],
        out_specs=near,
        name="unpack_halves",
        compiler_params=pltpu.CompilerParams(vmem_limit_bytes=32 << 20),
    )(own, other)


def gather_tokens(block, ident, after=()):
    whole = gather_rows(block, ident, 1, after)
    return whole.reshape(-1, block.shape[-1])


def scatter_tokens(partial, items, ident, after=()):
    ranks = lax.axis_size("rows")
    blocks = partial.astype(jnp.bfloat16).reshape(items, ranks, -1, partial.shape[-1])
    return scatter_rows(blocks, ident, 1, after)


NEAR = pl.BlockSpec(memory_space=pltpu.VMEM)
SCALARS = pl.BlockSpec(memory_space=pltpu.SMEM)
NT = (((1,), (1,)), ((), ()))


def local_params():
    return pltpu.CompilerParams(vmem_limit_bytes=48 << 20)


def text_item(text, item):
    block = text[:, item]
    return block.reshape(block.shape[0] * block.shape[1], block.shape[2])


def lanes_to_rows(columns, rows):
    lane = lax.broadcasted_iota(jnp.int32, (128, 128), 1)
    held = jnp.zeros((128, 128), jnp.float32)
    for place, column in enumerate(columns):
        held = jnp.where(lane == place, column, held)
    return jnp.transpose(held)[:rows]


def rows_to_lanes(rows):
    missing = jnp.zeros((128 - rows.shape[0], 128), jnp.float32)
    return jnp.transpose(jnp.concatenate([rows, missing], axis=0))


def project_kernel(attn, weight, text, proj, squares):
    span = text.shape[-1] // 2
    tokens = attn.shape[0]
    for start in range(0, tokens, 256):
        proj[start : start + 256] = jnp.dot(
            attn[start : start + 256], weight[...], preferred_element_type=jnp.float32
        )
    columns = []
    for part in range(2):
        for start in range(0, tokens, 128):
            block = proj[start : start + 128, part * span : (part + 1) * span]
            columns.append(jnp.sum(block * block, axis=1, keepdims=True))
    for item in range(text.shape[1]):
        block = text_item(text, item)[:, :span]
        columns.append(jnp.sum(block * block, axis=1, keepdims=True))
    squares[...] = lanes_to_rows(columns, squares.shape[0])


def project(attn, weight, text):
    count = 2 * attn.shape[0] // 128 + text.shape[1]
    return pl.pallas_call(
        project_kernel,
        out_shape=[
            jax.ShapeDtypeStruct((attn.shape[0], weight.shape[1]), jnp.float32),
            jax.ShapeDtypeStruct((-(-count // 8) * 8, 128), jnp.float32),
        ],
        in_specs=[NEAR] * 3,
        out_specs=[NEAR] * 2,
        name="project",
        compiler_params=local_params(),
    )(attn, weight, text)


def tile_lane():
    return lax.broadcasted_iota(jnp.int32, (1, 128), 1)


def swap_halves(tile):
    low = lax.rem(tile_lane(), 64) < 32
    return jnp.where(low, pltpu.roll(tile, 96, 1), pltpu.roll(tile, 32, 1))


def block_tables(tab, block, frame_lanes):
    by_row = lax.rem(tile_lane(), 32) < frame_lanes
    rows = 128 // COLS
    cosines, sines = [], []
    for row in range(rows):
        at = pl.ds(block * rows + row, 1)
        cosines.append(jnp.where(by_row, tab[0, at], tab[2, :COLS]))
        sines.append(jnp.where(by_row, tab[1, at], tab[3, :COLS]))
    return jnp.concatenate(cosines, axis=0), jnp.concatenate(sines, axis=0)


def block_inverse(inverse, block, blocks):
    lane = lax.broadcasted_iota(jnp.int32, (128, 128), 1)

    def column(place):
        return jnp.sum(jnp.where(lane == place, inverse, 0.0), axis=1, keepdims=True)

    query, key = column(block), column(blocks + block)
    return [query, jnp.where(tile_lane() < 64, query, key), key]


def attend_kernel(
    scale, width, counts, heights, text_lens, proj, totals, text, gains, text_gain, gate, w_out,
    parts, qkv, text_kv, tab, biases, text_biases,
):
    ranks, items = text.shape[0], text.shape[1]
    span = gate.shape[-1]
    heads, size = span // 64, 64
    tokens = proj.shape[0]
    blocks, item_blocks = tokens // 128, tokens // 128 // items
    seq = tokens // items
    slots = seq // ranks
    row_slots = slots // COLS
    frame_pairs = size // 8
    space_pairs = (size // 2 - frame_pairs) // 2

    place = lax.rem(tile_lane(), 32)
    frame_rate = jnp.exp(place.astype(jnp.float32) * (-math.log(10000.0) / frame_pairs))
    row_rate = jnp.exp((place - frame_pairs).astype(jnp.float32) * (-math.log(10000.0) / space_pairs))
    column_rate = jnp.exp(
        (place - frame_pairs - space_pairs).astype(jnp.float32) * (-math.log(10000.0) / space_pairs)
    )
    is_frame = place < frame_pairs
    rows = items * ranks * row_slots
    which = lax.broadcasted_iota(jnp.int32, (rows, 1), 0)
    frame_index = jnp.zeros((rows, 1), jnp.float32)
    frame_row = jnp.zeros((rows, 1), jnp.float32)
    seq_place = lax.broadcasted_iota(jnp.int32, (seq, 128), 0)
    for item in range(items):
        below = jnp.int32(0)
        bias = jnp.zeros((seq, 128), jnp.float32)
        for rank in range(ranks):
            live = counts[rank * items + item]
            for row in range(row_slots):
                index = below + row
                at = which == (item * ranks + rank) * row_slots + row
                frame_index = jnp.where(at, (index // heights[item]).astype(jnp.float32), frame_index)
                frame_row = jnp.where(at, lax.rem(index, heights[item]).astype(jnp.float32), frame_row)
            start = rank * slots
            inside = (seq_place >= start + live * COLS) & (seq_place < start + slots)
            bias = jnp.where(inside, masked_score, bias)
            below = below + live
        biases[item] = bias
        text_place = lax.broadcasted_iota(jnp.int32, text_biases.shape[1:], 0)
        text_biases[item] = jnp.where(text_place >= text_lens[item], masked_score, 0.0)
    column = lax.broadcasted_iota(jnp.int32, (COLS, 1), 0).astype(jnp.float32)
    row_angles = jnp.where(is_frame, frame_index * frame_rate, frame_row * row_rate)
    column_angles = column * column_rate
    sign = jnp.where(lax.rem(tile_lane(), 64) < 32, -1.0, 1.0)
    tab[0, :rows] = jnp.cos(row_angles)
    tab[1, :rows] = jnp.sin(row_angles) * sign
    tab[2, :COLS] = jnp.cos(column_angles)
    tab[3, :COLS] = jnp.sin(column_angles) * sign

    inverse = rows_to_lanes(lax.rsqrt(totals[...] / width + epsilon))
    for item in range(items):
        block = text_item(text, item)
        column = inverse[:, 2 * blocks + item : 2 * blocks + item + 1]
        text_kv[item] = jnp.concatenate(
            [block[:, :span] * column * text_gain[...], block[:, span:]], axis=1
        ).astype(text_kv.dtype)

    @pl.loop(0, blocks)
    def _(block):
        at = pl.ds(pl.multiple_of(block * 128, 128), 128)
        cosine, sine = block_tables(tab, block, frame_pairs + space_pairs)
        inverses = block_inverse(inverse, block, blocks)
        tiles = []
        for tile in range(3):
            lanes = slice(tile * 128, (tile + 1) * 128)
            value = proj[at, lanes] * inverses[tile] * gains[:, lanes]
            tiles.append(value * cosine + swap_halves(value) * sine)
        qkv[at] = jnp.concatenate(tiles + [proj[at, 2 * span :]], axis=1).astype(qkv.dtype)

    @pl.loop(0, blocks)
    def _(block):
        at = pl.ds(pl.multiple_of(block * 128, 128), 128)
        item = block // item_blocks
        keys_at = pl.ds(pl.multiple_of(item * seq, seq), seq)
        bias, text_bias = biases[item], text_biases[item]
        mixed = []
        for head in range(heads):
            lanes = slice(head * size, (head + 1) * size)

            def part_of(ref, rows, part):
                start = part * span + head * size
                return ref[rows, start : start + size]

            query = part_of(qkv, at, 0)

            def mix(keys, values, mask):
                scores = lax.dot_general(keys, query, NT, preferred_element_type=jnp.float32)
                scores = scores * scale + mask
                terms = jnp.exp(scores - jnp.max(scores, axis=0, keepdims=True))
                probs = terms * (1.0 / jnp.sum(terms, axis=0, keepdims=True))
                return lax.dot_general(
                    values,
                    probs.astype(jnp.bfloat16),
                    (((0,), (0,)), ((), ())),
                    preferred_element_type=jnp.float32,
                )

            out = mix(part_of(qkv, keys_at, 1), part_of(qkv, keys_at, 2), bias)
            text_keys = text_kv[item]
            cross = mix(
                text_keys[:, lanes], text_keys[:, span + head * size : span + (head + 1) * size], text_bias
            )
            mixed.append(jnp.transpose(out) + gate[:, lanes] * jnp.transpose(cross))
        combined = jnp.concatenate(mixed, axis=1).astype(jnp.bfloat16)
        parts[1][at] = combined
        parts[0][at] = jnp.dot(combined, w_out[...], preferred_element_type=jnp.float32).astype(jnp.bfloat16)


def attend(proj, totals, text, gains, text_gain, gate, w_out, counts, heights, text_lens, head_size):
    tokens, span, width = proj.shape[0], gate.shape[-1], w_out.shape[1]
    items, text_rows = text.shape[1], text.shape[0] * text.shape[2]
    low = jnp.bfloat16

    def body(*refs):
        ins, outs, scratch = refs[:10], refs[10:15], refs[15:]
        attend_kernel(
            head_size**-0.5, width, *ins, (outs[0], outs[1]), outs[2], outs[3], outs[4], *scratch
        )

    return pl.pallas_call(
        body,
        out_shape=[
            jax.ShapeDtypeStruct((tokens, width), low),
            jax.ShapeDtypeStruct((tokens, span), low),
            jax.ShapeDtypeStruct((tokens, 3 * span), low),
            jax.ShapeDtypeStruct((items, text_rows, 2 * span), low),
            jax.ShapeDtypeStruct((4, max(tokens // COLS, COLS), 128), jnp.float32),
        ],
        in_specs=[SCALARS] * 3 + [NEAR] * 7,
        out_specs=[NEAR] * 5,
        scratch_shapes=[
            pltpu.VMEM((items, tokens // items, 128), jnp.float32),
            pltpu.VMEM((items, text_rows, 128), jnp.float32),
        ],
        name="attend",
        compiler_params=local_params(),
    )(counts, heights, text_lens, proj, totals, text, gains, text_gain, gate, w_out)


def attend_back_kernel(
    scale, width, counts, text_lens, grad, w_out, qkv, text_kv, tab, proj, totals, text, gains, text_gain, gate,
    scaled, grad_value, text_scaled, text_value, sums, gain_sums, gate_sums,
    grad_query, key_sum, value_sum, text_key_sum, text_value_sum, biases, text_biases,
):
    ranks, items = text.shape[0], text.shape[1]
    span = gate.shape[-1]
    heads, size = span // 64, 64
    tokens = proj.shape[0]
    blocks, item_blocks = tokens // 128, tokens // 128 // items
    seq = tokens // items
    slots = seq // ranks
    frame_pairs = size // 8
    space_pairs = (size // 2 - frame_pairs) // 2
    seq_place = lax.broadcasted_iota(jnp.int32, (seq, 128), 0)
    for item in range(items):
        bias = jnp.zeros((seq, 128), jnp.float32)
        for rank in range(ranks):
            start = rank * slots
            live = counts[rank * items + item]
            inside = (seq_place >= start + live * COLS) & (seq_place < start + slots)
            bias = jnp.where(inside, masked_score, bias)
        biases[item] = bias
        text_place = lax.broadcasted_iota(jnp.int32, text_biases.shape[1:], 0)
        text_biases[item] = jnp.where(text_place >= text_lens[item], masked_score, 0.0)
    key_sum[...] = jnp.zeros_like(key_sum)
    value_sum[...] = jnp.zeros_like(value_sum)
    text_key_sum[...] = jnp.zeros_like(text_key_sum)
    text_value_sum[...] = jnp.zeros_like(text_value_sum)
    gate_sums[...] = jnp.zeros_like(gate_sums)
    gain_sums[...] = jnp.zeros_like(gain_sums)

    @pl.loop(0, blocks)
    def _(block):
        at = pl.ds(pl.multiple_of(block * 128, 128), 128)
        item = block // item_blocks
        keys_at = pl.ds(pl.multiple_of(item * seq, seq), seq)
        bias, text_bias = biases[item], text_biases[item]
        text_keys = text_kv[item]
        grad_combined = lax.dot_general(grad[at], w_out[...], NT, preferred_element_type=jnp.float32)
        self_low = grad_combined.astype(jnp.bfloat16)
        cross_low = (gate[...] * grad_combined).astype(jnp.bfloat16)
        queries, crossed = [], []
        for head in range(heads):
            lanes = slice(head * size, (head + 1) * size)
            query = qkv[at, lanes]

            def back(keys, values, low_grad, mask, key_total, value_total, rows):
                scores = lax.dot_general(keys, query, NT, preferred_element_type=jnp.float32)
                scores = scores * scale + mask
                terms = jnp.exp(scores - jnp.max(scores, axis=0, keepdims=True))
                probs = terms * (1.0 / jnp.sum(terms, axis=0, keepdims=True))
                grad_probs = lax.dot_general(values, low_grad, NT, preferred_element_type=jnp.float32)
                inner = jnp.sum(probs * grad_probs, axis=0, keepdims=True)
                score_low = (probs * (grad_probs - inner)).astype(jnp.bfloat16)
                probs_low = probs.astype(jnp.bfloat16)
                key_total[head, rows] += jnp.dot(score_low, query, preferred_element_type=jnp.float32)
                value_total[head, rows] += jnp.dot(probs_low, low_grad, preferred_element_type=jnp.float32)
                to_query = lax.dot_general(
                    keys, score_low, (((0,), (0,)), ((), ())), preferred_element_type=jnp.float32
                )
                return to_query, probs_low

            to_query, _ = back(
                qkv[keys_at, span + head * size : span + (head + 1) * size],
                qkv[keys_at, 2 * span + head * size : 2 * span + (head + 1) * size],
                self_low[:, lanes],
                bias,
                key_sum,
                value_sum,
                keys_at,
            )
            text_values = text_keys[:, span + head * size : span + (head + 1) * size]
            text_rows = pl.ds(pl.multiple_of(item * 128, 128), 128)
            cross_query, cross_probs = back(
                text_keys[:, lanes],
                text_values,
                cross_low[:, lanes],
                text_bias,
                text_key_sum,
                text_value_sum,
                text_rows,
            )
            crossed.append(
                jnp.transpose(
                    lax.dot_general(
                        text_values, cross_probs, (((0,), (0,)), ((), ())), preferred_element_type=jnp.float32
                    )
                )
            )
            queries.append(jnp.transpose(to_query + cross_query))
        grad_query[at] = jnp.concatenate(queries, axis=1) * scale
        gate_sums[...] += jnp.sum(
            grad_combined * jnp.concatenate(crossed, axis=1), axis=0, keepdims=True
        )

    inverse = rows_to_lanes(lax.rsqrt(totals[...] / width + epsilon))
    columns = [[], []]
    for block in range(blocks):
        at = slice(block * 128, (block + 1) * 128)
        cosine, sine = block_tables(tab, block, frame_pairs + space_pairs)
        inverses = block_inverse(inverse, block, blocks)
        keys = jnp.concatenate([key_sum[head, at] for head in range(heads)], axis=1) * scale
        both = jnp.concatenate([grad_query[at], keys], axis=1)
        products = []
        for tile in range(3):
            lanes = slice(tile * 128, (tile + 1) * 128)
            value = both[:, lanes]
            value = value * cosine - swap_halves(value) * sine
            unit = proj[at, lanes] * inverses[tile]
            gain_sums[0:1, lanes] += jnp.sum(value * unit, axis=0, keepdims=True)
            value = value * gains[:, lanes]
            scaled[at, lanes] = value
            products.append(value * unit)
        first = tile_lane() < 64
        query_part = products[0] + jnp.where(first, products[1], 0.0)
        key_part = products[2] + jnp.where(first, 0.0, products[1])
        columns[0].append(jnp.sum(query_part, axis=1, keepdims=True))
        columns[1].append(jnp.sum(key_part, axis=1, keepdims=True))
        grad_value[at] = jnp.concatenate([value_sum[head, at] for head in range(heads)], axis=1).astype(
            grad_value.dtype
        )
    for item in range(items):
        at = slice(item * 128, (item + 1) * 128)
        unit = text_item(text, item)[:, :span] * inverse[:, 2 * blocks + item : 2 * blocks + item + 1]
        value = jnp.concatenate([text_key_sum[head, at] for head in range(heads)], axis=1) * scale
        gain_sums[1:2, :span] += jnp.sum(value * unit, axis=0, keepdims=True)
        value = value * text_gain[...]
        text_scaled[at] = value
        text_value[at] = jnp.concatenate([text_value_sum[head, at] for head in range(heads)], axis=1).astype(
            text_value.dtype
        )
        columns[1].append(jnp.sum(value * unit, axis=1, keepdims=True))
    sums[...] = lanes_to_rows(columns[0] + columns[1], sums.shape[0])


def attend_back(
    grad, w_out, qkv, text_kv, tab, proj, totals, text, gains, text_gain, gate, counts, text_lens, head_size
):
    tokens, span, width = proj.shape[0], gate.shape[-1], w_out.shape[1]
    items, text_rows = text.shape[1], text.shape[0] * text.shape[2]
    heads = span // head_size
    low, single = jnp.bfloat16, jnp.float32
    return pl.pallas_call(
        functools.partial(attend_back_kernel, head_size**-0.5, width),
        out_shape=[
            jax.ShapeDtypeStruct((tokens, 2 * span), single),
            jax.ShapeDtypeStruct((tokens, span), low),
            jax.ShapeDtypeStruct((items * text_rows, span), single),
            jax.ShapeDtypeStruct((items * text_rows, span), low),
            jax.ShapeDtypeStruct(totals.shape, single),
            jax.ShapeDtypeStruct((8, 2 * span), single),
            jax.ShapeDtypeStruct((1, span), single),
        ],
        in_specs=[SCALARS] * 2 + [NEAR] * 11,
        out_specs=[NEAR] * 7,
        scratch_shapes=[
            pltpu.VMEM((tokens, span), single),
            pltpu.VMEM((heads, tokens, head_size), single),
            pltpu.VMEM((heads, tokens, head_size), single),
            pltpu.VMEM((heads, items * text_rows, head_size), single),
            pltpu.VMEM((heads, items * text_rows, head_size), single),
            pltpu.VMEM((items, tokens // items, 128), single),
            pltpu.VMEM((items, text_rows, 128), single),
        ],
        name="attend_back",
        compiler_params=local_params(),
    )(counts, text_lens, grad, w_out, qkv, text_kv, tab, proj, totals, text, gains, text_gain, gate)


def norms_back_kernel(width, proj, totals, sums, scaled, grad_value, text, text_scaled, text_value, qkv_low, text_low):
    items, span = text.shape[1], grad_value.shape[-1]
    tokens = proj.shape[0]
    blocks = tokens // 128
    inverse = rows_to_lanes(lax.rsqrt(totals[...] / width + epsilon))
    means = rows_to_lanes(sums[...] / width)
    first = tile_lane() < 64
    for block in range(blocks):
        at = slice(block * 128, (block + 1) * 128)

        def by_tile(columns):
            query = columns[:, block : block + 1]
            key = columns[:, blocks + block : blocks + block + 1]
            return [query, jnp.where(first, query, key), key]

        inverses, mean = by_tile(inverse), by_tile(means)
        tiles = []
        for tile in range(3):
            lanes = slice(tile * 128, (tile + 1) * 128)
            unit = proj[at, lanes] * inverses[tile]
            tiles.append((inverses[tile] * (scaled[at, lanes] - unit * mean[tile])).astype(qkv_low.dtype))
        qkv_low[at] = jnp.concatenate(tiles + [grad_value[at]], axis=1)
    for item in range(items):
        at = slice(item * 128, (item + 1) * 128)
        place = 2 * blocks + item
        column, mean = inverse[:, place : place + 1], means[:, place : place + 1]
        unit = text_item(text, item)[:, :span] * column
        low = (column * (text_scaled[at] - unit * mean)).astype(text_low.dtype)
        low = jnp.concatenate([low, text_value[at]], axis=1)
        text_low[:, item] = low.reshape(text_low.shape[0], text_low.shape[2], 2 * span)


def norms_back(proj, totals, sums, scaled, grad_value, text, text_scaled, text_value, width):
    low = jnp.bfloat16
    return pl.pallas_call(
        functools.partial(norms_back_kernel, width),
        out_shape=[
            jax.ShapeDtypeStruct(proj.shape, low),
            jax.ShapeDtypeStruct(text.shape, low),
        ],
        in_specs=[NEAR] * 8,
        out_specs=[NEAR] * 2,
        name="norms_back",
        compiler_params=local_params(),
    )(proj, totals, sums, scaled, grad_value, text, text_scaled, text_value)


def join_kernel(bit, own, other, out):
    mine = pl.program_id(0) == bit()

    @pl.when(mine)
    def _():
        out[0] = own[...].astype(out.dtype)

    @pl.when(jnp.logical_not(mine))
    def _():
        out[0] = other[...].astype(out.dtype)


def join_rows(own, other, bit, dtype):
    rows, width = own.shape
    step = min(rows, 128)
    near = pl.BlockSpec((step, width), lambda half, at: (at, 0))
    return pl.pallas_call(
        functools.partial(join_kernel, bit),
        grid=(2, rows // step),
        out_shape=jax.ShapeDtypeStruct((2, rows, width), dtype),
        in_specs=[near, near],
        out_specs=pl.BlockSpec((1, step, width), lambda half, at: (half, at, 0)),
        name="join_rows",
        compiler_params=local_params(),
    )(own, other)


def core_bit():
    return lax.rem(lax.axis_index("items"), 2)


def far_bit():
    return lax.axis_index("items") // 2


def join_blocks(own, other, bit):
    ranks, rows, width = own.shape
    block = pl.BlockSpec((1, rows, width), lambda rank: (rank, 0, 0))

    def kernel(one, two, out):
        mine = bit()
        for half in range(2):

            @pl.when(mine == half)
            def _(half=half):
                out[0, half * rows : (half + 1) * rows] = one[0]
                out[0, (1 - half) * rows : (2 - half) * rows] = two[0]

    return pl.pallas_call(
        kernel,
        grid=(ranks,),
        out_shape=jax.ShapeDtypeStruct((ranks, 2 * rows, width), own.dtype),
        in_specs=[block, block],
        out_specs=pl.BlockSpec((1, 2 * rows, width), lambda rank: (rank, 0, 0)),
        name="join_blocks",
        compiler_params=local_params(),
    )(own, other)


def lay_flat(vectors):
    flat = jnp.concatenate([vector.reshape(-1) for vector in vectors])
    rows = -(-flat.size // 1024) * 8
    return jnp.pad(flat, (0, rows * 128 - flat.size)).reshape(rows, 128)


def take_apart(total, vectors):
    flat, parts, start = total.reshape(-1), [], 0
    for vector in vectors:
        parts.append(flat[start : start + vector.size].reshape(vector.shape))
        start += vector.size
    return parts


def sum_vectors(vectors, ident):
    return take_apart(sum_rows(lay_flat(vectors), ident), vectors)


def first_sums(vectors, qkv, text, ident):
    total, qkv_here, text_in = first_transfers(lay_flat(vectors), qkv, text, ident)
    return take_apart(total, vectors), qkv_here, text_in


CORES = [(0, 1), (1, 0), (2, 3), (3, 2)]
FARS = [(0, 2), (1, 3), (2, 0), (3, 1)]


def swap(array, pairs):
    return lax.ppermute(array, "items", pairs)


def give_keep(grad, index, axis):
    keep = lax.dynamic_index_in_dim(grad, index, axis, keepdims=False)
    give = lax.dynamic_index_in_dim(grad, 1 - index, axis, keepdims=False)
    return give, keep


def add_low(one, other):
    return (one.astype(jnp.float32) + other.astype(jnp.float32)).astype(jnp.bfloat16)


def head_parallel_plan(
    hidden_in,
    cotangent,
    text_states,
    time_embed,
    live_rows,
    frame_rows,
    text_len,
    w_qkv,
    w_out,
    w_text,
    w_gu,
    w_down,
    w_ada,
    gains,
    cross_gate,
    ada_bias,
    text_gain,
):
    single = jnp.float32
    narrow = jnp.bfloat16
    ranks = lax.axis_size("rows")
    place = lax.axis_index("rows")
    width = hidden_in.shape[2]
    heads = cross_gate.shape[0]
    head_size = width // heads
    score_scale = head_size ** (-0.5)
    items = time_embed.shape[1]
    slots = hidden_in.shape[1] // items
    row_slots = slots // COLS
    seq_len = ranks * slots
    text_local = text_states.shape[2]
    text_all = text_local * ranks
    text_width = text_states.shape[3]
    span = width // ranks
    heads_here = heads // ranks
    tokens = items * seq_len

    def dot(left, right):
        return jnp.dot(left, right, preferred_element_type=single)

    def dot_back(left, weight):
        return jnp.einsum("tn,kn->tk", left, weight, preferred_element_type=single)

    def weight_grad(left, right):
        return jnp.einsum("tk,tn->kn", left, right, preferred_element_type=single)

    time_silu = jax.nn.silu(time_embed[0].astype(single)).astype(narrow)
    ada_depth = w_ada.shape[0]
    time_here = lax.dynamic_slice_in_dim(time_silu, place * ada_depth, ada_depth, 1)

    def spread(part, whole):
        return lax.dynamic_update_slice_in_dim(
            jnp.zeros((whole,), single), part.reshape(-1), place * part.size, 0
        )

    group = lax.axis_index("items")
    core, far = lax.rem(group, 2), group // 2
    counts_here = live_rows[0]
    text_float = text_states[0].astype(single).reshape(items * text_local, text_width)
    text_inverse = norm_parts(text_float)[1]
    (modulation, counts, text_inverse), qkv_here, text_in = first_sums(
        [
            dot(time_here, w_ada),
            spread(counts_here.astype(single), ranks * items),
            spread(text_inverse, ranks * items * text_local),
        ],
        w_qkv,
        text_states[0],
        0,
    )
    qkv_here = qkv_here.reshape(width, -1)
    modulation = modulation + ada_bias
    counts = counts.astype(jnp.int32)
    text_inverse = text_inverse.reshape(-1, 1)
    scale_attn = modulation[:, None, 0:width]
    gate_attn = jnp.tanh(modulation[:, None, width : 2 * width])
    scale_ffn = modulation[:, None, 2 * width : 3 * width]
    gate_ffn = jnp.tanh(modulation[:, None, 3 * width :])

    slot_in_row = jnp.arange(slots) // COLS
    live_mask = (slot_in_row[None, :] < counts_here[0][:, None]).astype(single)[..., None]
    def gain_here(index):
        return lax.dynamic_slice_in_dim(gains[index], place * span, span, 0)

    states = hidden_in[0].reshape(items, slots, width)
    unit_in, inverse_in = norm_parts(states)
    norm_in = unit_in * gains[0]
    attn_in = gather_tokens((norm_in * (1.0 + scale_attn)).astype(narrow), 1)
    hidden = w_down.shape[0]
    gu_depth = w_gu.shape[0] // 4
    gu_rows = lax.dynamic_slice_in_dim(w_gu, (2 * core + far) * gu_depth, gu_depth, 0)
    gu_rows = jnp.transpose(gu_rows.reshape(gu_depth, 2, ranks, hidden), (2, 0, 1, 3))
    gu_rows, attn_in = lax.optimization_barrier(
        (gu_rows.reshape(ranks, gu_depth, 2 * hidden), attn_in)
    )
    gu_part = lax.all_to_all(gu_rows, "rows", 0, 0, tiled=True)
    gu_pair = join_blocks(gu_part, swap(gu_part, FARS), far_bit)

    features = text_width // ranks
    features = text_width // ranks
    text_in = text_in.reshape(items * text_all, features)
    text_unit = text_in.astype(single) * text_inverse
    gain_text = lax.dynamic_slice_in_dim(text_gain, place * features, features, 0)
    text_norm = (text_unit * gain_text).astype(narrow)

    text_parts = pack_blocks(dot(text_norm, w_text).astype(narrow), 2, ranks, narrow)
    text_proj = scatter_rows(text_parts, 2, 0).reshape(ranks, items, text_local, 2 * span)
    qkv_proj, squares = project(attn_in, qkv_here, text_proj)
    totals = sum_rows(squares, 3)
    gains_both = jnp.concatenate([gain_here(1), gain_here(2)])[None]
    gain_t = gain_here(6)[None]
    gate_here = jnp.tanh(lax.dynamic_slice_in_dim(cross_gate, place * heads_here, heads_here, 0))
    gate_lanes = jnp.repeat(gate_here, head_size)[None]
    out_parts, combined, qkv_bf, text_kv, tables = attend(
        qkv_proj,
        totals,
        text_proj,
        gains_both,
        gain_t,
        gate_lanes,
        w_out,
        counts,
        frame_rows[0],
        text_len[0],
        head_size,
    )
    projected = scatter_tokens(out_parts, items, 4)

    unit_proj, inverse_proj = norm_parts(projected)
    norm_proj = unit_proj * gains[3]
    middle = states + gate_attn * norm_proj
    unit_mid, inverse_mid = norm_parts(middle)
    norm_mid = unit_mid * gains[4]
    ffn_in = gather_tokens((norm_mid * (1.0 + scale_ffn)).astype(narrow), 5)
    gu_columns = join_blocks(gu_pair, swap(gu_pair, CORES), core_bit)
    gu_here = gu_columns.reshape(width, 2 * w_down.shape[0])
    gate_up = dot(ffn_in, gu_here)
    gate_part, up_part = jnp.split(gate_up, 2, axis=1)
    sigmoid = 1.0 / (1.0 + jnp.exp(-gate_part))
    inner_act = (gate_part * sigmoid * up_part).astype(narrow)
    ffn_out = scatter_tokens(dot(inner_act, w_down), items, 6)
    unit_ffn, inverse_ffn = norm_parts(ffn_out)
    norm_ffn = unit_ffn * gains[5]
    output = live_mask * (middle + gate_ffn * norm_ffn)

    def over_tokens(values):
        return jnp.sum(values, axis=(0, 1))

    grad_result = live_mask * cotangent[0].reshape(items, slots, width)
    grad_gate_ffn = (1.0 - gate_ffn * gate_ffn)[:, 0] * jnp.sum(grad_result * norm_ffn, axis=1)
    grad_norm = gate_ffn * grad_result
    grad_five = over_tokens(grad_norm * unit_ffn)
    ffn_low = gather_tokens(
        norm_back(unit_ffn, inverse_ffn, grad_norm * gains[5]).astype(narrow), 7
    )
    grad_down = weight_grad(inner_act, ffn_low).astype(narrow).reshape(2, -1, width)
    give_down, keep_down = give_keep(grad_down, core, 0)
    grad_inner = dot_back(ffn_low, w_down)
    gate_up_low = jnp.concatenate(
        [
            grad_inner * up_part * sigmoid * (1.0 + gate_part * (1.0 - sigmoid)),
            grad_inner * gate_part * sigmoid,
        ],
        axis=1,
    ).astype(narrow)
    grad_gu = weight_grad(ffn_in, gate_up_low).astype(narrow)
    give_gu, keep_gu = give_keep(grad_gu.reshape(ranks, 2, -1, 2 * hidden), core, 1)
    grad_ffn_in = scatter_tokens(
        dot_back(gate_up_low, gu_here), items, 8, after=(give_down, give_gu)
    )
    half_down = add_low(keep_down, swap(give_down, CORES))
    half_gu = add_low(keep_gu, swap(give_gu, CORES))
    give_gu, keep_gu = give_keep(half_gu.reshape(ranks, 2, -1, 2 * hidden), far, 1)
    grad_scale_ffn = jnp.sum(grad_ffn_in * norm_mid, axis=1)
    grad_norm = grad_ffn_in * (1.0 + scale_ffn)
    grad_four = over_tokens(grad_norm * unit_mid)
    grad_middle = grad_result + norm_back(unit_mid, inverse_mid, grad_norm * gains[4])

    grad_gate_attn = (1.0 - gate_attn * gate_attn)[:, 0] * jnp.sum(grad_middle * norm_proj, axis=1)
    grad_norm = gate_attn * grad_middle
    grad_three = over_tokens(grad_norm * unit_proj)
    projected_low = gather_tokens(
        norm_back(unit_proj, inverse_proj, grad_norm * gains[3]).astype(narrow),
        9,
        after=(half_down, give_gu),
    )
    sum_down = add_low(half_down, swap(half_down, FARS))
    sum_gu = add_low(keep_gu, swap(give_gu, FARS))
    rows_gu = lax.all_to_all(sum_gu, "rows", 0, 0, tiled=True)
    grad_out = weight_grad(combined, projected_low).astype(narrow).reshape(2, -1, width)
    give_out, keep_out = give_keep(grad_out, core, 0)
    scaled, grad_value, text_scaled, text_value, sums, gain_sums, gate_sums = attend_back(
        projected_low,
        w_out,
        qkv_bf,
        text_kv,
        tables,
        qkv_proj,
        totals,
        text_proj,
        gains_both,
        gain_t,
        gate_lanes,
        counts,
        text_len[0],
        head_size,
    )
    grad_gate = (1.0 - gate_here * gate_here) * jnp.sum(
        gate_sums.reshape(heads_here, head_size), axis=1
    )
    qkv_low, text_low = norms_back(
        qkv_proj,
        totals,
        sum_rows(sums, 10),
        scaled,
        grad_value,
        text_proj,
        text_scaled,
        text_value,
        width,
    )
    grad_qkv = weight_grad(attn_in, qkv_low).astype(narrow)
    give_qkv, keep_qkv = give_keep(grad_qkv.reshape(ranks, 2, -1, 3 * span), core, 1)

    text_low = text_low.reshape(items * text_all, 2 * span)
    all_low = unpack_blocks(gather_rows(text_low, 12, 0, after=(give_qkv, give_out)), 2, narrow)
    half_out = add_low(keep_out, swap(give_out, CORES))
    half_qkv = add_low(keep_qkv, swap(give_qkv, CORES))
    give_qkv, keep_qkv = give_keep(half_qkv.reshape(ranks, 2, -1, 3 * span), far, 1)
    grad_text = weight_grad(text_norm, all_low).astype(narrow).reshape(2, -1, 2 * width)
    give_text, keep_text = give_keep(grad_text, core, 0)
    half_text = add_low(keep_text, swap(give_text, CORES))
    got_gu, got_out, got_qkv, got_text, got_down = (
        swap(rows_gu, FARS),
        swap(half_out, FARS),
        swap(give_qkv, FARS),
        swap(half_text, FARS),
        swap(sum_down, CORES),
    )
    grad_attn_in = scatter_tokens(
        dot_back(qkv_low, qkv_here),
        items,
        11,
        after=(half_out, give_qkv, half_text, rows_gu, sum_down),
    )
    grad_attn_in, got_gu, got_out, got_qkv, got_text, got_down = lax.optimization_barrier(
        (grad_attn_in, got_gu, got_out, got_qkv, got_text, got_down)
    )
    pair_gu = join_blocks(rows_gu, got_gu, far_bit)
    sum_out = add_low(half_out, got_out)
    sum_qkv = add_low(keep_qkv, got_qkv)
    sum_text = add_low(half_text, got_text)
    grad_scale_attn = jnp.sum(grad_attn_in * norm_in, axis=1)
    grad_norm = grad_attn_in * (1.0 + scale_attn)
    grad_zero = over_tokens(grad_norm * unit_in)
    grad_x = grad_middle + norm_back(unit_in, inverse_in, grad_norm * gains[0])

    grad_text_gain = jnp.sum(dot_back(all_low, w_text) * text_unit, axis=0)
    grad_modulation = jnp.stack([grad_scale_attn, grad_gate_attn, grad_scale_ffn, grad_gate_ffn], 1)
    grad_gains = jnp.stack(
        [
            grad_zero,
            spread(gain_sums[0, :span], width),
            spread(gain_sums[0, span:], width),
            grad_three,
            grad_four,
            grad_five,
            spread(gain_sums[1, :span], width),
        ]
    )
    flat = jnp.concatenate(
        [
            grad_gains.reshape(-1),
            spread(grad_text_gain, text_width),
            spread(grad_gate, heads),
        ]
    )
    lanes = ranks * 128
    sum_depth = -(-flat.size // lanes)
    flat = jnp.pad(flat, (0, sum_depth * lanes - flat.size)).reshape(ranks, sum_depth, 128)
    time_rows = spread(time_here.astype(single), ranks * time_here.size).reshape(ranks, -1, 128)
    grad_depth, time_depth = grad_modulation.size // lanes, time_rows.shape[1]
    keep_depth = grad_depth + time_depth
    reduced = final_sums(
        jnp.concatenate([flat, grad_modulation.reshape(ranks, grad_depth, 128), time_rows], axis=1),
        sum_depth,
        13,
    )
    flat = reduced[:, :sum_depth].reshape(-1)
    total_gains = flat[: gains.size].reshape(gains.shape)
    total_text_gain = flat[gains.size : gains.size + text_width]
    total_gate = flat[gains.size + text_width : gains.size + text_width + heads]
    groups = lax.axis_size("items")
    kept = reduced[:, sum_depth:].reshape(ranks, groups, keep_depth, 128)
    all_modulation = jnp.swapaxes(kept[:, :, :grad_depth], 0, 1).reshape(groups * items, 4 * width)
    all_time = lax.dynamic_index_in_dim(kept[:, :, grad_depth:], place, 0, keepdims=False)
    all_time = all_time.reshape(groups * items, ada_depth)
    final_ada = jnp.einsum(
        "tk,tn->kn",
        all_time,
        all_modulation,
        precision=lax.Precision.HIGHEST,
        preferred_element_type=single,
    )
    total_bias = jnp.sum(all_modulation, axis=0)
    rows_qkv = lax.all_to_all(sum_qkv, "rows", 0, 0, tiled=True)
    pair_qkv = join_blocks(rows_qkv, swap(rows_qkv, FARS), far_bit)

    def whole_rows(half, got):
        return join_rows(half, got, core_bit, single).reshape(-1, half.shape[-1])

    sums = [
        unpack_halves(pair_qkv, swap(pair_qkv, CORES), 3),
        whole_rows(sum_out, swap(sum_out, CORES)),
        whole_rows(sum_text, swap(sum_text, CORES)),
        unpack_halves(pair_gu, swap(pair_gu, CORES), 2),
        whole_rows(sum_down, got_down),
    ]
    return (
        output.reshape(1, items * slots, width),
        grad_x.reshape(1, items * slots, width),
        *sums,
        final_ada,
        total_gains,
        total_gate,
        total_bias,
        total_text_gain,
    )


def per_device(*arrays):
    heads = arrays[14].shape[0]
    plan = gathered_plan if heads % lax.axis_size("rows") else head_parallel_plan
    return plan(*arrays)


def solution(mesh):
    in_specs = (
        P("items", "rows", None),
        P("items", "rows", None),
        P("items", None, "rows", None),
        P("items", None, None),
        P("items", "rows", None),
        P("items", None),
        P("items", None),
        P("rows", None),
        P("rows", None),
        P("rows", None),
        P("rows", None),
        P("rows", None),
        P("rows", None),
        P(),
        P(),
        P(),
        P(),
    )
    out_specs = (
        P("items", "rows", None),
        P("items", "rows", None),
        P("rows", None),
        P("rows", None),
        P("rows", None),
        P("rows", None),
        P("rows", None),
        P("rows", None),
        P(),
        P(),
        P(),
        P(),
    )
    return jax.shard_map(
        per_device, mesh=mesh, in_specs=in_specs, out_specs=out_specs, check_vma=False
    )
```

```python
import functools
import math

import jax
import jax.numpy as jnp
from jax import lax
from jax.experimental import pallas as pl
from jax.experimental.pallas import tpu as pltpu
from jax.sharding import PartitionSpec as P

COLS = 32


epsilon = 1e-06
masked_score = -1e30
group_heads = 4


def norm_gain(values, scaling):
    return values * lax.rsqrt(jnp.mean(values * values, axis=-1, keepdims=True) + epsilon) * scaling


def pre_norm(values, shift_scale, scaling):
    return norm_gain(values, scaling) * (1.0 + shift_scale)


def post_add(residual, branch, gate_in, scaling):
    return residual + jnp.tanh(gate_in) * norm_gain(branch, scaling)


def swiglu(gate_up):
    middle_col = gate_up.shape[-1] // 2
    return jax.nn.silu(gate_up[..., :middle_col]) * gate_up[..., middle_col:]


def freq_rates(number):
    return 10000.0 ** (-jnp.arange(number).astype(jnp.float32) / number)


def rotary_angles(frame_index, frame_row, column, head_size):
    frame_pairs = head_size // 8
    space_pairs = (head_size // 2 - frame_pairs) // 2
    return jnp.concatenate(
        [
            frame_index.astype(jnp.float32)[..., None] * freq_rates(frame_pairs),
            frame_row.astype(jnp.float32)[..., None] * freq_rates(space_pairs),
            column.astype(jnp.float32)[..., None] * freq_rates(space_pairs),
        ],
        axis=-1,
    )


def rotate(values, cos_table, sin_table, head_count):
    shaped = values.reshape(values.shape[:-1] + (head_count, values.shape[-1] // head_count))
    half_size = shaped.shape[-1] // 2
    upper_half = shaped[..., :half_size]
    lower_half = shaped[..., half_size:]
    cos_heads = cos_table[..., None, :]
    sin_heads = sin_table[..., None, :]
    turned = jnp.concatenate(
        [
            upper_half * cos_heads - lower_half * sin_heads,
            upper_half * sin_heads + lower_half * cos_heads,
        ],
        axis=-1,
    )
    return turned.reshape(values.shape)


def text_split(projected, key_gain):
    half_cols = projected.shape[-1] // 2
    return (norm_gain(projected[..., :half_cols], key_gain), projected[..., half_cols:])


def gathered_plan(
    hidden_in,
    cotangent,
    text_states,
    time_embed,
    live_rows,
    frame_rows,
    text_len,
    w_qkv,
    w_out,
    w_text,
    w_gu,
    w_down,
    w_ada,
    gains,
    cross_gate,
    ada_bias,
    text_gain,
):
    single = jnp.float32
    narrow = jnp.bfloat16
    model_width = hidden_in.shape[2]
    head_count = cross_gate.shape[0]
    head_size = model_width // head_count
    score_scale = head_size ** (-0.5)
    item_count = time_embed.shape[1]
    item_slots = hidden_in.shape[1] // item_count
    row_devices = lax.axis_size("rows")
    seq_len = row_devices * item_slots
    text_local = text_states.shape[2]
    text_all = text_local * row_devices
    text_width = text_states.shape[3]
    group_span = group_heads * head_size
    block_count = head_count // group_heads
    token_count = item_count * item_slots

    def weight_term(left, right, accuracy):
        return jnp.einsum(
            "tk,tn->kn", left, right, precision=accuracy, preferred_element_type=single
        )

    def reduce_term(term):
        return lax.psum_scatter(
            term.astype(jnp.bfloat16), "rows", scatter_dimension=0, tiled=True
        ).astype(jnp.float32)

    full_qkv, full_out, full_text, full_gu, full_down, full_ada = (
        lax.all_gather(w_qkv, "rows", axis=0, tiled=True),
        lax.all_gather(w_out, "rows", axis=0, tiled=True),
        lax.all_gather(w_text, "rows", axis=0, tiled=True),
        lax.all_gather(w_gu, "rows", axis=0, tiled=True),
        lax.all_gather(w_down, "rows", axis=0, tiled=True),
        lax.all_gather(w_ada, "rows", axis=0, tiled=True),
    )
    counts_here = live_rows[0]
    every_count = lax.all_gather(counts_here, "rows", axis=0, tiled=True)
    device_place = lax.axis_index("rows")
    ranks = jnp.arange(row_devices)
    rows_below = jnp.sum(jnp.where(ranks[:, None] < device_place, every_count, 0), axis=0)
    slot_row = jnp.arange(item_slots) // COLS
    column = jnp.arange(item_slots) % COLS
    row_index = rows_below[:, None] + slot_row[None, :]
    heights = frame_rows[0][:, None]
    frame_index = row_index // heights
    frame_row = row_index % heights
    live_mask = (slot_row[None, :] < counts_here[0][:, None]).astype(single)
    key_live = (slot_row[None, None, :] < jnp.transpose(every_count)[:, :, None]).reshape(
        item_count, seq_len
    )
    text_live = jnp.arange(text_all)[None, :] < text_len[0][:, None]
    angles = rotary_angles(
        frame_index, frame_row, jnp.broadcast_to(column, row_index.shape), head_size
    )
    cos_table = jnp.cos(angles)
    sin_table = jnp.sin(angles)

    def qkv_split(projected, gain_query, gain_key):
        queries = rotate(
            norm_gain(projected[..., :model_width], gain_query), cos_table, sin_table, head_count
        )
        keys_here = rotate(
            norm_gain(projected[..., model_width : 2 * model_width], gain_key),
            cos_table,
            sin_table,
            head_count,
        )
        return (queries, keys_here, projected[..., 2 * model_width :])

    states = hidden_in[0].reshape(item_count, item_slots, model_width)
    time_silu = jax.nn.silu(time_embed[0].astype(single)).astype(narrow)
    modulation = jnp.dot(time_silu, full_ada, preferred_element_type=single) + ada_bias
    scale_attn = modulation[:, None, 0:model_width]
    gate_attn = modulation[:, None, model_width : 2 * model_width]
    scale_ffn = modulation[:, None, 2 * model_width : 3 * model_width]
    gate_ffn = modulation[:, None, 3 * model_width :]
    attn_in = (
        pre_norm(states, scale_attn, gains[0]).astype(narrow).reshape(token_count, model_width)
    )
    qkv_proj = jnp.dot(attn_in, full_qkv, preferred_element_type=single).reshape(
        item_count, item_slots, 3 * model_width
    )
    query_full, key_full, value_full = qkv_split(qkv_proj, gains[1], gains[2])
    query_low = query_full.astype(narrow)
    key_low = key_full.astype(narrow)
    value_low = value_full.astype(narrow)
    text_float = text_states[0].astype(single)
    text_norm = norm_gain(text_float, text_gain).astype(narrow)
    text_proj = jnp.einsum("ctd,dn->ctn", text_norm, full_text, preferred_element_type=single)
    tkey_full, tval_full = text_split(text_proj, gains[6])
    key_all, value_all, tkey_all, tval_all = (
        lax.all_gather(key_low, "rows", axis=1, tiled=True),
        lax.all_gather(value_low, "rows", axis=1, tiled=True),
        lax.all_gather(tkey_full.astype(narrow), "rows", axis=1, tiled=True),
        lax.all_gather(tval_full.astype(narrow), "rows", axis=1, tiled=True),
    )

    def block_slices(block_index, key_source, value_source):
        offset = block_index * group_span
        query_part = lax.dynamic_slice_in_dim(query_low, offset, group_span, 2).reshape(
            item_count, item_slots, group_heads, head_size
        )
        key_part = lax.dynamic_slice_in_dim(key_source, offset, group_span, 2).reshape(
            item_count, seq_len, group_heads, head_size
        )
        value_part = lax.dynamic_slice_in_dim(value_source, offset, group_span, 2).reshape(
            item_count, seq_len, group_heads, head_size
        )
        return (query_part, key_part, value_part)

    def self_step(carry, block_index):
        query_part, key_part, value_part = block_slices(block_index, key_all, value_all)
        scores = (
            jnp.einsum("iphe,ikhe->ihpk", query_part, key_part, preferred_element_type=single)
            * score_scale
        )
        scores = jnp.where(key_live[:, None, None, :], scores, masked_score)
        row_max = jnp.max(scores, axis=-1, keepdims=True)
        exp_terms = jnp.exp(scores - row_max)
        exp_total = jnp.sum(exp_terms, axis=-1, keepdims=True)
        probs_low = (exp_terms / exp_total).astype(narrow)
        attended = jnp.einsum(
            "ihpk,ikhe->iphe", probs_low, value_part, preferred_element_type=single
        )
        return (
            carry,
            (
                attended.reshape(item_count, item_slots, group_span),
                (row_max + jnp.log(exp_total))[..., 0],
            ),
        )

    _, (self_parts, log_totals) = lax.scan(
        self_step, jnp.zeros((), single), jnp.arange(block_count)
    )

    def heads_last(parts):
        return jnp.transpose(parts, (1, 2, 0, 3)).reshape(item_count, item_slots, model_width)

    self_out = heads_last(self_parts)
    query_heads = query_low.reshape(item_count, item_slots, head_count, head_size)
    tkey_heads = tkey_all.reshape(item_count, text_all, head_count, head_size)
    tval_heads = tval_all.reshape(item_count, text_all, head_count, head_size)
    cross_scores = (
        jnp.einsum("iphe,ikhe->ihpk", query_heads, tkey_heads, preferred_element_type=single)
        * score_scale
    )
    cross_scores = jnp.where(text_live[:, None, None, :], cross_scores, masked_score)
    cross_max = jnp.max(cross_scores, axis=-1, keepdims=True)
    cross_exp = jnp.exp(cross_scores - cross_max)
    cross_probs = cross_exp / jnp.sum(cross_exp, axis=-1, keepdims=True)
    cross_low = cross_probs.astype(narrow)
    cross_out = jnp.einsum("ihpk,ikhe->iphe", cross_low, tval_heads, preferred_element_type=single)
    tanh_gate = jnp.tanh(cross_gate)
    combined = (
        self_out.reshape(item_count, item_slots, head_count, head_size)
        + tanh_gate[:, None] * cross_out
    )
    combined = combined.reshape(token_count, model_width).astype(narrow)
    projected = jnp.dot(combined, full_out, preferred_element_type=single).reshape(
        item_count, item_slots, model_width
    )
    middle = post_add(states, projected, gate_attn, gains[3])
    ffn_in = pre_norm(middle, scale_ffn, gains[4]).astype(narrow).reshape(token_count, model_width)
    gate_up = jnp.dot(ffn_in, full_gu, preferred_element_type=single)
    inner_act = swiglu(gate_up).astype(narrow)
    ffn_out = jnp.dot(inner_act, full_down, preferred_element_type=single).reshape(
        item_count, item_slots, model_width
    )
    result = post_add(middle, ffn_out, gate_ffn, gains[5])
    output = (live_mask[..., None] * result).reshape(1, token_count, model_width)
    grad_result = live_mask[..., None] * cotangent[0].reshape(item_count, item_slots, model_width)
    _, back_ffn_out = jax.vjp(post_add, middle, ffn_out, gate_ffn, gains[5])
    grad_middle, grad_ffn_out, grad_gate_ffn, grad_gain_five = back_ffn_out(grad_result)
    ffn_low = grad_ffn_out.astype(narrow).reshape(token_count, model_width)
    shard_down = reduce_term(weight_term(inner_act, ffn_low, None))
    grad_inner = jnp.einsum("tn,kn->tk", ffn_low, full_down, preferred_element_type=single)
    _, back_glu = jax.vjp(swiglu, gate_up)
    gate_up_low = back_glu(grad_inner)[0].astype(narrow)
    shard_gu = reduce_term(weight_term(ffn_in, gate_up_low, None))
    grad_ffn_in = jnp.einsum("tn,kn->tk", gate_up_low, full_gu, preferred_element_type=single)
    _, back_ffn_in = jax.vjp(pre_norm, middle, scale_ffn, gains[4])
    part_middle, grad_scale_ffn, grad_gain_four = back_ffn_in(
        grad_ffn_in.reshape(item_count, item_slots, model_width)
    )
    grad_middle = grad_middle + part_middle
    _, back_attn_out = jax.vjp(post_add, states, projected, gate_attn, gains[3])
    grad_hidden, grad_projected, grad_gate_attn, grad_gain_three = back_attn_out(grad_middle)
    projected_low = grad_projected.astype(narrow).reshape(token_count, model_width)
    shard_out = reduce_term(weight_term(combined, projected_low, None))
    grad_combined = jnp.einsum("tn,kn->tk", projected_low, full_out, preferred_element_type=single)
    grad_combined = grad_combined.reshape(item_count, item_slots, head_count, head_size)
    self_low = grad_combined.reshape(item_count, item_slots, model_width).astype(narrow)
    cross_grad_low = (tanh_gate[:, None] * grad_combined).astype(narrow)
    grad_cross_gate = (1.0 - tanh_gate * tanh_gate) * jnp.sum(
        grad_combined * cross_out, axis=(0, 1, 3)
    )

    def self_back(carry, packed):
        block_index, log_total = packed
        query_part, key_part, value_part = block_slices(block_index, key_all, value_all)
        offset = block_index * group_span
        grad_part = lax.dynamic_slice_in_dim(self_low, offset, group_span, 2).reshape(
            item_count, item_slots, group_heads, head_size
        )
        scores = (
            jnp.einsum("iphe,ikhe->ihpk", query_part, key_part, preferred_element_type=single)
            * score_scale
        )
        scores = jnp.where(key_live[:, None, None, :], scores, masked_score)
        attn_probs = jnp.exp(scores - log_total[..., None])
        grad_probs = jnp.einsum(
            "iphe,ikhe->ihpk", grad_part, value_part, preferred_element_type=single
        )
        row_inner = jnp.sum(attn_probs * grad_probs, axis=-1, keepdims=True)
        score_low = (attn_probs * (grad_probs - row_inner)).astype(narrow)
        grad_query = (
            jnp.einsum("ihpk,ikhe->iphe", score_low, key_part, preferred_element_type=single)
            * score_scale
        )
        grad_value = jnp.einsum(
            "ihpk,iphe->ikhe", attn_probs.astype(narrow), grad_part, preferred_element_type=single
        )
        grad_key = (
            jnp.einsum("ihpk,iphe->ikhe", score_low, query_part, preferred_element_type=single)
            * score_scale
        )
        owned_key, owned_value = (
            lax.psum_scatter(
                grad_key.reshape(item_count, seq_len, group_span).astype(jnp.bfloat16),
                "rows",
                scatter_dimension=1,
                tiled=True,
            ).astype(jnp.float32),
            lax.psum_scatter(
                grad_value.reshape(item_count, seq_len, group_span).astype(jnp.bfloat16),
                "rows",
                scatter_dimension=1,
                tiled=True,
            ).astype(jnp.float32),
        )
        return (
            carry,
            (grad_query.reshape(item_count, item_slots, group_span), owned_key, owned_value),
        )

    _, (query_parts, key_parts, value_parts) = lax.scan(
        self_back, jnp.zeros((), single), (jnp.arange(block_count), log_totals)
    )
    cross_grad_probs = jnp.einsum(
        "iphe,ikhe->ihpk", cross_grad_low, tval_heads, preferred_element_type=single
    )
    cross_inner = jnp.sum(cross_probs * cross_grad_probs, axis=-1, keepdims=True)
    cross_score_low = (cross_probs * (cross_grad_probs - cross_inner)).astype(narrow)
    grad_query_cross = (
        jnp.einsum("ihpk,ikhe->iphe", cross_score_low, tkey_heads, preferred_element_type=single)
        * score_scale
    )
    grad_text_key = (
        jnp.einsum("ihpk,iphe->ikhe", cross_score_low, query_heads, preferred_element_type=single)
        * score_scale
    )
    grad_text_value = jnp.einsum(
        "ihpk,iphe->ikhe", cross_low, cross_grad_low, preferred_element_type=single
    )
    owned_tkey, owned_tval = (
        lax.psum_scatter(
            grad_text_key.reshape(item_count, text_all, model_width).astype(jnp.bfloat16),
            "rows",
            scatter_dimension=1,
            tiled=True,
        ).astype(jnp.float32),
        lax.psum_scatter(
            grad_text_value.reshape(item_count, text_all, model_width).astype(jnp.bfloat16),
            "rows",
            scatter_dimension=1,
            tiled=True,
        ).astype(jnp.float32),
    )
    grad_query_all = heads_last(query_parts) + grad_query_cross.reshape(
        item_count, item_slots, model_width
    )
    _, back_qkv = jax.vjp(qkv_split, qkv_proj, gains[1], gains[2])
    grad_qkv, grad_gain_one, grad_gain_two = back_qkv(
        (grad_query_all, heads_last(key_parts), heads_last(value_parts))
    )
    qkv_low = grad_qkv.astype(narrow).reshape(token_count, 3 * model_width)
    shard_qkv = reduce_term(weight_term(attn_in, qkv_low, None))
    grad_attn_in = jnp.einsum("tn,kn->tk", qkv_low, full_qkv, preferred_element_type=single)
    _, back_attn_in = jax.vjp(pre_norm, states, scale_attn, gains[0])
    part_states, grad_scale_attn, grad_gain_zero = back_attn_in(
        grad_attn_in.reshape(item_count, item_slots, model_width)
    )
    grad_x = (grad_hidden + part_states).reshape(1, token_count, model_width)
    _, back_text = jax.vjp(text_split, text_proj, gains[6])
    grad_text_proj, grad_gain_six = back_text((owned_tkey, owned_tval))
    text_low = grad_text_proj.astype(narrow).reshape(item_count * text_local, 2 * model_width)
    shard_text = reduce_term(
        weight_term(text_norm.reshape(item_count * text_local, text_width), text_low, None)
    )
    grad_text_norm = jnp.einsum("tn,kn->tk", text_low, full_text, preferred_element_type=single)
    _, back_text_norm = jax.vjp(norm_gain, text_float, text_gain)
    grad_text_gain = back_text_norm(grad_text_norm.reshape(text_float.shape))[1]
    grad_modulation = jnp.concatenate(
        [grad_scale_attn, grad_gate_attn, grad_scale_ffn, grad_gate_ffn], axis=-1
    )[:, 0, :]
    shard_ada = reduce_term(
        weight_term(time_silu.astype(single), grad_modulation, lax.Precision.HIGHEST)
    )
    grad_ada_bias = jnp.sum(grad_modulation, axis=0)
    grad_gains = jnp.stack(
        [
            grad_gain_zero,
            grad_gain_one,
            grad_gain_two,
            grad_gain_three,
            grad_gain_four,
            grad_gain_five,
            grad_gain_six,
        ],
        axis=0,
    )
    final_qkv, final_out, final_text, final_gu, final_down, final_ada = (
        lax.psum(shard_qkv.astype(jnp.bfloat16), "items").astype(jnp.float32),
        lax.psum(shard_out.astype(jnp.bfloat16), "items").astype(jnp.float32),
        lax.psum(shard_text.astype(jnp.bfloat16), "items").astype(jnp.float32),
        lax.psum(shard_gu.astype(jnp.bfloat16), "items").astype(jnp.float32),
        lax.psum(shard_down.astype(jnp.bfloat16), "items").astype(jnp.float32),
        lax.psum(shard_ada.astype(jnp.bfloat16), "items").astype(jnp.float32),
    )
    total_gains, total_gate, total_bias, total_text_gain = lax.psum(
        (grad_gains, grad_cross_gate, grad_ada_bias, grad_text_gain), ("items", "rows")
    )
    return (
        output,
        grad_x,
        final_qkv,
        final_out,
        final_text,
        final_gu,
        final_down,
        final_ada,
        total_gains,
        total_gate,
        total_bias,
        total_text_gain,
    )


def norm_parts(values):
    inverse = lax.rsqrt(jnp.mean(values * values, axis=-1, keepdims=True) + epsilon)
    return values * inverse, inverse


def norm_back(unit, inverse, scaled_grad):
    return inverse * (scaled_grad - unit * jnp.mean(scaled_grad * unit, axis=-1, keepdims=True))


MESH = pl.DeviceIdType.MESH
DEPTH, BREADTH = 4, 2


def row_place():
    place = lax.axis_index("rows")
    return place // BREADTH, lax.rem(place, BREADTH)


def on_rows(line, side):
    return {"rows": line * BREADTH + side}


def greet(devices):
    barrier = pltpu.get_barrier_semaphore()
    for condition, device in devices:

        @pl.when(condition)
        def _(device=device):
            pl.semaphore_signal(barrier, inc=1, device_id=device, device_id_type=MESH)

    count = 0
    for condition, _ in devices:
        count = count + jnp.where(condition, 1, 0)
    pl.semaphore_wait(barrier, count)


def remote(source, target, send, receive, device):
    return pltpu.make_async_remote_copy(
        src_ref=source,
        dst_ref=target,
        send_sem=send,
        recv_sem=receive,
        device_id=device,
        device_id_type=MESH,
    )


def shard_of(ref, place, axis):
    return ref.at[place] if axis == 0 else ref.at[:, place]


CHUNKS = 2


def partner(kind):
    group = lax.axis_index("items")
    if kind == "core":
        return {"items": group + 1 - 2 * lax.rem(group, 2)}
    return {"items": lax.rem(group + 2, 4)}


def chunk_part(ref, chunk, start, size):
    rows = ref.shape[0] // CHUNKS
    middle = (slice(None),) * (len(ref.shape) - 2)
    return ref.at[(pl.ds(chunk * rows, rows),) + middle + (pl.ds(start, size),)]


def streams_of(width):
    first = split_lanes(width)
    streams = [(0, chunk, 0, first) for chunk in range(CHUNKS)]
    if first < width:
        streams += [(which, chunk, first, width - first) for which in range(2) for chunk in range(CHUNKS)]
    return streams


class Swaps:
    def __init__(self, pairs):
        self.arrays = tuple(array for array, _ in pairs)
        self.kinds = tuple(kind for _, kind in pairs)

    def shapes(self):
        return [jax.ShapeDtypeStruct(array.shape, array.dtype) for array in self.arrays]

    def specs(self):
        return [pl.BlockSpec(memory_space=pl.ANY)] * len(self.arrays)

    def scratch(self):
        return [pltpu.SemaphoreType.DMA((2, max(1, len(self.arrays))))]

    def partners(self, always):
        return [(always, partner(kind)) for kind in sorted(set(self.kinds))]

    def copies(self, sources, targets, semaphores):
        return [
            remote(source, target, semaphores.at[0, at], semaphores.at[1, at], partner(kind))
            for at, (source, target, kind) in enumerate(zip(sources, targets, self.kinds))
        ]


def split_lanes(width):
    return width - 128 * round(width / 128 / 6)


def gather_kernel(axis, swaps, count, own, *rest):
    number = len(swaps.kinds)
    sources, rest = rest[:number], rest[number + count :]
    whole, targets, rest = rest[0], rest[1 : 1 + number], rest[1 + number :]
    local, z_send, z_recv, x_send, x_recv, beside = rest
    line, side = row_place()
    above, below, across = on_rows(line + 1, side), on_rows(line - 1, side), on_rows(line, 1 - side)
    has_above, has_below, always = line < DEPTH - 1, line > 0, line >= 0
    greet([(has_above, above), (has_below, below), (always, across)] + swaps.partners(always))
    extra = swaps.copies(sources, targets, beside)
    for copy in extra:
        copy.start()
    streams = streams_of(own.shape[-1])
    along, over = range(CHUNKS), range(CHUNKS, len(streams))

    def block(at, stream):
        which, *piece = streams[stream]
        return chunk_part(shard_of(whole, at * BREADTH + (1 - side if which else side), axis), *piece)

    def mine(stream):
        return chunk_part(own, *streams[stream][1:])

    def pass_on(stream, source, at, way):
        return remote(
            source,
            block(at, stream),
            z_send.at[stream, way, at],
            z_recv.at[stream, at],
            below if way else above,
        )

    def cross(source, at, stream):
        slot = stream * DEPTH + at if stream < CHUNKS else CHUNKS * DEPTH + stream - CHUNKS
        return remote(source, block(at, stream), x_send.at[slot], x_recv.at[slot], across)

    def onward(stream, source):
        @pl.when(has_above)
        def _():
            pass_on(stream, source, line, 0).start()

        @pl.when(has_below)
        def _():
            pass_on(stream, source, line, 1).start()

    handed = [stream for stream in over if streams[stream][0] == 0]
    for stream in handed + list(along):
        cross(mine(stream), line, stream).start()
    for stream in list(along) + handed:
        onward(stream, mine(stream))
    keep = pltpu.make_async_copy(own, shard_of(whole, line * BREADTH + side, axis), local)
    keep.start()
    for stream in handed:
        cross(mine(stream), line, stream).wait_recv()
        onward(stream + CHUNKS, block(line, stream + CHUNKS))
    for step in range(1, DEPTH):
        for way, at, there, more in (
            (0, line - step, line - step >= 0, has_above),
            (1, line + step, line + step < DEPTH, has_below),
        ):

            @pl.when(there)
            def _(way=way, at=at, more=more):
                for stream in range(len(streams)):
                    pass_on(stream, block(at, stream), at, way).wait_recv()
                    if stream in along:
                        cross(block(at, stream), at, stream).start()

                    @pl.when(more)
                    def _(stream=stream):
                        pass_on(stream, block(at, stream), at, way).start()

    keep.wait()
    for at in range(DEPTH):
        for stream in along:
            cross(mine(stream), at, stream).wait_recv()
            cross(mine(stream), at, stream).wait_send()
        for stream in range(len(streams)):

            @pl.when(has_above & (at <= line))
            def _(at=at, stream=stream):
                pass_on(stream, block(at, stream), at, 0).wait_send()

            @pl.when(has_below & (at >= line))
            def _(at=at, stream=stream):
                pass_on(stream, block(at, stream), at, 1).wait_send()

    for stream in handed:
        cross(mine(stream), line, stream).wait_send()
    for copy in extra:
        copy.wait()


def gather_rows(block, ident, axis, after=(), swaps=()):
    ranks = DEPTH * BREADTH
    swaps = Swaps(swaps)
    shape = block.shape[:axis] + (ranks,) + block.shape[axis:]
    anywhere = pl.BlockSpec(memory_space=pl.ANY)
    wave = pltpu.SemaphoreType.DMA
    whole, *others = pl.pallas_call(
        functools.partial(gather_kernel, axis, swaps, len(after)),
        out_shape=[jax.ShapeDtypeStruct(shape, block.dtype)] + swaps.shapes(),
        in_specs=[anywhere] * (1 + len(swaps.kinds) + len(after)),
        out_specs=[anywhere] + swaps.specs(),
        scratch_shapes=[
            wave,
            wave((3 * CHUNKS, 2, DEPTH)),
            wave((3 * CHUNKS, DEPTH)),
            wave((CHUNKS * (DEPTH + 1),)),
            wave((CHUNKS * (DEPTH + 1),)),
        ]
        + swaps.scratch(),
        name=f"gather_rows_{ident}",
        compiler_params=pltpu.CompilerParams(collective_id=ident, has_side_effects=True),
    )(block, *swaps.arrays, *after)
    return (whole, *others) if others else whole


def scatter_kernel(axis, swaps, count, parts, *rest):
    number = len(swaps.kinds)
    sources, rest = rest[:number], rest[number + count :]
    total, targets, rest = rest[0], rest[1 : 1 + number], rest[1 + number :]
    crossed, flow, x_send, x_recv, z_send, z_recv, beside = rest[0], rest[1:-5], *rest[-5:]
    line, side = row_place()
    above, below, across = on_rows(line + 1, side), on_rows(line - 1, side), on_rows(line, 1 - side)
    has_above, has_below, always = line < DEPTH - 1, line > 0, line >= 0
    greet([(has_above, above), (has_below, below), (always, across)] + swaps.partners(always))
    extra = swaps.copies(sources, targets, beside)
    for copy in extra:
        copy.start()
    streams = streams_of(parts.shape[-1])
    along, over = range(CHUNKS), range(CHUNKS, len(streams))
    handed = [stream for stream in over if streams[stream][0] == 1]

    def part(at, stream, turned=False):
        other, *piece = streams[stream]
        return chunk_part(shard_of(parts, at * BREADTH + (1 - side if other or turned else side), axis), *piece)

    def slot(ref, at, stream):
        chunk = streams[stream][1]
        rows = ref.shape[1] // CHUNKS
        return ref.at[at, pl.ds(chunk * rows, rows)]

    def cross(at, stream):
        place = stream * DEPTH + at
        return remote(
            part(at, stream, True), slot(crossed, at, stream), x_send.at[place], x_recv.at[place], across
        )

    def hand(stream):
        place = CHUNKS * DEPTH + stream - handed[0]
        leave, arrive = flow[12], flow[13]
        return remote(
            slot(leave, 0, stream), slot(arrive, 0, stream), x_send.at[place], x_recv.at[place], across
        )

    def held(stream, way, leaving):
        group = 0 if stream in along else 1 + streams[stream][0]
        return flow[4 * group + 2 * way + leaving]

    def moving(stream, at, way):
        return remote(
            slot(held(stream, way, 1), at, stream),
            slot(held(stream, way, 0), at, stream),
            z_send.at[stream, way, at],
            z_recv.at[stream, way, at],
            below if way else above,
        )

    def add_up(stream, at, ways, target, others=()):
        value = part(at, stream)[...].astype(jnp.float32)
        if stream in along:
            value = value + slot(crossed, at, stream)[...].astype(jnp.float32)
        for way in ways:
            value = value + slot(held(stream, way, 0), at, stream)[...].astype(jnp.float32)
        for other in others:
            value = value + other[...].astype(jnp.float32)
        target[...] = value.astype(target.dtype)

    def send_on(stream, at, way, comes):
        leaving = slot(held(stream, way, 1), at, stream)

        @pl.when(comes)
        def _():
            moving(stream, at, way).wait_recv()
            add_up(stream, at, [way], leaving)

        @pl.when(jnp.logical_not(comes))
        def _():
            add_up(stream, at, [], leaving)

        moving(stream, at, way).start()

    def finish(stream, target, others=()):
        for below_there, above_there, ways in ((True, True, [0, 1]), (True, False, [0]), (False, True, [1])):

            @pl.when((has_below == below_there) & (has_above == above_there))
            def _(ways=ways):
                for way in ways:
                    moving(stream, line, way).wait_recv()
                add_up(stream, line, ways, target, others)

    for step in range(DEPTH - 1, 0, -1):
        for at, there in ((line + step, line + step < DEPTH), (line - step, line - step >= 0)):

            @pl.when(there)
            def _(at=at):
                for stream in along:
                    cross(at, stream).start()

    for stream in along:
        cross(line, stream).start()
    for some in (over, along):
        for step in range(DEPTH - 1, 0, -1):
            for way, at, there, comes in (
                (0, line + step, line + step < DEPTH, has_below),
                (1, line - step, line - step >= 0, has_above),
            ):
                for stream in some:

                    @pl.when(there)
                    def _(way=way, at=at, comes=comes, stream=stream):
                        if stream in along:
                            cross(at, stream).wait_recv()
                        send_on(stream, at, way, comes)

        if some is over:
            for stream in handed:
                finish(stream, slot(flow[12], 0, stream))
                hand(stream).start()

    for stream in along:
        cross(line, stream).wait_recv()
        finish(stream, chunk_part(total, *streams[stream][1:]))
    for stream in handed:
        hand(stream).wait_recv()
        mate = stream - CHUNKS
        finish(mate, chunk_part(total, *streams[mate][1:]), (slot(flow[13], 0, stream),))
        hand(stream).wait_send()
    for at in range(DEPTH):
        for stream in along:
            cross(at, stream).wait_send()
        for stream in range(len(streams)):

            @pl.when(at > line)
            def _(at=at, stream=stream):
                moving(stream, at, 0).wait_send()

            @pl.when(at < line)
            def _(at=at, stream=stream):
                moving(stream, at, 1).wait_send()

    for copy in extra:
        copy.wait()


def scatter_rows(parts, ident, axis, after=(), swaps=()):
    swaps = Swaps(swaps)
    shape = parts.shape[:axis] + parts.shape[axis + 1 :]
    width = shape[-1]
    first = split_lanes(width)
    near = pl.BlockSpec(memory_space=pltpu.VMEM)
    wave = pltpu.SemaphoreType.DMA

    def slots(size, count=(DEPTH,)):
        return pltpu.VMEM(count + shape[:-1] + (size,), parts.dtype)

    flow = [slots(first)] * 4
    if first < width:
        flow = flow + [slots(width - first)] * 8 + [slots(width - first, (1,))] * 2
    total, *others = pl.pallas_call(
        functools.partial(scatter_kernel, axis, swaps, len(after)),
        out_shape=[jax.ShapeDtypeStruct(shape, jnp.float32)] + swaps.shapes(),
        in_specs=[near] + [pl.BlockSpec(memory_space=pl.ANY)] * (len(swaps.kinds) + len(after)),
        out_specs=[near] + swaps.specs(),
        scratch_shapes=[slots(first)]
        + flow
        + [wave((CHUNKS * (DEPTH + 1),))] * 2
        + [wave((3 * CHUNKS, 2, DEPTH))] * 2
        + swaps.scratch(),
        name=f"scatter_rows_{ident}",
        compiler_params=pltpu.CompilerParams(
            collective_id=ident, has_side_effects=True, vmem_limit_bytes=32 << 20
        ),
    )(parts, *swaps.arrays, *after)
    return (total, *others) if others else total


def sum_kernel(count, own, *rest):
    total, held, send, receive = rest[count:]
    ranks = DEPTH * BREADTH
    place = lax.axis_index("rows")
    others = [lax.rem(place + step, ranks) for step in range(1, ranks)]
    greet([(place >= 0, {"rows": other}) for other in others])

    def push(step, other, slot):
        return remote(own, held.at[slot], send.at[step], receive.at[slot], {"rows": other})

    for step, other in enumerate(others):
        push(step, other, place).start()
    held[pl.ds(place, 1)] = own[...][None]
    for step, other in enumerate(others):
        push(step, other, other).wait_recv()
    value = held[0]
    for rank in range(1, ranks):
        value = value + held[rank]
    total[...] = value
    for step, other in enumerate(others):
        push(step, other, place).wait_send()


def sum_rows(own, ident, after=()):
    ranks = DEPTH * BREADTH
    near = pl.BlockSpec(memory_space=pltpu.VMEM)
    return pl.pallas_call(
        functools.partial(sum_kernel, len(after)),
        out_shape=jax.ShapeDtypeStruct(own.shape, own.dtype),
        in_specs=[near] + [pl.BlockSpec(memory_space=pl.ANY)] * len(after),
        out_specs=near,
        scratch_shapes=[
            pltpu.VMEM((ranks,) + own.shape, own.dtype),
            pltpu.SemaphoreType.DMA((ranks,)),
            pltpu.SemaphoreType.DMA((ranks,)),
        ],
        name=f"sum_rows_{ident}",
        compiler_params=pltpu.CompilerParams(collective_id=ident, has_side_effects=True),
    )(own, *after)


def final_kernel(ranks, groups, sums, swaps, own, *rest):
    number = len(swaps.kinds)
    sources, out, targets, rest = rest[:number], rest[number], rest[number + 1 : 2 * number + 1], rest[2 * number + 1 :]
    held, kept, part, h_send, h_recv, g_send, g_recv, o_send, o_recv, beside = rest
    place, group = lax.axis_index("rows"), lax.axis_index("items")
    rows = [lax.rem(place + step, ranks) for step in range(1, ranks)]
    items = [lax.rem(group + step, groups) for step in range(1, groups)]
    greet([(place >= 0, {"rows": other}) for other in rows] + [(place >= 0, {"items": other}) for other in items])
    extra = swaps.copies(sources, targets, beside)
    for copy in extra:
        copy.start()

    def push(step, other, slot):
        return remote(own.at[other], held.at[slot], h_send.at[step], h_recv.at[slot], {"rows": other})

    def swap(step, other, slot):
        return remote(part, kept.at[slot], g_send.at[step], g_recv.at[slot], {"items": other})

    def share(step, other, slot):
        return remote(out.at[place], out.at[slot], o_send.at[step], o_recv.at[slot], {"rows": other})

    for step, other in enumerate(rows):
        push(step, other, place).start()
    held[pl.ds(place, 1)] = own[pl.ds(place, 1)]
    for step, other in enumerate(rows):
        push(step, other, other).wait_recv()
    value = held[0]
    for rank in range(1, ranks):
        value = value + held[rank]
    part[...] = value
    for step, other in enumerate(items):
        swap(step, other, group).start()
    kept[pl.ds(group, 1)] = value[None]
    for step, other in enumerate(items):
        swap(step, other, other).wait_recv()
    total = kept[0, :sums]
    for item in range(1, groups):
        total = total + kept[item, :sums]
    depth = own.shape[1] - sums
    out[pl.ds(place, 1), :sums] = total[None]
    for item in range(groups):
        out[pl.ds(place, 1), sums + item * depth : sums + (item + 1) * depth] = kept[item, sums:][None]
    for step, other in enumerate(rows):
        share(step, other, place).start()
    for step, other in enumerate(rows):
        share(step, other, other).wait_recv()
    for step, other in enumerate(rows):
        push(step, other, place).wait_send()
        share(step, other, place).wait_send()
    for step, other in enumerate(items):
        swap(step, other, group).wait_send()
    for copy in extra:
        copy.wait()


def final_sums(own, sums, ident, swaps=()):
    ranks, groups = lax.axis_size("rows"), lax.axis_size("items")
    near = pl.BlockSpec(memory_space=pltpu.VMEM)
    depth = own.shape[1]
    swaps = Swaps(swaps)
    return pl.pallas_call(
        functools.partial(final_kernel, ranks, groups, sums, swaps),
        out_shape=[jax.ShapeDtypeStruct((ranks, sums + groups * (depth - sums), 128), own.dtype)] + swaps.shapes(),
        in_specs=[near] + swaps.specs(),
        out_specs=[near] + swaps.specs(),
        scratch_shapes=[
            pltpu.VMEM(own.shape, own.dtype),
            pltpu.VMEM((groups,) + own.shape[1:], own.dtype),
            pltpu.VMEM(own.shape[1:], own.dtype),
            pltpu.SemaphoreType.DMA((ranks,)),
            pltpu.SemaphoreType.DMA((ranks,)),
            pltpu.SemaphoreType.DMA((groups,)),
            pltpu.SemaphoreType.DMA((groups,)),
            pltpu.SemaphoreType.DMA((ranks,)),
            pltpu.SemaphoreType.DMA((ranks,)),
        ]
        + swaps.scratch(),
        name=f"final_sums_{ident}",
        compiler_params=pltpu.CompilerParams(collective_id=ident, has_side_effects=True),
    )(own, *swaps.arrays)


def first_kernel(
    ranks, quarters, own, qkv, text, total, qkv_out, text_out, held, packed, local,
    s_send, s_recv, t_send, t_recv, a_send, a_recv, y_send, y_recv, c_send, c_recv,
):
    place, group = lax.axis_index("rows"), lax.axis_index("items")
    others = [lax.rem(place + step, ranks) for step in range(1, ranks)]
    far = lax.rem(group + 2, 4)
    twin = group + 1 - 2 * lax.rem(group, 2)
    depth = qkv.shape[0] // quarters
    mine = pl.ds(pl.multiple_of(group * depth, 16), depth)
    fars = pl.ds(pl.multiple_of(far * depth, 16), depth)
    features = text_out.shape[-1]
    span = qkv.shape[1] // (3 * ranks)

    def columns(other):
        return pl.ds(pl.multiple_of(other * features, features), features)

    keeps = [pltpu.make_async_copy(text.at[:, :, columns(place)], text_out.at[place], local.at[0])]
    keeps[0].start()
    greet(
        [(place >= 0, {"rows": other}) for other in others]
        + [(place >= 0, {"items": far}), (place >= 0, {"items": twin})]
    )

    def sum_push(step, other, slot):
        return remote(own, held.at[slot], s_send.at[step], s_recv.at[slot], {"rows": other})

    def text_push(step, other, slot):
        return remote(
            text.at[:, :, columns(other)], text_out.at[slot], t_send.at[step], t_recv.at[slot], {"rows": other}
        )

    def push(step, other, slot):
        return remote(
            packed.at[other, mine], qkv_out.at[slot, mine], a_send.at[step], a_recv.at[slot], {"rows": other}
        )

    def pass_far(slot):
        block = qkv_out.at[slot, mine]
        return remote(block, block, y_send.at[slot], y_recv.at[slot], {"items": far})

    def pass_twin(which, slot):
        block = qkv_out.at[slot, fars if which else mine]
        return remote(block, block, c_send.at[which, slot], c_recv.at[which, slot], {"items": twin})

    for step, other in enumerate(others):
        sum_push(step, other, place).start()
    for rank in range(ranks):
        packed[rank] = jnp.concatenate(
            [
                qkv[:, (part * ranks + rank) * span : (part * ranks + rank + 1) * span]
                for part in range(3)
            ],
            axis=1,
        )
    for step, other in enumerate(others):
        push(step, other, place).start()
    for step, other in enumerate(others):
        text_push(step, other, place).start()
    keeps.append(pltpu.make_async_copy(packed.at[place], qkv_out.at[place], local.at[1]))
    keeps[1].start()
    held[pl.ds(place, 1)] = own[...][None]
    for step, other in enumerate(others):
        sum_push(step, other, other).wait_recv()
    value = held[0]
    for rank in range(1, ranks):
        value = value + held[rank]
    total[...] = value
    for step, other in enumerate(others):
        push(step, other, other).wait_recv()
        pass_far(other).start()
        pass_twin(0, other).start()
    for other in others:
        pass_far(other).wait_recv()
        pass_twin(1, other).start()
    for step, other in enumerate(others):
        sum_push(step, other, place).wait_send()
        text_push(step, other, other).wait_recv()
        text_push(step, other, place).wait_send()
        push(step, other, place).wait_send()
        pass_far(other).wait_send()
        for which in range(2):
            pass_twin(which, other).wait_recv()
            pass_twin(which, other).wait_send()
    for copy in keeps:
        copy.wait()


def first_transfers(own, qkv, text, ident):
    ranks, quarters = lax.axis_size("rows"), lax.axis_size("items")
    depth = qkv.shape[0]
    anywhere = pl.BlockSpec(memory_space=pl.ANY)
    near = pl.BlockSpec(memory_space=pltpu.VMEM)
    outs = [
        jax.ShapeDtypeStruct(own.shape, own.dtype),
        jax.ShapeDtypeStruct((ranks, depth, qkv.shape[1] // ranks), qkv.dtype),
        jax.ShapeDtypeStruct((ranks,) + text.shape[:-1] + (text.shape[-1] // ranks,), text.dtype),
    ]
    wave = pltpu.SemaphoreType.DMA
    return pl.pallas_call(
        functools.partial(first_kernel, ranks, quarters),
        out_shape=outs,
        in_specs=[near, near, anywhere],
        out_specs=[near, anywhere, anywhere],
        scratch_shapes=[
            pltpu.VMEM((ranks,) + own.shape, own.dtype),
            pltpu.VMEM(outs[1].shape, qkv.dtype),
            wave((2,)),
        ]
        + [wave((ranks,))] * 8
        + [wave((2, ranks))] * 2,
        name=f"first_transfers_{ident}",
        compiler_params=pltpu.CompilerParams(
            collective_id=ident, has_side_effects=True, vmem_limit_bytes=24 << 20
        ),
    )(own, qkv, text)


def quarter_kernel(pieces, at, whole, packed):
    ranks, span = packed.shape[0], packed.shape[2] // pieces
    for rank in range(ranks):
        for piece in range(pieces):
            start = (piece * ranks + rank) * span
            packed[rank, :, piece * span : (piece + 1) * span] = whole[:, start : start + span]


def pack_quarter(whole, at, pieces, ranks):
    rows, width = whole.shape[0] // 4, whole.shape[1]
    out = (ranks, rows, width // ranks)
    return pl.pallas_call(
        functools.partial(quarter_kernel, pieces),
        grid_spec=pltpu.PrefetchScalarGridSpec(
            num_scalar_prefetch=1,
            grid=(1,),
            in_specs=[pl.BlockSpec((rows, width), lambda step, at: (at[0], 0))],
            out_specs=pl.BlockSpec(out, lambda step, at: (0, 0, 0)),
        ),
        out_shape=jax.ShapeDtypeStruct(out, whole.dtype),
        name="pack_quarter",
        compiler_params=local_params(),
    )(at, whole)


def pack_kernel(pieces, whole, packed):
    ranks, span = packed.shape[0], packed.shape[2] // pieces
    for rank in range(ranks):
        packed[rank] = jnp.concatenate(
            [whole[:, (piece * ranks + rank) * span : (piece * ranks + rank + 1) * span] for piece in range(pieces)],
            axis=1,
        ).astype(packed.dtype)


def pack_blocks(whole, pieces, ranks, dtype):
    near = pl.BlockSpec(memory_space=pltpu.VMEM)
    return pl.pallas_call(
        functools.partial(pack_kernel, pieces),
        out_shape=jax.ShapeDtypeStruct((ranks, whole.shape[0], whole.shape[1] // ranks), dtype),
        in_specs=[near],
        out_specs=near,
        name="pack_blocks",
        compiler_params=pltpu.CompilerParams(vmem_limit_bytes=24 << 20),
    )(whole)


def unpack_kernel(pieces, packed, whole):
    ranks, span = packed.shape[0], packed.shape[2] // pieces
    for piece in range(pieces):
        for rank in range(0, ranks, 2):
            start = (piece * ranks + rank) * span
            whole[:, start : start + 2 * span] = jnp.concatenate(
                [packed[rank + k, :, piece * span : (piece + 1) * span] for k in range(2)], axis=1
            ).astype(whole.dtype)


def unpack_blocks(packed, pieces, dtype):
    near = pl.BlockSpec(memory_space=pltpu.VMEM)
    ranks, rows, width = packed.shape
    return pl.pallas_call(
        functools.partial(unpack_kernel, pieces),
        out_shape=jax.ShapeDtypeStruct((rows, ranks * width), dtype),
        in_specs=[near],
        out_specs=near,
        name="unpack_blocks",
        compiler_params=pltpu.CompilerParams(vmem_limit_bytes=24 << 20),
    )(packed)


def halves_kernel(pieces, own, other, whole):
    ranks, half, span = own.shape[0], own.shape[1], own.shape[2] // pieces
    first = lax.rem(lax.axis_index("items"), 2) == 0
    for low in range(2):

        @pl.when(first == (low == 0))
        def _(low=low):
            for source, start in ((own, low * half), (other, (1 - low) * half)):
                for piece in range(pieces):
                    for rank in range(0, ranks, 2):
                        column = (piece * ranks + rank) * span
                        whole[start : start + half, column : column + 2 * span] = jnp.concatenate(
                            [source[rank + k, :, piece * span : (piece + 1) * span] for k in range(2)], axis=1
                        ).astype(whole.dtype)


def unpack_halves(own, other, pieces):
    near = pl.BlockSpec(memory_space=pltpu.VMEM)
    ranks, half, width = own.shape
    return pl.pallas_call(
        functools.partial(halves_kernel, pieces),
        out_shape=jax.ShapeDtypeStruct((2 * half, ranks * width), jnp.float32),
        in_specs=[near, near],
        out_specs=near,
        name="unpack_halves",
        compiler_params=pltpu.CompilerParams(vmem_limit_bytes=32 << 20),
    )(own, other)


def gather_tokens(block, ident, swaps=()):
    whole = gather_rows(block, ident, 1, swaps=swaps)
    if not swaps:
        return whole.reshape(-1, block.shape[-1])
    return (whole[0].reshape(-1, block.shape[-1]), *whole[1:])


def scatter_tokens(partial, items, ident, swaps=()):
    ranks = lax.axis_size("rows")
    blocks = partial.astype(jnp.bfloat16).reshape(items, ranks, -1, partial.shape[-1])
    return scatter_rows(blocks, ident, 1, swaps=swaps)


NEAR = pl.BlockSpec(memory_space=pltpu.VMEM)
SCALARS = pl.BlockSpec(memory_space=pltpu.SMEM)
NT = (((1,), (1,)), ((), ()))


def local_params():
    return pltpu.CompilerParams(vmem_limit_bytes=48 << 20)


def text_item(text, item):
    block = text[:, item]
    return block.reshape(block.shape[0] * block.shape[1], block.shape[2])


def lanes_to_rows(columns, rows):
    lane = lax.broadcasted_iota(jnp.int32, (128, 128), 1)
    held = jnp.zeros((128, 128), jnp.float32)
    for place, column in enumerate(columns):
        held = jnp.where(lane == place, column, held)
    return jnp.transpose(held)[:rows]


def rows_to_lanes(rows):
    missing = jnp.zeros((128 - rows.shape[0], 128), jnp.float32)
    return jnp.transpose(jnp.concatenate([rows, missing], axis=0))


def project_kernel(attn, weight, text, proj, squares):
    span = text.shape[-1] // 2
    tokens = attn.shape[0]
    for start in range(0, tokens, 256):
        proj[start : start + 256] = jnp.dot(
            attn[start : start + 256], weight[...], preferred_element_type=jnp.float32
        )
    columns = []
    for part in range(2):
        for start in range(0, tokens, 128):
            block = proj[start : start + 128, part * span : (part + 1) * span]
            columns.append(jnp.sum(block * block, axis=1, keepdims=True))
    for item in range(text.shape[1]):
        block = text_item(text, item)[:, :span]
        columns.append(jnp.sum(block * block, axis=1, keepdims=True))
    squares[...] = lanes_to_rows(columns, squares.shape[0])


def project(attn, weight, text):
    count = 2 * attn.shape[0] // 128 + text.shape[1]
    return pl.pallas_call(
        project_kernel,
        out_shape=[
            jax.ShapeDtypeStruct((attn.shape[0], weight.shape[1]), jnp.float32),
            jax.ShapeDtypeStruct((-(-count // 8) * 8, 128), jnp.float32),
        ],
        in_specs=[NEAR] * 3,
        out_specs=[NEAR] * 2,
        name="project",
        compiler_params=local_params(),
    )(attn, weight, text)


def tile_lane():
    return lax.broadcasted_iota(jnp.int32, (1, 128), 1)


def swap_halves(tile):
    low = lax.rem(tile_lane(), 64) < 32
    return jnp.where(low, pltpu.roll(tile, 96, 1), pltpu.roll(tile, 32, 1))


def block_tables(tab, block, frame_lanes):
    by_row = lax.rem(tile_lane(), 32) < frame_lanes
    rows = 128 // COLS
    cosines, sines = [], []
    for row in range(rows):
        at = pl.ds(block * rows + row, 1)
        cosines.append(jnp.where(by_row, tab[0, at], tab[2, :COLS]))
        sines.append(jnp.where(by_row, tab[1, at], tab[3, :COLS]))
    return jnp.concatenate(cosines, axis=0), jnp.concatenate(sines, axis=0)


def block_inverse(inverse, block, blocks):
    lane = lax.broadcasted_iota(jnp.int32, (128, 128), 1)

    def column(place):
        return jnp.sum(jnp.where(lane == place, inverse, 0.0), axis=1, keepdims=True)

    query, key = column(block), column(blocks + block)
    return [query, jnp.where(tile_lane() < 64, query, key), key]


def attend_kernel(
    scale, width, counts, heights, text_lens, proj, totals, text, gains, text_gain, gate, w_out,
    parts, qkv, text_kv, tab, biases, text_biases,
):
    ranks, items = text.shape[0], text.shape[1]
    span = gate.shape[-1]
    heads, size = span // 64, 64
    tokens = proj.shape[0]
    blocks, item_blocks = tokens // 128, tokens // 128 // items
    seq = tokens // items
    slots = seq // ranks
    row_slots = slots // COLS
    frame_pairs = size // 8
    space_pairs = (size // 2 - frame_pairs) // 2

    place = lax.rem(tile_lane(), 32)
    frame_rate = jnp.exp(place.astype(jnp.float32) * (-math.log(10000.0) / frame_pairs))
    row_rate = jnp.exp((place - frame_pairs).astype(jnp.float32) * (-math.log(10000.0) / space_pairs))
    column_rate = jnp.exp(
        (place - frame_pairs - space_pairs).astype(jnp.float32) * (-math.log(10000.0) / space_pairs)
    )
    is_frame = place < frame_pairs
    rows = items * ranks * row_slots
    which = lax.broadcasted_iota(jnp.int32, (rows, 1), 0)
    frame_index = jnp.zeros((rows, 1), jnp.float32)
    frame_row = jnp.zeros((rows, 1), jnp.float32)
    seq_place = lax.broadcasted_iota(jnp.int32, (seq, 128), 0)
    for item in range(items):
        below = jnp.int32(0)
        bias = jnp.zeros((seq, 128), jnp.float32)
        for rank in range(ranks):
            live = counts[rank * items + item]
            for row in range(row_slots):
                index = below + row
                at = which == (item * ranks + rank) * row_slots + row
                frame_index = jnp.where(at, (index // heights[item]).astype(jnp.float32), frame_index)
                frame_row = jnp.where(at, lax.rem(index, heights[item]).astype(jnp.float32), frame_row)
            start = rank * slots
            inside = (seq_place >= start + live * COLS) & (seq_place < start + slots)
            bias = jnp.where(inside, masked_score, bias)
            below = below + live
        biases[item] = bias
        text_place = lax.broadcasted_iota(jnp.int32, text_biases.shape[1:], 0)
        text_biases[item] = jnp.where(text_place >= text_lens[item], masked_score, 0.0)
    column = lax.broadcasted_iota(jnp.int32, (COLS, 1), 0).astype(jnp.float32)
    row_angles = jnp.where(is_frame, frame_index * frame_rate, frame_row * row_rate)
    column_angles = column * column_rate
    sign = jnp.where(lax.rem(tile_lane(), 64) < 32, -1.0, 1.0)
    tab[0, :rows] = jnp.cos(row_angles)
    tab[1, :rows] = jnp.sin(row_angles) * sign
    tab[2, :COLS] = jnp.cos(column_angles)
    tab[3, :COLS] = jnp.sin(column_angles) * sign

    inverse = rows_to_lanes(lax.rsqrt(totals[...] / width + epsilon))
    for item in range(items):
        block = text_item(text, item)
        column = inverse[:, 2 * blocks + item : 2 * blocks + item + 1]
        text_kv[item] = jnp.concatenate(
            [block[:, :span] * column * text_gain[...], block[:, span:]], axis=1
        ).astype(text_kv.dtype)

    @pl.loop(0, blocks)
    def _(block):
        at = pl.ds(pl.multiple_of(block * 128, 128), 128)
        cosine, sine = block_tables(tab, block, frame_pairs + space_pairs)
        inverses = block_inverse(inverse, block, blocks)
        tiles = []
        for tile in range(3):
            lanes = slice(tile * 128, (tile + 1) * 128)
            value = proj[at, lanes] * inverses[tile] * gains[:, lanes]
            tiles.append(value * cosine + swap_halves(value) * sine)
        qkv[at] = jnp.concatenate(tiles + [proj[at, 2 * span :]], axis=1).astype(qkv.dtype)

    @pl.loop(0, blocks)
    def _(block):
        at = pl.ds(pl.multiple_of(block * 128, 128), 128)
        item = block // item_blocks
        keys_at = pl.ds(pl.multiple_of(item * seq, seq), seq)
        bias, text_bias = biases[item], text_biases[item]
        mixed = []
        for head in range(heads):
            lanes = slice(head * size, (head + 1) * size)

            def part_of(ref, rows, part):
                start = part * span + head * size
                return ref[rows, start : start + size]

            query = part_of(qkv, at, 0)

            def mix(keys, values, mask):
                scores = lax.dot_general(keys, query, NT, preferred_element_type=jnp.float32)
                scores = scores * scale + mask
                terms = jnp.exp(scores - jnp.max(scores, axis=0, keepdims=True))
                probs = terms * (1.0 / jnp.sum(terms, axis=0, keepdims=True))
                return lax.dot_general(
                    values,
                    probs.astype(jnp.bfloat16),
                    (((0,), (0,)), ((), ())),
                    preferred_element_type=jnp.float32,
                )

            out = mix(part_of(qkv, keys_at, 1), part_of(qkv, keys_at, 2), bias)
            text_keys = text_kv[item]
            cross = mix(
                text_keys[:, lanes], text_keys[:, span + head * size : span + (head + 1) * size], text_bias
            )
            mixed.append(jnp.transpose(out) + gate[:, lanes] * jnp.transpose(cross))
        combined = jnp.concatenate(mixed, axis=1).astype(jnp.bfloat16)
        parts[1][at] = combined
        parts[0][at] = jnp.dot(combined, w_out[...], preferred_element_type=jnp.float32).astype(jnp.bfloat16)


def attend(proj, totals, text, gains, text_gain, gate, w_out, counts, heights, text_lens, head_size):
    tokens, span, width = proj.shape[0], gate.shape[-1], w_out.shape[1]
    items, text_rows = text.shape[1], text.shape[0] * text.shape[2]
    low = jnp.bfloat16

    def body(*refs):
        ins, outs, scratch = refs[:10], refs[10:15], refs[15:]
        attend_kernel(
            head_size**-0.5, width, *ins, (outs[0], outs[1]), outs[2], outs[3], outs[4], *scratch
        )

    return pl.pallas_call(
        body,
        out_shape=[
            jax.ShapeDtypeStruct((tokens, width), low),
            jax.ShapeDtypeStruct((tokens, span), low),
            jax.ShapeDtypeStruct((tokens, 3 * span), low),
            jax.ShapeDtypeStruct((items, text_rows, 2 * span), low),
            jax.ShapeDtypeStruct((4, max(tokens // COLS, COLS), 128), jnp.float32),
        ],
        in_specs=[SCALARS] * 3 + [NEAR] * 7,
        out_specs=[NEAR] * 5,
        scratch_shapes=[
            pltpu.VMEM((items, tokens // items, 128), jnp.float32),
            pltpu.VMEM((items, text_rows, 128), jnp.float32),
        ],
        name="attend",
        compiler_params=local_params(),
    )(counts, heights, text_lens, proj, totals, text, gains, text_gain, gate, w_out)


def attend_back_kernel(
    scale, width, counts, text_lens, grad, w_out, qkv, text_kv, tab, proj, totals, text, gains, text_gain, gate,
    scaled, grad_value, text_scaled, text_value, sums, gain_sums, gate_sums,
    grad_query, key_sum, value_sum, text_key_sum, text_value_sum, biases, text_biases,
):
    ranks, items = text.shape[0], text.shape[1]
    span = gate.shape[-1]
    heads, size = span // 64, 64
    tokens = proj.shape[0]
    blocks, item_blocks = tokens // 128, tokens // 128 // items
    seq = tokens // items
    slots = seq // ranks
    frame_pairs = size // 8
    space_pairs = (size // 2 - frame_pairs) // 2
    seq_place = lax.broadcasted_iota(jnp.int32, (seq, 128), 0)
    for item in range(items):
        bias = jnp.zeros((seq, 128), jnp.float32)
        for rank in range(ranks):
            start = rank * slots
            live = counts[rank * items + item]
            inside = (seq_place >= start + live * COLS) & (seq_place < start + slots)
            bias = jnp.where(inside, masked_score, bias)
        biases[item] = bias
        text_place = lax.broadcasted_iota(jnp.int32, text_biases.shape[1:], 0)
        text_biases[item] = jnp.where(text_place >= text_lens[item], masked_score, 0.0)
    key_sum[...] = jnp.zeros_like(key_sum)
    value_sum[...] = jnp.zeros_like(value_sum)
    text_key_sum[...] = jnp.zeros_like(text_key_sum)
    text_value_sum[...] = jnp.zeros_like(text_value_sum)
    gate_sums[...] = jnp.zeros_like(gate_sums)
    gain_sums[...] = jnp.zeros_like(gain_sums)

    @pl.loop(0, blocks)
    def _(block):
        at = pl.ds(pl.multiple_of(block * 128, 128), 128)
        item = block // item_blocks
        keys_at = pl.ds(pl.multiple_of(item * seq, seq), seq)
        bias, text_bias = biases[item], text_biases[item]
        text_keys = text_kv[item]
        grad_combined = lax.dot_general(grad[at], w_out[...], NT, preferred_element_type=jnp.float32)
        self_low = grad_combined.astype(jnp.bfloat16)
        cross_low = (gate[...] * grad_combined).astype(jnp.bfloat16)
        queries, crossed = [], []
        for head in range(heads):
            lanes = slice(head * size, (head + 1) * size)
            query = qkv[at, lanes]

            def back(keys, values, low_grad, mask, key_total, value_total, rows):
                scores = lax.dot_general(keys, query, NT, preferred_element_type=jnp.float32)
                scores = scores * scale + mask
                terms = jnp.exp(scores - jnp.max(scores, axis=0, keepdims=True))
                probs = terms * (1.0 / jnp.sum(terms, axis=0, keepdims=True))
                grad_probs = lax.dot_general(values, low_grad, NT, preferred_element_type=jnp.float32)
                inner = jnp.sum(probs * grad_probs, axis=0, keepdims=True)
                score_low = (probs * (grad_probs - inner)).astype(jnp.bfloat16)
                probs_low = probs.astype(jnp.bfloat16)
                key_total[head, rows] += jnp.dot(score_low, query, preferred_element_type=jnp.float32)
                value_total[head, rows] += jnp.dot(probs_low, low_grad, preferred_element_type=jnp.float32)
                to_query = lax.dot_general(
                    keys, score_low, (((0,), (0,)), ((), ())), preferred_element_type=jnp.float32
                )
                return to_query, probs_low

            to_query, _ = back(
                qkv[keys_at, span + head * size : span + (head + 1) * size],
                qkv[keys_at, 2 * span + head * size : 2 * span + (head + 1) * size],
                self_low[:, lanes],
                bias,
                key_sum,
                value_sum,
                keys_at,
            )
            text_values = text_keys[:, span + head * size : span + (head + 1) * size]
            text_rows = pl.ds(pl.multiple_of(item * 128, 128), 128)
            cross_query, cross_probs = back(
                text_keys[:, lanes],
                text_values,
                cross_low[:, lanes],
                text_bias,
                text_key_sum,
                text_value_sum,
                text_rows,
            )
            crossed.append(
                jnp.transpose(
                    lax.dot_general(
                        text_values, cross_probs, (((0,), (0,)), ((), ())), preferred_element_type=jnp.float32
                    )
                )
            )
            queries.append(jnp.transpose(to_query + cross_query))
        grad_query[at] = jnp.concatenate(queries, axis=1) * scale
        gate_sums[...] += jnp.sum(
            grad_combined * jnp.concatenate(crossed, axis=1), axis=0, keepdims=True
        )

    inverse = rows_to_lanes(lax.rsqrt(totals[...] / width + epsilon))
    columns = [[], []]
    for block in range(blocks):
        at = slice(block * 128, (block + 1) * 128)
        cosine, sine = block_tables(tab, block, frame_pairs + space_pairs)
        inverses = block_inverse(inverse, block, blocks)
        keys = jnp.concatenate([key_sum[head, at] for head in range(heads)], axis=1) * scale
        both = jnp.concatenate([grad_query[at], keys], axis=1)
        products = []
        for tile in range(3):
            lanes = slice(tile * 128, (tile + 1) * 128)
            value = both[:, lanes]
            value = value * cosine - swap_halves(value) * sine
            unit = proj[at, lanes] * inverses[tile]
            gain_sums[0:1, lanes] += jnp.sum(value * unit, axis=0, keepdims=True)
            value = value * gains[:, lanes]
            scaled[at, lanes] = value
            products.append(value * unit)
        first = tile_lane() < 64
        query_part = products[0] + jnp.where(first, products[1], 0.0)
        key_part = products[2] + jnp.where(first, 0.0, products[1])
        columns[0].append(jnp.sum(query_part, axis=1, keepdims=True))
        columns[1].append(jnp.sum(key_part, axis=1, keepdims=True))
        grad_value[at] = jnp.concatenate([value_sum[head, at] for head in range(heads)], axis=1).astype(
            grad_value.dtype
        )
    for item in range(items):
        at = slice(item * 128, (item + 1) * 128)
        unit = text_item(text, item)[:, :span] * inverse[:, 2 * blocks + item : 2 * blocks + item + 1]
        value = jnp.concatenate([text_key_sum[head, at] for head in range(heads)], axis=1) * scale
        gain_sums[1:2, :span] += jnp.sum(value * unit, axis=0, keepdims=True)
        value = value * text_gain[...]
        text_scaled[at] = value
        text_value[at] = jnp.concatenate([text_value_sum[head, at] for head in range(heads)], axis=1).astype(
            text_value.dtype
        )
        columns[1].append(jnp.sum(value * unit, axis=1, keepdims=True))
    sums[...] = lanes_to_rows(columns[0] + columns[1], sums.shape[0])


def attend_back(
    grad, w_out, qkv, text_kv, tab, proj, totals, text, gains, text_gain, gate, counts, text_lens, head_size, after
):
    tokens, span, width = proj.shape[0], gate.shape[-1], w_out.shape[1]
    items, text_rows = text.shape[1], text.shape[0] * text.shape[2]
    heads = span // head_size
    low, single = jnp.bfloat16, jnp.float32

    def body(*refs):
        attend_back_kernel(head_size**-0.5, width, *refs[:13], *refs[13 + len(after) :])

    return pl.pallas_call(
        body,
        out_shape=[
            jax.ShapeDtypeStruct((tokens, 2 * span), single),
            jax.ShapeDtypeStruct((tokens, span), low),
            jax.ShapeDtypeStruct((items * text_rows, span), single),
            jax.ShapeDtypeStruct((items * text_rows, span), low),
            jax.ShapeDtypeStruct(totals.shape, single),
            jax.ShapeDtypeStruct((8, 2 * span), single),
            jax.ShapeDtypeStruct((1, span), single),
        ],
        in_specs=[SCALARS] * 2 + [NEAR] * 11 + [pl.BlockSpec(memory_space=pl.ANY)] * len(after),
        out_specs=[NEAR] * 7,
        scratch_shapes=[
            pltpu.VMEM((tokens, span), single),
            pltpu.VMEM((heads, tokens, head_size), single),
            pltpu.VMEM((heads, tokens, head_size), single),
            pltpu.VMEM((heads, items * text_rows, head_size), single),
            pltpu.VMEM((heads, items * text_rows, head_size), single),
            pltpu.VMEM((items, tokens // items, 128), single),
            pltpu.VMEM((items, text_rows, 128), single),
        ],
        name="attend_back",
        compiler_params=local_params(),
    )(counts, text_lens, grad, w_out, qkv, text_kv, tab, proj, totals, text, gains, text_gain, gate, *after)


def norms_back_kernel(width, proj, totals, sums, scaled, grad_value, text, text_scaled, text_value, qkv_low, text_low):
    items, span = text.shape[1], grad_value.shape[-1]
    tokens = proj.shape[0]
    blocks = tokens // 128
    inverse = rows_to_lanes(lax.rsqrt(totals[...] / width + epsilon))
    means = rows_to_lanes(sums[...] / width)
    first = tile_lane() < 64
    for block in range(blocks):
        at = slice(block * 128, (block + 1) * 128)

        def by_tile(columns):
            query = columns[:, block : block + 1]
            key = columns[:, blocks + block : blocks + block + 1]
            return [query, jnp.where(first, query, key), key]

        inverses, mean = by_tile(inverse), by_tile(means)
        tiles = []
        for tile in range(3):
            lanes = slice(tile * 128, (tile + 1) * 128)
            unit = proj[at, lanes] * inverses[tile]
            tiles.append((inverses[tile] * (scaled[at, lanes] - unit * mean[tile])).astype(qkv_low.dtype))
        qkv_low[at] = jnp.concatenate(tiles + [grad_value[at]], axis=1)
    for item in range(items):
        at = slice(item * 128, (item + 1) * 128)
        place = 2 * blocks + item
        column, mean = inverse[:, place : place + 1], means[:, place : place + 1]
        unit = text_item(text, item)[:, :span] * column
        low = (column * (text_scaled[at] - unit * mean)).astype(text_low.dtype)
        low = jnp.concatenate([low, text_value[at]], axis=1)
        text_low[:, item] = low.reshape(text_low.shape[0], text_low.shape[2], 2 * span)


def norms_back(proj, totals, sums, scaled, grad_value, text, text_scaled, text_value, width):
    low = jnp.bfloat16
    return pl.pallas_call(
        functools.partial(norms_back_kernel, width),
        out_shape=[
            jax.ShapeDtypeStruct(proj.shape, low),
            jax.ShapeDtypeStruct(text.shape, low),
        ],
        in_specs=[NEAR] * 8,
        out_specs=[NEAR] * 2,
        name="norms_back",
        compiler_params=local_params(),
    )(proj, totals, sums, scaled, grad_value, text, text_scaled, text_value)


def join_kernel(bit, own, other, out):
    mine = pl.program_id(0) == bit()

    @pl.when(mine)
    def _():
        out[0] = own[...].astype(out.dtype)

    @pl.when(jnp.logical_not(mine))
    def _():
        out[0] = other[...].astype(out.dtype)


def join_rows(own, other, bit, dtype):
    rows, width = own.shape
    step = min(rows, 128)
    near = pl.BlockSpec((step, width), lambda half, at: (at, 0))
    return pl.pallas_call(
        functools.partial(join_kernel, bit),
        grid=(2, rows // step),
        out_shape=jax.ShapeDtypeStruct((2, rows, width), dtype),
        in_specs=[near, near],
        out_specs=pl.BlockSpec((1, step, width), lambda half, at: (half, at, 0)),
        name="join_rows",
        compiler_params=local_params(),
    )(own, other)


def core_bit():
    return lax.rem(lax.axis_index("items"), 2)


def far_bit():
    return lax.axis_index("items") // 2


def join_blocks(own, other, bit):
    ranks, rows, width = own.shape
    block = pl.BlockSpec((1, rows, width), lambda rank: (rank, 0, 0))

    def kernel(one, two, out):
        mine = bit()
        for half in range(2):

            @pl.when(mine == half)
            def _(half=half):
                out[0, half * rows : (half + 1) * rows] = one[0]
                out[0, (1 - half) * rows : (2 - half) * rows] = two[0]

    return pl.pallas_call(
        kernel,
        grid=(ranks,),
        out_shape=jax.ShapeDtypeStruct((ranks, 2 * rows, width), own.dtype),
        in_specs=[block, block],
        out_specs=pl.BlockSpec((1, 2 * rows, width), lambda rank: (rank, 0, 0)),
        name="join_blocks",
        compiler_params=local_params(),
    )(own, other)


def lay_flat(vectors):
    flat = jnp.concatenate([vector.reshape(-1) for vector in vectors])
    rows = -(-flat.size // 1024) * 8
    return jnp.pad(flat, (0, rows * 128 - flat.size)).reshape(rows, 128)


def take_apart(total, vectors):
    flat, parts, start = total.reshape(-1), [], 0
    for vector in vectors:
        parts.append(flat[start : start + vector.size].reshape(vector.shape))
        start += vector.size
    return parts


def sum_vectors(vectors, ident):
    return take_apart(sum_rows(lay_flat(vectors), ident), vectors)


def first_sums(vectors, qkv, text, ident):
    total, qkv_here, text_in = first_transfers(lay_flat(vectors), qkv, text, ident)
    return take_apart(total, vectors), qkv_here, text_in


CORES = [(0, 1), (1, 0), (2, 3), (3, 2)]
FARS = [(0, 2), (1, 3), (2, 0), (3, 1)]


def swap(array, pairs):
    return lax.ppermute(array, "items", pairs)


def give_keep(grad, index, axis):
    keep = lax.dynamic_index_in_dim(grad, index, axis, keepdims=False)
    give = lax.dynamic_index_in_dim(grad, 1 - index, axis, keepdims=False)
    return give, keep


def add_low(one, other):
    return (one.astype(jnp.float32) + other.astype(jnp.float32)).astype(jnp.bfloat16)


def head_parallel_plan(
    hidden_in,
    cotangent,
    text_states,
    time_embed,
    live_rows,
    frame_rows,
    text_len,
    w_qkv,
    w_out,
    w_text,
    w_gu,
    w_down,
    w_ada,
    gains,
    cross_gate,
    ada_bias,
    text_gain,
):
    single = jnp.float32
    narrow = jnp.bfloat16
    ranks = lax.axis_size("rows")
    place = lax.axis_index("rows")
    width = hidden_in.shape[2]
    heads = cross_gate.shape[0]
    head_size = width // heads
    score_scale = head_size ** (-0.5)
    items = time_embed.shape[1]
    slots = hidden_in.shape[1] // items
    row_slots = slots // COLS
    seq_len = ranks * slots
    text_local = text_states.shape[2]
    text_all = text_local * ranks
    text_width = text_states.shape[3]
    span = width // ranks
    heads_here = heads // ranks
    tokens = items * seq_len

    def dot(left, right):
        return jnp.dot(left, right, preferred_element_type=single)

    def dot_back(left, weight):
        return jnp.einsum("tn,kn->tk", left, weight, preferred_element_type=single)

    def weight_grad(left, right):
        return jnp.einsum("tk,tn->kn", left, right, preferred_element_type=single)

    time_silu = jax.nn.silu(time_embed[0].astype(single)).astype(narrow)
    ada_depth = w_ada.shape[0]
    time_here = lax.dynamic_slice_in_dim(time_silu, place * ada_depth, ada_depth, 1)

    def spread(part, whole):
        return lax.dynamic_update_slice_in_dim(
            jnp.zeros((whole,), single), part.reshape(-1), place * part.size, 0
        )

    group = lax.axis_index("items")
    core, far = lax.rem(group, 2), group // 2
    counts_here = live_rows[0]
    text_float = text_states[0].astype(single).reshape(items * text_local, text_width)
    text_inverse = norm_parts(text_float)[1]
    (modulation, counts, text_inverse), qkv_here, text_in = first_sums(
        [
            dot(time_here, w_ada),
            spread(counts_here.astype(single), ranks * items),
            spread(text_inverse, ranks * items * text_local),
        ],
        w_qkv,
        text_states[0],
        0,
    )
    qkv_here = qkv_here.reshape(width, -1)
    modulation = modulation + ada_bias
    counts = counts.astype(jnp.int32)
    text_inverse = text_inverse.reshape(-1, 1)
    scale_attn = modulation[:, None, 0:width]
    gate_attn = jnp.tanh(modulation[:, None, width : 2 * width])
    scale_ffn = modulation[:, None, 2 * width : 3 * width]
    gate_ffn = jnp.tanh(modulation[:, None, 3 * width :])

    slot_in_row = jnp.arange(slots) // COLS
    live_mask = (slot_in_row[None, :] < counts_here[0][:, None]).astype(single)[..., None]
    def gain_here(index):
        return lax.dynamic_slice_in_dim(gains[index], place * span, span, 0)

    states = hidden_in[0].reshape(items, slots, width)
    unit_in, inverse_in = norm_parts(states)
    norm_in = unit_in * gains[0]
    attn_in = gather_tokens((norm_in * (1.0 + scale_attn)).astype(narrow), 1)
    hidden = w_down.shape[0]
    gu_rows = pack_quarter(w_gu, (2 * core + far).reshape(1), 2, ranks)
    gu_rows, attn_in = lax.optimization_barrier((gu_rows, attn_in))
    gu_part = lax.all_to_all(gu_rows, "rows", 0, 0, tiled=True)
    gu_pair = join_blocks(gu_part, swap(gu_part, FARS), far_bit)

    features = text_width // ranks
    features = text_width // ranks
    text_in = text_in.reshape(items * text_all, features)
    text_unit = text_in.astype(single) * text_inverse
    gain_text = lax.dynamic_slice_in_dim(text_gain, place * features, features, 0)
    text_norm = (text_unit * gain_text).astype(narrow)

    text_parts = pack_blocks(dot(text_norm, w_text).astype(narrow), 2, ranks, narrow)
    text_proj = scatter_rows(text_parts, 2, 0).reshape(ranks, items, text_local, 2 * span)
    qkv_proj, squares = project(attn_in, qkv_here, text_proj)
    totals = sum_rows(squares, 3)
    gains_both = jnp.concatenate([gain_here(1), gain_here(2)])[None]
    gain_t = gain_here(6)[None]
    gate_here = jnp.tanh(lax.dynamic_slice_in_dim(cross_gate, place * heads_here, heads_here, 0))
    gate_lanes = jnp.repeat(gate_here, head_size)[None]
    out_parts, combined, qkv_bf, text_kv, tables = attend(
        qkv_proj,
        totals,
        text_proj,
        gains_both,
        gain_t,
        gate_lanes,
        w_out,
        counts,
        frame_rows[0],
        text_len[0],
        head_size,
    )
    projected = scatter_tokens(out_parts, items, 4)

    unit_proj, inverse_proj = norm_parts(projected)
    norm_proj = unit_proj * gains[3]
    middle = states + gate_attn * norm_proj
    unit_mid, inverse_mid = norm_parts(middle)
    norm_mid = unit_mid * gains[4]
    ffn_in = gather_tokens((norm_mid * (1.0 + scale_ffn)).astype(narrow), 5)
    gu_columns = join_blocks(gu_pair, swap(gu_pair, CORES), core_bit)
    gu_here = gu_columns.reshape(width, 2 * w_down.shape[0])
    gate_up = dot(ffn_in, gu_here)
    gate_part, up_part = jnp.split(gate_up, 2, axis=1)
    sigmoid = 1.0 / (1.0 + jnp.exp(-gate_part))
    inner_act = (gate_part * sigmoid * up_part).astype(narrow)
    ffn_out = scatter_tokens(dot(inner_act, w_down), items, 6)
    unit_ffn, inverse_ffn = norm_parts(ffn_out)
    norm_ffn = unit_ffn * gains[5]
    output = live_mask * (middle + gate_ffn * norm_ffn)

    def over_tokens(values):
        return jnp.sum(values, axis=(0, 1))

    grad_result = live_mask * cotangent[0].reshape(items, slots, width)
    grad_gate_ffn = (1.0 - gate_ffn * gate_ffn)[:, 0] * jnp.sum(grad_result * norm_ffn, axis=1)
    grad_norm = gate_ffn * grad_result
    grad_five = over_tokens(grad_norm * unit_ffn)
    ffn_low = gather_tokens(
        norm_back(unit_ffn, inverse_ffn, grad_norm * gains[5]).astype(narrow), 7
    )
    grad_down = weight_grad(inner_act, ffn_low).astype(narrow).reshape(2, -1, width)
    give_down, keep_down = give_keep(grad_down, core, 0)
    grad_inner = dot_back(ffn_low, w_down)
    gate_up_low = jnp.concatenate(
        [
            grad_inner * up_part * sigmoid * (1.0 + gate_part * (1.0 - sigmoid)),
            grad_inner * gate_part * sigmoid,
        ],
        axis=1,
    ).astype(narrow)
    grad_gu = weight_grad(ffn_in, gate_up_low).astype(narrow)
    give_gu, keep_gu = give_keep(grad_gu.reshape(ranks, 2, -1, 2 * hidden), core, 1)
    grad_ffn_in, got_down, got_gu = scatter_tokens(
        dot_back(gate_up_low, gu_here), items, 8, swaps=((give_down, "core"), (give_gu, "core"))
    )
    half_down = add_low(keep_down, got_down)
    half_gu = add_low(keep_gu, got_gu)
    give_gu, keep_gu = give_keep(half_gu.reshape(ranks, 2, -1, 2 * hidden), far, 1)
    grad_scale_ffn = jnp.sum(grad_ffn_in * norm_mid, axis=1)
    grad_norm = grad_ffn_in * (1.0 + scale_ffn)
    grad_four = over_tokens(grad_norm * unit_mid)
    grad_middle = grad_result + norm_back(unit_mid, inverse_mid, grad_norm * gains[4])

    grad_gate_attn = (1.0 - gate_attn * gate_attn)[:, 0] * jnp.sum(grad_middle * norm_proj, axis=1)
    grad_norm = gate_attn * grad_middle
    grad_three = over_tokens(grad_norm * unit_proj)
    projected_low, got_gu, got_down = gather_tokens(
        norm_back(unit_proj, inverse_proj, grad_norm * gains[3]).astype(narrow),
        9,
        swaps=((give_gu, "far"), (half_down, "far")),
    )
    sum_gu = add_low(keep_gu, got_gu)
    rows_gu = lax.all_to_all(sum_gu, "rows", 0, 0, tiled=True)
    grad_out = weight_grad(combined, projected_low).astype(narrow).reshape(2, -1, width)
    give_out, keep_out = give_keep(grad_out, core, 0)
    scaled, grad_value, text_scaled, text_value, sums, gain_sums, gate_sums = attend_back(
        projected_low,
        w_out,
        qkv_bf,
        text_kv,
        tables,
        qkv_proj,
        totals,
        text_proj,
        gains_both,
        gain_t,
        gate_lanes,
        counts,
        text_len[0],
        head_size,
        (sum_gu, give_out),
    )
    sum_down = add_low(half_down, got_down)
    half_out = add_low(keep_out, swap(give_out, CORES))
    grad_gate = (1.0 - gate_here * gate_here) * jnp.sum(
        gate_sums.reshape(heads_here, head_size), axis=1
    )
    qkv_low, text_low = norms_back(
        qkv_proj,
        totals,
        sum_rows(sums, 10, after=(sum_down, half_out, rows_gu)),
        scaled,
        grad_value,
        text_proj,
        text_scaled,
        text_value,
        width,
    )
    grad_qkv = weight_grad(attn_in, qkv_low).astype(narrow)
    give_qkv, keep_qkv = give_keep(grad_qkv.reshape(ranks, 2, -1, 3 * span), core, 1)

    text_low = text_low.reshape(items * text_all, 2 * span)
    all_low, got_gu, got_out, got_qkv, got_down = gather_rows(
        text_low,
        12,
        0,
        swaps=((rows_gu, "far"), (half_out, "far"), (give_qkv, "core"), (sum_down, "core")),
    )
    all_low = unpack_blocks(all_low, 2, narrow)
    grad_text = weight_grad(text_norm, all_low).astype(narrow).reshape(2, -1, 2 * width)
    give_text, keep_text = give_keep(grad_text, core, 0)
    half_text = add_low(keep_text, swap(give_text, CORES))
    middle_row = half_text.shape[0] // 2
    pair_gu = join_blocks(rows_gu, got_gu, far_bit)
    sum_out, half_qkv = add_low(half_out, got_out), add_low(keep_qkv, got_qkv)
    grad_attn_in, got_qkv, got_text, got_out, got_gu = scatter_tokens(
        dot_back(qkv_low, qkv_here),
        items,
        11,
        swaps=(
            (half_qkv, "far"),
            (half_text[:middle_row], "far"),
            (sum_out, "core"),
            (pair_gu, "core"),
        ),
    )
    sum_qkv = add_low(half_qkv, got_qkv)
    rows_qkv = lax.all_to_all(sum_qkv, "rows", 0, 0, tiled=True)
    sum_text = [add_low(half_text[:middle_row], got_text)]
    grad_scale_attn = jnp.sum(grad_attn_in * norm_in, axis=1)
    grad_norm = grad_attn_in * (1.0 + scale_attn)
    grad_zero = over_tokens(grad_norm * unit_in)
    grad_x = grad_middle + norm_back(unit_in, inverse_in, grad_norm * gains[0])

    grad_text_gain = jnp.sum(dot_back(all_low, w_text) * text_unit, axis=0)
    grad_modulation = jnp.stack([grad_scale_attn, grad_gate_attn, grad_scale_ffn, grad_gate_ffn], 1)
    grad_gains = jnp.stack(
        [
            grad_zero,
            spread(gain_sums[0, :span], width),
            spread(gain_sums[0, span:], width),
            grad_three,
            grad_four,
            grad_five,
            spread(gain_sums[1, :span], width),
        ]
    )
    flat = jnp.concatenate(
        [
            grad_gains.reshape(-1),
            spread(grad_text_gain, text_width),
            spread(grad_gate, heads),
        ]
    )
    lanes = ranks * 128
    sum_depth = -(-flat.size // lanes)
    flat = jnp.pad(flat, (0, sum_depth * lanes - flat.size)).reshape(ranks, sum_depth, 128)
    time_rows = spread(time_here.astype(single), ranks * time_here.size).reshape(ranks, -1, 128)
    grad_depth, time_depth = grad_modulation.size // lanes, time_rows.shape[1]
    keep_depth = grad_depth + time_depth
    reduced, got_text, other_text = final_sums(
        jnp.concatenate([flat, grad_modulation.reshape(ranks, grad_depth, 128), time_rows], axis=1),
        sum_depth,
        13,
        swaps=((half_text[middle_row:], "far"), (sum_text[0], "core")),
    )
    sum_text.append(add_low(half_text[middle_row:], got_text))
    sum_text = jnp.concatenate(sum_text)
    got_text = jnp.concatenate([other_text, swap(sum_text[middle_row:], CORES)])
    flat = reduced[:, :sum_depth].reshape(-1)
    total_gains = flat[: gains.size].reshape(gains.shape)
    total_text_gain = flat[gains.size : gains.size + text_width]
    total_gate = flat[gains.size + text_width : gains.size + text_width + heads]
    groups = lax.axis_size("items")
    kept = reduced[:, sum_depth:].reshape(ranks, groups, keep_depth, 128)
    all_modulation = jnp.swapaxes(kept[:, :, :grad_depth], 0, 1).reshape(groups * items, 4 * width)
    all_time = lax.dynamic_index_in_dim(kept[:, :, grad_depth:], place, 0, keepdims=False)
    all_time = all_time.reshape(groups * items, ada_depth)
    final_ada = jnp.einsum(
        "tk,tn->kn",
        all_time,
        all_modulation,
        precision=lax.Precision.HIGHEST,
        preferred_element_type=single,
    )
    total_bias = jnp.sum(all_modulation, axis=0)
    def whole_rows(half, got):
        return join_rows(half, got, core_bit, single).reshape(-1, half.shape[-1])

    sums = [
        unpack_halves(rows_qkv, swap(rows_qkv, CORES), 3),
        whole_rows(sum_out, got_out),
        whole_rows(sum_text, swap(sum_text, CORES)),
        unpack_halves(pair_gu, got_gu, 2),
        whole_rows(sum_down, got_down),
    ]
    return (
        output.reshape(1, items * slots, width),
        grad_x.reshape(1, items * slots, width),
        *sums,
        final_ada,
        total_gains,
        total_gate,
        total_bias,
        total_text_gain,
    )


def per_device(*arrays):
    heads = arrays[14].shape[0]
    plan = gathered_plan if heads % lax.axis_size("rows") else head_parallel_plan
    return plan(*arrays)


def solution(mesh):
    in_specs = (
        P("items", "rows", None),
        P("items", "rows", None),
        P("items", None, "rows", None),
        P("items", None, None),
        P("items", "rows", None),
        P("items", None),
        P("items", None),
        P("rows", None),
        P("rows", None),
        P("rows", None),
        P("rows", None),
        P("rows", None),
        P("rows", None),
        P(),
        P(),
        P(),
        P(),
    )
    out_specs = (
        P("items", "rows", None),
        P("items", "rows", None),
        P("rows", None),
        P("rows", None),
        P("rows", None),
        P("rows", None),
        P("rows", None),
        P("rows", None),
        P(),
        P(),
        P(),
        P(),
    )
    return jax.shard_map(
        per_device, mesh=mesh, in_specs=in_specs, out_specs=out_specs, check_vma=False
    )
```

```python
import functools
import itertools
import math

import jax
import jax.numpy as jnp
from jax import lax
from jax.experimental import pallas as pl
from jax.experimental.pallas import tpu as pltpu
from jax.sharding import PartitionSpec as P

COLS = 32


epsilon = 1e-06
masked_score = -1e30
group_heads = 4


def norm_gain(values, scaling):
    return values * lax.rsqrt(jnp.mean(values * values, axis=-1, keepdims=True) + epsilon) * scaling


def pre_norm(values, shift_scale, scaling):
    return norm_gain(values, scaling) * (1.0 + shift_scale)


def post_add(residual, branch, gate_in, scaling):
    return residual + jnp.tanh(gate_in) * norm_gain(branch, scaling)


def swiglu(gate_up):
    middle_col = gate_up.shape[-1] // 2
    return jax.nn.silu(gate_up[..., :middle_col]) * gate_up[..., middle_col:]


def freq_rates(number):
    return 10000.0 ** (-jnp.arange(number).astype(jnp.float32) / number)


def rotary_angles(frame_index, frame_row, column, head_size):
    frame_pairs = head_size // 8
    space_pairs = (head_size // 2 - frame_pairs) // 2
    return jnp.concatenate(
        [
            frame_index.astype(jnp.float32)[..., None] * freq_rates(frame_pairs),
            frame_row.astype(jnp.float32)[..., None] * freq_rates(space_pairs),
            column.astype(jnp.float32)[..., None] * freq_rates(space_pairs),
        ],
        axis=-1,
    )


def rotate(values, cos_table, sin_table, head_count):
    shaped = values.reshape(values.shape[:-1] + (head_count, values.shape[-1] // head_count))
    half_size = shaped.shape[-1] // 2
    upper_half = shaped[..., :half_size]
    lower_half = shaped[..., half_size:]
    cos_heads = cos_table[..., None, :]
    sin_heads = sin_table[..., None, :]
    turned = jnp.concatenate(
        [
            upper_half * cos_heads - lower_half * sin_heads,
            upper_half * sin_heads + lower_half * cos_heads,
        ],
        axis=-1,
    )
    return turned.reshape(values.shape)


def text_split(projected, key_gain):
    half_cols = projected.shape[-1] // 2
    return (norm_gain(projected[..., :half_cols], key_gain), projected[..., half_cols:])


def gathered_plan(
    hidden_in,
    cotangent,
    text_states,
    time_embed,
    live_rows,
    frame_rows,
    text_len,
    w_qkv,
    w_out,
    w_text,
    w_gu,
    w_down,
    w_ada,
    gains,
    cross_gate,
    ada_bias,
    text_gain,
):
    single = jnp.float32
    narrow = jnp.bfloat16
    model_width = hidden_in.shape[2]
    head_count = cross_gate.shape[0]
    head_size = model_width // head_count
    score_scale = head_size ** (-0.5)
    item_count = time_embed.shape[1]
    item_slots = hidden_in.shape[1] // item_count
    row_devices = lax.axis_size("rows")
    seq_len = row_devices * item_slots
    text_local = text_states.shape[2]
    text_all = text_local * row_devices
    text_width = text_states.shape[3]
    group_span = group_heads * head_size
    block_count = head_count // group_heads
    token_count = item_count * item_slots

    def weight_term(left, right, accuracy):
        return jnp.einsum(
            "tk,tn->kn", left, right, precision=accuracy, preferred_element_type=single
        )

    def reduce_term(term):
        return lax.psum_scatter(
            term.astype(jnp.bfloat16), "rows", scatter_dimension=0, tiled=True
        ).astype(jnp.float32)

    full_qkv, full_out, full_text, full_gu, full_down, full_ada = (
        lax.all_gather(w_qkv, "rows", axis=0, tiled=True),
        lax.all_gather(w_out, "rows", axis=0, tiled=True),
        lax.all_gather(w_text, "rows", axis=0, tiled=True),
        lax.all_gather(w_gu, "rows", axis=0, tiled=True),
        lax.all_gather(w_down, "rows", axis=0, tiled=True),
        lax.all_gather(w_ada, "rows", axis=0, tiled=True),
    )
    counts_here = live_rows[0]
    every_count = lax.all_gather(counts_here, "rows", axis=0, tiled=True)
    device_place = lax.axis_index("rows")
    ranks = jnp.arange(row_devices)
    rows_below = jnp.sum(jnp.where(ranks[:, None] < device_place, every_count, 0), axis=0)
    slot_row = jnp.arange(item_slots) // COLS
    column = jnp.arange(item_slots) % COLS
    row_index = rows_below[:, None] + slot_row[None, :]
    heights = frame_rows[0][:, None]
    frame_index = row_index // heights
    frame_row = row_index % heights
    live_mask = (slot_row[None, :] < counts_here[0][:, None]).astype(single)
    key_live = (slot_row[None, None, :] < jnp.transpose(every_count)[:, :, None]).reshape(
        item_count, seq_len
    )
    text_live = jnp.arange(text_all)[None, :] < text_len[0][:, None]
    angles = rotary_angles(
        frame_index, frame_row, jnp.broadcast_to(column, row_index.shape), head_size
    )
    cos_table = jnp.cos(angles)
    sin_table = jnp.sin(angles)

    def qkv_split(projected, gain_query, gain_key):
        queries = rotate(
            norm_gain(projected[..., :model_width], gain_query), cos_table, sin_table, head_count
        )
        keys_here = rotate(
            norm_gain(projected[..., model_width : 2 * model_width], gain_key),
            cos_table,
            sin_table,
            head_count,
        )
        return (queries, keys_here, projected[..., 2 * model_width :])

    states = hidden_in[0].reshape(item_count, item_slots, model_width)
    time_silu = jax.nn.silu(time_embed[0].astype(single)).astype(narrow)
    modulation = jnp.dot(time_silu, full_ada, preferred_element_type=single) + ada_bias
    scale_attn = modulation[:, None, 0:model_width]
    gate_attn = modulation[:, None, model_width : 2 * model_width]
    scale_ffn = modulation[:, None, 2 * model_width : 3 * model_width]
    gate_ffn = modulation[:, None, 3 * model_width :]
    attn_in = (
        pre_norm(states, scale_attn, gains[0]).astype(narrow).reshape(token_count, model_width)
    )
    qkv_proj = jnp.dot(attn_in, full_qkv, preferred_element_type=single).reshape(
        item_count, item_slots, 3 * model_width
    )
    query_full, key_full, value_full = qkv_split(qkv_proj, gains[1], gains[2])
    query_low = query_full.astype(narrow)
    key_low = key_full.astype(narrow)
    value_low = value_full.astype(narrow)
    text_float = text_states[0].astype(single)
    text_norm = norm_gain(text_float, text_gain).astype(narrow)
    text_proj = jnp.einsum("ctd,dn->ctn", text_norm, full_text, preferred_element_type=single)
    tkey_full, tval_full = text_split(text_proj, gains[6])
    key_all, value_all, tkey_all, tval_all = (
        lax.all_gather(key_low, "rows", axis=1, tiled=True),
        lax.all_gather(value_low, "rows", axis=1, tiled=True),
        lax.all_gather(tkey_full.astype(narrow), "rows", axis=1, tiled=True),
        lax.all_gather(tval_full.astype(narrow), "rows", axis=1, tiled=True),
    )

    def block_slices(block_index, key_source, value_source):
        offset = block_index * group_span
        query_part = lax.dynamic_slice_in_dim(query_low, offset, group_span, 2).reshape(
            item_count, item_slots, group_heads, head_size
        )
        key_part = lax.dynamic_slice_in_dim(key_source, offset, group_span, 2).reshape(
            item_count, seq_len, group_heads, head_size
        )
        value_part = lax.dynamic_slice_in_dim(value_source, offset, group_span, 2).reshape(
            item_count, seq_len, group_heads, head_size
        )
        return (query_part, key_part, value_part)

    def self_step(carry, block_index):
        query_part, key_part, value_part = block_slices(block_index, key_all, value_all)
        scores = (
            jnp.einsum("iphe,ikhe->ihpk", query_part, key_part, preferred_element_type=single)
            * score_scale
        )
        scores = jnp.where(key_live[:, None, None, :], scores, masked_score)
        row_max = jnp.max(scores, axis=-1, keepdims=True)
        exp_terms = jnp.exp(scores - row_max)
        exp_total = jnp.sum(exp_terms, axis=-1, keepdims=True)
        probs_low = (exp_terms / exp_total).astype(narrow)
        attended = jnp.einsum(
            "ihpk,ikhe->iphe", probs_low, value_part, preferred_element_type=single
        )
        return (
            carry,
            (
                attended.reshape(item_count, item_slots, group_span),
                (row_max + jnp.log(exp_total))[..., 0],
            ),
        )

    _, (self_parts, log_totals) = lax.scan(
        self_step, jnp.zeros((), single), jnp.arange(block_count)
    )

    def heads_last(parts):
        return jnp.transpose(parts, (1, 2, 0, 3)).reshape(item_count, item_slots, model_width)

    self_out = heads_last(self_parts)
    query_heads = query_low.reshape(item_count, item_slots, head_count, head_size)
    tkey_heads = tkey_all.reshape(item_count, text_all, head_count, head_size)
    tval_heads = tval_all.reshape(item_count, text_all, head_count, head_size)
    cross_scores = (
        jnp.einsum("iphe,ikhe->ihpk", query_heads, tkey_heads, preferred_element_type=single)
        * score_scale
    )
    cross_scores = jnp.where(text_live[:, None, None, :], cross_scores, masked_score)
    cross_max = jnp.max(cross_scores, axis=-1, keepdims=True)
    cross_exp = jnp.exp(cross_scores - cross_max)
    cross_probs = cross_exp / jnp.sum(cross_exp, axis=-1, keepdims=True)
    cross_low = cross_probs.astype(narrow)
    cross_out = jnp.einsum("ihpk,ikhe->iphe", cross_low, tval_heads, preferred_element_type=single)
    tanh_gate = jnp.tanh(cross_gate)
    combined = (
        self_out.reshape(item_count, item_slots, head_count, head_size)
        + tanh_gate[:, None] * cross_out
    )
    combined = combined.reshape(token_count, model_width).astype(narrow)
    projected = jnp.dot(combined, full_out, preferred_element_type=single).reshape(
        item_count, item_slots, model_width
    )
    middle = post_add(states, projected, gate_attn, gains[3])
    ffn_in = pre_norm(middle, scale_ffn, gains[4]).astype(narrow).reshape(token_count, model_width)
    gate_up = jnp.dot(ffn_in, full_gu, preferred_element_type=single)
    inner_act = swiglu(gate_up).astype(narrow)
    ffn_out = jnp.dot(inner_act, full_down, preferred_element_type=single).reshape(
        item_count, item_slots, model_width
    )
    result = post_add(middle, ffn_out, gate_ffn, gains[5])
    output = (live_mask[..., None] * result).reshape(1, token_count, model_width)
    grad_result = live_mask[..., None] * cotangent[0].reshape(item_count, item_slots, model_width)
    _, back_ffn_out = jax.vjp(post_add, middle, ffn_out, gate_ffn, gains[5])
    grad_middle, grad_ffn_out, grad_gate_ffn, grad_gain_five = back_ffn_out(grad_result)
    ffn_low = grad_ffn_out.astype(narrow).reshape(token_count, model_width)
    shard_down = reduce_term(weight_term(inner_act, ffn_low, None))
    grad_inner = jnp.einsum("tn,kn->tk", ffn_low, full_down, preferred_element_type=single)
    _, back_glu = jax.vjp(swiglu, gate_up)
    gate_up_low = back_glu(grad_inner)[0].astype(narrow)
    shard_gu = reduce_term(weight_term(ffn_in, gate_up_low, None))
    grad_ffn_in = jnp.einsum("tn,kn->tk", gate_up_low, full_gu, preferred_element_type=single)
    _, back_ffn_in = jax.vjp(pre_norm, middle, scale_ffn, gains[4])
    part_middle, grad_scale_ffn, grad_gain_four = back_ffn_in(
        grad_ffn_in.reshape(item_count, item_slots, model_width)
    )
    grad_middle = grad_middle + part_middle
    _, back_attn_out = jax.vjp(post_add, states, projected, gate_attn, gains[3])
    grad_hidden, grad_projected, grad_gate_attn, grad_gain_three = back_attn_out(grad_middle)
    projected_low = grad_projected.astype(narrow).reshape(token_count, model_width)
    shard_out = reduce_term(weight_term(combined, projected_low, None))
    grad_combined = jnp.einsum("tn,kn->tk", projected_low, full_out, preferred_element_type=single)
    grad_combined = grad_combined.reshape(item_count, item_slots, head_count, head_size)
    self_low = grad_combined.reshape(item_count, item_slots, model_width).astype(narrow)
    cross_grad_low = (tanh_gate[:, None] * grad_combined).astype(narrow)
    grad_cross_gate = (1.0 - tanh_gate * tanh_gate) * jnp.sum(
        grad_combined * cross_out, axis=(0, 1, 3)
    )

    def self_back(carry, packed):
        block_index, log_total = packed
        query_part, key_part, value_part = block_slices(block_index, key_all, value_all)
        offset = block_index * group_span
        grad_part = lax.dynamic_slice_in_dim(self_low, offset, group_span, 2).reshape(
            item_count, item_slots, group_heads, head_size
        )
        scores = (
            jnp.einsum("iphe,ikhe->ihpk", query_part, key_part, preferred_element_type=single)
            * score_scale
        )
        scores = jnp.where(key_live[:, None, None, :], scores, masked_score)
        attn_probs = jnp.exp(scores - log_total[..., None])
        grad_probs = jnp.einsum(
            "iphe,ikhe->ihpk", grad_part, value_part, preferred_element_type=single
        )
        row_inner = jnp.sum(attn_probs * grad_probs, axis=-1, keepdims=True)
        score_low = (attn_probs * (grad_probs - row_inner)).astype(narrow)
        grad_query = (
            jnp.einsum("ihpk,ikhe->iphe", score_low, key_part, preferred_element_type=single)
            * score_scale
        )
        grad_value = jnp.einsum(
            "ihpk,iphe->ikhe", attn_probs.astype(narrow), grad_part, preferred_element_type=single
        )
        grad_key = (
            jnp.einsum("ihpk,iphe->ikhe", score_low, query_part, preferred_element_type=single)
            * score_scale
        )
        owned_key, owned_value = (
            lax.psum_scatter(
                grad_key.reshape(item_count, seq_len, group_span).astype(jnp.bfloat16),
                "rows",
                scatter_dimension=1,
                tiled=True,
            ).astype(jnp.float32),
            lax.psum_scatter(
                grad_value.reshape(item_count, seq_len, group_span).astype(jnp.bfloat16),
                "rows",
                scatter_dimension=1,
                tiled=True,
            ).astype(jnp.float32),
        )
        return (
            carry,
            (grad_query.reshape(item_count, item_slots, group_span), owned_key, owned_value),
        )

    _, (query_parts, key_parts, value_parts) = lax.scan(
        self_back, jnp.zeros((), single), (jnp.arange(block_count), log_totals)
    )
    cross_grad_probs = jnp.einsum(
        "iphe,ikhe->ihpk", cross_grad_low, tval_heads, preferred_element_type=single
    )
    cross_inner = jnp.sum(cross_probs * cross_grad_probs, axis=-1, keepdims=True)
    cross_score_low = (cross_probs * (cross_grad_probs - cross_inner)).astype(narrow)
    grad_query_cross = (
        jnp.einsum("ihpk,ikhe->iphe", cross_score_low, tkey_heads, preferred_element_type=single)
        * score_scale
    )
    grad_text_key = (
        jnp.einsum("ihpk,iphe->ikhe", cross_score_low, query_heads, preferred_element_type=single)
        * score_scale
    )
    grad_text_value = jnp.einsum(
        "ihpk,iphe->ikhe", cross_low, cross_grad_low, preferred_element_type=single
    )
    owned_tkey, owned_tval = (
        lax.psum_scatter(
            grad_text_key.reshape(item_count, text_all, model_width).astype(jnp.bfloat16),
            "rows",
            scatter_dimension=1,
            tiled=True,
        ).astype(jnp.float32),
        lax.psum_scatter(
            grad_text_value.reshape(item_count, text_all, model_width).astype(jnp.bfloat16),
            "rows",
            scatter_dimension=1,
            tiled=True,
        ).astype(jnp.float32),
    )
    grad_query_all = heads_last(query_parts) + grad_query_cross.reshape(
        item_count, item_slots, model_width
    )
    _, back_qkv = jax.vjp(qkv_split, qkv_proj, gains[1], gains[2])
    grad_qkv, grad_gain_one, grad_gain_two = back_qkv(
        (grad_query_all, heads_last(key_parts), heads_last(value_parts))
    )
    qkv_low = grad_qkv.astype(narrow).reshape(token_count, 3 * model_width)
    shard_qkv = reduce_term(weight_term(attn_in, qkv_low, None))
    grad_attn_in = jnp.einsum("tn,kn->tk", qkv_low, full_qkv, preferred_element_type=single)
    _, back_attn_in = jax.vjp(pre_norm, states, scale_attn, gains[0])
    part_states, grad_scale_attn, grad_gain_zero = back_attn_in(
        grad_attn_in.reshape(item_count, item_slots, model_width)
    )
    grad_x = (grad_hidden + part_states).reshape(1, token_count, model_width)
    _, back_text = jax.vjp(text_split, text_proj, gains[6])
    grad_text_proj, grad_gain_six = back_text((owned_tkey, owned_tval))
    text_low = grad_text_proj.astype(narrow).reshape(item_count * text_local, 2 * model_width)
    shard_text = reduce_term(
        weight_term(text_norm.reshape(item_count * text_local, text_width), text_low, None)
    )
    grad_text_norm = jnp.einsum("tn,kn->tk", text_low, full_text, preferred_element_type=single)
    _, back_text_norm = jax.vjp(norm_gain, text_float, text_gain)
    grad_text_gain = back_text_norm(grad_text_norm.reshape(text_float.shape))[1]
    grad_modulation = jnp.concatenate(
        [grad_scale_attn, grad_gate_attn, grad_scale_ffn, grad_gate_ffn], axis=-1
    )[:, 0, :]
    shard_ada = reduce_term(
        weight_term(time_silu.astype(single), grad_modulation, lax.Precision.HIGHEST)
    )
    grad_ada_bias = jnp.sum(grad_modulation, axis=0)
    grad_gains = jnp.stack(
        [
            grad_gain_zero,
            grad_gain_one,
            grad_gain_two,
            grad_gain_three,
            grad_gain_four,
            grad_gain_five,
            grad_gain_six,
        ],
        axis=0,
    )
    final_qkv, final_out, final_text, final_gu, final_down, final_ada = (
        lax.psum(shard_qkv.astype(jnp.bfloat16), "items").astype(jnp.float32),
        lax.psum(shard_out.astype(jnp.bfloat16), "items").astype(jnp.float32),
        lax.psum(shard_text.astype(jnp.bfloat16), "items").astype(jnp.float32),
        lax.psum(shard_gu.astype(jnp.bfloat16), "items").astype(jnp.float32),
        lax.psum(shard_down.astype(jnp.bfloat16), "items").astype(jnp.float32),
        lax.psum(shard_ada.astype(jnp.bfloat16), "items").astype(jnp.float32),
    )
    total_gains, total_gate, total_bias, total_text_gain = lax.psum(
        (grad_gains, grad_cross_gate, grad_ada_bias, grad_text_gain), ("items", "rows")
    )
    return (
        output,
        grad_x,
        final_qkv,
        final_out,
        final_text,
        final_gu,
        final_down,
        final_ada,
        total_gains,
        total_gate,
        total_bias,
        total_text_gain,
    )


def norm_parts(values):
    inverse = lax.rsqrt(jnp.mean(values * values, axis=-1, keepdims=True) + epsilon)
    return values * inverse, inverse


def norm_back(unit, inverse, scaled_grad):
    return inverse * (scaled_grad - unit * jnp.mean(scaled_grad * unit, axis=-1, keepdims=True))


MESH = pl.DeviceIdType.MESH
DEPTH, BREADTH = 4, 2


def row_place():
    place = lax.axis_index("rows")
    return place // BREADTH, lax.rem(place, BREADTH)


def on_rows(line, side):
    return {"rows": line * BREADTH + side}


def greet(devices):
    barrier = pltpu.get_barrier_semaphore()
    for condition, device in devices:

        @pl.when(condition)
        def _(device=device):
            pl.semaphore_signal(barrier, inc=1, device_id=device, device_id_type=MESH)

    count = 0
    for condition, _ in devices:
        count = count + jnp.where(condition, 1, 0)
    pl.semaphore_wait(barrier, count)


def remote(source, target, send, receive, device):
    return pltpu.make_async_remote_copy(
        src_ref=source,
        dst_ref=target,
        send_sem=send,
        recv_sem=receive,
        device_id=device,
        device_id_type=MESH,
    )


def shard_of(ref, place, axis):
    return ref.at[place] if axis == 0 else ref.at[:, place]


CHUNKS = 2


def partner(kind):
    group = lax.axis_index("items")
    if kind == "core":
        return {"items": group + 1 - 2 * lax.rem(group, 2)}
    return {"items": lax.rem(group + 2, 4)}


def chunk_part(ref, chunk, start, size):
    rows = ref.shape[0] // CHUNKS
    middle = (slice(None),) * (len(ref.shape) - 2)
    return ref.at[(pl.ds(chunk * rows, rows),) + middle + (pl.ds(start, size),)]


def streams_of(width):
    first = split_lanes(width)
    streams = [(0, chunk, 0, first) for chunk in range(CHUNKS)]
    if first < width:
        streams += [(which, chunk, first, width - first) for which in range(2) for chunk in range(CHUNKS)]
    return streams


class Swaps:
    def __init__(self, pairs):
        self.arrays = tuple(array for array, _ in pairs)
        self.kinds = tuple(kind for _, kind in pairs)

    def shapes(self):
        return [jax.ShapeDtypeStruct(array.shape, array.dtype) for array in self.arrays]

    def specs(self):
        return [pl.BlockSpec(memory_space=pl.ANY)] * len(self.arrays)

    def scratch(self):
        return [pltpu.SemaphoreType.DMA((2, max(1, len(self.arrays))))]

    def partners(self, always):
        return [(always, partner(kind)) for kind in sorted(set(self.kinds))]

    def copies(self, sources, targets, semaphores):
        return [
            remote(source, target, semaphores.at[0, at], semaphores.at[1, at], partner(kind))
            for at, (source, target, kind) in enumerate(zip(sources, targets, self.kinds))
        ]


def split_lanes(width):
    return width - 128 * round(width / 128 / 6)


def gather_kernel(axis, swaps, count, own, *rest):
    number = len(swaps.kinds)
    sources, rest = rest[:number], rest[number + count :]
    whole, targets, rest = rest[0], rest[1 : 1 + number], rest[1 + number :]
    local, z_send, z_recv, x_send, x_recv, beside = rest
    line, side = row_place()
    above, below, across = on_rows(line + 1, side), on_rows(line - 1, side), on_rows(line, 1 - side)
    has_above, has_below, always = line < DEPTH - 1, line > 0, line >= 0
    greet([(has_above, above), (has_below, below), (always, across)] + swaps.partners(always))
    extra = swaps.copies(sources, targets, beside)
    for copy in extra:
        copy.start()
    streams = streams_of(own.shape[-1])
    along, over = range(CHUNKS), range(CHUNKS, len(streams))

    def block(at, stream):
        which, *piece = streams[stream]
        return chunk_part(shard_of(whole, at * BREADTH + (1 - side if which else side), axis), *piece)

    def mine(stream):
        return chunk_part(own, *streams[stream][1:])

    def pass_on(stream, source, at, way):
        return remote(
            source,
            block(at, stream),
            z_send.at[stream, way, at],
            z_recv.at[stream, at],
            below if way else above,
        )

    def cross(source, at, stream):
        slot = stream * DEPTH + at if stream < CHUNKS else CHUNKS * DEPTH + stream - CHUNKS
        return remote(source, block(at, stream), x_send.at[slot], x_recv.at[slot], across)

    def onward(stream, source):
        @pl.when(has_above)
        def _():
            pass_on(stream, source, line, 0).start()

        @pl.when(has_below)
        def _():
            pass_on(stream, source, line, 1).start()

    handed = [stream for stream in over if streams[stream][0] == 0]
    for stream in handed + list(along):
        cross(mine(stream), line, stream).start()
    for stream in list(along) + handed:
        onward(stream, mine(stream))
    keep = pltpu.make_async_copy(own, shard_of(whole, line * BREADTH + side, axis), local)
    keep.start()
    for stream in handed:
        cross(mine(stream), line, stream).wait_recv()
        onward(stream + CHUNKS, block(line, stream + CHUNKS))
    for step in range(1, DEPTH):
        for way, at, there, more in (
            (0, line - step, line - step >= 0, has_above),
            (1, line + step, line + step < DEPTH, has_below),
        ):

            @pl.when(there)
            def _(way=way, at=at, more=more):
                for stream in range(len(streams)):
                    pass_on(stream, block(at, stream), at, way).wait_recv()
                    if stream in along:
                        cross(block(at, stream), at, stream).start()

                    @pl.when(more)
                    def _(stream=stream):
                        pass_on(stream, block(at, stream), at, way).start()

    keep.wait()
    for at in range(DEPTH):
        for stream in along:
            cross(mine(stream), at, stream).wait_recv()
            cross(mine(stream), at, stream).wait_send()
        for stream in range(len(streams)):

            @pl.when(has_above & (at <= line))
            def _(at=at, stream=stream):
                pass_on(stream, block(at, stream), at, 0).wait_send()

            @pl.when(has_below & (at >= line))
            def _(at=at, stream=stream):
                pass_on(stream, block(at, stream), at, 1).wait_send()

    for stream in handed:
        cross(mine(stream), line, stream).wait_send()
    for copy in extra:
        copy.wait()


def gather_rows(block, ident, axis, after=(), swaps=()):
    ranks = DEPTH * BREADTH
    swaps = Swaps(swaps)
    shape = block.shape[:axis] + (ranks,) + block.shape[axis:]
    anywhere = pl.BlockSpec(memory_space=pl.ANY)
    wave = pltpu.SemaphoreType.DMA
    whole, *others = pl.pallas_call(
        functools.partial(gather_kernel, axis, swaps, len(after)),
        out_shape=[jax.ShapeDtypeStruct(shape, block.dtype)] + swaps.shapes(),
        in_specs=[anywhere] * (1 + len(swaps.kinds) + len(after)),
        out_specs=[anywhere] + swaps.specs(),
        scratch_shapes=[
            wave,
            wave((3 * CHUNKS, 2, DEPTH)),
            wave((3 * CHUNKS, DEPTH)),
            wave((CHUNKS * (DEPTH + 1),)),
            wave((CHUNKS * (DEPTH + 1),)),
        ]
        + swaps.scratch(),
        name=f"gather_rows_{ident}",
        compiler_params=pltpu.CompilerParams(collective_id=ident, has_side_effects=True),
    )(block, *swaps.arrays, *after)
    return (whole, *others) if others else whole


def scatter_kernel(axis, swaps, count, parts, *rest):
    number = len(swaps.kinds)
    sources, rest = rest[:number], rest[number + count :]
    total, targets, rest = rest[0], rest[1 : 1 + number], rest[1 + number :]
    crossed, flow, x_send, x_recv, z_send, z_recv, beside = rest[0], rest[1:-5], *rest[-5:]
    line, side = row_place()
    above, below, across = on_rows(line + 1, side), on_rows(line - 1, side), on_rows(line, 1 - side)
    has_above, has_below, always = line < DEPTH - 1, line > 0, line >= 0
    greet([(has_above, above), (has_below, below), (always, across)] + swaps.partners(always))
    extra = swaps.copies(sources, targets, beside)
    for copy in extra:
        copy.start()
    streams = streams_of(parts.shape[-1])
    along, over = range(CHUNKS), range(CHUNKS, len(streams))
    handed = [stream for stream in over if streams[stream][0] == 1]

    def part(at, stream, turned=False):
        other, *piece = streams[stream]
        return chunk_part(shard_of(parts, at * BREADTH + (1 - side if other or turned else side), axis), *piece)

    def slot(ref, at, stream):
        chunk = streams[stream][1]
        rows = ref.shape[1] // CHUNKS
        return ref.at[at, pl.ds(chunk * rows, rows)]

    def cross(at, stream):
        place = stream * DEPTH + at
        return remote(
            part(at, stream, True), slot(crossed, at, stream), x_send.at[place], x_recv.at[place], across
        )

    def hand(stream):
        place = CHUNKS * DEPTH + stream - handed[0]
        leave, arrive = flow[12], flow[13]
        return remote(
            slot(leave, 0, stream), slot(arrive, 0, stream), x_send.at[place], x_recv.at[place], across
        )

    def held(stream, way, leaving):
        group = 0 if stream in along else 1 + streams[stream][0]
        return flow[4 * group + 2 * way + leaving]

    def moving(stream, at, way):
        return remote(
            slot(held(stream, way, 1), at, stream),
            slot(held(stream, way, 0), at, stream),
            z_send.at[stream, way, at],
            z_recv.at[stream, way, at],
            below if way else above,
        )

    def add_up(stream, at, ways, target, others=()):
        value = part(at, stream)[...].astype(jnp.float32)
        if stream in along:
            value = value + slot(crossed, at, stream)[...].astype(jnp.float32)
        for way in ways:
            value = value + slot(held(stream, way, 0), at, stream)[...].astype(jnp.float32)
        for other in others:
            value = value + other[...].astype(jnp.float32)
        target[...] = value.astype(target.dtype)

    def send_on(stream, at, way, comes):
        leaving = slot(held(stream, way, 1), at, stream)

        @pl.when(comes)
        def _():
            moving(stream, at, way).wait_recv()
            add_up(stream, at, [way], leaving)

        @pl.when(jnp.logical_not(comes))
        def _():
            add_up(stream, at, [], leaving)

        moving(stream, at, way).start()

    def finish(stream, target, others=()):
        for below_there, above_there, ways in ((True, True, [0, 1]), (True, False, [0]), (False, True, [1])):

            @pl.when((has_below == below_there) & (has_above == above_there))
            def _(ways=ways):
                for way in ways:
                    moving(stream, line, way).wait_recv()
                add_up(stream, line, ways, target, others)

    for step in range(DEPTH - 1, 0, -1):
        for at, there in ((line + step, line + step < DEPTH), (line - step, line - step >= 0)):

            @pl.when(there)
            def _(at=at):
                for stream in along:
                    cross(at, stream).start()

    for stream in along:
        cross(line, stream).start()
    for some in (over, along):
        for step in range(DEPTH - 1, 0, -1):
            for way, at, there, comes in (
                (0, line + step, line + step < DEPTH, has_below),
                (1, line - step, line - step >= 0, has_above),
            ):
                for stream in some:

                    @pl.when(there)
                    def _(way=way, at=at, comes=comes, stream=stream):
                        if stream in along:
                            cross(at, stream).wait_recv()
                        send_on(stream, at, way, comes)

        if some is over:
            for stream in handed:
                finish(stream, slot(flow[12], 0, stream))
                hand(stream).start()

    for stream in along:
        cross(line, stream).wait_recv()
        finish(stream, chunk_part(total, *streams[stream][1:]))
    for stream in handed:
        hand(stream).wait_recv()
        mate = stream - CHUNKS
        finish(mate, chunk_part(total, *streams[mate][1:]), (slot(flow[13], 0, stream),))
        hand(stream).wait_send()
    for at in range(DEPTH):
        for stream in along:
            cross(at, stream).wait_send()
        for stream in range(len(streams)):

            @pl.when(at > line)
            def _(at=at, stream=stream):
                moving(stream, at, 0).wait_send()

            @pl.when(at < line)
            def _(at=at, stream=stream):
                moving(stream, at, 1).wait_send()

    for copy in extra:
        copy.wait()


def scatter_rows(parts, ident, axis, after=(), swaps=()):
    swaps = Swaps(swaps)
    shape = parts.shape[:axis] + parts.shape[axis + 1 :]
    width = shape[-1]
    first = split_lanes(width)
    near = pl.BlockSpec(memory_space=pltpu.VMEM)
    wave = pltpu.SemaphoreType.DMA

    def slots(size, count=(DEPTH,)):
        return pltpu.VMEM(count + shape[:-1] + (size,), parts.dtype)

    flow = [slots(first)] * 4
    if first < width:
        flow = flow + [slots(width - first)] * 8 + [slots(width - first, (1,))] * 2
    total, *others = pl.pallas_call(
        functools.partial(scatter_kernel, axis, swaps, len(after)),
        out_shape=[jax.ShapeDtypeStruct(shape, jnp.float32)] + swaps.shapes(),
        in_specs=[near] + [pl.BlockSpec(memory_space=pl.ANY)] * (len(swaps.kinds) + len(after)),
        out_specs=[near] + swaps.specs(),
        scratch_shapes=[slots(first)]
        + flow
        + [wave((CHUNKS * (DEPTH + 1),))] * 2
        + [wave((3 * CHUNKS, 2, DEPTH))] * 2
        + swaps.scratch(),
        name=f"scatter_rows_{ident}",
        compiler_params=pltpu.CompilerParams(
            collective_id=ident, has_side_effects=True, vmem_limit_bytes=32 << 20
        ),
    )(parts, *swaps.arrays, *after)
    return (total, *others) if others else total


def sum_kernel(count, own, *rest):
    total, held, send, receive = rest[count:]
    ranks = DEPTH * BREADTH
    place = lax.axis_index("rows")
    others = [lax.rem(place + step, ranks) for step in range(1, ranks)]
    greet([(place >= 0, {"rows": other}) for other in others])

    def push(step, other, slot):
        return remote(own, held.at[slot], send.at[step], receive.at[slot], {"rows": other})

    for step, other in enumerate(others):
        push(step, other, place).start()
    held[pl.ds(place, 1)] = own[...][None]
    for step, other in enumerate(others):
        push(step, other, other).wait_recv()
    value = held[0]
    for rank in range(1, ranks):
        value = value + held[rank]
    total[...] = value
    for step, other in enumerate(others):
        push(step, other, place).wait_send()


def sum_rows(own, ident, after=()):
    ranks = DEPTH * BREADTH
    near = pl.BlockSpec(memory_space=pltpu.VMEM)
    return pl.pallas_call(
        functools.partial(sum_kernel, len(after)),
        out_shape=jax.ShapeDtypeStruct(own.shape, own.dtype),
        in_specs=[near] + [pl.BlockSpec(memory_space=pl.ANY)] * len(after),
        out_specs=near,
        scratch_shapes=[
            pltpu.VMEM((ranks,) + own.shape, own.dtype),
            pltpu.SemaphoreType.DMA((ranks,)),
            pltpu.SemaphoreType.DMA((ranks,)),
        ],
        name=f"sum_rows_{ident}",
        compiler_params=pltpu.CompilerParams(collective_id=ident, has_side_effects=True),
    )(own, *after)


def final_kernel(ranks, groups, sums, swaps, own, *rest):
    number = len(swaps.kinds)
    sources, out, targets, rest = rest[:number], rest[number], rest[number + 1 : 2 * number + 1], rest[2 * number + 1 :]
    held, kept, part, h_send, h_recv, g_send, g_recv, o_send, o_recv, beside = rest
    place, group = lax.axis_index("rows"), lax.axis_index("items")
    rows = [lax.rem(place + step, ranks) for step in range(1, ranks)]
    items = [lax.rem(group + step, groups) for step in range(1, groups)]
    greet([(place >= 0, {"rows": other}) for other in rows] + [(place >= 0, {"items": other}) for other in items])
    extra = swaps.copies(sources, targets, beside)
    for copy in extra:
        copy.start()

    def push(step, other, slot):
        return remote(own.at[other], held.at[slot], h_send.at[step], h_recv.at[slot], {"rows": other})

    def swap(step, other, slot):
        return remote(part, kept.at[slot], g_send.at[step], g_recv.at[slot], {"items": other})

    def share(step, other, slot):
        return remote(out.at[place], out.at[slot], o_send.at[step], o_recv.at[slot], {"rows": other})

    for step, other in enumerate(rows):
        push(step, other, place).start()
    held[pl.ds(place, 1)] = own[pl.ds(place, 1)]
    for step, other in enumerate(rows):
        push(step, other, other).wait_recv()
    value = held[0]
    for rank in range(1, ranks):
        value = value + held[rank]
    part[...] = value
    for step, other in enumerate(items):
        swap(step, other, group).start()
    kept[pl.ds(group, 1)] = value[None]
    for step, other in enumerate(items):
        swap(step, other, other).wait_recv()
    total = kept[0, :sums]
    for item in range(1, groups):
        total = total + kept[item, :sums]
    depth = own.shape[1] - sums
    out[pl.ds(place, 1), :sums] = total[None]
    for item in range(groups):
        out[pl.ds(place, 1), sums + item * depth : sums + (item + 1) * depth] = kept[item, sums:][None]
    for step, other in enumerate(rows):
        share(step, other, place).start()
    for step, other in enumerate(rows):
        share(step, other, other).wait_recv()
    for step, other in enumerate(rows):
        push(step, other, place).wait_send()
        share(step, other, place).wait_send()
    for step, other in enumerate(items):
        swap(step, other, group).wait_send()
    for copy in extra:
        copy.wait()


def final_sums(own, sums, ident, swaps=()):
    ranks, groups = lax.axis_size("rows"), lax.axis_size("items")
    near = pl.BlockSpec(memory_space=pltpu.VMEM)
    depth = own.shape[1]
    swaps = Swaps(swaps)
    return pl.pallas_call(
        functools.partial(final_kernel, ranks, groups, sums, swaps),
        out_shape=[jax.ShapeDtypeStruct((ranks, sums + groups * (depth - sums), 128), own.dtype)] + swaps.shapes(),
        in_specs=[near] + swaps.specs(),
        out_specs=[near] + swaps.specs(),
        scratch_shapes=[
            pltpu.VMEM(own.shape, own.dtype),
            pltpu.VMEM((groups,) + own.shape[1:], own.dtype),
            pltpu.VMEM(own.shape[1:], own.dtype),
            pltpu.SemaphoreType.DMA((ranks,)),
            pltpu.SemaphoreType.DMA((ranks,)),
            pltpu.SemaphoreType.DMA((groups,)),
            pltpu.SemaphoreType.DMA((groups,)),
            pltpu.SemaphoreType.DMA((ranks,)),
            pltpu.SemaphoreType.DMA((ranks,)),
        ]
        + swaps.scratch(),
        name=f"final_sums_{ident}",
        compiler_params=pltpu.CompilerParams(collective_id=ident, has_side_effects=True),
    )(own, *swaps.arrays)


def first_kernel(
    ranks, quarters, own, qkv, text, total, qkv_out, text_out, held, packed, local,
    s_send, s_recv, t_send, t_recv, a_send, a_recv, y_send, y_recv, c_send, c_recv,
):
    place, group = lax.axis_index("rows"), lax.axis_index("items")
    others = [lax.rem(place + step, ranks) for step in range(1, ranks)]
    far = lax.rem(group + 2, 4)
    twin = group + 1 - 2 * lax.rem(group, 2)
    depth = qkv.shape[0] // quarters
    mine = pl.ds(pl.multiple_of(group * depth, 16), depth)
    fars = pl.ds(pl.multiple_of(far * depth, 16), depth)
    features = text_out.shape[-1]
    span = qkv.shape[1] // (3 * ranks)

    def columns(other):
        return pl.ds(pl.multiple_of(other * features, features), features)

    keeps = [pltpu.make_async_copy(text.at[:, :, columns(place)], text_out.at[place], local.at[0])]
    keeps[0].start()
    greet(
        [(place >= 0, {"rows": other}) for other in others]
        + [(place >= 0, {"items": far}), (place >= 0, {"items": twin})]
    )

    def sum_push(step, other, slot):
        return remote(own, held.at[slot], s_send.at[step], s_recv.at[slot], {"rows": other})

    def text_push(step, other, slot):
        return remote(
            text.at[:, :, columns(other)], text_out.at[slot], t_send.at[step], t_recv.at[slot], {"rows": other}
        )

    def push(step, other, slot):
        return remote(
            packed.at[other, mine], qkv_out.at[slot, mine], a_send.at[step], a_recv.at[slot], {"rows": other}
        )

    def pass_far(slot):
        block = qkv_out.at[slot, mine]
        return remote(block, block, y_send.at[slot], y_recv.at[slot], {"items": far})

    def pass_twin(which, slot):
        block = qkv_out.at[slot, fars if which else mine]
        return remote(block, block, c_send.at[which, slot], c_recv.at[which, slot], {"items": twin})

    for step, other in enumerate(others):
        sum_push(step, other, place).start()
    for rank in range(ranks):
        packed[rank] = jnp.concatenate(
            [
                qkv[:, (part * ranks + rank) * span : (part * ranks + rank + 1) * span]
                for part in range(3)
            ],
            axis=1,
        )
    for step, other in enumerate(others):
        push(step, other, place).start()
    for step, other in enumerate(others):
        text_push(step, other, place).start()
    keeps.append(pltpu.make_async_copy(packed.at[place], qkv_out.at[place], local.at[1]))
    keeps[1].start()
    held[pl.ds(place, 1)] = own[...][None]
    for step, other in enumerate(others):
        sum_push(step, other, other).wait_recv()
    value = held[0]
    for rank in range(1, ranks):
        value = value + held[rank]
    total[...] = value
    for step, other in enumerate(others):
        push(step, other, other).wait_recv()
        pass_far(other).start()
        pass_twin(0, other).start()
    for other in others:
        pass_far(other).wait_recv()
        pass_twin(1, other).start()
    for step, other in enumerate(others):
        sum_push(step, other, place).wait_send()
        text_push(step, other, other).wait_recv()
        text_push(step, other, place).wait_send()
        push(step, other, place).wait_send()
        pass_far(other).wait_send()
        for which in range(2):
            pass_twin(which, other).wait_recv()
            pass_twin(which, other).wait_send()
    for copy in keeps:
        copy.wait()


def first_transfers(own, qkv, text, ident):
    ranks, quarters = lax.axis_size("rows"), lax.axis_size("items")
    depth = qkv.shape[0]
    anywhere = pl.BlockSpec(memory_space=pl.ANY)
    near = pl.BlockSpec(memory_space=pltpu.VMEM)
    outs = [
        jax.ShapeDtypeStruct(own.shape, own.dtype),
        jax.ShapeDtypeStruct((ranks, depth, qkv.shape[1] // ranks), qkv.dtype),
        jax.ShapeDtypeStruct((ranks,) + text.shape[:-1] + (text.shape[-1] // ranks,), text.dtype),
    ]
    wave = pltpu.SemaphoreType.DMA
    return pl.pallas_call(
        functools.partial(first_kernel, ranks, quarters),
        out_shape=outs,
        in_specs=[near, near, anywhere],
        out_specs=[near, anywhere, anywhere],
        scratch_shapes=[
            pltpu.VMEM((ranks,) + own.shape, own.dtype),
            pltpu.VMEM(outs[1].shape, qkv.dtype),
            wave((2,)),
        ]
        + [wave((ranks,))] * 8
        + [wave((2, ranks))] * 2,
        name=f"first_transfers_{ident}",
        compiler_params=pltpu.CompilerParams(
            collective_id=ident, has_side_effects=True, vmem_limit_bytes=24 << 20
        ),
    )(own, qkv, text)


def quarter_kernel(pieces, at, whole, packed):
    ranks, span = packed.shape[0], packed.shape[2] // pieces
    for rank in range(ranks):
        for piece in range(pieces):
            start = (piece * ranks + rank) * span
            packed[rank, :, piece * span : (piece + 1) * span] = whole[:, start : start + span]


def pack_quarter(whole, at, pieces, ranks):
    rows, width = whole.shape[0] // 4, whole.shape[1]
    out = (ranks, rows, width // ranks)
    return pl.pallas_call(
        functools.partial(quarter_kernel, pieces),
        grid_spec=pltpu.PrefetchScalarGridSpec(
            num_scalar_prefetch=1,
            grid=(1,),
            in_specs=[pl.BlockSpec((rows, width), lambda step, at: (at[0], 0))],
            out_specs=pl.BlockSpec(out, lambda step, at: (0, 0, 0)),
        ),
        out_shape=jax.ShapeDtypeStruct(out, whole.dtype),
        name="pack_quarter",
        compiler_params=local_params(),
    )(at, whole)


def pack_kernel(pieces, whole, packed):
    ranks, span = packed.shape[0], packed.shape[2] // pieces
    for rank in range(ranks):
        packed[rank] = jnp.concatenate(
            [whole[:, (piece * ranks + rank) * span : (piece * ranks + rank + 1) * span] for piece in range(pieces)],
            axis=1,
        ).astype(packed.dtype)


def pack_blocks(whole, pieces, ranks, dtype):
    near = pl.BlockSpec(memory_space=pltpu.VMEM)
    return pl.pallas_call(
        functools.partial(pack_kernel, pieces),
        out_shape=jax.ShapeDtypeStruct((ranks, whole.shape[0], whole.shape[1] // ranks), dtype),
        in_specs=[near],
        out_specs=near,
        name="pack_blocks",
        compiler_params=pltpu.CompilerParams(vmem_limit_bytes=24 << 20),
    )(whole)


def unpack_kernel(pieces, packed, whole):
    ranks, span = packed.shape[0], packed.shape[2] // pieces
    for piece in range(pieces):
        for rank in range(0, ranks, 2):
            start = (piece * ranks + rank) * span
            whole[:, start : start + 2 * span] = jnp.concatenate(
                [packed[rank + k, :, piece * span : (piece + 1) * span] for k in range(2)], axis=1
            ).astype(whole.dtype)


def unpack_blocks(packed, pieces, dtype):
    near = pl.BlockSpec(memory_space=pltpu.VMEM)
    ranks, rows, width = packed.shape
    return pl.pallas_call(
        functools.partial(unpack_kernel, pieces),
        out_shape=jax.ShapeDtypeStruct((rows, ranks * width), dtype),
        in_specs=[near],
        out_specs=near,
        name="unpack_blocks",
        compiler_params=pltpu.CompilerParams(vmem_limit_bytes=24 << 20),
    )(packed)


def halves_kernel(pieces, own, other, whole):
    ranks, half, span = own.shape[0], own.shape[1], own.shape[2] // pieces
    first = lax.rem(lax.axis_index("items"), 2) == 0
    for low in range(2):

        @pl.when(first == (low == 0))
        def _(low=low):
            for source, start in ((own, low * half), (other, (1 - low) * half)):
                for piece in range(pieces):
                    for rank in range(0, ranks, 2):
                        column = (piece * ranks + rank) * span
                        whole[start : start + half, column : column + 2 * span] = jnp.concatenate(
                            [source[rank + k, :, piece * span : (piece + 1) * span] for k in range(2)], axis=1
                        ).astype(whole.dtype)


def unpack_halves(own, other, pieces):
    near = pl.BlockSpec(memory_space=pltpu.VMEM)
    ranks, half, width = own.shape
    return pl.pallas_call(
        functools.partial(halves_kernel, pieces),
        out_shape=jax.ShapeDtypeStruct((2 * half, ranks * width), jnp.float32),
        in_specs=[near, near],
        out_specs=near,
        name="unpack_halves",
        compiler_params=pltpu.CompilerParams(vmem_limit_bytes=32 << 20),
    )(own, other)


def gather_tokens(block, ident, swaps=()):
    whole = gather_rows(block, ident, 1, swaps=swaps)
    if not swaps:
        return whole.reshape(-1, block.shape[-1])
    return (whole[0].reshape(-1, block.shape[-1]), *whole[1:])


def scatter_tokens(partial, items, ident, swaps=()):
    ranks = lax.axis_size("rows")
    blocks = partial.astype(jnp.bfloat16).reshape(items, ranks, -1, partial.shape[-1])
    return scatter_rows(blocks, ident, 1, swaps=swaps)


NEAR = pl.BlockSpec(memory_space=pltpu.VMEM)
SCALARS = pl.BlockSpec(memory_space=pltpu.SMEM)
NT = (((1,), (1,)), ((), ()))
TN = (((0,), (0,)), ((), ()))


def local_params():
    return pltpu.CompilerParams(vmem_limit_bytes=48 << 20)


def text_item(text, item):
    block = text[:, item]
    return block.reshape(block.shape[0] * block.shape[1], block.shape[2])


def lanes_to_rows(columns, rows):
    lane = lax.broadcasted_iota(jnp.int32, (128, 128), 1)
    held = jnp.zeros((128, 128), jnp.float32)
    for place, column in enumerate(columns):
        held = jnp.where(lane == place, column, held)
    return jnp.transpose(held)[:rows]


def rows_to_lanes(rows):
    missing = jnp.zeros((128 - rows.shape[0], 128), jnp.float32)
    return jnp.transpose(jnp.concatenate([rows, missing], axis=0))


def project_kernel(attn, weight, text, proj, squares):
    span = text.shape[-1] // 2
    tokens = attn.shape[0]
    for start in range(0, tokens, 256):
        proj[start : start + 256] = jnp.dot(
            attn[start : start + 256], weight[...], preferred_element_type=jnp.float32
        )
    columns = []
    for part in range(2):
        for start in range(0, tokens, 128):
            block = proj[start : start + 128, part * span : (part + 1) * span]
            columns.append(jnp.sum(block * block, axis=1, keepdims=True))
    for item in range(text.shape[1]):
        block = text_item(text, item)[:, :span]
        columns.append(jnp.sum(block * block, axis=1, keepdims=True))
    squares[...] = lanes_to_rows(columns, squares.shape[0])


def project(attn, weight, text):
    count = 2 * attn.shape[0] // 128 + text.shape[1]
    return pl.pallas_call(
        project_kernel,
        out_shape=[
            jax.ShapeDtypeStruct((attn.shape[0], weight.shape[1]), jnp.float32),
            jax.ShapeDtypeStruct((-(-count // 8) * 8, 128), jnp.float32),
        ],
        in_specs=[NEAR] * 3,
        out_specs=[NEAR] * 2,
        name="project",
        compiler_params=local_params(),
    )(attn, weight, text)


def tile_lane():
    return lax.broadcasted_iota(jnp.int32, (1, 128), 1)


def swap_halves(tile):
    low = lax.rem(tile_lane(), 64) < 32
    return jnp.where(low, pltpu.roll(tile, 96, 1), pltpu.roll(tile, 32, 1))


def block_tables(tab, block, frame_lanes):
    by_row = lax.rem(tile_lane(), 32) < frame_lanes
    rows = 128 // COLS
    cosines, sines = [], []
    for row in range(rows):
        at = pl.ds(block * rows + row, 1)
        cosines.append(jnp.where(by_row, tab[0, at], tab[2, :COLS]))
        sines.append(jnp.where(by_row, tab[1, at], tab[3, :COLS]))
    return jnp.concatenate(cosines, axis=0), jnp.concatenate(sines, axis=0)


def block_inverse(inverse, block, blocks):
    lane = lax.broadcasted_iota(jnp.int32, (128, 128), 1)

    def column(place):
        return jnp.sum(jnp.where(lane == place, inverse, 0.0), axis=1, keepdims=True)

    query, key = column(block), column(blocks + block)
    return [query, jnp.where(tile_lane() < 64, query, key), key]


def attend_kernel(
    scale, width, counts, heights, text_lens, proj, totals, text, gains, text_gain, gate, w_out,
    parts, qkv, text_kv, tab, biases, text_biases,
):
    ranks, items = text.shape[0], text.shape[1]
    span = gate.shape[-1]
    heads, size = span // 64, 64
    tokens = proj.shape[0]
    blocks, item_blocks = tokens // 128, tokens // 128 // items
    seq = tokens // items
    slots = seq // ranks
    row_slots = slots // COLS
    frame_pairs = size // 8
    space_pairs = (size // 2 - frame_pairs) // 2

    place = lax.rem(tile_lane(), 32)
    frame_rate = jnp.exp(place.astype(jnp.float32) * (-math.log(10000.0) / frame_pairs))
    row_rate = jnp.exp((place - frame_pairs).astype(jnp.float32) * (-math.log(10000.0) / space_pairs))
    column_rate = jnp.exp(
        (place - frame_pairs - space_pairs).astype(jnp.float32) * (-math.log(10000.0) / space_pairs)
    )
    is_frame = place < frame_pairs
    rows = items * ranks * row_slots
    which = lax.broadcasted_iota(jnp.int32, (rows, 1), 0)
    frame_index = jnp.zeros((rows, 1), jnp.float32)
    frame_row = jnp.zeros((rows, 1), jnp.float32)
    seq_place = lax.broadcasted_iota(jnp.int32, (seq, 128), 0)
    for item in range(items):
        below = jnp.int32(0)
        bias = jnp.zeros((seq, 128), jnp.float32)
        for rank in range(ranks):
            live = counts[rank * items + item]
            for row in range(row_slots):
                index = below + row
                at = which == (item * ranks + rank) * row_slots + row
                frame_index = jnp.where(at, (index // heights[item]).astype(jnp.float32), frame_index)
                frame_row = jnp.where(at, lax.rem(index, heights[item]).astype(jnp.float32), frame_row)
            start = rank * slots
            inside = (seq_place >= start + live * COLS) & (seq_place < start + slots)
            bias = jnp.where(inside, masked_score, bias)
            below = below + live
        biases[item] = bias
        text_place = lax.broadcasted_iota(jnp.int32, text_biases.shape[1:], 0)
        text_biases[item] = jnp.where(text_place >= text_lens[item], masked_score, 0.0)
    column = lax.broadcasted_iota(jnp.int32, (COLS, 1), 0).astype(jnp.float32)
    row_angles = jnp.where(is_frame, frame_index * frame_rate, frame_row * row_rate)
    column_angles = column * column_rate
    sign = jnp.where(lax.rem(tile_lane(), 64) < 32, -1.0, 1.0)
    tab[0, :rows] = jnp.cos(row_angles)
    tab[1, :rows] = jnp.sin(row_angles) * sign
    tab[2, :COLS] = jnp.cos(column_angles)
    tab[3, :COLS] = jnp.sin(column_angles) * sign

    inverse = rows_to_lanes(lax.rsqrt(totals[...] / width + epsilon))
    for item in range(items):
        block = text_item(text, item)
        column = inverse[:, 2 * blocks + item : 2 * blocks + item + 1]
        text_kv[item] = jnp.concatenate(
            [block[:, :span] * column * text_gain[...], block[:, span:]], axis=1
        ).astype(text_kv.dtype)

    @pl.loop(0, blocks)
    def _(block):
        at = pl.ds(pl.multiple_of(block * 128, 128), 128)
        cosine, sine = block_tables(tab, block, frame_pairs + space_pairs)
        inverses = block_inverse(inverse, block, blocks)
        tiles = []
        for tile in range(3):
            lanes = slice(tile * 128, (tile + 1) * 128)
            value = proj[at, lanes] * inverses[tile] * gains[:, lanes]
            tiles.append(value * cosine + swap_halves(value) * sine)
        qkv[at] = jnp.concatenate(tiles + [proj[at, 2 * span :]], axis=1).astype(qkv.dtype)

    @pl.loop(0, blocks)
    def _(block):
        at = pl.ds(pl.multiple_of(block * 128, 128), 128)
        item = block // item_blocks
        keys_at = pl.ds(pl.multiple_of(item * seq, seq), seq)
        bias, text_bias = biases[item], text_biases[item]
        mixed = []
        for head in range(heads):
            lanes = slice(head * size, (head + 1) * size)

            def part_of(ref, rows, part):
                start = part * span + head * size
                return ref[rows, start : start + size]

            query = part_of(qkv, at, 0)

            def mix(keys, values, mask):
                scores = lax.dot_general(keys, query, NT, preferred_element_type=jnp.float32)
                scores = scores * scale + mask
                terms = jnp.exp(scores - jnp.max(scores, axis=0, keepdims=True))
                probs = terms * (1.0 / jnp.sum(terms, axis=0, keepdims=True))
                return lax.dot_general(
                    values,
                    probs.astype(jnp.bfloat16),
                    (((0,), (0,)), ((), ())),
                    preferred_element_type=jnp.float32,
                )

            out = mix(part_of(qkv, keys_at, 1), part_of(qkv, keys_at, 2), bias)
            text_keys = text_kv[item]
            cross = mix(
                text_keys[:, lanes], text_keys[:, span + head * size : span + (head + 1) * size], text_bias
            )
            mixed.append(jnp.transpose(out) + gate[:, lanes] * jnp.transpose(cross))
        combined = jnp.concatenate(mixed, axis=1).astype(jnp.bfloat16)
        parts[1][at] = combined
        parts[0][at] = jnp.dot(combined, w_out[...], preferred_element_type=jnp.float32).astype(jnp.bfloat16)


def attend(proj, totals, text, gains, text_gain, gate, w_out, counts, heights, text_lens, head_size):
    tokens, span, width = proj.shape[0], gate.shape[-1], w_out.shape[1]
    items, text_rows = text.shape[1], text.shape[0] * text.shape[2]
    low = jnp.bfloat16

    def body(*refs):
        ins, outs, scratch = refs[:10], refs[10:15], refs[15:]
        attend_kernel(
            head_size**-0.5, width, *ins, (outs[0], outs[1]), outs[2], outs[3], outs[4], *scratch
        )

    return pl.pallas_call(
        body,
        out_shape=[
            jax.ShapeDtypeStruct((tokens, width), low),
            jax.ShapeDtypeStruct((tokens, span), low),
            jax.ShapeDtypeStruct((tokens, 3 * span), low),
            jax.ShapeDtypeStruct((items, text_rows, 2 * span), low),
            jax.ShapeDtypeStruct((4, max(tokens // COLS, COLS), 128), jnp.float32),
        ],
        in_specs=[SCALARS] * 3 + [NEAR] * 7,
        out_specs=[NEAR] * 5,
        scratch_shapes=[
            pltpu.VMEM((items, tokens // items, 128), jnp.float32),
            pltpu.VMEM((items, text_rows, 128), jnp.float32),
        ],
        name="attend",
        compiler_params=local_params(),
    )(counts, heights, text_lens, proj, totals, text, gains, text_gain, gate, w_out)


def attend_back_kernel(
    scale, width, counts, text_lens, grad, w_out, qkv, text_kv, tab, proj, totals, text, gains, text_gain, gate,
    scaled, grad_value, text_scaled, text_value, sums, gain_sums, gate_sums,
    grad_query, key_sum, value_sum, text_key_sum, text_value_sum, biases, text_biases,
):
    ranks, items = text.shape[0], text.shape[1]
    span = gate.shape[-1]
    heads, size = span // 64, 64
    tokens = proj.shape[0]
    blocks, item_blocks = tokens // 128, tokens // 128 // items
    seq = tokens // items
    slots = seq // ranks
    frame_pairs = size // 8
    space_pairs = (size // 2 - frame_pairs) // 2
    seq_place = lax.broadcasted_iota(jnp.int32, (seq, 128), 0)
    for item in range(items):
        bias = jnp.zeros((seq, 128), jnp.float32)
        for rank in range(ranks):
            start = rank * slots
            live = counts[rank * items + item]
            inside = (seq_place >= start + live * COLS) & (seq_place < start + slots)
            bias = jnp.where(inside, masked_score, bias)
        biases[item] = bias
        text_place = lax.broadcasted_iota(jnp.int32, text_biases.shape[1:], 0)
        text_biases[item] = jnp.where(text_place >= text_lens[item], masked_score, 0.0)
    key_sum[...] = jnp.zeros_like(key_sum)
    value_sum[...] = jnp.zeros_like(value_sum)
    text_key_sum[...] = jnp.zeros_like(text_key_sum)
    text_value_sum[...] = jnp.zeros_like(text_value_sum)
    gate_sums[...] = jnp.zeros_like(gate_sums)
    gain_sums[...] = jnp.zeros_like(gain_sums)

    @pl.loop(0, blocks)
    def _(block):
        at = pl.ds(pl.multiple_of(block * 128, 128), 128)
        item = block // item_blocks
        keys_at = pl.ds(pl.multiple_of(item * seq, seq), seq)
        bias, text_bias = biases[item], text_biases[item]
        text_keys = text_kv[item]
        grad_combined = lax.dot_general(grad[at], w_out[...], NT, preferred_element_type=jnp.float32)
        self_low = grad_combined.astype(jnp.bfloat16)
        cross_low = (gate[...] * grad_combined).astype(jnp.bfloat16)
        queries, crossed = [], []
        for head in range(heads):
            lanes = slice(head * size, (head + 1) * size)
            query = qkv[at, lanes]

            def back(keys, values, low_grad, mask, key_total, value_total, rows):
                scores = lax.dot_general(keys, query, NT, preferred_element_type=jnp.float32)
                scores = scores * scale + mask
                terms = jnp.exp(scores - jnp.max(scores, axis=0, keepdims=True))
                probs = terms * (1.0 / jnp.sum(terms, axis=0, keepdims=True))
                grad_probs = lax.dot_general(values, low_grad, NT, preferred_element_type=jnp.float32)
                inner = jnp.sum(probs * grad_probs, axis=0, keepdims=True)
                score_low = (probs * (grad_probs - inner)).astype(jnp.bfloat16)
                probs_low = probs.astype(jnp.bfloat16)
                key_total[head, rows] += jnp.dot(score_low, query, preferred_element_type=jnp.float32)
                value_total[head, rows] += jnp.dot(probs_low, low_grad, preferred_element_type=jnp.float32)
                to_query = lax.dot_general(
                    keys, score_low, (((0,), (0,)), ((), ())), preferred_element_type=jnp.float32
                )
                return to_query, probs_low

            to_query, _ = back(
                qkv[keys_at, span + head * size : span + (head + 1) * size],
                qkv[keys_at, 2 * span + head * size : 2 * span + (head + 1) * size],
                self_low[:, lanes],
                bias,
                key_sum,
                value_sum,
                keys_at,
            )
            text_values = text_keys[:, span + head * size : span + (head + 1) * size]
            text_rows = pl.ds(pl.multiple_of(item * 128, 128), 128)
            cross_query, cross_probs = back(
                text_keys[:, lanes],
                text_values,
                cross_low[:, lanes],
                text_bias,
                text_key_sum,
                text_value_sum,
                text_rows,
            )
            crossed.append(
                jnp.transpose(
                    lax.dot_general(
                        text_values, cross_probs, (((0,), (0,)), ((), ())), preferred_element_type=jnp.float32
                    )
                )
            )
            queries.append(jnp.transpose(to_query + cross_query))
        grad_query[at] = jnp.concatenate(queries, axis=1) * scale
        gate_sums[...] += jnp.sum(
            grad_combined * jnp.concatenate(crossed, axis=1), axis=0, keepdims=True
        )

    inverse = rows_to_lanes(lax.rsqrt(totals[...] / width + epsilon))
    columns = [[], []]
    for block in range(blocks):
        at = slice(block * 128, (block + 1) * 128)
        cosine, sine = block_tables(tab, block, frame_pairs + space_pairs)
        inverses = block_inverse(inverse, block, blocks)
        keys = jnp.concatenate([key_sum[head, at] for head in range(heads)], axis=1) * scale
        both = jnp.concatenate([grad_query[at], keys], axis=1)
        products = []
        for tile in range(3):
            lanes = slice(tile * 128, (tile + 1) * 128)
            value = both[:, lanes]
            value = value * cosine - swap_halves(value) * sine
            unit = proj[at, lanes] * inverses[tile]
            gain_sums[0:1, lanes] += jnp.sum(value * unit, axis=0, keepdims=True)
            value = value * gains[:, lanes]
            scaled[at, lanes] = value
            products.append(value * unit)
        first = tile_lane() < 64
        query_part = products[0] + jnp.where(first, products[1], 0.0)
        key_part = products[2] + jnp.where(first, 0.0, products[1])
        columns[0].append(jnp.sum(query_part, axis=1, keepdims=True))
        columns[1].append(jnp.sum(key_part, axis=1, keepdims=True))
        grad_value[at] = jnp.concatenate([value_sum[head, at] for head in range(heads)], axis=1).astype(
            grad_value.dtype
        )
    for item in range(items):
        at = slice(item * 128, (item + 1) * 128)
        unit = text_item(text, item)[:, :span] * inverse[:, 2 * blocks + item : 2 * blocks + item + 1]
        value = jnp.concatenate([text_key_sum[head, at] for head in range(heads)], axis=1) * scale
        gain_sums[1:2, :span] += jnp.sum(value * unit, axis=0, keepdims=True)
        value = value * text_gain[...]
        text_scaled[at] = value
        text_value[at] = jnp.concatenate([text_value_sum[head, at] for head in range(heads)], axis=1).astype(
            text_value.dtype
        )
        columns[1].append(jnp.sum(value * unit, axis=1, keepdims=True))
    sums[...] = lanes_to_rows(columns[0] + columns[1], sums.shape[0])


def attend_back(
    grad, w_out, qkv, text_kv, tab, proj, totals, text, gains, text_gain, gate, counts, text_lens, head_size, after
):
    tokens, span, width = proj.shape[0], gate.shape[-1], w_out.shape[1]
    items, text_rows = text.shape[1], text.shape[0] * text.shape[2]
    heads = span // head_size
    low, single = jnp.bfloat16, jnp.float32

    def body(*refs):
        attend_back_kernel(head_size**-0.5, width, *refs[:13], *refs[13 + len(after) :])

    return pl.pallas_call(
        body,
        out_shape=[
            jax.ShapeDtypeStruct((tokens, 2 * span), single),
            jax.ShapeDtypeStruct((tokens, span), low),
            jax.ShapeDtypeStruct((items * text_rows, span), single),
            jax.ShapeDtypeStruct((items * text_rows, span), low),
            jax.ShapeDtypeStruct(totals.shape, single),
            jax.ShapeDtypeStruct((8, 2 * span), single),
            jax.ShapeDtypeStruct((1, span), single),
        ],
        in_specs=[SCALARS] * 2 + [NEAR] * 11 + [pl.BlockSpec(memory_space=pl.ANY)] * len(after),
        out_specs=[NEAR] * 7,
        scratch_shapes=[
            pltpu.VMEM((tokens, span), single),
            pltpu.VMEM((heads, tokens, head_size), single),
            pltpu.VMEM((heads, tokens, head_size), single),
            pltpu.VMEM((heads, items * text_rows, head_size), single),
            pltpu.VMEM((heads, items * text_rows, head_size), single),
            pltpu.VMEM((items, tokens // items, 128), single),
            pltpu.VMEM((items, text_rows, 128), single),
        ],
        name="attend_back",
        compiler_params=local_params(),
    )(counts, text_lens, grad, w_out, qkv, text_kv, tab, proj, totals, text, gains, text_gain, gate, *after)


def norms_back_kernel(width, proj, totals, sums, scaled, grad_value, text, text_scaled, text_value, qkv_low, text_low):
    items, span = text.shape[1], grad_value.shape[-1]
    tokens = proj.shape[0]
    blocks = tokens // 128
    inverse = rows_to_lanes(lax.rsqrt(totals[...] / width + epsilon))
    means = rows_to_lanes(sums[...] / width)
    first = tile_lane() < 64
    for block in range(blocks):
        at = slice(block * 128, (block + 1) * 128)

        def by_tile(columns):
            query = columns[:, block : block + 1]
            key = columns[:, blocks + block : blocks + block + 1]
            return [query, jnp.where(first, query, key), key]

        inverses, mean = by_tile(inverse), by_tile(means)
        tiles = []
        for tile in range(3):
            lanes = slice(tile * 128, (tile + 1) * 128)
            unit = proj[at, lanes] * inverses[tile]
            tiles.append((inverses[tile] * (scaled[at, lanes] - unit * mean[tile])).astype(qkv_low.dtype))
        qkv_low[at] = jnp.concatenate(tiles + [grad_value[at]], axis=1)
    for item in range(items):
        at = slice(item * 128, (item + 1) * 128)
        place = 2 * blocks + item
        column, mean = inverse[:, place : place + 1], means[:, place : place + 1]
        unit = text_item(text, item)[:, :span] * column
        low = (column * (text_scaled[at] - unit * mean)).astype(text_low.dtype)
        low = jnp.concatenate([low, text_value[at]], axis=1)
        text_low[:, item] = low.reshape(text_low.shape[0], text_low.shape[2], 2 * span)


def norms_back(proj, totals, sums, scaled, grad_value, text, text_scaled, text_value, width):
    low = jnp.bfloat16
    return pl.pallas_call(
        functools.partial(norms_back_kernel, width),
        out_shape=[
            jax.ShapeDtypeStruct(proj.shape, low),
            jax.ShapeDtypeStruct(text.shape, low),
        ],
        in_specs=[NEAR] * 8,
        out_specs=[NEAR] * 2,
        name="norms_back",
        compiler_params=local_params(),
    )(proj, totals, sums, scaled, grad_value, text, text_scaled, text_value)


SUM_DEPTH = 16


def finish_kernel(
    grad, states, grad_middle, modulation, gains, vectors, gain_sums, gate_sums, text_gain, time, grad_x, small
):
    items, _, width = states.shape
    ranks = small.shape[0]
    place = lax.axis_index("rows")
    scales, zero = [], jnp.zeros((1, width), jnp.float32)
    for item in range(items):
        unit, inverse = norm_unit(states[item])
        value = grad[item]
        scales.append(jnp.sum(value * (unit * gains[0:1]), axis=0, keepdims=True))
        value = value * (1.0 + modulation[item : item + 1, :width])
        zero = zero + jnp.sum(value * unit, axis=0, keepdims=True)
        value = value * gains[0:1]
        value = inverse * (value - unit * jnp.mean(value * unit, axis=-1, keepdims=True))
        grad_x[item] = grad_middle[item] + value

    def spread(part):
        size = part.shape[1]
        owner = lax.broadcasted_iota(jnp.int32, (1, ranks * size), 1) // size
        return jnp.where(owner == place, jnp.concatenate([part] * ranks, axis=1), 0.0)

    span = gate_sums.shape[1]
    rows = [
        zero,
        spread(gain_sums[0:1, :span]),
        spread(gain_sums[0:1, span:]),
        vectors[8:9],
        vectors[7:8],
        vectors[6:7],
        spread(gain_sums[1:2, :span]),
        spread(text_gain[...]),
        spread(gate_sums[...]),
    ]
    number = 0
    for row in rows:
        for start in range(0, row.shape[1], 128):
            rank, depth = divmod(number, SUM_DEPTH)
            small[rank, depth : depth + 1] = row[:, start : start + 128]
            number += 1
    for item in range(items):
        kinds = (scales[item], vectors[4 + item : 5 + item], vectors[2 + item : 3 + item], vectors[item : item + 1])
        for which, row in enumerate(kinds):
            for at in range(width // 128):
                depth = SUM_DEPTH + at
                small[item * 4 + which, depth : depth + 1] = row[:, at * 128 : (at + 1) * 128]
    for rank in range(ranks):
        small[rank, SUM_DEPTH + width // 128 :] = jnp.where(rank == place, time[...], 0.0)


def finish(grad, states, grad_middle, modulation, gains, vectors, gain_sums, gate_sums, text_gain, time):
    ranks, width = lax.axis_size("rows"), states.shape[-1]
    depth = SUM_DEPTH + width // 128 + time.shape[0]
    return pl.pallas_call(
        finish_kernel,
        out_shape=[
            jax.ShapeDtypeStruct(states.shape, jnp.float32),
            jax.ShapeDtypeStruct((ranks, depth, 128), jnp.float32),
        ],
        in_specs=[NEAR] * 10,
        out_specs=[NEAR] * 2,
        name="finish",
        compiler_params=local_params(),
    )(grad, states, grad_middle, modulation, gains, vectors, gain_sums, gate_sums, text_gain, time)


def join_kernel(bit, own, other, out):
    mine = pl.program_id(0) == bit()

    @pl.when(mine)
    def _():
        out[0] = own[...].astype(out.dtype)

    @pl.when(jnp.logical_not(mine))
    def _():
        out[0] = other[...].astype(out.dtype)


def join_rows(own, other, bit, dtype):
    rows, width = own.shape
    step = min(rows, 128)
    near = pl.BlockSpec((step, width), lambda half, at: (at, 0))
    return pl.pallas_call(
        functools.partial(join_kernel, bit),
        grid=(2, rows // step),
        out_shape=jax.ShapeDtypeStruct((2, rows, width), dtype),
        in_specs=[near, near],
        out_specs=pl.BlockSpec((1, step, width), lambda half, at: (half, at, 0)),
        name="join_rows",
        compiler_params=local_params(),
    )(own, other)


def core_bit():
    return lax.rem(lax.axis_index("items"), 2)


def far_bit():
    return lax.axis_index("items") // 2


def join_blocks(own, other, bit):
    ranks, rows, width = own.shape
    block = pl.BlockSpec((1, rows, width), lambda rank: (rank, 0, 0))

    def kernel(one, two, out):
        mine = bit()
        for half in range(2):

            @pl.when(mine == half)
            def _(half=half):
                out[0, half * rows : (half + 1) * rows] = one[0]
                out[0, (1 - half) * rows : (2 - half) * rows] = two[0]

    return pl.pallas_call(
        kernel,
        grid=(ranks,),
        out_shape=jax.ShapeDtypeStruct((ranks, 2 * rows, width), own.dtype),
        in_specs=[block, block],
        out_specs=pl.BlockSpec((1, 2 * rows, width), lambda rank: (rank, 0, 0)),
        name="join_blocks",
        compiler_params=local_params(),
    )(own, other)


ORDER = (
    "gs", "wf", "sf", "wn", "sn", "t", "b0", "g1", "b1", "b2", "a0", "g2",
    "a1", "h", "g3", "a2", "ge", "se",
)
LAST_ORDER = (
    "gs", "wf", "sf", "wn", "sn", "t", "d0", "b0", "d1", "g1", "b1", "b2",
    "u0", "a0", "u1", "g2", "a1", "u2", "h", "g3", "u3", "c", "a2", "ge",
    "se",
)
END_ORDER = (
    "gs", "t", "g1", "y", "g2", "g3", "ge",
)


def split_chain(width):
    return width - 128 * round(width / 384)


class Chain:
    def __init__(self, place, width, flow, scatter_waves, gather_waves):
        self.line, self.side = place
        line = self.line
        self.across = on_rows(line, 1 - self.side)
        self.ways = (on_rows(line + 1, self.side), on_rows(line - 1, self.side))
        self.more = (line < DEPTH - 1, line > 0)
        low = line < 2
        self.pair = jnp.where(low, 1, 0)
        self.order = (jnp.where(low, 3, 0), jnp.where(low, 2, 1), line + 1 - 2 * lax.rem(line, 2))
        even = lax.rem(line, 2) == 0
        self.upward = (low, low, even)
        first = split_chain(width)
        self.pieces = ((0, 0, first), (0, first, width - first), (1, first, width - first))
        self.crossed, self.flow = flow[0], flow[1:]
        self.x_send, self.x_recv, self.z_send, self.z_recv = scatter_waves
        self.gx_send, self.gx_recv, self.gz_send, self.gz_recv = gather_waves

    def shard(self, ref, at, stream, turned=False):
        which, start, size = self.pieces[stream]
        other = which or turned
        return ref.at[at * BREADTH + (1 - self.side if other else self.side), :, pl.ds(start, size)]


    def cross(self, parts, at):
        return remote(
            self.shard(parts, at, 0, True), self.crossed.at[at], self.x_send.at[at], self.x_recv.at[at], self.across
        )

    def hand(self):
        leave, arrive = self.flow[12], self.flow[13]
        return remote(leave, arrive, self.x_send.at[DEPTH], self.x_recv.at[DEPTH], self.across)

    def moving(self, stream, at, way):
        return remote(
            self.flow[4 * stream + 2 * way + 1].at[at],
            self.flow[4 * stream + 2 * way].at[at],
            self.z_send.at[stream, way, at],
            self.z_recv.at[stream, way, at],
            self.ways[way],
        )

    def add_up(self, parts, stream, at, ways, target, others=()):
        value = self.shard(parts, at, stream)[...].astype(jnp.float32)
        if stream == 0:
            value = value + self.crossed[at].astype(jnp.float32)
        for way in ways:
            value = value + self.flow[4 * stream + 2 * way][at].astype(jnp.float32)
        for other in others:
            value = value + other[...].astype(jnp.float32)
        target[...] = value.astype(target.dtype)

    def send_on(self, parts, stream, number):
        at = self.order[number]
        for way in range(2):
            going = self.upward[number] if way == 0 else jnp.logical_not(self.upward[number])
            comes = self.more[1 - way]
            leaving = self.flow[4 * stream + 2 * way + 1].at[at]

            @pl.when(going & comes)
            def _(way=way, leaving=leaving):
                self.moving(stream, at, way).wait_recv()
                self.add_up(parts, stream, at, [way], leaving)

            @pl.when(going & jnp.logical_not(comes))
            def _(leaving=leaving):
                self.add_up(parts, stream, at, [], leaving)

            @pl.when(going)
            def _(way=way):
                self.moving(stream, at, way).start()

    def finish(self, parts, stream, target, others=()):
        for above_there, below_there, ways in ((True, True, [0, 1]), (False, True, [0]), (True, False, [1])):

            @pl.when((self.more[0] == above_there) & (self.more[1] == below_there))
            def _(ways=ways):
                for way in ways:
                    self.moving(stream, self.line, way).wait_recv()
                self.add_up(parts, stream, self.line, ways, target, others)

    def scatter_start(self, parts, near):
        for at in (self.order[2], self.line) if near else self.order[:2]:
            self.cross(parts, at).start()

    def scatter_over(self, parts, number):
        for stream in (1, 2):
            self.send_on(parts, stream, number)

    def scatter_along(self, parts, number):
        self.cross(parts, self.order[number]).wait_recv()
        self.send_on(parts, 0, number)

    def scatter_hand(self, parts):
        self.finish(parts, 2, self.flow[12])
        self.hand().start()

    def scatter_end(self, parts, total):
        first = self.pieces[0][2]
        self.cross(parts, self.line).wait_recv()
        self.finish(parts, 0, total.at[:, pl.ds(0, first)])
        self.hand().wait_recv()
        self.finish(parts, 1, total.at[:, pl.ds(*self.pieces[1][1:])], (self.flow[13],))
        self.hand().wait_send()
        for at in range(DEPTH):
            self.cross(parts, at).wait_send()
        for number in range(3):
            for way in range(2):
                going = self.upward[number] if way == 0 else jnp.logical_not(self.upward[number])

                @pl.when(going)
                def _(number=number, way=way):
                    for stream in range(3):
                        self.moving(stream, self.order[number], way).wait_send()


    def mine(self, own, stream):
        return own.at[:, pl.ds(*self.pieces[stream][1:])]

    def pass_on(self, whole, stream, source, at, way):
        return remote(
            source,
            self.shard(whole, at, stream),
            self.gz_send.at[stream, way, at],
            self.gz_recv.at[stream, at],
            self.ways[way],
        )

    def give(self, whole, stream, source, at):
        slot = DEPTH if stream else at
        return remote(source, self.shard(whole, at, stream), self.gx_send.at[slot], self.gx_recv.at[slot], self.across)

    def onward(self, whole, stream, source):
        for way in range(2):

            @pl.when(self.more[way])
            def _(way=way):
                self.pass_on(whole, stream, source, self.line, way).start()

    def gather_start(self, own, whole):
        self.give(whole, 1, self.mine(own, 1), self.line).start()
        self.give(whole, 0, self.mine(own, 0), self.line).start()
        for stream in range(2):
            self.onward(whole, stream, self.mine(own, stream))
        whole[self.line * BREADTH + self.side] = own[...]

    def gather_turn(self, own, whole):
        self.give(whole, 1, self.mine(own, 1), self.line).wait_recv()
        self.onward(whole, 2, self.shard(whole, self.line, 2))

    def gather_step(self, whole, step):
        line = self.line
        for way, at, there in ((0, line - step, line - step >= 0), (1, line + step, line + step < DEPTH)):

            @pl.when(there)
            def _(way=way, at=at):
                for stream in range(3):
                    block = self.shard(whole, at, stream)
                    self.pass_on(whole, stream, block, at, way).wait_recv()
                    if stream == 0:
                        self.give(whole, 0, block, at).start()

                    @pl.when(self.more[way])
                    def _(stream=stream, block=block):
                        self.pass_on(whole, stream, block, at, way).start()

    def gather_end(self, own, whole):
        for at in range(DEPTH):
            self.give(whole, 0, self.mine(own, 0), at).wait_recv()
            self.give(whole, 0, self.mine(own, 0), at).wait_send()
            for stream in range(3):
                for way, holds in ((0, at <= self.line), (1, at >= self.line)):

                    @pl.when(self.more[way] & holds)
                    def _(at=at, stream=stream, way=way):
                        self.pass_on(whole, stream, self.shard(whole, at, stream), at, way).wait_send()

        self.give(whole, 1, self.mine(own, 1), self.line).wait_send()


def norm_unit(values):
    inverse = lax.rsqrt(jnp.mean(values * values, axis=-1, keepdims=True) + epsilon)
    return values * inverse, inverse


def feed_forward_kernel(
    parts, states, cotangent, live, modulation, gains, gu_part, w_down,
    output, grad_middle, ffn_in, inner_act, ffn_low, gate_up_low, projected_low, vectors, sum_gu, half_down,
    gate_up, projected, middle, result, own, partial, w_gu, grad_gu, grad_down, got_gu, got_down, half_gu,
    far_gu, swap_send, swap_recv, *rest,
):
    items = states.shape[0]
    width, hidden = states.shape[2], w_down.shape[0]
    rows = states.shape[1]
    half = 4 * rows
    flows, waves = rest[: 15 * items], rest[15 * items :]
    place = row_place()
    line = place[0]
    chains = [
        Chain(place, width, flows[15 * item : 15 * item + 15], waves[8 * item : 8 * item + 4], waves[8 * item + 4 : 8 * item + 8])
        for item in range(items)
    ]
    one = chains[0]
    core, far = core_bit(), far_bit()
    twin, across_y = partner("core"), partner("far")
    greet(
        [(one.more[0], one.ways[0]), (one.more[1], one.ways[1]), (line >= 0, one.across)]
        + [(line >= 0, twin), (line >= 0, across_y)]
    )

    def quarter_on(number):
        which = 2 * core + (far if number < 2 else 1 - far)
        block = w_gu.at[:, which]
        return remote(block, block, swap_send.at[number], swap_recv.at[number], across_y if number == 0 else twin)

    w_gu[:, 2 * core + far] = gu_part[...]
    quarter_on(0).start()
    quarter_on(1).start()
    vectors[...] = jnp.zeros_like(vectors)

    def scale_of(item, which):
        return modulation[item : item + 1, which * width : (which + 1) * width]

    def over_rows(values):
        return jnp.sum(values, axis=0, keepdims=True)

    def middle_of(item):
        projected[item] = result[item]
        unit, _ = norm_unit(projected[item])
        middle[item] = states[item] + jnp.tanh(scale_of(item, 1)) * (unit * gains[3:4])
        unit, _ = norm_unit(middle[item])
        own[item] = (unit * gains[4:5] * (1.0 + scale_of(item, 2))).astype(own.dtype)

    def outcome(item):
        mask = live[item][:, 0:1]
        gate = jnp.tanh(scale_of(item, 3))
        unit, inverse = norm_unit(result[item])
        normed = unit * gains[5:6]
        output[item] = mask * (middle[item] + gate * normed)
        grad = mask * cotangent[item]
        vectors[item : item + 1] = (1.0 - gate * gate) * over_rows(grad * normed)
        grad = gate * grad
        vectors[6:7] += over_rows(grad * unit)
        grad = grad * gains[5:6]
        grad = inverse * (grad - unit * jnp.mean(grad * unit, axis=-1, keepdims=True))
        own[items + item] = grad.astype(own.dtype)

    def back_to_attention(item):
        unit, inverse = norm_unit(middle[item])
        grad = result[item]
        vectors[2 + item : 3 + item] = over_rows(grad * (unit * gains[4:5]))
        grad = grad * (1.0 + scale_of(item, 2))
        vectors[7:8] += over_rows(grad * unit)
        grad = grad * gains[4:5]
        grad = inverse * (grad - unit * jnp.mean(grad * unit, axis=-1, keepdims=True))
        grad = live[item][:, 0:1] * cotangent[item] + grad
        grad_middle[item] = grad
        gate = jnp.tanh(scale_of(item, 1))
        unit, inverse = norm_unit(projected[item])
        vectors[4 + item : 5 + item] = (1.0 - gate * gate) * over_rows(grad * (unit * gains[3:4]))
        grad = gate * grad
        vectors[8:9] += over_rows(grad * unit)
        grad = grad * gains[3:4]
        grad = inverse * (grad - unit * jnp.mean(grad * unit, axis=-1, keepdims=True))
        own[2 * items + item] = grad.astype(own.dtype)

    def pair_of(near):
        return jnp.where(near, 1 - one.pair, one.pair)

    def forward(item, near):
        pair = pair_of(near)
        at = pl.ds(pl.multiple_of(item * 2 * half + pair * half, half), half)
        tokens = ffn_in[item, pl.ds(pair * 4, 4)].reshape(half, width)

        @pl.loop(0, hidden // 256)
        def _(tile):
            lanes = pl.ds(pl.multiple_of(tile * 256, 256), 256)
            up_lanes = pl.ds(pl.multiple_of(hidden + tile * 256, 256), 256)
            gate = jnp.dot(tokens, w_gu[:, :, :, lanes].reshape(width, 256), preferred_element_type=jnp.float32)
            up = jnp.dot(tokens, w_gu[:, :, :, up_lanes].reshape(width, 256), preferred_element_type=jnp.float32)
            gate_up[at, lanes] = gate
            gate_up[at, up_lanes] = up
            inner_act[at, lanes] = (gate * (1.0 / (1.0 + jnp.exp(-gate))) * up).astype(inner_act.dtype)

        inner = inner_act[at]

        @pl.loop(0, width // 256)
        def _(tile):
            lanes = pl.ds(pl.multiple_of(tile * 256, 256), 256)
            out = jnp.dot(inner, w_down[:, lanes], preferred_element_type=jnp.float32)
            partial[item, pl.ds(pair * 4, 4), :, lanes] = out.astype(partial.dtype).reshape(4, rows, 256)

    def backward(item, near):
        pair = pair_of(near)
        at = pl.ds(pl.multiple_of(item * 2 * half + pair * half, half), half)
        grads = ffn_low[item, pl.ds(pair * 4, 4)].reshape(half, width)

        @pl.loop(0, hidden // 256)
        def _(tile):
            lanes = pl.ds(pl.multiple_of(tile * 256, 256), 256)
            up_lanes = pl.ds(pl.multiple_of(hidden + tile * 256, 256), 256)
            grad = lax.dot_general(grads, w_down[lanes], NT, preferred_element_type=jnp.float32)
            gate, up = gate_up[at, lanes], gate_up[at, up_lanes]
            sigmoid = 1.0 / (1.0 + jnp.exp(-gate))
            gate_up_low[at, lanes] = (grad * up * sigmoid * (1.0 + gate * (1.0 - sigmoid))).astype(gate_up_low.dtype)
            gate_up_low[at, up_lanes] = (grad * (gate * sigmoid)).astype(gate_up_low.dtype)

        low = gate_up_low[at]

        @pl.loop(0, 4)
        def _(tile):
            lanes = pl.ds(pl.multiple_of(tile * (width // 4), 128), width // 4)
            weight = w_gu[pl.ds(tile * 2, 2)].reshape(width // 4, 2 * hidden)
            out = lax.dot_general(low, weight, NT, preferred_element_type=jnp.float32)
            partial[item, pl.ds(pair * 4, 4), :, lanes] = out.astype(partial.dtype).reshape(4, rows, width // 4)

    def down_part(half):
        at = slice(half * 256, (half + 1) * 256)
        left = inner_act[:, at]
        right = ffn_low[...].reshape(left.shape[0], width)
        grad_down[half] = lax.dot_general(left, right, TN, preferred_element_type=jnp.float32).astype(grad_down.dtype)

    def gu_columns(tile):
        lanes = slice(tile * (width // 4), (tile + 1) * (width // 4))
        left = ffn_in[:, :, :, lanes].reshape(gate_up_low.shape[0], width // 4)
        out = lax.dot_general(left, gate_up_low[...], TN, preferred_element_type=jnp.float32)
        grad_gu[2 * tile : 2 * tile + 2] = out.astype(grad_gu.dtype).reshape((2,) + grad_gu.shape[1:])

    def to_twin(number):
        pairs = ((grad_gu.at[:, pl.ds(2 * (1 - core), 2)], got_gu), (grad_down.at[1 - core], got_down))
        return remote(*pairs[number], swap_send.at[3 + number], swap_recv.at[3 + number], twin)

    def to_far():
        return remote(half_gu.at[:, 1 - far], far_gu, swap_send.at[5], swap_recv.at[5], across_y)

    def exchange():
        to_twin(0).start()
        to_twin(1).start()

    def exchange_far():
        to_twin(0).wait()
        to_twin(1).wait()
        mine = grad_gu[:, pl.ds(2 * core, 2)].astype(jnp.float32)
        half_gu[...] = (mine + got_gu[...].astype(jnp.float32)).astype(half_gu.dtype)
        to_far().start()
        mine = grad_down[core].astype(jnp.float32)
        half_down[...] = (mine + got_down[...].astype(jnp.float32)).astype(half_down.dtype)

    def scatter(item, source):
        chain, ref = chains[item], source.at[item]
        steps = {
            "sf": functools.partial(chain.scatter_start, ref, False),
            "sn": functools.partial(chain.scatter_start, ref, True),
            "h": functools.partial(chain.scatter_hand, ref),
            "se": functools.partial(chain.scatter_end, ref, result.at[item]),
        }
        for number in range(3):
            steps[f"b{number}"] = functools.partial(chain.scatter_over, ref, number)
            steps[f"a{number}"] = functools.partial(chain.scatter_along, ref, number)
        return steps

    def gather(item, phase, target):
        chain, mine, ref = chains[item], own.at[phase * items + item], target.at[item]
        steps = {
            "gs": functools.partial(chain.gather_start, mine, ref),
            "t": functools.partial(chain.gather_turn, mine, ref),
            "ge": functools.partial(chain.gather_end, mine, ref),
        }
        for step in range(1, DEPTH):
            steps[f"g{step}"] = functools.partial(chain.gather_step, ref, step)
        return steps

    def working(item, work):
        return {"wf": functools.partial(work, item, False), "wn": functools.partial(work, item, True)}

    def run(order, *tables):
        steps = {}
        for table in tables:
            steps.update(table)
        for name in order:
            if name in steps:
                steps[name]()

    weights = {f"d{half}": functools.partial(down_part, half) for half in range(2)}
    weights.update({f"u{tile}": functools.partial(gu_columns, tile) for tile in range(4)})
    weights.update({"c": exchange, "y": exchange_far})
    run(ORDER, scatter(0, parts))
    middle_of(0)
    quarter_on(0).wait()
    quarter_on(2).start()
    run(ORDER, gather(0, 0, ffn_in), scatter(1, parts))
    middle_of(1)
    quarter_on(1).wait()
    quarter_on(2).wait()
    run(ORDER, gather(1, 0, ffn_in), scatter(0, partial), working(0, forward))
    outcome(0)
    run(ORDER, gather(0, 1, ffn_low), scatter(1, partial), working(1, forward))
    outcome(1)
    run(ORDER, gather(1, 1, ffn_low), scatter(0, partial), working(0, backward))
    back_to_attention(0)
    run(LAST_ORDER, gather(0, 2, projected_low), scatter(1, partial), working(1, backward), weights)
    back_to_attention(1)
    run(END_ORDER, gather(1, 2, projected_low), weights)
    to_far().wait()
    mine = half_gu[:, pl.ds(far, 1)][:, 0].astype(jnp.float32)
    sum_gu[...] = (mine + far_gu[...].astype(jnp.float32)).astype(sum_gu.dtype)


def feed_forward(parts, states, cotangent, live, modulation, gains, gu_part, w_down, ident):
    items, ranks, rows, width = parts.shape
    tokens, hidden = items * ranks * rows, w_down.shape[0]
    low, single = parts.dtype, jnp.float32
    first = split_chain(width)
    wave = pltpu.SemaphoreType.DMA

    def slots(size, count=(DEPTH,)):
        return pltpu.VMEM(count + (rows, size), low)

    flow = [slots(first)] * 5 + [slots(width - first)] * 8 + [slots(width - first, ())] * 2
    waves = [wave((DEPTH + 1,))] * 2 + [wave((3, 2, DEPTH))] * 2
    waves += [wave((DEPTH + 1,))] * 2 + [wave((3, 2, DEPTH)), wave((3, DEPTH))]
    quarters, pair = ((ranks, count) + gu_part.shape[1:] for count in (4, 2))
    local = jax.ShapeDtypeStruct(states.shape, single)
    everywhere = jax.ShapeDtypeStruct(parts.shape, low)
    return pl.pallas_call(
        feed_forward_kernel,
        out_shape=[
            local,
            local,
            everywhere,
            jax.ShapeDtypeStruct((tokens, hidden), low),
            everywhere,
            jax.ShapeDtypeStruct((tokens, 2 * hidden), low),
            everywhere,
            jax.ShapeDtypeStruct((16, width), single),
            jax.ShapeDtypeStruct(gu_part.shape, low),
            jax.ShapeDtypeStruct((hidden // 2, width), low),
        ],
        in_specs=[NEAR] * 8,
        out_specs=[NEAR] * 10,
        scratch_shapes=[
            pltpu.VMEM((tokens, 2 * hidden), single),
            pltpu.VMEM(states.shape, single),
            pltpu.VMEM(states.shape, single),
            pltpu.VMEM(states.shape, single),
            pltpu.VMEM((3 * items, rows, width), low),
            pltpu.VMEM(parts.shape, low),
            pltpu.VMEM(quarters, low),
            pltpu.VMEM(quarters, low),
            pltpu.VMEM((2, hidden // 2, width), low),
            pltpu.VMEM(pair, low),
            pltpu.VMEM((hidden // 2, width), low),
            pltpu.VMEM(pair, low),
            pltpu.VMEM(gu_part.shape, low),
            wave((6,)),
            wave((6,)),
        ]
        + flow * items
        + waves * items,
        name=f"feed_forward_{ident}",
        compiler_params=pltpu.CompilerParams(
            collective_id=ident, has_side_effects=True, vmem_limit_bytes=58 << 20
        ),
    )(parts, states, cotangent, live, modulation, gains, gu_part, w_down)


def lay_flat(vectors):
    flat = jnp.concatenate([vector.reshape(-1) for vector in vectors])
    rows = -(-flat.size // 1024) * 8
    return jnp.pad(flat, (0, rows * 128 - flat.size)).reshape(rows, 128)


def take_apart(total, vectors):
    flat, parts, start = total.reshape(-1), [], 0
    for vector in vectors:
        parts.append(flat[start : start + vector.size].reshape(vector.shape))
        start += vector.size
    return parts


def sum_vectors(vectors, ident):
    return take_apart(sum_rows(lay_flat(vectors), ident), vectors)


def first_sums(vectors, qkv, text, ident):
    total, qkv_here, text_in = first_transfers(lay_flat(vectors), qkv, text, ident)
    return take_apart(total, vectors), qkv_here, text_in


CORES = [(0, 1), (1, 0), (2, 3), (3, 2)]
FARS = [(0, 2), (1, 3), (2, 0), (3, 1)]


def swap(array, pairs):
    return lax.ppermute(array, "items", pairs)


def give_keep(grad, index, axis):
    keep = lax.dynamic_index_in_dim(grad, index, axis, keepdims=False)
    give = lax.dynamic_index_in_dim(grad, 1 - index, axis, keepdims=False)
    return give, keep


def add_low(one, other):
    return (one.astype(jnp.float32) + other.astype(jnp.float32)).astype(jnp.bfloat16)


def head_parallel_plan(
    hidden_in,
    cotangent,
    text_states,
    time_embed,
    live_rows,
    frame_rows,
    text_len,
    w_qkv,
    w_out,
    w_text,
    w_gu,
    w_down,
    w_ada,
    gains,
    cross_gate,
    ada_bias,
    text_gain,
):
    single = jnp.float32
    narrow = jnp.bfloat16
    ranks = lax.axis_size("rows")
    place = lax.axis_index("rows")
    width = hidden_in.shape[2]
    heads = cross_gate.shape[0]
    head_size = width // heads
    score_scale = head_size ** (-0.5)
    items = time_embed.shape[1]
    slots = hidden_in.shape[1] // items
    row_slots = slots // COLS
    seq_len = ranks * slots
    text_local = text_states.shape[2]
    text_all = text_local * ranks
    text_width = text_states.shape[3]
    span = width // ranks
    heads_here = heads // ranks
    tokens = items * seq_len

    def dot(left, right):
        return jnp.dot(left, right, preferred_element_type=single)

    def dot_back(left, weight):
        return jnp.einsum("tn,kn->tk", left, weight, preferred_element_type=single)

    def weight_grad(left, right):
        return jnp.einsum("tk,tn->kn", left, right, preferred_element_type=single)

    time_silu = jax.nn.silu(time_embed[0].astype(single)).astype(narrow)
    ada_depth = w_ada.shape[0]
    time_here = lax.dynamic_slice_in_dim(time_silu, place * ada_depth, ada_depth, 1)

    def spread(part, whole):
        return lax.dynamic_update_slice_in_dim(
            jnp.zeros((whole,), single), part.reshape(-1), place * part.size, 0
        )

    group = lax.axis_index("items")
    core, far = lax.rem(group, 2), group // 2
    counts_here = live_rows[0]
    text_float = text_states[0].astype(single).reshape(items * text_local, text_width)
    text_inverse = norm_parts(text_float)[1]
    (modulation, counts, text_inverse), qkv_here, text_in = first_sums(
        [
            dot(time_here, w_ada),
            spread(counts_here.astype(single), ranks * items),
            spread(text_inverse, ranks * items * text_local),
        ],
        w_qkv,
        text_states[0],
        0,
    )
    qkv_here = qkv_here.reshape(width, -1)
    modulation = modulation + ada_bias
    counts = counts.astype(jnp.int32)
    text_inverse = text_inverse.reshape(-1, 1)
    scale_attn = modulation[:, None, 0:width]

    slot_in_row = jnp.arange(slots) // COLS
    live_mask = (slot_in_row[None, :] < counts_here[0][:, None]).astype(single)[..., None]
    def gain_here(index):
        return lax.dynamic_slice_in_dim(gains[index], place * span, span, 0)

    states = hidden_in[0].reshape(items, slots, width)
    unit_in, inverse_in = norm_parts(states)
    norm_in = unit_in * gains[0]
    attn_in = gather_tokens((norm_in * (1.0 + scale_attn)).astype(narrow), 1)
    hidden = w_down.shape[0]
    gu_rows = pack_quarter(w_gu, (2 * core + far).reshape(1), 2, ranks)

    features = text_width // ranks
    features = text_width // ranks
    text_in = text_in.reshape(items * text_all, features)
    text_unit = text_in.astype(single) * text_inverse
    gain_text = lax.dynamic_slice_in_dim(text_gain, place * features, features, 0)
    text_norm = (text_unit * gain_text).astype(narrow)

    text_parts = pack_blocks(dot(text_norm, w_text).astype(narrow), 2, ranks, narrow)
    text_proj = scatter_rows(text_parts, 2, 0).reshape(ranks, items, text_local, 2 * span)
    gu_rows, text_proj = lax.optimization_barrier((gu_rows, text_proj))
    gu_part = lax.all_to_all(gu_rows, "rows", 0, 0, tiled=True)
    qkv_proj, squares = project(attn_in, qkv_here, text_proj)
    totals = sum_rows(squares, 3)
    gains_both = jnp.concatenate([gain_here(1), gain_here(2)])[None]
    gain_t = gain_here(6)[None]
    gate_here = jnp.tanh(lax.dynamic_slice_in_dim(cross_gate, place * heads_here, heads_here, 0))
    gate_lanes = jnp.repeat(gate_here, head_size)[None]
    out_parts, combined, qkv_bf, text_kv, tables = attend(
        qkv_proj,
        totals,
        text_proj,
        gains_both,
        gain_t,
        gate_lanes,
        w_out,
        counts,
        frame_rows[0],
        text_len[0],
        head_size,
    )
    live_lanes = jnp.broadcast_to(live_mask, (items, slots, 128))
    output, grad_middle, _, _, _, _, projected_low, vectors, sum_gu, half_down = feed_forward(
        out_parts.reshape(items, ranks, slots, width),
        states,
        cotangent[0].reshape(items, slots, width),
        live_lanes,
        modulation,
        gains,
        gu_part,
        w_down,
        4,
    )
    projected_low = projected_low.reshape(tokens, width)
    rows_gu = lax.all_to_all(sum_gu, "rows", 0, 0, tiled=True)
    got_down = swap(half_down, FARS)
    grad_out = weight_grad(combined, projected_low).astype(narrow).reshape(2, -1, width)
    give_out, keep_out = give_keep(grad_out, core, 0)

    scaled, grad_value, text_scaled, text_value, sums, gain_sums, gate_sums = attend_back(
        projected_low,
        w_out,
        qkv_bf,
        text_kv,
        tables,
        qkv_proj,
        totals,
        text_proj,
        gains_both,
        gain_t,
        gate_lanes,
        counts,
        text_len[0],
        head_size,
        (give_out,),
    )
    half_out = add_low(keep_out, swap(give_out, CORES))
    sum_down = add_low(half_down, got_down)
    qkv_low, text_low = norms_back(
        qkv_proj,
        totals,
        sum_rows(sums, 10, after=(sum_down, half_out)),
        scaled,
        grad_value,
        text_proj,
        text_scaled,
        text_value,
        width,
    )
    grad_qkv = weight_grad(attn_in, qkv_low).astype(narrow)
    give_qkv, keep_qkv = give_keep(grad_qkv.reshape(ranks, 2, -1, 3 * span), core, 1)

    text_low = text_low.reshape(items * text_all, 2 * span)
    half_qkv = add_low(keep_qkv, swap(give_qkv, CORES))
    attn_parts = dot_back(qkv_low, qkv_here)
    got_gu = swap(rows_gu, FARS)
    all_low, got_out, got_qkv, got_down = gather_rows(
        text_low,
        12,
        0,
        after=(got_gu, attn_parts),
        swaps=((half_out, "far"), (half_qkv, "far"), (sum_down, "core")),
    )
    pair_gu = join_blocks(rows_gu, got_gu, far_bit)
    all_low = unpack_blocks(all_low, 2, narrow)
    grad_text = weight_grad(text_norm, all_low).astype(narrow).reshape(2, -1, 2 * width)
    give_text, keep_text = give_keep(grad_text, core, 0)
    half_text = add_low(keep_text, swap(give_text, CORES))
    sum_out, sum_qkv = add_low(half_out, got_out), add_low(half_qkv, got_qkv)
    grad_attn_in, got_text, got_out, got_gu = scatter_tokens(
        attn_parts,
        items,
        11,
        swaps=((half_text, "far"), (sum_out, "core"), (pair_gu, "core")),
    )
    sum_qkv, grad_attn_in = lax.optimization_barrier((sum_qkv, grad_attn_in))
    rows_qkv = lax.all_to_all(sum_qkv, "rows", 0, 0, tiled=True)
    sum_text = add_low(half_text, got_text)
    grad_text_gain = jnp.sum(dot_back(all_low, w_text) * text_unit, axis=0)
    grad_x, small = finish(
        grad_attn_in,
        states,
        grad_middle,
        modulation,
        gains,
        vectors,
        gain_sums,
        gate_sums,
        grad_text_gain[None],
        time_here.astype(single),
    )
    reduced, got_text = final_sums(small, SUM_DEPTH, 13, swaps=((sum_text, "core"),))
    flat = reduced[:, :SUM_DEPTH].reshape(-1)
    total_gains = flat[: gains.size].reshape(gains.shape)
    total_text_gain = flat[gains.size : gains.size + text_width]
    total_gate = jnp.sum(flat[-width:].reshape(heads, head_size), axis=1)
    total_gate = total_gate * (1.0 - jnp.tanh(cross_gate) ** 2)
    groups = lax.axis_size("items")
    kept = reduced[:, SUM_DEPTH:].reshape(ranks, groups, -1, 128)
    all_modulation = jnp.swapaxes(kept[:, :, : width // 128], 0, 1).reshape(groups * items, 4 * width)
    all_time = lax.dynamic_index_in_dim(kept[:, :, width // 128 :], place, 0, keepdims=False)
    all_time = all_time.reshape(groups * items, ada_depth)
    final_ada = jnp.einsum(
        "tk,tn->kn",
        all_time,
        all_modulation,
        precision=lax.Precision.HIGHEST,
        preferred_element_type=single,
    )
    total_bias = jnp.sum(all_modulation, axis=0)
    def whole_rows(half, got):
        return join_rows(half, got, core_bit, single).reshape(-1, half.shape[-1])

    sums = [
        unpack_halves(rows_qkv, swap(rows_qkv, CORES), 3),
        whole_rows(sum_out, got_out),
        whole_rows(sum_text, got_text),
        unpack_halves(pair_gu, got_gu, 2),
        whole_rows(sum_down, got_down),
    ]
    return (
        output.reshape(1, items * slots, width),
        grad_x.reshape(1, items * slots, width),
        *sums,
        final_ada,
        total_gains,
        total_gate,
        total_bias,
        total_text_gain,
    )


def per_device(*arrays):
    heads = arrays[14].shape[0]
    plan = gathered_plan if heads % lax.axis_size("rows") else head_parallel_plan
    return plan(*arrays)


def solution(mesh):
    in_specs = (
        P("items", "rows", None),
        P("items", "rows", None),
        P("items", None, "rows", None),
        P("items", None, None),
        P("items", "rows", None),
        P("items", None),
        P("items", None),
        P("rows", None),
        P("rows", None),
        P("rows", None),
        P("rows", None),
        P("rows", None),
        P("rows", None),
        P(),
        P(),
        P(),
        P(),
    )
    out_specs = (
        P("items", "rows", None),
        P("items", "rows", None),
        P("rows", None),
        P("rows", None),
        P("rows", None),
        P("rows", None),
        P("rows", None),
        P("rows", None),
        P(),
        P(),
        P(),
        P(),
    )
    return jax.shard_map(
        per_device, mesh=mesh, in_specs=in_specs, out_specs=out_specs, check_vma=False
    )
```

```python
import functools
import itertools
import math

import jax
import jax.numpy as jnp
from jax import lax
from jax.experimental import pallas as pl
from jax.experimental.pallas import tpu as pltpu
from jax.sharding import PartitionSpec as P

COLS = 32


epsilon = 1e-06
masked_score = -1e30
group_heads = 4


def norm_gain(values, scaling):
    return values * lax.rsqrt(jnp.mean(values * values, axis=-1, keepdims=True) + epsilon) * scaling


def pre_norm(values, shift_scale, scaling):
    return norm_gain(values, scaling) * (1.0 + shift_scale)


def post_add(residual, branch, gate_in, scaling):
    return residual + jnp.tanh(gate_in) * norm_gain(branch, scaling)


def swiglu(gate_up):
    middle_col = gate_up.shape[-1] // 2
    return jax.nn.silu(gate_up[..., :middle_col]) * gate_up[..., middle_col:]


def freq_rates(number):
    return 10000.0 ** (-jnp.arange(number).astype(jnp.float32) / number)


def rotary_angles(frame_index, frame_row, column, head_size):
    frame_pairs = head_size // 8
    space_pairs = (head_size // 2 - frame_pairs) // 2
    return jnp.concatenate(
        [
            frame_index.astype(jnp.float32)[..., None] * freq_rates(frame_pairs),
            frame_row.astype(jnp.float32)[..., None] * freq_rates(space_pairs),
            column.astype(jnp.float32)[..., None] * freq_rates(space_pairs),
        ],
        axis=-1,
    )


def rotate(values, cos_table, sin_table, head_count):
    shaped = values.reshape(values.shape[:-1] + (head_count, values.shape[-1] // head_count))
    half_size = shaped.shape[-1] // 2
    upper_half = shaped[..., :half_size]
    lower_half = shaped[..., half_size:]
    cos_heads = cos_table[..., None, :]
    sin_heads = sin_table[..., None, :]
    turned = jnp.concatenate(
        [
            upper_half * cos_heads - lower_half * sin_heads,
            upper_half * sin_heads + lower_half * cos_heads,
        ],
        axis=-1,
    )
    return turned.reshape(values.shape)


def text_split(projected, key_gain):
    half_cols = projected.shape[-1] // 2
    return (norm_gain(projected[..., :half_cols], key_gain), projected[..., half_cols:])


def gathered_plan(
    hidden_in,
    cotangent,
    text_states,
    time_embed,
    live_rows,
    frame_rows,
    text_len,
    w_qkv,
    w_out,
    w_text,
    w_gu,
    w_down,
    w_ada,
    gains,
    cross_gate,
    ada_bias,
    text_gain,
):
    single = jnp.float32
    narrow = jnp.bfloat16
    model_width = hidden_in.shape[2]
    head_count = cross_gate.shape[0]
    head_size = model_width // head_count
    score_scale = head_size ** (-0.5)
    item_count = time_embed.shape[1]
    item_slots = hidden_in.shape[1] // item_count
    row_devices = lax.axis_size("rows")
    seq_len = row_devices * item_slots
    text_local = text_states.shape[2]
    text_all = text_local * row_devices
    text_width = text_states.shape[3]
    group_span = group_heads * head_size
    block_count = head_count // group_heads
    token_count = item_count * item_slots

    def weight_term(left, right, accuracy):
        return jnp.einsum(
            "tk,tn->kn", left, right, precision=accuracy, preferred_element_type=single
        )

    def reduce_term(term):
        return lax.psum_scatter(
            term.astype(jnp.bfloat16), "rows", scatter_dimension=0, tiled=True
        ).astype(jnp.float32)

    full_qkv, full_out, full_text, full_gu, full_down, full_ada = (
        lax.all_gather(w_qkv, "rows", axis=0, tiled=True),
        lax.all_gather(w_out, "rows", axis=0, tiled=True),
        lax.all_gather(w_text, "rows", axis=0, tiled=True),
        lax.all_gather(w_gu, "rows", axis=0, tiled=True),
        lax.all_gather(w_down, "rows", axis=0, tiled=True),
        lax.all_gather(w_ada, "rows", axis=0, tiled=True),
    )
    counts_here = live_rows[0]
    every_count = lax.all_gather(counts_here, "rows", axis=0, tiled=True)
    device_place = lax.axis_index("rows")
    ranks = jnp.arange(row_devices)
    rows_below = jnp.sum(jnp.where(ranks[:, None] < device_place, every_count, 0), axis=0)
    slot_row = jnp.arange(item_slots) // COLS
    column = jnp.arange(item_slots) % COLS
    row_index = rows_below[:, None] + slot_row[None, :]
    heights = frame_rows[0][:, None]
    frame_index = row_index // heights
    frame_row = row_index % heights
    live_mask = (slot_row[None, :] < counts_here[0][:, None]).astype(single)
    key_live = (slot_row[None, None, :] < jnp.transpose(every_count)[:, :, None]).reshape(
        item_count, seq_len
    )
    text_live = jnp.arange(text_all)[None, :] < text_len[0][:, None]
    angles = rotary_angles(
        frame_index, frame_row, jnp.broadcast_to(column, row_index.shape), head_size
    )
    cos_table = jnp.cos(angles)
    sin_table = jnp.sin(angles)

    def qkv_split(projected, gain_query, gain_key):
        queries = rotate(
            norm_gain(projected[..., :model_width], gain_query), cos_table, sin_table, head_count
        )
        keys_here = rotate(
            norm_gain(projected[..., model_width : 2 * model_width], gain_key),
            cos_table,
            sin_table,
            head_count,
        )
        return (queries, keys_here, projected[..., 2 * model_width :])

    states = hidden_in[0].reshape(item_count, item_slots, model_width)
    time_silu = jax.nn.silu(time_embed[0].astype(single)).astype(narrow)
    modulation = jnp.dot(time_silu, full_ada, preferred_element_type=single) + ada_bias
    scale_attn = modulation[:, None, 0:model_width]
    gate_attn = modulation[:, None, model_width : 2 * model_width]
    scale_ffn = modulation[:, None, 2 * model_width : 3 * model_width]
    gate_ffn = modulation[:, None, 3 * model_width :]
    attn_in = (
        pre_norm(states, scale_attn, gains[0]).astype(narrow).reshape(token_count, model_width)
    )
    qkv_proj = jnp.dot(attn_in, full_qkv, preferred_element_type=single).reshape(
        item_count, item_slots, 3 * model_width
    )
    query_full, key_full, value_full = qkv_split(qkv_proj, gains[1], gains[2])
    query_low = query_full.astype(narrow)
    key_low = key_full.astype(narrow)
    value_low = value_full.astype(narrow)
    text_float = text_states[0].astype(single)
    text_norm = norm_gain(text_float, text_gain).astype(narrow)
    text_proj = jnp.einsum("ctd,dn->ctn", text_norm, full_text, preferred_element_type=single)
    tkey_full, tval_full = text_split(text_proj, gains[6])
    key_all, value_all, tkey_all, tval_all = (
        lax.all_gather(key_low, "rows", axis=1, tiled=True),
        lax.all_gather(value_low, "rows", axis=1, tiled=True),
        lax.all_gather(tkey_full.astype(narrow), "rows", axis=1, tiled=True),
        lax.all_gather(tval_full.astype(narrow), "rows", axis=1, tiled=True),
    )

    def block_slices(block_index, key_source, value_source):
        offset = block_index * group_span
        query_part = lax.dynamic_slice_in_dim(query_low, offset, group_span, 2).reshape(
            item_count, item_slots, group_heads, head_size
        )
        key_part = lax.dynamic_slice_in_dim(key_source, offset, group_span, 2).reshape(
            item_count, seq_len, group_heads, head_size
        )
        value_part = lax.dynamic_slice_in_dim(value_source, offset, group_span, 2).reshape(
            item_count, seq_len, group_heads, head_size
        )
        return (query_part, key_part, value_part)

    def self_step(carry, block_index):
        query_part, key_part, value_part = block_slices(block_index, key_all, value_all)
        scores = (
            jnp.einsum("iphe,ikhe->ihpk", query_part, key_part, preferred_element_type=single)
            * score_scale
        )
        scores = jnp.where(key_live[:, None, None, :], scores, masked_score)
        row_max = jnp.max(scores, axis=-1, keepdims=True)
        exp_terms = jnp.exp(scores - row_max)
        exp_total = jnp.sum(exp_terms, axis=-1, keepdims=True)
        probs_low = (exp_terms / exp_total).astype(narrow)
        attended = jnp.einsum(
            "ihpk,ikhe->iphe", probs_low, value_part, preferred_element_type=single
        )
        return (
            carry,
            (
                attended.reshape(item_count, item_slots, group_span),
                (row_max + jnp.log(exp_total))[..., 0],
            ),
        )

    _, (self_parts, log_totals) = lax.scan(
        self_step, jnp.zeros((), single), jnp.arange(block_count)
    )

    def heads_last(parts):
        return jnp.transpose(parts, (1, 2, 0, 3)).reshape(item_count, item_slots, model_width)

    self_out = heads_last(self_parts)
    query_heads = query_low.reshape(item_count, item_slots, head_count, head_size)
    tkey_heads = tkey_all.reshape(item_count, text_all, head_count, head_size)
    tval_heads = tval_all.reshape(item_count, text_all, head_count, head_size)
    cross_scores = (
        jnp.einsum("iphe,ikhe->ihpk", query_heads, tkey_heads, preferred_element_type=single)
        * score_scale
    )
    cross_scores = jnp.where(text_live[:, None, None, :], cross_scores, masked_score)
    cross_max = jnp.max(cross_scores, axis=-1, keepdims=True)
    cross_exp = jnp.exp(cross_scores - cross_max)
    cross_probs = cross_exp / jnp.sum(cross_exp, axis=-1, keepdims=True)
    cross_low = cross_probs.astype(narrow)
    cross_out = jnp.einsum("ihpk,ikhe->iphe", cross_low, tval_heads, preferred_element_type=single)
    tanh_gate = jnp.tanh(cross_gate)
    combined = (
        self_out.reshape(item_count, item_slots, head_count, head_size)
        + tanh_gate[:, None] * cross_out
    )
    combined = combined.reshape(token_count, model_width).astype(narrow)
    projected = jnp.dot(combined, full_out, preferred_element_type=single).reshape(
        item_count, item_slots, model_width
    )
    middle = post_add(states, projected, gate_attn, gains[3])
    ffn_in = pre_norm(middle, scale_ffn, gains[4]).astype(narrow).reshape(token_count, model_width)
    gate_up = jnp.dot(ffn_in, full_gu, preferred_element_type=single)
    inner_act = swiglu(gate_up).astype(narrow)
    ffn_out = jnp.dot(inner_act, full_down, preferred_element_type=single).reshape(
        item_count, item_slots, model_width
    )
    result = post_add(middle, ffn_out, gate_ffn, gains[5])
    output = (live_mask[..., None] * result).reshape(1, token_count, model_width)
    grad_result = live_mask[..., None] * cotangent[0].reshape(item_count, item_slots, model_width)
    _, back_ffn_out = jax.vjp(post_add, middle, ffn_out, gate_ffn, gains[5])
    grad_middle, grad_ffn_out, grad_gate_ffn, grad_gain_five = back_ffn_out(grad_result)
    ffn_low = grad_ffn_out.astype(narrow).reshape(token_count, model_width)
    shard_down = reduce_term(weight_term(inner_act, ffn_low, None))
    grad_inner = jnp.einsum("tn,kn->tk", ffn_low, full_down, preferred_element_type=single)
    _, back_glu = jax.vjp(swiglu, gate_up)
    gate_up_low = back_glu(grad_inner)[0].astype(narrow)
    shard_gu = reduce_term(weight_term(ffn_in, gate_up_low, None))
    grad_ffn_in = jnp.einsum("tn,kn->tk", gate_up_low, full_gu, preferred_element_type=single)
    _, back_ffn_in = jax.vjp(pre_norm, middle, scale_ffn, gains[4])
    part_middle, grad_scale_ffn, grad_gain_four = back_ffn_in(
        grad_ffn_in.reshape(item_count, item_slots, model_width)
    )
    grad_middle = grad_middle + part_middle
    _, back_attn_out = jax.vjp(post_add, states, projected, gate_attn, gains[3])
    grad_hidden, grad_projected, grad_gate_attn, grad_gain_three = back_attn_out(grad_middle)
    projected_low = grad_projected.astype(narrow).reshape(token_count, model_width)
    shard_out = reduce_term(weight_term(combined, projected_low, None))
    grad_combined = jnp.einsum("tn,kn->tk", projected_low, full_out, preferred_element_type=single)
    grad_combined = grad_combined.reshape(item_count, item_slots, head_count, head_size)
    self_low = grad_combined.reshape(item_count, item_slots, model_width).astype(narrow)
    cross_grad_low = (tanh_gate[:, None] * grad_combined).astype(narrow)
    grad_cross_gate = (1.0 - tanh_gate * tanh_gate) * jnp.sum(
        grad_combined * cross_out, axis=(0, 1, 3)
    )

    def self_back(carry, packed):
        block_index, log_total = packed
        query_part, key_part, value_part = block_slices(block_index, key_all, value_all)
        offset = block_index * group_span
        grad_part = lax.dynamic_slice_in_dim(self_low, offset, group_span, 2).reshape(
            item_count, item_slots, group_heads, head_size
        )
        scores = (
            jnp.einsum("iphe,ikhe->ihpk", query_part, key_part, preferred_element_type=single)
            * score_scale
        )
        scores = jnp.where(key_live[:, None, None, :], scores, masked_score)
        attn_probs = jnp.exp(scores - log_total[..., None])
        grad_probs = jnp.einsum(
            "iphe,ikhe->ihpk", grad_part, value_part, preferred_element_type=single
        )
        row_inner = jnp.sum(attn_probs * grad_probs, axis=-1, keepdims=True)
        score_low = (attn_probs * (grad_probs - row_inner)).astype(narrow)
        grad_query = (
            jnp.einsum("ihpk,ikhe->iphe", score_low, key_part, preferred_element_type=single)
            * score_scale
        )
        grad_value = jnp.einsum(
            "ihpk,iphe->ikhe", attn_probs.astype(narrow), grad_part, preferred_element_type=single
        )
        grad_key = (
            jnp.einsum("ihpk,iphe->ikhe", score_low, query_part, preferred_element_type=single)
            * score_scale
        )
        owned_key, owned_value = (
            lax.psum_scatter(
                grad_key.reshape(item_count, seq_len, group_span).astype(jnp.bfloat16),
                "rows",
                scatter_dimension=1,
                tiled=True,
            ).astype(jnp.float32),
            lax.psum_scatter(
                grad_value.reshape(item_count, seq_len, group_span).astype(jnp.bfloat16),
                "rows",
                scatter_dimension=1,
                tiled=True,
            ).astype(jnp.float32),
        )
        return (
            carry,
            (grad_query.reshape(item_count, item_slots, group_span), owned_key, owned_value),
        )

    _, (query_parts, key_parts, value_parts) = lax.scan(
        self_back, jnp.zeros((), single), (jnp.arange(block_count), log_totals)
    )
    cross_grad_probs = jnp.einsum(
        "iphe,ikhe->ihpk", cross_grad_low, tval_heads, preferred_element_type=single
    )
    cross_inner = jnp.sum(cross_probs * cross_grad_probs, axis=-1, keepdims=True)
    cross_score_low = (cross_probs * (cross_grad_probs - cross_inner)).astype(narrow)
    grad_query_cross = (
        jnp.einsum("ihpk,ikhe->iphe", cross_score_low, tkey_heads, preferred_element_type=single)
        * score_scale
    )
    grad_text_key = (
        jnp.einsum("ihpk,iphe->ikhe", cross_score_low, query_heads, preferred_element_type=single)
        * score_scale
    )
    grad_text_value = jnp.einsum(
        "ihpk,iphe->ikhe", cross_low, cross_grad_low, preferred_element_type=single
    )
    owned_tkey, owned_tval = (
        lax.psum_scatter(
            grad_text_key.reshape(item_count, text_all, model_width).astype(jnp.bfloat16),
            "rows",
            scatter_dimension=1,
            tiled=True,
        ).astype(jnp.float32),
        lax.psum_scatter(
            grad_text_value.reshape(item_count, text_all, model_width).astype(jnp.bfloat16),
            "rows",
            scatter_dimension=1,
            tiled=True,
        ).astype(jnp.float32),
    )
    grad_query_all = heads_last(query_parts) + grad_query_cross.reshape(
        item_count, item_slots, model_width
    )
    _, back_qkv = jax.vjp(qkv_split, qkv_proj, gains[1], gains[2])
    grad_qkv, grad_gain_one, grad_gain_two = back_qkv(
        (grad_query_all, heads_last(key_parts), heads_last(value_parts))
    )
    qkv_low = grad_qkv.astype(narrow).reshape(token_count, 3 * model_width)
    shard_qkv = reduce_term(weight_term(attn_in, qkv_low, None))
    grad_attn_in = jnp.einsum("tn,kn->tk", qkv_low, full_qkv, preferred_element_type=single)
    _, back_attn_in = jax.vjp(pre_norm, states, scale_attn, gains[0])
    part_states, grad_scale_attn, grad_gain_zero = back_attn_in(
        grad_attn_in.reshape(item_count, item_slots, model_width)
    )
    grad_x = (grad_hidden + part_states).reshape(1, token_count, model_width)
    _, back_text = jax.vjp(text_split, text_proj, gains[6])
    grad_text_proj, grad_gain_six = back_text((owned_tkey, owned_tval))
    text_low = grad_text_proj.astype(narrow).reshape(item_count * text_local, 2 * model_width)
    shard_text = reduce_term(
        weight_term(text_norm.reshape(item_count * text_local, text_width), text_low, None)
    )
    grad_text_norm = jnp.einsum("tn,kn->tk", text_low, full_text, preferred_element_type=single)
    _, back_text_norm = jax.vjp(norm_gain, text_float, text_gain)
    grad_text_gain = back_text_norm(grad_text_norm.reshape(text_float.shape))[1]
    grad_modulation = jnp.concatenate(
        [grad_scale_attn, grad_gate_attn, grad_scale_ffn, grad_gate_ffn], axis=-1
    )[:, 0, :]
    shard_ada = reduce_term(
        weight_term(time_silu.astype(single), grad_modulation, lax.Precision.HIGHEST)
    )
    grad_ada_bias = jnp.sum(grad_modulation, axis=0)
    grad_gains = jnp.stack(
        [
            grad_gain_zero,
            grad_gain_one,
            grad_gain_two,
            grad_gain_three,
            grad_gain_four,
            grad_gain_five,
            grad_gain_six,
        ],
        axis=0,
    )
    final_qkv, final_out, final_text, final_gu, final_down, final_ada = (
        lax.psum(shard_qkv.astype(jnp.bfloat16), "items").astype(jnp.float32),
        lax.psum(shard_out.astype(jnp.bfloat16), "items").astype(jnp.float32),
        lax.psum(shard_text.astype(jnp.bfloat16), "items").astype(jnp.float32),
        lax.psum(shard_gu.astype(jnp.bfloat16), "items").astype(jnp.float32),
        lax.psum(shard_down.astype(jnp.bfloat16), "items").astype(jnp.float32),
        lax.psum(shard_ada.astype(jnp.bfloat16), "items").astype(jnp.float32),
    )
    total_gains, total_gate, total_bias, total_text_gain = lax.psum(
        (grad_gains, grad_cross_gate, grad_ada_bias, grad_text_gain), ("items", "rows")
    )
    return (
        output,
        grad_x,
        final_qkv,
        final_out,
        final_text,
        final_gu,
        final_down,
        final_ada,
        total_gains,
        total_gate,
        total_bias,
        total_text_gain,
    )


def norm_parts(values):
    inverse = lax.rsqrt(jnp.mean(values * values, axis=-1, keepdims=True) + epsilon)
    return values * inverse, inverse


def norm_back(unit, inverse, scaled_grad):
    return inverse * (scaled_grad - unit * jnp.mean(scaled_grad * unit, axis=-1, keepdims=True))


MESH = pl.DeviceIdType.MESH
DEPTH, BREADTH = 4, 2


def row_place():
    place = lax.axis_index("rows")
    return place // BREADTH, lax.rem(place, BREADTH)


def on_rows(line, side):
    return {"rows": line * BREADTH + side}


def greet(devices):
    barrier = pltpu.get_barrier_semaphore()
    for condition, device in devices:

        @pl.when(condition)
        def _(device=device):
            pl.semaphore_signal(barrier, inc=1, device_id=device, device_id_type=MESH)

    count = 0
    for condition, _ in devices:
        count = count + jnp.where(condition, 1, 0)
    pl.semaphore_wait(barrier, count)


def remote(source, target, send, receive, device):
    return pltpu.make_async_remote_copy(
        src_ref=source,
        dst_ref=target,
        send_sem=send,
        recv_sem=receive,
        device_id=device,
        device_id_type=MESH,
    )


def shard_of(ref, place, axis):
    return ref.at[place] if axis == 0 else ref.at[:, place]


CHUNKS = 2


def partner(kind):
    group = lax.axis_index("items")
    if kind == "core":
        return {"items": group + 1 - 2 * lax.rem(group, 2)}
    return {"items": lax.rem(group + 2, 4)}


def chunk_part(ref, chunk, start, size):
    rows = ref.shape[0] // CHUNKS
    middle = (slice(None),) * (len(ref.shape) - 2)
    return ref.at[(pl.ds(chunk * rows, rows),) + middle + (pl.ds(start, size),)]


def streams_of(width):
    first = split_lanes(width)
    streams = [(0, chunk, 0, first) for chunk in range(CHUNKS)]
    if first < width:
        streams += [(which, chunk, first, width - first) for which in range(2) for chunk in range(CHUNKS)]
    return streams


class Swaps:
    def __init__(self, pairs):
        self.arrays = tuple(array for array, _ in pairs)
        self.kinds = tuple(kind for _, kind in pairs)

    def shapes(self):
        return [jax.ShapeDtypeStruct(array.shape, array.dtype) for array in self.arrays]

    def specs(self):
        return [pl.BlockSpec(memory_space=pl.ANY)] * len(self.arrays)

    def scratch(self):
        return [pltpu.SemaphoreType.DMA((2, max(1, len(self.arrays))))]

    def partners(self, always):
        return [(always, partner(kind)) for kind in sorted(set(self.kinds))]

    def copies(self, sources, targets, semaphores):
        return [
            remote(source, target, semaphores.at[0, at], semaphores.at[1, at], partner(kind))
            for at, (source, target, kind) in enumerate(zip(sources, targets, self.kinds))
        ]


def split_lanes(width):
    return width - 128 * round(width / 128 / 6)


def gather_kernel(axis, swaps, count, own, *rest):
    number = len(swaps.kinds)
    sources, rest = rest[:number], rest[number + count :]
    whole, targets, rest = rest[0], rest[1 : 1 + number], rest[1 + number :]
    local, z_send, z_recv, x_send, x_recv, beside = rest
    line, side = row_place()
    above, below, across = on_rows(line + 1, side), on_rows(line - 1, side), on_rows(line, 1 - side)
    has_above, has_below, always = line < DEPTH - 1, line > 0, line >= 0
    greet([(has_above, above), (has_below, below), (always, across)] + swaps.partners(always))
    extra = swaps.copies(sources, targets, beside)
    for copy in extra:
        copy.start()
    streams = streams_of(own.shape[-1])
    along, over = range(CHUNKS), range(CHUNKS, len(streams))

    def block(at, stream):
        which, *piece = streams[stream]
        return chunk_part(shard_of(whole, at * BREADTH + (1 - side if which else side), axis), *piece)

    def mine(stream):
        return chunk_part(own, *streams[stream][1:])

    def pass_on(stream, source, at, way):
        return remote(
            source,
            block(at, stream),
            z_send.at[stream, way, at],
            z_recv.at[stream, at],
            below if way else above,
        )

    def cross(source, at, stream):
        slot = stream * DEPTH + at if stream < CHUNKS else CHUNKS * DEPTH + stream - CHUNKS
        return remote(source, block(at, stream), x_send.at[slot], x_recv.at[slot], across)

    def onward(stream, source):
        @pl.when(has_above)
        def _():
            pass_on(stream, source, line, 0).start()

        @pl.when(has_below)
        def _():
            pass_on(stream, source, line, 1).start()

    handed = [stream for stream in over if streams[stream][0] == 0]
    for stream in handed + list(along):
        cross(mine(stream), line, stream).start()
    for stream in list(along) + handed:
        onward(stream, mine(stream))
    keep = pltpu.make_async_copy(own, shard_of(whole, line * BREADTH + side, axis), local)
    keep.start()
    for stream in handed:
        cross(mine(stream), line, stream).wait_recv()
        onward(stream + CHUNKS, block(line, stream + CHUNKS))
    for step in range(1, DEPTH):
        for way, at, there, more in (
            (0, line - step, line - step >= 0, has_above),
            (1, line + step, line + step < DEPTH, has_below),
        ):

            @pl.when(there)
            def _(way=way, at=at, more=more):
                for stream in range(len(streams)):
                    pass_on(stream, block(at, stream), at, way).wait_recv()
                    if stream in along:
                        cross(block(at, stream), at, stream).start()

                    @pl.when(more)
                    def _(stream=stream):
                        pass_on(stream, block(at, stream), at, way).start()

    keep.wait()
    for at in range(DEPTH):
        for stream in along:
            cross(mine(stream), at, stream).wait_recv()
            cross(mine(stream), at, stream).wait_send()
        for stream in range(len(streams)):

            @pl.when(has_above & (at <= line))
            def _(at=at, stream=stream):
                pass_on(stream, block(at, stream), at, 0).wait_send()

            @pl.when(has_below & (at >= line))
            def _(at=at, stream=stream):
                pass_on(stream, block(at, stream), at, 1).wait_send()

    for stream in handed:
        cross(mine(stream), line, stream).wait_send()
    for copy in extra:
        copy.wait()


def gather_rows(block, ident, axis, after=(), swaps=()):
    ranks = DEPTH * BREADTH
    swaps = Swaps(swaps)
    shape = block.shape[:axis] + (ranks,) + block.shape[axis:]
    anywhere = pl.BlockSpec(memory_space=pl.ANY)
    wave = pltpu.SemaphoreType.DMA
    whole, *others = pl.pallas_call(
        functools.partial(gather_kernel, axis, swaps, len(after)),
        out_shape=[jax.ShapeDtypeStruct(shape, block.dtype)] + swaps.shapes(),
        in_specs=[anywhere] * (1 + len(swaps.kinds) + len(after)),
        out_specs=[anywhere] + swaps.specs(),
        scratch_shapes=[
            wave,
            wave((3 * CHUNKS, 2, DEPTH)),
            wave((3 * CHUNKS, DEPTH)),
            wave((CHUNKS * (DEPTH + 1),)),
            wave((CHUNKS * (DEPTH + 1),)),
        ]
        + swaps.scratch(),
        compiler_params=pltpu.CompilerParams(collective_id=ident, has_side_effects=True),
    )(block, *swaps.arrays, *after)
    return (whole, *others) if others else whole


def scatter_kernel(axis, swaps, count, parts, *rest):
    number = len(swaps.kinds)
    sources, rest = rest[:number], rest[number + count :]
    total, targets, rest = rest[0], rest[1 : 1 + number], rest[1 + number :]
    crossed, flow, x_send, x_recv, z_send, z_recv, beside = rest[0], rest[1:-5], *rest[-5:]
    line, side = row_place()
    above, below, across = on_rows(line + 1, side), on_rows(line - 1, side), on_rows(line, 1 - side)
    has_above, has_below, always = line < DEPTH - 1, line > 0, line >= 0
    greet([(has_above, above), (has_below, below), (always, across)] + swaps.partners(always))
    extra = swaps.copies(sources, targets, beside)
    for copy in extra:
        copy.start()
    streams = streams_of(parts.shape[-1])
    along, over = range(CHUNKS), range(CHUNKS, len(streams))
    handed = [stream for stream in over if streams[stream][0] == 1]

    def part(at, stream, turned=False):
        other, *piece = streams[stream]
        return chunk_part(shard_of(parts, at * BREADTH + (1 - side if other or turned else side), axis), *piece)

    def slot(ref, at, stream):
        chunk = streams[stream][1]
        rows = ref.shape[1] // CHUNKS
        return ref.at[at, pl.ds(chunk * rows, rows)]

    def cross(at, stream):
        place = stream * DEPTH + at
        return remote(
            part(at, stream, True), slot(crossed, at, stream), x_send.at[place], x_recv.at[place], across
        )

    def hand(stream):
        place = CHUNKS * DEPTH + stream - handed[0]
        leave, arrive = flow[12], flow[13]
        return remote(
            slot(leave, 0, stream), slot(arrive, 0, stream), x_send.at[place], x_recv.at[place], across
        )

    def held(stream, way, leaving):
        group = 0 if stream in along else 1 + streams[stream][0]
        return flow[4 * group + 2 * way + leaving]

    def moving(stream, at, way):
        return remote(
            slot(held(stream, way, 1), at, stream),
            slot(held(stream, way, 0), at, stream),
            z_send.at[stream, way, at],
            z_recv.at[stream, way, at],
            below if way else above,
        )

    def add_up(stream, at, ways, target, others=()):
        value = part(at, stream)[...].astype(jnp.float32)
        if stream in along:
            value = value + slot(crossed, at, stream)[...].astype(jnp.float32)
        for way in ways:
            value = value + slot(held(stream, way, 0), at, stream)[...].astype(jnp.float32)
        for other in others:
            value = value + other[...].astype(jnp.float32)
        target[...] = value.astype(target.dtype)

    def send_on(stream, at, way, comes):
        leaving = slot(held(stream, way, 1), at, stream)

        @pl.when(comes)
        def _():
            moving(stream, at, way).wait_recv()
            add_up(stream, at, [way], leaving)

        @pl.when(jnp.logical_not(comes))
        def _():
            add_up(stream, at, [], leaving)

        moving(stream, at, way).start()

    def finish(stream, target, others=()):
        for below_there, above_there, ways in ((True, True, [0, 1]), (True, False, [0]), (False, True, [1])):

            @pl.when((has_below == below_there) & (has_above == above_there))
            def _(ways=ways):
                for way in ways:
                    moving(stream, line, way).wait_recv()
                add_up(stream, line, ways, target, others)

    for step in range(DEPTH - 1, 0, -1):
        for at, there in ((line + step, line + step < DEPTH), (line - step, line - step >= 0)):

            @pl.when(there)
            def _(at=at):
                for stream in along:
                    cross(at, stream).start()

    for stream in along:
        cross(line, stream).start()
    for some in (over, along):
        for step in range(DEPTH - 1, 0, -1):
            for way, at, there, comes in (
                (0, line + step, line + step < DEPTH, has_below),
                (1, line - step, line - step >= 0, has_above),
            ):
                for stream in some:

                    @pl.when(there)
                    def _(way=way, at=at, comes=comes, stream=stream):
                        if stream in along:
                            cross(at, stream).wait_recv()
                        send_on(stream, at, way, comes)

        if some is over:
            for stream in handed:
                finish(stream, slot(flow[12], 0, stream))
                hand(stream).start()

    for stream in along:
        cross(line, stream).wait_recv()
        finish(stream, chunk_part(total, *streams[stream][1:]))
    for stream in handed:
        hand(stream).wait_recv()
        mate = stream - CHUNKS
        finish(mate, chunk_part(total, *streams[mate][1:]), (slot(flow[13], 0, stream),))
        hand(stream).wait_send()
    for at in range(DEPTH):
        for stream in along:
            cross(at, stream).wait_send()
        for stream in range(len(streams)):

            @pl.when(at > line)
            def _(at=at, stream=stream):
                moving(stream, at, 0).wait_send()

            @pl.when(at < line)
            def _(at=at, stream=stream):
                moving(stream, at, 1).wait_send()

    for copy in extra:
        copy.wait()


def scatter_rows(parts, ident, axis, after=(), swaps=()):
    swaps = Swaps(swaps)
    shape = parts.shape[:axis] + parts.shape[axis + 1 :]
    width = shape[-1]
    first = split_lanes(width)
    near = pl.BlockSpec(memory_space=pltpu.VMEM)
    wave = pltpu.SemaphoreType.DMA

    def slots(size, count=(DEPTH,)):
        return pltpu.VMEM(count + shape[:-1] + (size,), parts.dtype)

    flow = [slots(first)] * 4
    if first < width:
        flow = flow + [slots(width - first)] * 8 + [slots(width - first, (1,))] * 2
    total, *others = pl.pallas_call(
        functools.partial(scatter_kernel, axis, swaps, len(after)),
        out_shape=[jax.ShapeDtypeStruct(shape, jnp.float32)] + swaps.shapes(),
        in_specs=[near] + [pl.BlockSpec(memory_space=pl.ANY)] * (len(swaps.kinds) + len(after)),
        out_specs=[near] + swaps.specs(),
        scratch_shapes=[slots(first)]
        + flow
        + [wave((CHUNKS * (DEPTH + 1),))] * 2
        + [wave((3 * CHUNKS, 2, DEPTH))] * 2
        + swaps.scratch(),
        compiler_params=pltpu.CompilerParams(
            collective_id=ident, has_side_effects=True, vmem_limit_bytes=32 << 20
        ),
    )(parts, *swaps.arrays, *after)
    return (total, *others) if others else total


def sum_kernel(count, own, *rest):
    total, held, send, receive = rest[count:]
    ranks = DEPTH * BREADTH
    place = lax.axis_index("rows")
    others = [lax.rem(place + step, ranks) for step in range(1, ranks)]
    greet([(place >= 0, {"rows": other}) for other in others])

    def push(step, other, slot):
        return remote(own, held.at[slot], send.at[step], receive.at[slot], {"rows": other})

    for step, other in enumerate(others):
        push(step, other, place).start()
    held[pl.ds(place, 1)] = own[...][None]
    for step, other in enumerate(others):
        push(step, other, other).wait_recv()
    value = held[0]
    for rank in range(1, ranks):
        value = value + held[rank]
    total[...] = value
    for step, other in enumerate(others):
        push(step, other, place).wait_send()


def sum_rows(own, ident, after=()):
    ranks = DEPTH * BREADTH
    near = pl.BlockSpec(memory_space=pltpu.VMEM)
    return pl.pallas_call(
        functools.partial(sum_kernel, len(after)),
        out_shape=jax.ShapeDtypeStruct(own.shape, own.dtype),
        in_specs=[near] + [pl.BlockSpec(memory_space=pl.ANY)] * len(after),
        out_specs=near,
        scratch_shapes=[
            pltpu.VMEM((ranks,) + own.shape, own.dtype),
            pltpu.SemaphoreType.DMA((ranks,)),
            pltpu.SemaphoreType.DMA((ranks,)),
        ],
        compiler_params=pltpu.CompilerParams(collective_id=ident, has_side_effects=True),
    )(own, *after)


def final_kernel(ranks, groups, sums, swaps, own, *rest):
    number = len(swaps.kinds)
    sources, out, targets, rest = rest[:number], rest[number], rest[number + 1 : 2 * number + 1], rest[2 * number + 1 :]
    held, kept, part, h_send, h_recv, g_send, g_recv, o_send, o_recv, beside = rest
    place, group = lax.axis_index("rows"), lax.axis_index("items")
    rows = [lax.rem(place + step, ranks) for step in range(1, ranks)]
    items = [lax.rem(group + step, groups) for step in range(1, groups)]
    greet([(place >= 0, {"rows": other}) for other in rows] + [(place >= 0, {"items": other}) for other in items])
    extra = swaps.copies(sources, targets, beside)
    for copy in extra:
        copy.start()

    def push(step, other, slot):
        return remote(own.at[other], held.at[slot], h_send.at[step], h_recv.at[slot], {"rows": other})

    def swap(step, other, slot):
        return remote(part, kept.at[slot], g_send.at[step], g_recv.at[slot], {"items": other})

    def share(step, other, slot):
        return remote(out.at[place], out.at[slot], o_send.at[step], o_recv.at[slot], {"rows": other})

    for step, other in enumerate(rows):
        push(step, other, place).start()
    held[pl.ds(place, 1)] = own[pl.ds(place, 1)]
    for step, other in enumerate(rows):
        push(step, other, other).wait_recv()
    value = held[0]
    for rank in range(1, ranks):
        value = value + held[rank]
    part[...] = value
    for step, other in enumerate(items):
        swap(step, other, group).start()
    kept[pl.ds(group, 1)] = value[None]
    for step, other in enumerate(items):
        swap(step, other, other).wait_recv()
    total = kept[0, :sums]
    for item in range(1, groups):
        total = total + kept[item, :sums]
    depth = own.shape[1] - sums
    out[pl.ds(place, 1), :sums] = total[None]
    for item in range(groups):
        out[pl.ds(place, 1), sums + item * depth : sums + (item + 1) * depth] = kept[item, sums:][None]
    for step, other in enumerate(rows):
        share(step, other, place).start()
    for step, other in enumerate(rows):
        share(step, other, other).wait_recv()
    for step, other in enumerate(rows):
        push(step, other, place).wait_send()
        share(step, other, place).wait_send()
    for step, other in enumerate(items):
        swap(step, other, group).wait_send()
    for copy in extra:
        copy.wait()


def final_sums(own, sums, ident, swaps=()):
    ranks, groups = lax.axis_size("rows"), lax.axis_size("items")
    near = pl.BlockSpec(memory_space=pltpu.VMEM)
    depth = own.shape[1]
    swaps = Swaps(swaps)
    return pl.pallas_call(
        functools.partial(final_kernel, ranks, groups, sums, swaps),
        out_shape=[jax.ShapeDtypeStruct((ranks, sums + groups * (depth - sums), 128), own.dtype)] + swaps.shapes(),
        in_specs=[near] + swaps.specs(),
        out_specs=[near] + swaps.specs(),
        scratch_shapes=[
            pltpu.VMEM(own.shape, own.dtype),
            pltpu.VMEM((groups,) + own.shape[1:], own.dtype),
            pltpu.VMEM(own.shape[1:], own.dtype),
            pltpu.SemaphoreType.DMA((ranks,)),
            pltpu.SemaphoreType.DMA((ranks,)),
            pltpu.SemaphoreType.DMA((groups,)),
            pltpu.SemaphoreType.DMA((groups,)),
            pltpu.SemaphoreType.DMA((ranks,)),
            pltpu.SemaphoreType.DMA((ranks,)),
        ]
        + swaps.scratch(),
        compiler_params=pltpu.CompilerParams(collective_id=ident, has_side_effects=True),
    )(own, *swaps.arrays)


def first_kernel(ranks, own, text, total, text_out, held, local, s_send, s_recv, t_send, t_recv):
    place = lax.axis_index("rows")
    others = [lax.rem(place + step, ranks) for step in range(1, ranks)]
    features = text_out.shape[-1]

    def columns(other):
        return pl.ds(pl.multiple_of(other * features, features), features)

    keep = pltpu.make_async_copy(text.at[:, :, columns(place)], text_out.at[place], local)
    keep.start()
    greet([(place >= 0, {"rows": other}) for other in others])

    def sum_push(step, other, slot):
        return remote(own, held.at[slot], s_send.at[step], s_recv.at[slot], {"rows": other})

    def text_push(step, other, slot):
        return remote(
            text.at[:, :, columns(other)], text_out.at[slot], t_send.at[step], t_recv.at[slot], {"rows": other}
        )

    for step, other in enumerate(others):
        sum_push(step, other, place).start()
    for step, other in enumerate(others):
        text_push(step, other, place).start()
    held[pl.ds(place, 1)] = own[...][None]
    for step, other in enumerate(others):
        sum_push(step, other, other).wait_recv()
    value = held[0]
    for rank in range(1, ranks):
        value = value + held[rank]
    total[...] = value
    for step, other in enumerate(others):
        sum_push(step, other, place).wait_send()
        text_push(step, other, other).wait_recv()
        text_push(step, other, place).wait_send()
    keep.wait()


def first_transfers(own, text, ident):
    ranks = lax.axis_size("rows")
    anywhere = pl.BlockSpec(memory_space=pl.ANY)
    outs = [
        jax.ShapeDtypeStruct(own.shape, own.dtype),
        jax.ShapeDtypeStruct((ranks,) + text.shape[:-1] + (text.shape[-1] // ranks,), text.dtype),
    ]
    wave = pltpu.SemaphoreType.DMA
    return pl.pallas_call(
        functools.partial(first_kernel, ranks),
        out_shape=outs,
        in_specs=[NEAR, anywhere],
        out_specs=[NEAR, anywhere],
        scratch_shapes=[pltpu.VMEM((ranks,) + own.shape, own.dtype), wave] + [wave((ranks,))] * 4,
        compiler_params=pltpu.CompilerParams(collective_id=ident, has_side_effects=True),
    )(own, text)


def quarter_kernel(pieces, at, whole, packed):
    ranks, span = packed.shape[0], packed.shape[2] // pieces
    for rank in range(ranks):
        for piece in range(pieces):
            start = (piece * ranks + rank) * span
            packed[rank, :, piece * span : (piece + 1) * span] = whole[:, start : start + span]


def pack_quarter(whole, at, pieces, ranks):
    rows, width = whole.shape[0] // 4, whole.shape[1]
    out = (ranks, rows, width // ranks)
    return pl.pallas_call(
        functools.partial(quarter_kernel, pieces),
        grid_spec=pltpu.PrefetchScalarGridSpec(
            num_scalar_prefetch=1,
            grid=(1,),
            in_specs=[pl.BlockSpec((rows, width), lambda step, at: (at[0], 0))],
            out_specs=pl.BlockSpec(out, lambda step, at: (0, 0, 0)),
        ),
        out_shape=jax.ShapeDtypeStruct(out, whole.dtype),
        compiler_params=local_params(),
    )(at, whole)


def pack_kernel(pieces, whole, packed):
    ranks, span = packed.shape[0], packed.shape[2] // pieces
    for rank in range(ranks):
        packed[rank] = jnp.concatenate(
            [whole[:, (piece * ranks + rank) * span : (piece * ranks + rank + 1) * span] for piece in range(pieces)],
            axis=1,
        ).astype(packed.dtype)


def pack_blocks(whole, pieces, ranks, dtype):
    near = pl.BlockSpec(memory_space=pltpu.VMEM)
    return pl.pallas_call(
        functools.partial(pack_kernel, pieces),
        out_shape=jax.ShapeDtypeStruct((ranks, whole.shape[0], whole.shape[1] // ranks), dtype),
        in_specs=[near],
        out_specs=near,
        compiler_params=pltpu.CompilerParams(vmem_limit_bytes=24 << 20),
    )(whole)


def unpack_kernel(pieces, packed, whole):
    ranks, span = packed.shape[0], packed.shape[2] // pieces
    for piece in range(pieces):
        for rank in range(0, ranks, 2):
            start = (piece * ranks + rank) * span
            whole[:, start : start + 2 * span] = jnp.concatenate(
                [packed[rank + k, :, piece * span : (piece + 1) * span] for k in range(2)], axis=1
            ).astype(whole.dtype)


def unpack_blocks(packed, pieces, dtype):
    near = pl.BlockSpec(memory_space=pltpu.VMEM)
    ranks, rows, width = packed.shape
    return pl.pallas_call(
        functools.partial(unpack_kernel, pieces),
        out_shape=jax.ShapeDtypeStruct((rows, ranks * width), dtype),
        in_specs=[near],
        out_specs=near,
        compiler_params=pltpu.CompilerParams(vmem_limit_bytes=24 << 20),
    )(packed)


def halves_kernel(pieces, own, other, whole):
    ranks, half, span = own.shape[0], own.shape[1], own.shape[2] // pieces
    first = lax.rem(lax.axis_index("items"), 2) == 0
    for low in range(2):

        @pl.when(first == (low == 0))
        def _(low=low):
            for source, start in ((own, low * half), (other, (1 - low) * half)):
                for piece in range(pieces):
                    for rank in range(0, ranks, 2):
                        column = (piece * ranks + rank) * span
                        whole[start : start + half, column : column + 2 * span] = jnp.concatenate(
                            [source[rank + k, :, piece * span : (piece + 1) * span] for k in range(2)], axis=1
                        ).astype(whole.dtype)


def unpack_halves(own, other, pieces):
    near = pl.BlockSpec(memory_space=pltpu.VMEM)
    ranks, half, width = own.shape
    return pl.pallas_call(
        functools.partial(halves_kernel, pieces),
        out_shape=jax.ShapeDtypeStruct((2 * half, ranks * width), jnp.float32),
        in_specs=[near, near],
        out_specs=near,
        compiler_params=pltpu.CompilerParams(vmem_limit_bytes=32 << 20),
    )(own, other)


def gather_tokens(block, ident, swaps=()):
    whole = gather_rows(block, ident, 1, swaps=swaps)
    if not swaps:
        return whole.reshape(-1, block.shape[-1])
    return (whole[0].reshape(-1, block.shape[-1]), *whole[1:])


def scatter_tokens(partial, items, ident, swaps=()):
    ranks = lax.axis_size("rows")
    blocks = partial.astype(jnp.bfloat16).reshape(items, ranks, -1, partial.shape[-1])
    return scatter_rows(blocks, ident, 1, swaps=swaps)


NEAR = pl.BlockSpec(memory_space=pltpu.VMEM)
SCALARS = pl.BlockSpec(memory_space=pltpu.SMEM)
NT = (((1,), (1,)), ((), ()))
TN = (((0,), (0,)), ((), ()))


def local_params():
    return pltpu.CompilerParams(vmem_limit_bytes=48 << 20)


def text_item(text, item):
    block = text[:, item]
    return block.reshape(block.shape[0] * block.shape[1], block.shape[2])


def lanes_to_rows(columns, rows):
    lane = lax.broadcasted_iota(jnp.int32, (128, 128), 1)
    held = jnp.zeros((128, 128), jnp.float32)
    for place, column in enumerate(columns):
        held = jnp.where(lane == place, column, held)
    return jnp.transpose(held)[:rows]


def rows_to_lanes(rows):
    missing = jnp.zeros((128 - rows.shape[0], 128), jnp.float32)
    return jnp.transpose(jnp.concatenate([rows, missing], axis=0))


def open_kernel(
    total, states, gains, bias, text_parts, qkv,
    attn, qkv_out, text_out, proj, totals, modulation,
    own, squares, held, packed, flow, *waves,
):
    items, rows, width = states.shape
    ranks, span = qkv_out.shape[0], text_out.shape[-1] // 2
    chunks = bias.shape[0]
    tokens = proj.shape[0]
    place = lax.axis_index("rows")
    group = lax.axis_index("items")
    others = [lax.rem(place + step, ranks) for step in range(1, ranks)]
    always = place >= 0
    twin, across_y = partner("core"), partner("far")
    depth = qkv.shape[0] // 4
    mine = pl.ds(pl.multiple_of(group * depth, 16), depth)
    fars = pl.ds(pl.multiple_of(lax.rem(group + 2, 4) * depth, 16), depth)
    s_send, s_recv, a_send, a_recv, y_send, y_recv, c_send, c_recv = waves[:8]
    greet([(always, {"rows": other}) for other in others] + [(always, twin), (always, across_y)])
    text_chain = Chain(row_place(), text_out.shape[-1], flow, waves[8:12], (None,) * 4)
    chains = [
        Chain(row_place(), width, (None,) * 15, (None,) * 4, waves[12 + 4 * item : 16 + 4 * item])
        for item in range(items)
    ]

    text_chain.scatter_start(text_parts, False)
    text_chain.scatter_start(text_parts, True)
    for item in range(items):
        for chunk in range(chunks):
            at = item * chunks + chunk
            modulation[item : item + 1, chunk * 128 : (chunk + 1) * 128] = total[at : at + 1] + bias[chunk : chunk + 1]
        unit, _ = norm_unit(states[item])
        own[item] = (unit * gains[0:1] * (1.0 + modulation[item : item + 1, :width])).astype(own.dtype)
        chains[item].gather_start(own.at[item], attn.at[item])

    def push(step, other, slot):
        return remote(
            packed.at[other, mine], qkv_out.at[slot, mine], a_send.at[step], a_recv.at[slot], {"rows": other}
        )

    def pass_far(slot):
        block = qkv_out.at[slot, mine]
        return remote(block, block, y_send.at[slot], y_recv.at[slot], across_y)

    def pass_twin(which, slot):
        block = qkv_out.at[slot, fars if which else mine]
        return remote(block, block, c_send.at[which, slot], c_recv.at[which, slot], twin)

    head_span = qkv.shape[1] // (3 * ranks)
    for rank in range(ranks):
        packed[rank] = jnp.concatenate(
            [
                qkv[:, (part * ranks + rank) * head_span : (part * ranks + rank + 1) * head_span]
                for part in range(3)
            ],
            axis=1,
        )
    for step, other in enumerate(others):
        push(step, other, place).start()
    qkv_out[pl.ds(place, 1)] = packed[pl.ds(place, 1)]

    for item in range(items):
        chains[item].gather_turn(own.at[item], attn.at[item])
    text_chain.scatter_over(text_parts, 0)
    for step in range(1, DEPTH):
        for item in range(items):
            chains[item].gather_step(attn.at[item], step)
        if step == 1:
            text_chain.scatter_over(text_parts, 1)
            text_chain.scatter_over(text_parts, 2)
        text_chain.scatter_along(text_parts, step - 1)
        if step == 2:
            text_chain.scatter_hand(text_parts)
    for step, other in enumerate(others):
        push(step, other, other).wait_recv()
        pass_far(other).start()
        pass_twin(0, other).start()
    text_chain.scatter_end(text_parts, text_out)
    for item in range(items):
        chains[item].gather_end(own.at[item], attn.at[item])
    for other in others:
        pass_far(other).wait_recv()
        pass_twin(1, other).start()
    for step, other in enumerate(others):
        push(step, other, place).wait_send()
        pass_far(other).wait_send()
        for which in range(2):
            pass_twin(which, other).wait_recv()
            pass_twin(which, other).wait_send()

    weight = qkv_out[...].reshape(width, proj.shape[1])
    half = tokens // (2 * items)
    for block in range(2 * items):
        item, pair = divmod(block, 2)
        left = attn[item, pair * ranks // 2 : (pair + 1) * ranks // 2].reshape(half, width)
        proj[block * half : (block + 1) * half] = jnp.dot(left, weight, preferred_element_type=jnp.float32)
    columns = []
    for part in range(2):
        for start in range(0, tokens, 128):
            block = proj[start : start + 128, part * span : (part + 1) * span]
            columns.append(jnp.sum(block * block, axis=1, keepdims=True))
    text_rows = text_out.shape[0] // (ranks * items)
    for item in range(items):
        block = text_out[...].reshape(ranks, items, text_rows, 2 * span)[:, item, :, :span]
        block = block.reshape(ranks * text_rows, span)
        columns.append(jnp.sum(block * block, axis=1, keepdims=True))
    squares[...] = lanes_to_rows(columns, squares.shape[0])

    def sum_push(step, other, slot):
        return remote(squares, held.at[slot], s_send.at[step], s_recv.at[slot], {"rows": other})

    for step, other in enumerate(others):
        sum_push(step, other, place).start()
    held[pl.ds(place, 1)] = squares[...][None]
    for step, other in enumerate(others):
        sum_push(step, other, other).wait_recv()
    value = held[0]
    for rank in range(1, ranks):
        value = value + held[rank]
    totals[...] = value
    for step, other in enumerate(others):
        sum_push(step, other, place).wait_send()


def open_attention(total, states, gains, bias, text_parts, qkv, ident):
    items, rows, width = states.shape
    ranks, text_rows, text_width = text_parts.shape
    low, single = text_parts.dtype, jnp.float32
    tokens, depth, columns = items * ranks * rows, qkv.shape[0], qkv.shape[1] // ranks
    count = 2 * tokens // 128 + items
    squares = (-(-count // 8) * 8, 128)
    first = split_chain(text_width)
    wave = pltpu.SemaphoreType.DMA

    def slots(size, count=(DEPTH,)):
        return pltpu.VMEM(count + (text_rows, size), low)

    flow = [slots(first)] * 5 + [slots(text_width - first)] * 8 + [slots(text_width - first, ())] * 2
    scatter_waves = [wave((DEPTH + 1,))] * 2 + [wave((3, 2, DEPTH))] * 2
    gather_waves = [wave((DEPTH + 1,))] * 2 + [wave((3, 2, DEPTH)), wave((3, DEPTH))]

    def body(*refs):
        ins, outs, rest = refs[:6], refs[6:12], refs[12:]
        open_kernel(*ins, *outs, *rest[:4], rest[4:19], *rest[19:])

    return pl.pallas_call(
        body,
        out_shape=[
            jax.ShapeDtypeStruct((items, ranks, rows, width), low),
            jax.ShapeDtypeStruct((ranks, depth, columns), low),
            jax.ShapeDtypeStruct((text_rows, text_width), single),
            jax.ShapeDtypeStruct((tokens, columns), single),
            jax.ShapeDtypeStruct(squares, single),
            jax.ShapeDtypeStruct((items, bias.size), single),
        ],
        in_specs=[NEAR] * 6,
        out_specs=[NEAR] * 6,
        scratch_shapes=[
            pltpu.VMEM(states.shape, low),
            pltpu.VMEM(squares, single),
            pltpu.VMEM((ranks,) + squares, single),
            pltpu.VMEM((ranks, depth, columns), low),
        ]
        + flow
        + [wave((ranks,))] * 6
        + [wave((2, ranks))] * 2
        + scatter_waves
        + gather_waves * items,
        compiler_params=pltpu.CompilerParams(
            collective_id=ident, has_side_effects=True, vmem_limit_bytes=48 << 20
        ),
    )(total, states, gains, bias, text_parts, qkv)


def tile_lane():
    return lax.broadcasted_iota(jnp.int32, (1, 128), 1)


def swap_halves(tile):
    low = lax.rem(tile_lane(), 64) < 32
    return jnp.where(low, pltpu.roll(tile, 96, 1), pltpu.roll(tile, 32, 1))


def block_tables(tab, block, frame_lanes):
    by_row = lax.rem(tile_lane(), 32) < frame_lanes
    rows = 128 // COLS
    cosines, sines = [], []
    for row in range(rows):
        at = pl.ds(block * rows + row, 1)
        cosines.append(jnp.where(by_row, tab[0, at], tab[2, :COLS]))
        sines.append(jnp.where(by_row, tab[1, at], tab[3, :COLS]))
    return jnp.concatenate(cosines, axis=0), jnp.concatenate(sines, axis=0)


def block_inverse(inverse, block, blocks):
    lane = lax.broadcasted_iota(jnp.int32, (128, 128), 1)

    def column(place):
        return jnp.sum(jnp.where(lane == place, inverse, 0.0), axis=1, keepdims=True)

    query, key = column(block), column(blocks + block)
    return [query, jnp.where(tile_lane() < 64, query, key), key]


def attend_kernel(
    scale, width, counts, heights, text_lens, proj, totals, text, gains, text_gain, gate, w_out,
    parts, qkv, text_kv, tab, biases, text_biases,
):
    ranks, items = text.shape[0], text.shape[1]
    span = gate.shape[-1]
    heads, size = span // 64, 64
    tokens = proj.shape[0]
    blocks, item_blocks = tokens // 128, tokens // 128 // items
    seq = tokens // items
    slots = seq // ranks
    row_slots = slots // COLS
    frame_pairs = size // 8
    space_pairs = (size // 2 - frame_pairs) // 2

    place = lax.rem(tile_lane(), 32)
    frame_rate = jnp.exp(place.astype(jnp.float32) * (-math.log(10000.0) / frame_pairs))
    row_rate = jnp.exp((place - frame_pairs).astype(jnp.float32) * (-math.log(10000.0) / space_pairs))
    column_rate = jnp.exp(
        (place - frame_pairs - space_pairs).astype(jnp.float32) * (-math.log(10000.0) / space_pairs)
    )
    is_frame = place < frame_pairs
    rows = items * ranks * row_slots
    which = lax.broadcasted_iota(jnp.int32, (rows, 1), 0)
    frame_index = jnp.zeros((rows, 1), jnp.float32)
    frame_row = jnp.zeros((rows, 1), jnp.float32)
    seq_place = lax.broadcasted_iota(jnp.int32, (seq, 128), 0)
    for item in range(items):
        below = jnp.int32(0)
        bias = jnp.zeros((seq, 128), jnp.float32)
        for rank in range(ranks):
            live = counts[rank * items + item]
            for row in range(row_slots):
                index = below + row
                at = which == (item * ranks + rank) * row_slots + row
                frame_index = jnp.where(at, (index // heights[item]).astype(jnp.float32), frame_index)
                frame_row = jnp.where(at, lax.rem(index, heights[item]).astype(jnp.float32), frame_row)
            start = rank * slots
            inside = (seq_place >= start + live * COLS) & (seq_place < start + slots)
            bias = jnp.where(inside, masked_score, bias)
            below = below + live
        biases[item] = bias
        text_place = lax.broadcasted_iota(jnp.int32, text_biases.shape[1:], 0)
        text_biases[item] = jnp.where(text_place >= text_lens[item], masked_score, 0.0)
    column = lax.broadcasted_iota(jnp.int32, (COLS, 1), 0).astype(jnp.float32)
    row_angles = jnp.where(is_frame, frame_index * frame_rate, frame_row * row_rate)
    column_angles = column * column_rate
    sign = jnp.where(lax.rem(tile_lane(), 64) < 32, -1.0, 1.0)
    tab[0, :rows] = jnp.cos(row_angles)
    tab[1, :rows] = jnp.sin(row_angles) * sign
    tab[2, :COLS] = jnp.cos(column_angles)
    tab[3, :COLS] = jnp.sin(column_angles) * sign

    inverse = rows_to_lanes(lax.rsqrt(totals[...] / width + epsilon))
    for item in range(items):
        block = text_item(text, item)
        column = inverse[:, 2 * blocks + item : 2 * blocks + item + 1]
        text_kv[item] = jnp.concatenate(
            [block[:, :span] * column * text_gain[...], block[:, span:]], axis=1
        ).astype(text_kv.dtype)

    @pl.loop(0, blocks)
    def _(block):
        at = pl.ds(pl.multiple_of(block * 128, 128), 128)
        cosine, sine = block_tables(tab, block, frame_pairs + space_pairs)
        inverses = block_inverse(inverse, block, blocks)
        tiles = []
        for tile in range(3):
            lanes = slice(tile * 128, (tile + 1) * 128)
            value = proj[at, lanes] * inverses[tile] * gains[:, lanes]
            tiles.append(value * cosine + swap_halves(value) * sine)
        qkv[at] = jnp.concatenate(tiles + [proj[at, 2 * span :]], axis=1).astype(qkv.dtype)

    @pl.loop(0, blocks)
    def _(block):
        at = pl.ds(pl.multiple_of(block * 128, 128), 128)
        item = block // item_blocks
        keys_at = pl.ds(pl.multiple_of(item * seq, seq), seq)
        bias, text_bias = biases[item], text_biases[item]
        mixed = []
        for head in range(heads):
            lanes = slice(head * size, (head + 1) * size)

            def part_of(ref, rows, part):
                start = part * span + head * size
                return ref[rows, start : start + size]

            query = part_of(qkv, at, 0)

            def mix(keys, values, mask):
                scores = lax.dot_general(keys, query, NT, preferred_element_type=jnp.float32)
                scores = scores * scale + mask
                terms = jnp.exp(scores - jnp.max(scores, axis=0, keepdims=True))
                probs = terms * (1.0 / jnp.sum(terms, axis=0, keepdims=True))
                return lax.dot_general(
                    values,
                    probs.astype(jnp.bfloat16),
                    (((0,), (0,)), ((), ())),
                    preferred_element_type=jnp.float32,
                )

            out = mix(part_of(qkv, keys_at, 1), part_of(qkv, keys_at, 2), bias)
            text_keys = text_kv[item]
            cross = mix(
                text_keys[:, lanes], text_keys[:, span + head * size : span + (head + 1) * size], text_bias
            )
            mixed.append(jnp.transpose(out) + gate[:, lanes] * jnp.transpose(cross))
        combined = jnp.concatenate(mixed, axis=1).astype(jnp.bfloat16)
        parts[1][at] = combined
        parts[0][at] = jnp.dot(combined, w_out[...], preferred_element_type=jnp.float32).astype(jnp.bfloat16)


def attend(proj, totals, text, gains, text_gain, gate, w_out, counts, heights, text_lens, head_size):
    tokens, span, width = proj.shape[0], gate.shape[-1], w_out.shape[1]
    items, text_rows = text.shape[1], text.shape[0] * text.shape[2]
    low = jnp.bfloat16

    def body(*refs):
        ins, outs, scratch = refs[:10], refs[10:15], refs[15:]
        attend_kernel(
            head_size**-0.5, width, *ins, (outs[0], outs[1]), outs[2], outs[3], outs[4], *scratch
        )

    return pl.pallas_call(
        body,
        out_shape=[
            jax.ShapeDtypeStruct((tokens, width), low),
            jax.ShapeDtypeStruct((tokens, span), low),
            jax.ShapeDtypeStruct((tokens, 3 * span), low),
            jax.ShapeDtypeStruct((items, text_rows, 2 * span), low),
            jax.ShapeDtypeStruct((4, max(tokens // COLS, COLS), 128), jnp.float32),
        ],
        in_specs=[SCALARS] * 3 + [NEAR] * 7,
        out_specs=[NEAR] * 5,
        scratch_shapes=[
            pltpu.VMEM((items, tokens // items, 128), jnp.float32),
            pltpu.VMEM((items, text_rows, 128), jnp.float32),
        ],
        compiler_params=local_params(),
    )(counts, heights, text_lens, proj, totals, text, gains, text_gain, gate, w_out)


def attend_back_kernel(
    scale, width, counts, text_lens, grad, w_out, qkv, text_kv, tab, proj, totals, text, gains, text_gain, gate,
    scaled, grad_value, text_scaled, text_value, sums, gain_sums, gate_sums,
    grad_query, key_sum, value_sum, text_key_sum, text_value_sum, biases, text_biases,
):
    ranks, items = text.shape[0], text.shape[1]
    span = gate.shape[-1]
    heads, size = span // 64, 64
    tokens = proj.shape[0]
    blocks, item_blocks = tokens // 128, tokens // 128 // items
    seq = tokens // items
    slots = seq // ranks
    frame_pairs = size // 8
    space_pairs = (size // 2 - frame_pairs) // 2
    seq_place = lax.broadcasted_iota(jnp.int32, (seq, 128), 0)
    for item in range(items):
        bias = jnp.zeros((seq, 128), jnp.float32)
        for rank in range(ranks):
            start = rank * slots
            live = counts[rank * items + item]
            inside = (seq_place >= start + live * COLS) & (seq_place < start + slots)
            bias = jnp.where(inside, masked_score, bias)
        biases[item] = bias
        text_place = lax.broadcasted_iota(jnp.int32, text_biases.shape[1:], 0)
        text_biases[item] = jnp.where(text_place >= text_lens[item], masked_score, 0.0)
    key_sum[...] = jnp.zeros_like(key_sum)
    value_sum[...] = jnp.zeros_like(value_sum)
    text_key_sum[...] = jnp.zeros_like(text_key_sum)
    text_value_sum[...] = jnp.zeros_like(text_value_sum)
    gate_sums[...] = jnp.zeros_like(gate_sums)
    gain_sums[...] = jnp.zeros_like(gain_sums)

    @pl.loop(0, blocks)
    def _(block):
        at = pl.ds(pl.multiple_of(block * 128, 128), 128)
        item = block // item_blocks
        keys_at = pl.ds(pl.multiple_of(item * seq, seq), seq)
        bias, text_bias = biases[item], text_biases[item]
        text_keys = text_kv[item]
        grad_combined = lax.dot_general(grad[at], w_out[...], NT, preferred_element_type=jnp.float32)
        self_low = grad_combined.astype(jnp.bfloat16)
        cross_low = (gate[...] * grad_combined).astype(jnp.bfloat16)
        queries, crossed = [], []
        for head in range(heads):
            lanes = slice(head * size, (head + 1) * size)
            query = qkv[at, lanes]

            def back(keys, values, low_grad, mask, key_total, value_total, rows):
                scores = lax.dot_general(keys, query, NT, preferred_element_type=jnp.float32)
                scores = scores * scale + mask
                terms = jnp.exp(scores - jnp.max(scores, axis=0, keepdims=True))
                probs = terms * (1.0 / jnp.sum(terms, axis=0, keepdims=True))
                grad_probs = lax.dot_general(values, low_grad, NT, preferred_element_type=jnp.float32)
                inner = jnp.sum(probs * grad_probs, axis=0, keepdims=True)
                score_low = (probs * (grad_probs - inner)).astype(jnp.bfloat16)
                probs_low = probs.astype(jnp.bfloat16)
                key_total[head, rows] += jnp.dot(score_low, query, preferred_element_type=jnp.float32)
                value_total[head, rows] += jnp.dot(probs_low, low_grad, preferred_element_type=jnp.float32)
                to_query = lax.dot_general(
                    keys, score_low, (((0,), (0,)), ((), ())), preferred_element_type=jnp.float32
                )
                return to_query, probs_low

            to_query, _ = back(
                qkv[keys_at, span + head * size : span + (head + 1) * size],
                qkv[keys_at, 2 * span + head * size : 2 * span + (head + 1) * size],
                self_low[:, lanes],
                bias,
                key_sum,
                value_sum,
                keys_at,
            )
            text_values = text_keys[:, span + head * size : span + (head + 1) * size]
            text_rows = pl.ds(pl.multiple_of(item * 128, 128), 128)
            cross_query, cross_probs = back(
                text_keys[:, lanes],
                text_values,
                cross_low[:, lanes],
                text_bias,
                text_key_sum,
                text_value_sum,
                text_rows,
            )
            crossed.append(
                jnp.transpose(
                    lax.dot_general(
                        text_values, cross_probs, (((0,), (0,)), ((), ())), preferred_element_type=jnp.float32
                    )
                )
            )
            queries.append(jnp.transpose(to_query + cross_query))
        grad_query[at] = jnp.concatenate(queries, axis=1) * scale
        gate_sums[...] += jnp.sum(
            grad_combined * jnp.concatenate(crossed, axis=1), axis=0, keepdims=True
        )

    inverse = rows_to_lanes(lax.rsqrt(totals[...] / width + epsilon))
    columns = [[], []]
    for block in range(blocks):
        at = slice(block * 128, (block + 1) * 128)
        cosine, sine = block_tables(tab, block, frame_pairs + space_pairs)
        inverses = block_inverse(inverse, block, blocks)
        keys = jnp.concatenate([key_sum[head, at] for head in range(heads)], axis=1) * scale
        both = jnp.concatenate([grad_query[at], keys], axis=1)
        products = []
        for tile in range(3):
            lanes = slice(tile * 128, (tile + 1) * 128)
            value = both[:, lanes]
            value = value * cosine - swap_halves(value) * sine
            unit = proj[at, lanes] * inverses[tile]
            gain_sums[0:1, lanes] += jnp.sum(value * unit, axis=0, keepdims=True)
            value = value * gains[:, lanes]
            scaled[at, lanes] = value
            products.append(value * unit)
        first = tile_lane() < 64
        query_part = products[0] + jnp.where(first, products[1], 0.0)
        key_part = products[2] + jnp.where(first, 0.0, products[1])
        columns[0].append(jnp.sum(query_part, axis=1, keepdims=True))
        columns[1].append(jnp.sum(key_part, axis=1, keepdims=True))
        grad_value[at] = jnp.concatenate([value_sum[head, at] for head in range(heads)], axis=1).astype(
            grad_value.dtype
        )
    for item in range(items):
        at = slice(item * 128, (item + 1) * 128)
        unit = text_item(text, item)[:, :span] * inverse[:, 2 * blocks + item : 2 * blocks + item + 1]
        value = jnp.concatenate([text_key_sum[head, at] for head in range(heads)], axis=1) * scale
        gain_sums[1:2, :span] += jnp.sum(value * unit, axis=0, keepdims=True)
        value = value * text_gain[...]
        text_scaled[at] = value
        text_value[at] = jnp.concatenate([text_value_sum[head, at] for head in range(heads)], axis=1).astype(
            text_value.dtype
        )
        columns[1].append(jnp.sum(value * unit, axis=1, keepdims=True))
    sums[...] = lanes_to_rows(columns[0] + columns[1], sums.shape[0])


def attend_back(
    grad, w_out, qkv, text_kv, tab, proj, totals, text, gains, text_gain, gate, counts, text_lens, head_size, after
):
    tokens, span, width = proj.shape[0], gate.shape[-1], w_out.shape[1]
    items, text_rows = text.shape[1], text.shape[0] * text.shape[2]
    heads = span // head_size
    low, single = jnp.bfloat16, jnp.float32

    def body(*refs):
        attend_back_kernel(head_size**-0.5, width, *refs[:13], *refs[13 + len(after) :])

    return pl.pallas_call(
        body,
        out_shape=[
            jax.ShapeDtypeStruct((tokens, 2 * span), single),
            jax.ShapeDtypeStruct((tokens, span), low),
            jax.ShapeDtypeStruct((items * text_rows, span), single),
            jax.ShapeDtypeStruct((items * text_rows, span), low),
            jax.ShapeDtypeStruct(totals.shape, single),
            jax.ShapeDtypeStruct((8, 2 * span), single),
            jax.ShapeDtypeStruct((1, span), single),
        ],
        in_specs=[SCALARS] * 2 + [NEAR] * 11 + [pl.BlockSpec(memory_space=pl.ANY)] * len(after),
        out_specs=[NEAR] * 7,
        scratch_shapes=[
            pltpu.VMEM((tokens, span), single),
            pltpu.VMEM((heads, tokens, head_size), single),
            pltpu.VMEM((heads, tokens, head_size), single),
            pltpu.VMEM((heads, items * text_rows, head_size), single),
            pltpu.VMEM((heads, items * text_rows, head_size), single),
            pltpu.VMEM((items, tokens // items, 128), single),
            pltpu.VMEM((items, text_rows, 128), single),
        ],
        compiler_params=local_params(),
    )(counts, text_lens, grad, w_out, qkv, text_kv, tab, proj, totals, text, gains, text_gain, gate, *after)


def project_back_kernel(
    width, proj, totals, sums, scaled, grad_value, text, text_scaled, text_value, attn, weight, rows_gu,
    parts, text_low, half, got_gu,
    qkv_low, grad_weight, got, send, receive,
):
    items, span = text.shape[1], grad_value.shape[-1]
    tokens = proj.shape[0]
    blocks = tokens // 128
    core = core_bit()
    twin, across_y = partner("core"), partner("far")
    always = lax.axis_index("rows") >= 0
    greet([(always, twin), (always, across_y)])
    far = remote(rows_gu, got_gu, send.at[0], receive.at[0], across_y)
    far.start()
    inverse = rows_to_lanes(lax.rsqrt(totals[...] / width + epsilon))
    means = rows_to_lanes(sums[...] / width)
    first = tile_lane() < 64
    for block in range(blocks):
        at = slice(block * 128, (block + 1) * 128)

        def by_tile(columns):
            query = columns[:, block : block + 1]
            key = columns[:, blocks + block : blocks + block + 1]
            return [query, jnp.where(first, query, key), key]

        inverses, mean = by_tile(inverse), by_tile(means)
        tiles = []
        for tile in range(3):
            lanes = slice(tile * 128, (tile + 1) * 128)
            unit = proj[at, lanes] * inverses[tile]
            tiles.append((inverses[tile] * (scaled[at, lanes] - unit * mean[tile])).astype(qkv_low.dtype))
        qkv_low[at] = jnp.concatenate(tiles + [grad_value[at]], axis=1)
    for item in range(items):
        at = slice(item * 128, (item + 1) * 128)
        place = 2 * blocks + item
        column, mean = inverse[:, place : place + 1], means[:, place : place + 1]
        unit = text_item(text, item)[:, :span] * column
        low = (column * (text_scaled[at] - unit * mean)).astype(text_low.dtype)
        low = jnp.concatenate([low, text_value[at]], axis=1)
        text_low[:, item] = low.reshape(text_low.shape[0], text_low.shape[2], 2 * span)

    quarter = width // 4

    @pl.loop(0, 4)
    def _(tile):
        left = attn[:, :, :, pl.ds(pl.multiple_of(tile * quarter, 128), quarter)].reshape(tokens, quarter)
        out = lax.dot_general(left, qkv_low[...], TN, preferred_element_type=jnp.float32)
        grad_weight[pl.ds(2 * tile, 2)] = out.astype(grad_weight.dtype).reshape((2,) + grad_weight.shape[1:])

    swap_halves_of = remote(grad_weight.at[:, 1 - core], got, send.at[1], receive.at[1], twin)
    swap_halves_of.start()
    groups = parts.shape[1] // 2

    @pl.loop(0, 2 * items)
    def _(block):
        item, pair = block // 2, lax.rem(block, 2)
        rows = tokens // (2 * items)
        low = qkv_low[pl.ds(pl.multiple_of(block * rows, rows), rows)]

        @pl.loop(0, 4)
        def _(tile):
            lanes = pl.ds(pl.multiple_of(tile * quarter, 128), quarter)
            out = lax.dot_general(low, weight[lanes], NT, preferred_element_type=jnp.float32)
            parts[item, pl.ds(pair * groups, groups), :, lanes] = out.astype(parts.dtype).reshape(
                groups, parts.shape[2], quarter
            )

    swap_halves_of.wait()
    mine = grad_weight[:, pl.ds(core, 1)][:, 0].astype(jnp.float32)
    half[...] = (mine + got[...].astype(jnp.float32)).astype(half.dtype)
    far.wait()


def project_back(
    proj, totals, sums, scaled, grad_value, text, text_scaled, text_value, attn, weight, rows_gu, ident
):
    low = jnp.bfloat16
    items, ranks, _, width = attn.shape
    halves = (ranks, 2, width // ranks // 2, proj.shape[1])
    half = (ranks,) + halves[2:]
    anywhere = pl.BlockSpec(memory_space=pl.ANY)
    return pl.pallas_call(
        functools.partial(project_back_kernel, width),
        out_shape=[
            jax.ShapeDtypeStruct(attn.shape, low),
            jax.ShapeDtypeStruct(text.shape, low),
            jax.ShapeDtypeStruct(half, low),
            jax.ShapeDtypeStruct(rows_gu.shape, low),
        ],
        in_specs=[NEAR] * 10 + [anywhere],
        out_specs=[NEAR] * 3 + [anywhere],
        scratch_shapes=[
            pltpu.VMEM(proj.shape, low),
            pltpu.VMEM(halves, low),
            pltpu.VMEM(half, low),
            pltpu.SemaphoreType.DMA((2,)),
            pltpu.SemaphoreType.DMA((2,)),
        ],
        compiler_params=pltpu.CompilerParams(
            collective_id=ident, has_side_effects=True, vmem_limit_bytes=48 << 20
        ),
    )(proj, totals, sums, scaled, grad_value, text, text_scaled, text_value, attn, weight, rows_gu)


SUM_DEPTH = 16


def finish_kernel(
    grad, states, grad_middle, modulation, gains, vectors, gain_sums, gate_sums, text_gain, time, grad_x, small
):
    items, _, width = states.shape
    ranks = small.shape[0]
    place = lax.axis_index("rows")
    scales, zero = [], jnp.zeros((1, width), jnp.float32)
    for item in range(items):
        unit, inverse = norm_unit(states[item])
        value = grad[item]
        scales.append(jnp.sum(value * (unit * gains[0:1]), axis=0, keepdims=True))
        value = value * (1.0 + modulation[item : item + 1, :width])
        zero = zero + jnp.sum(value * unit, axis=0, keepdims=True)
        value = value * gains[0:1]
        value = inverse * (value - unit * jnp.mean(value * unit, axis=-1, keepdims=True))
        grad_x[item] = grad_middle[item] + value

    def spread(part):
        size = part.shape[1]
        owner = lax.broadcasted_iota(jnp.int32, (1, ranks * size), 1) // size
        return jnp.where(owner == place, jnp.concatenate([part] * ranks, axis=1), 0.0)

    span = gate_sums.shape[1]
    rows = [
        zero,
        spread(gain_sums[0:1, :span]),
        spread(gain_sums[0:1, span:]),
        vectors[8:9],
        vectors[7:8],
        vectors[6:7],
        spread(gain_sums[1:2, :span]),
        spread(text_gain[...]),
        spread(gate_sums[...]),
    ]
    number = 0
    for row in rows:
        for start in range(0, row.shape[1], 128):
            rank, depth = divmod(number, SUM_DEPTH)
            small[rank, depth : depth + 1] = row[:, start : start + 128]
            number += 1
    for item in range(items):
        kinds = (scales[item], vectors[4 + item : 5 + item], vectors[2 + item : 3 + item], vectors[item : item + 1])
        for which, row in enumerate(kinds):
            for at in range(width // 128):
                depth = SUM_DEPTH + at
                small[item * 4 + which, depth : depth + 1] = row[:, at * 128 : (at + 1) * 128]
    for rank in range(ranks):
        small[rank, SUM_DEPTH + width // 128 :] = jnp.where(rank == place, time[...], 0.0)


def finish(grad, states, grad_middle, modulation, gains, vectors, gain_sums, gate_sums, text_gain, time):
    ranks, width = lax.axis_size("rows"), states.shape[-1]
    depth = SUM_DEPTH + width // 128 + time.shape[0]
    return pl.pallas_call(
        finish_kernel,
        out_shape=[
            jax.ShapeDtypeStruct(states.shape, jnp.float32),
            jax.ShapeDtypeStruct((ranks, depth, 128), jnp.float32),
        ],
        in_specs=[NEAR] * 10,
        out_specs=[NEAR] * 2,
        compiler_params=local_params(),
    )(grad, states, grad_middle, modulation, gains, vectors, gain_sums, gate_sums, text_gain, time)


def join_kernel(bit, own, other, out):
    mine = pl.program_id(0) == bit()

    @pl.when(mine)
    def _():
        out[0] = own[...].astype(out.dtype)

    @pl.when(jnp.logical_not(mine))
    def _():
        out[0] = other[...].astype(out.dtype)


def join_rows(own, other, bit, dtype):
    rows, width = own.shape
    step = min(rows, 128)
    near = pl.BlockSpec((step, width), lambda half, at: (at, 0))
    return pl.pallas_call(
        functools.partial(join_kernel, bit),
        grid=(2, rows // step),
        out_shape=jax.ShapeDtypeStruct((2, rows, width), dtype),
        in_specs=[near, near],
        out_specs=pl.BlockSpec((1, step, width), lambda half, at: (half, at, 0)),
        compiler_params=local_params(),
    )(own, other)


def core_bit():
    return lax.rem(lax.axis_index("items"), 2)


def far_bit():
    return lax.axis_index("items") // 2


def join_blocks(own, other, bit):
    ranks, rows, width = own.shape
    block = pl.BlockSpec((1, rows, width), lambda rank: (rank, 0, 0))

    def kernel(one, two, out):
        mine = bit()
        for half in range(2):

            @pl.when(mine == half)
            def _(half=half):
                out[0, half * rows : (half + 1) * rows] = one[0]
                out[0, (1 - half) * rows : (2 - half) * rows] = two[0]

    return pl.pallas_call(
        kernel,
        grid=(ranks,),
        out_shape=jax.ShapeDtypeStruct((ranks, 2 * rows, width), own.dtype),
        in_specs=[block, block],
        out_specs=pl.BlockSpec((1, 2 * rows, width), lambda rank: (rank, 0, 0)),
        compiler_params=local_params(),
    )(own, other)


ORDER = (
    "gs", "wf", "sf", "wn", "sn", "t", "b0", "g1", "b1", "b2", "a0", "g2",
    "a1", "h", "g3", "a2", "ge", "se",
)
LAST_ORDER = (
    "gs", "wf", "sf", "wn", "sn", "t", "d0", "b0", "d1", "g1", "b1", "b2",
    "u0", "a0", "u1", "g2", "a1", "u2", "h", "g3", "u3", "c", "a2", "ge",
    "se",
)
END_ORDER = (
    "gs", "t", "g1", "y", "g2", "g3", "ge",
)


def split_chain(width):
    return width - 128 * round(width / 384)


class Chain:
    def __init__(self, place, width, flow, scatter_waves, gather_waves):
        self.line, self.side = place
        line = self.line
        self.across = on_rows(line, 1 - self.side)
        self.ways = (on_rows(line + 1, self.side), on_rows(line - 1, self.side))
        self.more = (line < DEPTH - 1, line > 0)
        low = line < 2
        self.pair = jnp.where(low, 1, 0)
        self.order = (jnp.where(low, 3, 0), jnp.where(low, 2, 1), line + 1 - 2 * lax.rem(line, 2))
        even = lax.rem(line, 2) == 0
        self.upward = (low, low, even)
        first = split_chain(width)
        self.pieces = ((0, 0, first), (0, first, width - first), (1, first, width - first))
        self.crossed, self.flow = flow[0], flow[1:]
        self.x_send, self.x_recv, self.z_send, self.z_recv = scatter_waves
        self.gx_send, self.gx_recv, self.gz_send, self.gz_recv = gather_waves

    def shard(self, ref, at, stream, turned=False):
        which, start, size = self.pieces[stream]
        other = which or turned
        return ref.at[at * BREADTH + (1 - self.side if other else self.side), :, pl.ds(start, size)]


    def cross(self, parts, at):
        return remote(
            self.shard(parts, at, 0, True), self.crossed.at[at], self.x_send.at[at], self.x_recv.at[at], self.across
        )

    def hand(self):
        leave, arrive = self.flow[12], self.flow[13]
        return remote(leave, arrive, self.x_send.at[DEPTH], self.x_recv.at[DEPTH], self.across)

    def moving(self, stream, at, way):
        return remote(
            self.flow[4 * stream + 2 * way + 1].at[at],
            self.flow[4 * stream + 2 * way].at[at],
            self.z_send.at[stream, way, at],
            self.z_recv.at[stream, way, at],
            self.ways[way],
        )

    def add_up(self, parts, stream, at, ways, target, others=()):
        value = self.shard(parts, at, stream)[...].astype(jnp.float32)
        if stream == 0:
            value = value + self.crossed[at].astype(jnp.float32)
        for way in ways:
            value = value + self.flow[4 * stream + 2 * way][at].astype(jnp.float32)
        for other in others:
            value = value + other[...].astype(jnp.float32)
        target[...] = value.astype(target.dtype)

    def send_on(self, parts, stream, number):
        at = self.order[number]
        for way in range(2):
            going = self.upward[number] if way == 0 else jnp.logical_not(self.upward[number])
            comes = self.more[1 - way]
            leaving = self.flow[4 * stream + 2 * way + 1].at[at]

            @pl.when(going & comes)
            def _(way=way, leaving=leaving):
                self.moving(stream, at, way).wait_recv()
                self.add_up(parts, stream, at, [way], leaving)

            @pl.when(going & jnp.logical_not(comes))
            def _(leaving=leaving):
                self.add_up(parts, stream, at, [], leaving)

            @pl.when(going)
            def _(way=way):
                self.moving(stream, at, way).start()

    def finish(self, parts, stream, target, others=()):
        for above_there, below_there, ways in ((True, True, [0, 1]), (False, True, [0]), (True, False, [1])):

            @pl.when((self.more[0] == above_there) & (self.more[1] == below_there))
            def _(ways=ways):
                for way in ways:
                    self.moving(stream, self.line, way).wait_recv()
                self.add_up(parts, stream, self.line, ways, target, others)

    def scatter_start(self, parts, near):
        for at in (self.order[2], self.line) if near else self.order[:2]:
            self.cross(parts, at).start()

    def scatter_over(self, parts, number):
        for stream in (1, 2):
            self.send_on(parts, stream, number)

    def scatter_along(self, parts, number):
        self.cross(parts, self.order[number]).wait_recv()
        self.send_on(parts, 0, number)

    def scatter_hand(self, parts):
        self.finish(parts, 2, self.flow[12])
        self.hand().start()

    def scatter_end(self, parts, total):
        first = self.pieces[0][2]
        self.cross(parts, self.line).wait_recv()
        self.finish(parts, 0, total.at[:, pl.ds(0, first)])
        self.hand().wait_recv()
        self.finish(parts, 1, total.at[:, pl.ds(*self.pieces[1][1:])], (self.flow[13],))
        self.hand().wait_send()
        for at in range(DEPTH):
            self.cross(parts, at).wait_send()
        for number in range(3):
            for way in range(2):
                going = self.upward[number] if way == 0 else jnp.logical_not(self.upward[number])

                @pl.when(going)
                def _(number=number, way=way):
                    for stream in range(3):
                        self.moving(stream, self.order[number], way).wait_send()


    def mine(self, own, stream):
        return own.at[:, pl.ds(*self.pieces[stream][1:])]

    def pass_on(self, whole, stream, source, at, way):
        return remote(
            source,
            self.shard(whole, at, stream),
            self.gz_send.at[stream, way, at],
            self.gz_recv.at[stream, at],
            self.ways[way],
        )

    def give(self, whole, stream, source, at):
        slot = DEPTH if stream else at
        return remote(source, self.shard(whole, at, stream), self.gx_send.at[slot], self.gx_recv.at[slot], self.across)

    def onward(self, whole, stream, source):
        for way in range(2):

            @pl.when(self.more[way])
            def _(way=way):
                self.pass_on(whole, stream, source, self.line, way).start()

    def gather_start(self, own, whole):
        self.give(whole, 1, self.mine(own, 1), self.line).start()
        self.give(whole, 0, self.mine(own, 0), self.line).start()
        for stream in range(2):
            self.onward(whole, stream, self.mine(own, stream))
        whole[self.line * BREADTH + self.side] = own[...]

    def gather_turn(self, own, whole):
        self.give(whole, 1, self.mine(own, 1), self.line).wait_recv()
        self.onward(whole, 2, self.shard(whole, self.line, 2))

    def gather_step(self, whole, step):
        line = self.line
        for way, at, there in ((0, line - step, line - step >= 0), (1, line + step, line + step < DEPTH)):

            @pl.when(there)
            def _(way=way, at=at):
                for stream in range(3):
                    block = self.shard(whole, at, stream)
                    self.pass_on(whole, stream, block, at, way).wait_recv()
                    if stream == 0:
                        self.give(whole, 0, block, at).start()

                    @pl.when(self.more[way])
                    def _(stream=stream, block=block):
                        self.pass_on(whole, stream, block, at, way).start()

    def gather_end(self, own, whole):
        for at in range(DEPTH):
            self.give(whole, 0, self.mine(own, 0), at).wait_recv()
            self.give(whole, 0, self.mine(own, 0), at).wait_send()
            for stream in range(3):
                for way, holds in ((0, at <= self.line), (1, at >= self.line)):

                    @pl.when(self.more[way] & holds)
                    def _(at=at, stream=stream, way=way):
                        self.pass_on(whole, stream, self.shard(whole, at, stream), at, way).wait_send()

        self.give(whole, 1, self.mine(own, 1), self.line).wait_send()


def norm_unit(values):
    inverse = lax.rsqrt(jnp.mean(values * values, axis=-1, keepdims=True) + epsilon)
    return values * inverse, inverse


def feed_forward_kernel(
    parts, states, cotangent, live, modulation, gains, gu_part, w_down,
    output, grad_middle, ffn_in, inner_act, ffn_low, gate_up_low, projected_low, vectors, sum_gu, half_down,
    gate_up, projected, middle, result, own, partial, w_gu, grad_gu, grad_down, got_gu, got_down, half_gu,
    far_gu, swap_send, swap_recv, *rest,
):
    items = states.shape[0]
    width, hidden = states.shape[2], w_down.shape[0]
    rows = states.shape[1]
    half = 4 * rows
    flows, waves = rest[: 15 * items], rest[15 * items :]
    place = row_place()
    line = place[0]
    chains = [
        Chain(place, width, flows[15 * item : 15 * item + 15], waves[8 * item : 8 * item + 4], waves[8 * item + 4 : 8 * item + 8])
        for item in range(items)
    ]
    one = chains[0]
    core, far = core_bit(), far_bit()
    twin, across_y = partner("core"), partner("far")
    greet(
        [(one.more[0], one.ways[0]), (one.more[1], one.ways[1]), (line >= 0, one.across)]
        + [(line >= 0, twin), (line >= 0, across_y)]
    )

    def quarter_on(number):
        which = 2 * core + (far if number < 2 else 1 - far)
        block = w_gu.at[:, which]
        return remote(block, block, swap_send.at[number], swap_recv.at[number], across_y if number == 0 else twin)

    w_gu[:, 2 * core + far] = gu_part[...]
    quarter_on(0).start()
    quarter_on(1).start()
    vectors[...] = jnp.zeros_like(vectors)

    def scale_of(item, which):
        return modulation[item : item + 1, which * width : (which + 1) * width]

    def over_rows(values):
        return jnp.sum(values, axis=0, keepdims=True)

    def middle_of(item):
        projected[item] = result[item]
        unit, _ = norm_unit(projected[item])
        middle[item] = states[item] + jnp.tanh(scale_of(item, 1)) * (unit * gains[3:4])
        unit, _ = norm_unit(middle[item])
        own[item] = (unit * gains[4:5] * (1.0 + scale_of(item, 2))).astype(own.dtype)

    def outcome(item):
        mask = live[item][:, 0:1]
        gate = jnp.tanh(scale_of(item, 3))
        unit, inverse = norm_unit(result[item])
        normed = unit * gains[5:6]
        output[item] = mask * (middle[item] + gate * normed)
        grad = mask * cotangent[item]
        vectors[item : item + 1] = (1.0 - gate * gate) * over_rows(grad * normed)
        grad = gate * grad
        vectors[6:7] += over_rows(grad * unit)
        grad = grad * gains[5:6]
        grad = inverse * (grad - unit * jnp.mean(grad * unit, axis=-1, keepdims=True))
        own[items + item] = grad.astype(own.dtype)

    def back_to_attention(item):
        unit, inverse = norm_unit(middle[item])
        grad = result[item]
        vectors[2 + item : 3 + item] = over_rows(grad * (unit * gains[4:5]))
        grad = grad * (1.0 + scale_of(item, 2))
        vectors[7:8] += over_rows(grad * unit)
        grad = grad * gains[4:5]
        grad = inverse * (grad - unit * jnp.mean(grad * unit, axis=-1, keepdims=True))
        grad = live[item][:, 0:1] * cotangent[item] + grad
        grad_middle[item] = grad
        gate = jnp.tanh(scale_of(item, 1))
        unit, inverse = norm_unit(projected[item])
        vectors[4 + item : 5 + item] = (1.0 - gate * gate) * over_rows(grad * (unit * gains[3:4]))
        grad = gate * grad
        vectors[8:9] += over_rows(grad * unit)
        grad = grad * gains[3:4]
        grad = inverse * (grad - unit * jnp.mean(grad * unit, axis=-1, keepdims=True))
        own[2 * items + item] = grad.astype(own.dtype)

    def pair_of(near):
        return jnp.where(near, 1 - one.pair, one.pair)

    def forward(item, near):
        pair = pair_of(near)
        at = pl.ds(pl.multiple_of(item * 2 * half + pair * half, half), half)
        tokens = ffn_in[item, pl.ds(pair * 4, 4)].reshape(half, width)

        @pl.loop(0, hidden // 256)
        def _(tile):
            lanes = pl.ds(pl.multiple_of(tile * 256, 256), 256)
            up_lanes = pl.ds(pl.multiple_of(hidden + tile * 256, 256), 256)
            gate = jnp.dot(tokens, w_gu[:, :, :, lanes].reshape(width, 256), preferred_element_type=jnp.float32)
            up = jnp.dot(tokens, w_gu[:, :, :, up_lanes].reshape(width, 256), preferred_element_type=jnp.float32)
            gate_up[at, lanes] = gate
            gate_up[at, up_lanes] = up
            inner_act[at, lanes] = (gate * (1.0 / (1.0 + jnp.exp(-gate))) * up).astype(inner_act.dtype)

        inner = inner_act[at]

        @pl.loop(0, width // 256)
        def _(tile):
            lanes = pl.ds(pl.multiple_of(tile * 256, 256), 256)
            out = jnp.dot(inner, w_down[:, lanes], preferred_element_type=jnp.float32)
            partial[item, pl.ds(pair * 4, 4), :, lanes] = out.astype(partial.dtype).reshape(4, rows, 256)

    def backward(item, near):
        pair = pair_of(near)
        at = pl.ds(pl.multiple_of(item * 2 * half + pair * half, half), half)
        grads = ffn_low[item, pl.ds(pair * 4, 4)].reshape(half, width)

        @pl.loop(0, hidden // 256)
        def _(tile):
            lanes = pl.ds(pl.multiple_of(tile * 256, 256), 256)
            up_lanes = pl.ds(pl.multiple_of(hidden + tile * 256, 256), 256)
            grad = lax.dot_general(grads, w_down[lanes], NT, preferred_element_type=jnp.float32)
            gate, up = gate_up[at, lanes], gate_up[at, up_lanes]
            sigmoid = 1.0 / (1.0 + jnp.exp(-gate))
            gate_up_low[at, lanes] = (grad * up * sigmoid * (1.0 + gate * (1.0 - sigmoid))).astype(gate_up_low.dtype)
            gate_up_low[at, up_lanes] = (grad * (gate * sigmoid)).astype(gate_up_low.dtype)

        low = gate_up_low[at]

        @pl.loop(0, 4)
        def _(tile):
            lanes = pl.ds(pl.multiple_of(tile * (width // 4), 128), width // 4)
            weight = w_gu[pl.ds(tile * 2, 2)].reshape(width // 4, 2 * hidden)
            out = lax.dot_general(low, weight, NT, preferred_element_type=jnp.float32)
            partial[item, pl.ds(pair * 4, 4), :, lanes] = out.astype(partial.dtype).reshape(4, rows, width // 4)

    def down_part(half):
        at = slice(half * 256, (half + 1) * 256)
        left = inner_act[:, at]
        right = ffn_low[...].reshape(left.shape[0], width)
        grad_down[half] = lax.dot_general(left, right, TN, preferred_element_type=jnp.float32).astype(grad_down.dtype)

    def gu_columns(tile):
        lanes = slice(tile * (width // 4), (tile + 1) * (width // 4))
        left = ffn_in[:, :, :, lanes].reshape(gate_up_low.shape[0], width // 4)
        out = lax.dot_general(left, gate_up_low[...], TN, preferred_element_type=jnp.float32)
        grad_gu[2 * tile : 2 * tile + 2] = out.astype(grad_gu.dtype).reshape((2,) + grad_gu.shape[1:])

    def to_twin(number):
        pairs = ((grad_gu.at[:, pl.ds(2 * (1 - core), 2)], got_gu), (grad_down.at[1 - core], got_down))
        return remote(*pairs[number], swap_send.at[3 + number], swap_recv.at[3 + number], twin)

    def to_far():
        return remote(half_gu.at[:, 1 - far], far_gu, swap_send.at[5], swap_recv.at[5], across_y)

    def exchange():
        to_twin(0).start()
        to_twin(1).start()

    def exchange_far():
        to_twin(0).wait()
        to_twin(1).wait()
        mine = grad_gu[:, pl.ds(2 * core, 2)].astype(jnp.float32)
        half_gu[...] = (mine + got_gu[...].astype(jnp.float32)).astype(half_gu.dtype)
        to_far().start()
        mine = grad_down[core].astype(jnp.float32)
        half_down[...] = (mine + got_down[...].astype(jnp.float32)).astype(half_down.dtype)

    def scatter(item, source):
        chain, ref = chains[item], source.at[item]
        steps = {
            "sf": functools.partial(chain.scatter_start, ref, False),
            "sn": functools.partial(chain.scatter_start, ref, True),
            "h": functools.partial(chain.scatter_hand, ref),
            "se": functools.partial(chain.scatter_end, ref, result.at[item]),
        }
        for number in range(3):
            steps[f"b{number}"] = functools.partial(chain.scatter_over, ref, number)
            steps[f"a{number}"] = functools.partial(chain.scatter_along, ref, number)
        return steps

    def gather(item, phase, target):
        chain, mine, ref = chains[item], own.at[phase * items + item], target.at[item]
        steps = {
            "gs": functools.partial(chain.gather_start, mine, ref),
            "t": functools.partial(chain.gather_turn, mine, ref),
            "ge": functools.partial(chain.gather_end, mine, ref),
        }
        for step in range(1, DEPTH):
            steps[f"g{step}"] = functools.partial(chain.gather_step, ref, step)
        return steps

    def working(item, work):
        return {"wf": functools.partial(work, item, False), "wn": functools.partial(work, item, True)}

    def run(order, *tables):
        steps = {}
        for table in tables:
            steps.update(table)
        for name in order:
            if name in steps:
                steps[name]()

    weights = {f"d{half}": functools.partial(down_part, half) for half in range(2)}
    weights.update({f"u{tile}": functools.partial(gu_columns, tile) for tile in range(4)})
    weights.update({"c": exchange, "y": exchange_far})
    run(ORDER, scatter(0, parts))
    middle_of(0)
    quarter_on(0).wait()
    quarter_on(2).start()
    run(ORDER, gather(0, 0, ffn_in), scatter(1, parts))
    middle_of(1)
    quarter_on(1).wait()
    quarter_on(2).wait()
    run(ORDER, gather(1, 0, ffn_in), scatter(0, partial), working(0, forward))
    outcome(0)
    run(ORDER, gather(0, 1, ffn_low), scatter(1, partial), working(1, forward))
    outcome(1)
    run(ORDER, gather(1, 1, ffn_low), scatter(0, partial), working(0, backward))
    back_to_attention(0)
    run(LAST_ORDER, gather(0, 2, projected_low), scatter(1, partial), working(1, backward), weights)
    back_to_attention(1)
    run(END_ORDER, gather(1, 2, projected_low), weights)
    to_far().wait()
    mine = half_gu[:, pl.ds(far, 1)][:, 0].astype(jnp.float32)
    sum_gu[...] = (mine + far_gu[...].astype(jnp.float32)).astype(sum_gu.dtype)


def feed_forward(parts, states, cotangent, live, modulation, gains, gu_part, w_down, ident):
    items, ranks, rows, width = parts.shape
    tokens, hidden = items * ranks * rows, w_down.shape[0]
    low, single = parts.dtype, jnp.float32
    first = split_chain(width)
    wave = pltpu.SemaphoreType.DMA

    def slots(size, count=(DEPTH,)):
        return pltpu.VMEM(count + (rows, size), low)

    flow = [slots(first)] * 5 + [slots(width - first)] * 8 + [slots(width - first, ())] * 2
    waves = [wave((DEPTH + 1,))] * 2 + [wave((3, 2, DEPTH))] * 2
    waves += [wave((DEPTH + 1,))] * 2 + [wave((3, 2, DEPTH)), wave((3, DEPTH))]
    quarters, pair = ((ranks, count) + gu_part.shape[1:] for count in (4, 2))
    local = jax.ShapeDtypeStruct(states.shape, single)
    everywhere = jax.ShapeDtypeStruct(parts.shape, low)
    return pl.pallas_call(
        feed_forward_kernel,
        out_shape=[
            local,
            local,
            everywhere,
            jax.ShapeDtypeStruct((tokens, hidden), low),
            everywhere,
            jax.ShapeDtypeStruct((tokens, 2 * hidden), low),
            everywhere,
            jax.ShapeDtypeStruct((16, width), single),
            jax.ShapeDtypeStruct(gu_part.shape, low),
            jax.ShapeDtypeStruct((hidden // 2, width), low),
        ],
        in_specs=[NEAR] * 8,
        out_specs=[NEAR] * 10,
        scratch_shapes=[
            pltpu.VMEM((tokens, 2 * hidden), single),
            pltpu.VMEM(states.shape, single),
            pltpu.VMEM(states.shape, single),
            pltpu.VMEM(states.shape, single),
            pltpu.VMEM((3 * items, rows, width), low),
            pltpu.VMEM(parts.shape, low),
            pltpu.VMEM(quarters, low),
            pltpu.VMEM(quarters, low),
            pltpu.VMEM((2, hidden // 2, width), low),
            pltpu.VMEM(pair, low),
            pltpu.VMEM((hidden // 2, width), low),
            pltpu.VMEM(pair, low),
            pltpu.VMEM(gu_part.shape, low),
            wave((6,)),
            wave((6,)),
        ]
        + flow * items
        + waves * items,
        compiler_params=pltpu.CompilerParams(
            collective_id=ident, has_side_effects=True, vmem_limit_bytes=58 << 20
        ),
    )(parts, states, cotangent, live, modulation, gains, gu_part, w_down)


def lay_flat(vectors):
    flat = jnp.concatenate([vector.reshape(-1) for vector in vectors])
    rows = -(-flat.size // 1024) * 8
    return jnp.pad(flat, (0, rows * 128 - flat.size)).reshape(rows, 128)


def take_apart(total, vectors):
    flat, parts, start = total.reshape(-1), [], 0
    for vector in vectors:
        parts.append(flat[start : start + vector.size].reshape(vector.shape))
        start += vector.size
    return parts


def sum_vectors(vectors, ident):
    return take_apart(sum_rows(lay_flat(vectors), ident), vectors)


CORES = [(0, 1), (1, 0), (2, 3), (3, 2)]
FARS = [(0, 2), (1, 3), (2, 0), (3, 1)]


def swap(array, pairs):
    return lax.ppermute(array, "items", pairs)


def give_keep(grad, index, axis):
    keep = lax.dynamic_index_in_dim(grad, index, axis, keepdims=False)
    give = lax.dynamic_index_in_dim(grad, 1 - index, axis, keepdims=False)
    return give, keep


def add_low(one, other):
    return (one.astype(jnp.float32) + other.astype(jnp.float32)).astype(jnp.bfloat16)


def head_parallel_plan(
    hidden_in,
    cotangent,
    text_states,
    time_embed,
    live_rows,
    frame_rows,
    text_len,
    w_qkv,
    w_out,
    w_text,
    w_gu,
    w_down,
    w_ada,
    gains,
    cross_gate,
    ada_bias,
    text_gain,
):
    single = jnp.float32
    narrow = jnp.bfloat16
    ranks = lax.axis_size("rows")
    place = lax.axis_index("rows")
    width = hidden_in.shape[2]
    heads = cross_gate.shape[0]
    head_size = width // heads
    score_scale = head_size ** (-0.5)
    items = time_embed.shape[1]
    slots = hidden_in.shape[1] // items
    row_slots = slots // COLS
    seq_len = ranks * slots
    text_local = text_states.shape[2]
    text_all = text_local * ranks
    text_width = text_states.shape[3]
    span = width // ranks
    heads_here = heads // ranks
    tokens = items * seq_len

    def dot(left, right):
        return jnp.dot(left, right, preferred_element_type=single)

    def dot_back(left, weight):
        return jnp.einsum("tn,kn->tk", left, weight, preferred_element_type=single)

    def weight_grad(left, right):
        return jnp.einsum("tk,tn->kn", left, right, preferred_element_type=single)

    time_silu = jax.nn.silu(time_embed[0].astype(single)).astype(narrow)
    ada_depth = w_ada.shape[0]
    time_here = lax.dynamic_slice_in_dim(time_silu, place * ada_depth, ada_depth, 1)

    def spread(part, whole):
        return lax.dynamic_update_slice_in_dim(
            jnp.zeros((whole,), single), part.reshape(-1), place * part.size, 0
        )

    group = lax.axis_index("items")
    core, far = lax.rem(group, 2), group // 2
    counts_here = live_rows[0]
    text_float = text_states[0].astype(single).reshape(items * text_local, text_width)
    text_inverse = norm_parts(text_float)[1]
    small = [
        dot(time_here, w_ada),
        spread(counts_here.astype(single), ranks * items),
        spread(text_inverse, ranks * items * text_local),
    ]
    total, text_in = first_transfers(lay_flat(small), text_states[0], 0)
    _, counts, text_inverse = take_apart(total, small)
    counts = counts.astype(jnp.int32)
    text_inverse = text_inverse.reshape(-1, 1)

    slot_in_row = jnp.arange(slots) // COLS
    live_mask = (slot_in_row[None, :] < counts_here[0][:, None]).astype(single)[..., None]
    def gain_here(index):
        return lax.dynamic_slice_in_dim(gains[index], place * span, span, 0)

    states = hidden_in[0].reshape(items, slots, width)
    hidden = w_down.shape[0]
    gu_rows = pack_quarter(w_gu, (2 * core + far).reshape(1), 2, ranks)

    features = text_width // ranks
    features = text_width // ranks
    text_in = text_in.reshape(items * text_all, features)
    text_unit = text_in.astype(single) * text_inverse
    gain_text = lax.dynamic_slice_in_dim(text_gain, place * features, features, 0)
    text_norm = (text_unit * gain_text).astype(narrow)

    text_parts = pack_blocks(dot(text_norm, w_text).astype(narrow), 2, ranks, narrow)
    attn_in, qkv_here, text_proj, qkv_proj, totals, modulation = open_attention(
        total, states, gains, ada_bias.reshape(-1, 128), text_parts, w_qkv, 1
    )
    text_proj = text_proj.reshape(ranks, items, text_local, 2 * span)
    qkv_here = qkv_here.reshape(width, -1)
    gu_rows, totals = lax.optimization_barrier((gu_rows, totals))
    gu_part = lax.all_to_all(gu_rows, "rows", 0, 0, tiled=True)
    gains_both = jnp.concatenate([gain_here(1), gain_here(2)])[None]
    gain_t = gain_here(6)[None]
    gate_here = jnp.tanh(lax.dynamic_slice_in_dim(cross_gate, place * heads_here, heads_here, 0))
    gate_lanes = jnp.repeat(gate_here, head_size)[None]
    out_parts, combined, qkv_bf, text_kv, tables = attend(
        qkv_proj,
        totals,
        text_proj,
        gains_both,
        gain_t,
        gate_lanes,
        w_out,
        counts,
        frame_rows[0],
        text_len[0],
        head_size,
    )
    live_lanes = jnp.broadcast_to(live_mask, (items, slots, 128))
    output, grad_middle, _, _, _, _, projected_low, vectors, sum_gu, half_down = feed_forward(
        out_parts.reshape(items, ranks, slots, width),
        states,
        cotangent[0].reshape(items, slots, width),
        live_lanes,
        modulation,
        gains,
        gu_part,
        w_down,
        4,
    )
    projected_low = projected_low.reshape(tokens, width)
    rows_gu = lax.all_to_all(sum_gu, "rows", 0, 0, tiled=True)
    got_down = swap(half_down, FARS)
    grad_out = weight_grad(combined, projected_low).astype(narrow).reshape(2, -1, width)
    give_out, keep_out = give_keep(grad_out, core, 0)

    scaled, grad_value, text_scaled, text_value, sums, gain_sums, gate_sums = attend_back(
        projected_low,
        w_out,
        qkv_bf,
        text_kv,
        tables,
        qkv_proj,
        totals,
        text_proj,
        gains_both,
        gain_t,
        gate_lanes,
        counts,
        text_len[0],
        head_size,
        (give_out,),
    )
    half_out = add_low(keep_out, swap(give_out, CORES))
    sum_down = add_low(half_down, got_down)
    attn_parts, text_low, half_qkv, got_gu = project_back(
        qkv_proj,
        totals,
        sum_rows(sums, 10, after=(sum_down, half_out, rows_gu)),
        scaled,
        grad_value,
        text_proj,
        text_scaled,
        text_value,
        attn_in,
        qkv_here,
        rows_gu,
        14,
    )

    text_low = text_low.reshape(items * text_all, 2 * span)
    all_low, got_out, got_qkv, got_down = gather_rows(
        text_low,
        12,
        0,
        swaps=((half_out, "far"), (half_qkv, "far"), (sum_down, "core")),
    )
    pair_gu = join_blocks(rows_gu, got_gu, far_bit)
    all_low = unpack_blocks(all_low, 2, narrow)
    grad_text = weight_grad(text_norm, all_low).astype(narrow).reshape(2, -1, 2 * width)
    give_text, keep_text = give_keep(grad_text, core, 0)
    half_text = add_low(keep_text, swap(give_text, CORES))
    sum_out, sum_qkv = add_low(half_out, got_out), add_low(half_qkv, got_qkv)
    grad_attn_in, got_text, got_out, got_gu = scatter_rows(
        attn_parts,
        11,
        1,
        swaps=((half_text, "far"), (sum_out, "core"), (pair_gu, "core")),
    )
    sum_qkv, grad_attn_in = lax.optimization_barrier((sum_qkv, grad_attn_in))
    rows_qkv = lax.all_to_all(sum_qkv, "rows", 0, 0, tiled=True)
    sum_text = add_low(half_text, got_text)
    grad_text_gain = jnp.sum(dot_back(all_low, w_text) * text_unit, axis=0)
    grad_x, small = finish(
        grad_attn_in,
        states,
        grad_middle,
        modulation,
        gains,
        vectors,
        gain_sums,
        gate_sums,
        grad_text_gain[None],
        time_here.astype(single),
    )
    reduced, got_text = final_sums(small, SUM_DEPTH, 13, swaps=((sum_text, "core"),))
    flat = reduced[:, :SUM_DEPTH].reshape(-1)
    total_gains = flat[: gains.size].reshape(gains.shape)
    total_text_gain = flat[gains.size : gains.size + text_width]
    total_gate = jnp.sum(flat[-width:].reshape(heads, head_size), axis=1)
    total_gate = total_gate * (1.0 - jnp.tanh(cross_gate) ** 2)
    groups = lax.axis_size("items")
    kept = reduced[:, SUM_DEPTH:].reshape(ranks, groups, -1, 128)
    all_modulation = jnp.swapaxes(kept[:, :, : width // 128], 0, 1).reshape(groups * items, 4 * width)
    all_time = lax.dynamic_index_in_dim(kept[:, :, width // 128 :], place, 0, keepdims=False)
    all_time = all_time.reshape(groups * items, ada_depth)
    final_ada = jnp.einsum(
        "tk,tn->kn",
        all_time,
        all_modulation,
        precision=lax.Precision.HIGHEST,
        preferred_element_type=single,
    )
    total_bias = jnp.sum(all_modulation, axis=0)
    def whole_rows(half, got):
        return join_rows(half, got, core_bit, single).reshape(-1, half.shape[-1])

    sums = [
        unpack_halves(rows_qkv, swap(rows_qkv, CORES), 3),
        whole_rows(sum_out, got_out),
        whole_rows(sum_text, got_text),
        unpack_halves(pair_gu, got_gu, 2),
        whole_rows(sum_down, got_down),
    ]
    return (
        output.reshape(1, items * slots, width),
        grad_x.reshape(1, items * slots, width),
        *sums,
        final_ada,
        total_gains,
        total_gate,
        total_bias,
        total_text_gain,
    )


def per_device(*arrays):
    heads = arrays[14].shape[0]
    plan = gathered_plan if heads % lax.axis_size("rows") else head_parallel_plan
    return plan(*arrays)


def solution(mesh):
    in_specs = (
        P("items", "rows", None),
        P("items", "rows", None),
        P("items", None, "rows", None),
        P("items", None, None),
        P("items", "rows", None),
        P("items", None),
        P("items", None),
        P("rows", None),
        P("rows", None),
        P("rows", None),
        P("rows", None),
        P("rows", None),
        P("rows", None),
        P(),
        P(),
        P(),
        P(),
    )
    out_specs = (
        P("items", "rows", None),
        P("items", "rows", None),
        P("rows", None),
        P("rows", None),
        P("rows", None),
        P("rows", None),
        P("rows", None),
        P("rows", None),
        P(),
        P(),
        P(),
        P(),
    )
    return jax.shard_map(
        per_device, mesh=mesh, in_specs=in_specs, out_specs=out_specs, check_vma=False
    )
```
